32 devices in a mesh: fsdp: 16 (over z, y, core), rep: 2 (over x).
Axes of the slice: x: 2, y: 2, z: 4, core: 2. Of those that a mesh axis runs over, the one named last changes fastest.
Arguments:
- class_ids: int32 [32], P(('fsdp', 'rep')), may hold values from 0 to 999
- null_mask: int32 [32], P(('fsdp', 'rep')), may hold values 0 or 1
- code_ids: int32 [32, 256], P(('fsdp', 'rep')), may hold values from 0 to 16383
- lengths: int32 [32], P(('fsdp', 'rep')), may hold values from 0 to 256, as said below
- code_table: float32 [16384, 768], P('fsdp'), may hold values from -6 to 6
- code_first: float32 [16384, 768], P('fsdp'), may hold values from -1.1920929e-07 to 1.1920929e-07
- code_second: float32 [16384, 768], P('fsdp'), may hold values from 4.1392115e-16 to 1.6556846e-15
- class_table: float32 [1001, 768], P(None, 'fsdp'), may hold values from -6 to 6
- class_first: float32 [1001, 768], P(None, 'fsdp'), may hold values from -5.2154064e-08 to 5.2154064e-08
- class_second: float32 [1001, 768], P(None, 'fsdp'), may hold values from 7.9393464e-17 to 3.1757385e-16
- qkv_weight: float32 [2304, 768], P('fsdp'), may hold values from -0.21875 to 0.21875
- qkv_first: float32 [2304, 768], P('fsdp'), may hold values from -1.9073486e-06 to 1.9073486e-06
- qkv_second: float32 [2304, 768], P('fsdp'), may hold values from 1.2115784e-13 to 4.846314e-13
- out_weight: float32 [768, 768], P('fsdp'), may hold values from -0.625 to 0.625
- out_first: float32 [768, 768], P('fsdp'), may hold values from -1.9073486e-06 to 1.9073486e-06
- out_second: float32 [768, 768], P('fsdp'), may hold values from 1.2115784e-13 to 4.846314e-13
- gate_up: float32 [4096, 768], P('fsdp'), may hold values from -0.21875 to 0.21875
- gate_up_first: float32 [4096, 768], P('fsdp'), may hold values from -1.9073486e-06 to 1.9073486e-06
- gate_up_second: float32 [4096, 768], P('fsdp'), may hold values from 1.2115784e-13 to 4.846314e-13
- down_weight: float32 [768, 2048], P('fsdp'), may hold values from -0.125 to 0.125
- down_first: float32 [768, 2048], P('fsdp'), may hold values from -1.9073486e-06 to 1.9073486e-06
- down_second: float32 [768, 2048], P('fsdp'), may hold values from 1.2115784e-13 to 4.846314e-13
- head_weight: float32 [16384, 768], P('fsdp'), may hold values from -0.21875 to 0.21875
- head_first: float32 [16384, 768], P('fsdp'), may hold values from -1.9073486e-06 to 1.9073486e-06
- head_second: float32 [16384, 768], P('fsdp'), may hold values from 1.2115784e-13 to 4.846314e-13
- norm_gains: float32 [3, 768], P(None, 'fsdp'), may hold values from 0.5 to 1.5
- gains_first: float32 [3, 768], P(None, 'fsdp'), may hold values from -1.9073486e-06 to 1.9073486e-06
- gains_second: float32 [3, 768], P(None, 'fsdp'), may hold values from 1.2115784e-13 to 4.846314e-13
Outputs:
- loss_sum: float32 [], replicated
- token_count: float32 [], replicated
- grad_norm: float32 [], replicated
- new_code_table: float32 [16384, 768], P('fsdp')
- new_code_first: float32 [16384, 768], P('fsdp')
- new_code_second: float32 [16384, 768], P('fsdp')
- new_class_table: float32 [1001, 768], P(None, 'fsdp')
- new_class_first: float32 [1001, 768], P(None, 'fsdp')
- new_class_second: float32 [1001, 768], P(None, 'fsdp')
- new_qkv_weight: float32 [2304, 768], P('fsdp')
- new_qkv_first: float32 [2304, 768], P('fsdp')
- new_qkv_second: float32 [2304, 768], P('fsdp')
- new_out_weight: float32 [768, 768], P('fsdp')
- new_out_first: float32 [768, 768], P('fsdp')
- new_out_second: float32 [768, 768], P('fsdp')
- new_gate_up: float32 [4096, 768], P('fsdp')
- new_gate_up_first: float32 [4096, 768], P('fsdp')
- new_gate_up_second: float32 [4096, 768], P('fsdp')
- new_down_weight: float32 [768, 2048], P('fsdp')
- new_down_first: float32 [768, 2048], P('fsdp')
- new_down_second: float32 [768, 2048], P('fsdp')
- new_head_weight: float32 [16384, 768], P('fsdp')
- new_head_first: float32 [16384, 768], P('fsdp')
- new_head_second: float32 [16384, 768], P('fsdp')
- new_norm_gains: float32 [3, 768], P(None, 'fsdp')
- new_gains_first: float32 [3, 768], P(None, 'fsdp')
- new_gains_second: float32 [3, 768], P(None, 'fsdp')
The draws below stay inside these ranges and needn't reach their ends.
Inputs may be any that keep to these rules, and one draw needn't show every extreme that they name: `lengths`: image slot 0 is empty (0) and the last image slot counts all 256 positions; a counted prefix of an image slot is 0 or at least 42.
All inputs are finite; a program needn't handle non-finite values. No bound on the sum of `null_mask` on one device may be relied on, other than what follows from the above.
Results may differ from the reference program's by a relative error of at most 0.018.
Values may be sent and summed in bfloat16 or wider, within the bound.
A program may use at most 384 MiB of HBM per device.

```python
import math
import jax
import jax.numpy as jnp
from jax import lax

D = 768
HEADS = 12
HEAD_DIM = 64
FF = 2048
V = 16384
CLASSES = 1001
SEQ = 256
IMG_DEV = 1
CLIP_INV = 500
STEP = 10
IMAGES = 32
NPARAM = 33014784
N_FSDP = 16
N_REP = 2


def draw_lengths(key, part):
    key = jax.random.fold_in(key, 7)
    index = jnp.arange(IMAGES)
    column = index // (IMG_DEV * N_REP)
    upper = SEQ // 3 + (SEQ - SEQ // 3) * column // max(N_FSDP - 1, 1)
    first_key, second_key = jax.random.split(key)
    raw = jax.random.randint(first_key, (IMAGES,), 0, 1 << 20)
    drawn = raw % (upper - upper // 2 + 1) + upper // 2
    empty = jax.random.randint(second_key, (IMAGES,), 0, 8) == 0
    result = jnp.where(empty, 0, drawn)
    result = jnp.where(index == 0, 0, result)
    result = jnp.where(index == IMAGES - 1, SEQ, result)
    return result.astype(jnp.int32)


def plant(entries, key, low, top_value):
    spot = [jax.random.randint(jax.random.fold_in(key, axis), (), 0, length) for axis, length in enumerate(entries.shape)]
    widest = entries.shape.index(max(entries.shape))
    neighbour = spot[:widest] + [(spot[widest] + 1) % entries.shape[widest]] + spot[widest + 1:]
    return entries.at[tuple(spot)].set(low).at[tuple(neighbour)].set(top_value)


def steps_of(key, shape, cuts, least, high):
    factor_of, own = 1.0, jax.random.fold_in(key, 6)
    for axis_at, blocks in cuts:
        heights = jnp.exp(jax.random.uniform(jax.random.fold_in(own, axis_at), (blocks,), jnp.float32, least / len(cuts), high / len(cuts)))
        factor_of = factor_of * jnp.repeat(heights, shape[axis_at] // blocks).reshape([-1 if axis == axis_at else 1 for axis in range(len(shape))])
    return factor_of


def normal_values(key, extent, spread, reach, pieces=(), held_as=jnp.bfloat16):
    entries = jax.random.normal(key, extent, jnp.float32) * spread
    if len(pieces) > 0:
        entries = steps_of(key, extent, pieces, -0.22, 0.18) * entries
    return jnp.clip(entries, min=-reach, max=reach).astype(held_as)


def setup_inputs(seed: int = 0) -> dict:
    seeds = jax.random.split(jax.random.key(seed), 29)
    return {
        "class_ids": plant(jax.random.randint(seeds[0], (IMAGES,), 0, CLASSES - 1), jax.random.fold_in(seeds[0], 1), 0, (CLASSES - 1) - 1).astype(jnp.int32),
        "null_mask": plant((jax.random.randint(seeds[1], (IMAGES,), 0, 10) < 1).astype(jnp.int32), jax.random.fold_in(seeds[1], 1), 0, 1),
        "code_ids": plant(jax.random.randint(seeds[2], (IMAGES, SEQ), 0, V), jax.random.fold_in(seeds[2], 1), 0, V - 1).astype(jnp.int32),
        "lengths": draw_lengths(jax.random.fold_in(seeds[28], 71), 0),
        "code_table": normal_values(seeds[4], (V, D), 1.0, 6.0, ((0, 16),), jnp.float32),
        "code_first": normal_values(seeds[5], (V, D), ((CLIP_INV * CLIP_INV * D * D * V) ** -0.5), 1.1920928955078125e-07, ((0, 16),), jnp.float32),
        "code_second": jnp.clip(jnp.exp(math.log(1.6556846082070218e-15) - 1.3862944 * jax.random.uniform(seeds[6], (V, D), jnp.float32) ** steps_of(seeds[6], (V, D), ((0, 16),), -0.2, 0.2)), 4.1392115205175545e-16, 1.6556846082070218e-15),
        "class_table": normal_values(seeds[7], (CLASSES, D), 1.0, 6.0, ((1, 16),), jnp.float32),
        "class_first": normal_values(seeds[8], (CLASSES, D), ((CLIP_INV * CLIP_INV * D * D * CLASSES * SEQ // 3) ** -0.5), 5.21540641784668e-08, ((1, 16),), jnp.float32),
        "class_second": jnp.clip(jnp.exp(math.log(3.1757385421909816e-16) - 1.3862944 * jax.random.uniform(seeds[9], (CLASSES, D), jnp.float32) ** steps_of(seeds[9], (CLASSES, D), ((1, 16),), -0.2, 0.2)), 7.939346355477454e-17, 3.1757385421909816e-16),
        "qkv_weight": normal_values(seeds[10], (3 * D, D), D ** -0.5, 0.21875, ((0, 16),), jnp.float32),
        "qkv_first": normal_values(seeds[11], (3 * D, D), ((CLIP_INV * CLIP_INV * NPARAM) ** -0.5), 1.9073486328125e-06, ((0, 16),), jnp.float32),
        "qkv_second": jnp.clip(jnp.exp(math.log(4.84631377997008e-13) - 1.3862944 * jax.random.uniform(seeds[12], (3 * D, D), jnp.float32) ** steps_of(seeds[12], (3 * D, D), ((0, 16),), -0.2, 0.2)), 1.21157844499252e-13, 4.84631377997008e-13),
        "out_weight": normal_values(seeds[13], (D, D), (D // 8) ** -0.5, 0.625, ((0, 16),), jnp.float32),
        "out_first": normal_values(seeds[14], (D, D), ((CLIP_INV * CLIP_INV * NPARAM) ** -0.5), 1.9073486328125e-06, ((0, 16),), jnp.float32),
        "out_second": jnp.clip(jnp.exp(math.log(4.84631377997008e-13) - 1.3862944 * jax.random.uniform(seeds[15], (D, D), jnp.float32) ** steps_of(seeds[15], (D, D), ((0, 16),), -0.2, 0.2)), 1.21157844499252e-13, 4.84631377997008e-13),
        "gate_up": normal_values(seeds[16], (2 * FF, D), D ** -0.5, 0.21875, ((0, 16),), jnp.float32),
        "gate_up_first": normal_values(seeds[17], (2 * FF, D), ((CLIP_INV * CLIP_INV * NPARAM) ** -0.5), 1.9073486328125e-06, ((0, 16),), jnp.float32),
        "gate_up_second": jnp.clip(jnp.exp(math.log(4.84631377997008e-13) - 1.3862944 * jax.random.uniform(seeds[18], (2 * FF, D), jnp.float32) ** steps_of(seeds[18], (2 * FF, D), ((0, 16),), -0.2, 0.2)), 1.21157844499252e-13, 4.84631377997008e-13),
        "down_weight": normal_values(seeds[19], (D, FF), FF ** -0.5, 0.125, ((0, 16),), jnp.float32),
        "down_first": normal_values(seeds[20], (D, FF), ((CLIP_INV * CLIP_INV * NPARAM) ** -0.5), 1.9073486328125e-06, ((0, 16),), jnp.float32),
        "down_second": jnp.clip(jnp.exp(math.log(4.84631377997008e-13) - 1.3862944 * jax.random.uniform(seeds[21], (D, FF), jnp.float32) ** steps_of(seeds[21], (D, FF), ((0, 16),), -0.2, 0.2)), 1.21157844499252e-13, 4.84631377997008e-13),
        "head_weight": normal_values(seeds[22], (V, D), D ** -0.5, 0.21875, ((0, 16),), jnp.float32),
        "head_first": normal_values(seeds[23], (V, D), ((CLIP_INV * CLIP_INV * NPARAM) ** -0.5), 1.9073486328125e-06, ((0, 16),), jnp.float32),
        "head_second": jnp.clip(jnp.exp(math.log(4.84631377997008e-13) - 1.3862944 * jax.random.uniform(seeds[24], (V, D), jnp.float32) ** steps_of(seeds[24], (V, D), ((0, 16),), -0.2, 0.2)), 1.21157844499252e-13, 4.84631377997008e-13),
        "norm_gains": jnp.clip(1.0 + 0.1 * jax.random.normal(seeds[25], (3, D), jnp.float32), 0.5, 1.5),
        "gains_first": normal_values(seeds[26], (3, D), ((CLIP_INV * CLIP_INV * NPARAM) ** -0.5), 1.9073486328125e-06, ((1, 16),), jnp.float32),
        "gains_second": jnp.clip(jnp.exp(math.log(4.84631377997008e-13) - 1.3862944 * jax.random.uniform(seeds[27], (3, D), jnp.float32) ** steps_of(seeds[27], (3, D), ((1, 16),), -0.2, 0.2)), 1.21157844499252e-13, 4.84631377997008e-13),
    }


HIGH = lax.Precision.HIGHEST
NORM_EPS = 1e-05
BETA_ONE = 0.5
BETA_TWO = 0.5
ADAM_EPS = 1e-08

@jax.custom_vjp
def low(v):
    return lax.optimization_barrier(v.astype(jnp.bfloat16)).astype(jnp.float32)

@jax.custom_vjp
def low_back(v):
    return v

def low_keep(v):
    return (low(v), None)

def low_pass(kept, grad):
    return (grad,)

def back_keep(v):
    return (v, None)

def back_low(kept, grad):
    return (low(grad),)
low.defvjp(low_keep, low_pass)
low_back.defvjp(back_keep, back_low)

def rotary_tables(length, width):
    half = width // 2
    freq = 10000.0 ** (-jnp.arange(half, dtype=jnp.float32) * 2.0 / width)
    angles = jnp.arange(length, dtype=jnp.float32)[:, None] * freq[None, :]
    cosine = jnp.concatenate([jnp.cos(angles), jnp.cos(angles)], -1)
    sine = jnp.concatenate([jnp.sin(angles), jnp.sin(angles)], -1)
    return (cosine, sine)

def rotate(values, cosine, sine):
    half = values.shape[-1] // 2
    swapped = jnp.concatenate([-values[..., half:], values[..., :half]], -1)
    return values * cosine[:, None, :] + swapped * sine[:, None, :]

def rms_scale(stream, gain):
    return stream * lax.rsqrt(lax.optimization_barrier(jnp.mean(stream * stream, -1, keepdims=True)) + NORM_EPS) * gain

def group_loss(weights, classes, code_ids, lengths):
    code_w, class_w, qkv_w, out_w, gate_w, down_w, head_w, gain_w = weights
    batch, length = code_ids.shape
    stream0 = jnp.concatenate([class_w[classes][:, None, :], code_w[code_ids[:, :-1]]], 1)
    normed1 = low(rms_scale(stream0, gain_w[0]))
    mixed = low_back(jnp.einsum('btd,ed->bte', normed1, qkv_w, precision=HIGH))
    cosine, sine = rotary_tables(length, HEAD_DIM)
    split4 = (batch, length, HEADS, HEAD_DIM)
    queries = low(rotate(mixed[..., :D].reshape(split4), cosine, sine))
    keys_rot = low(rotate(mixed[..., D:2 * D].reshape(split4), cosine, sine))
    values = low(mixed[..., 2 * D:].reshape(split4))
    scores = low_back(jnp.einsum('bqhd,bkhd->bhqk', queries, keys_rot, precision=HIGH) * HEAD_DIM ** (-0.5))
    causal = jnp.arange(length)[:, None] >= jnp.arange(length)[None, :]
    scores = jnp.where(causal, scores, -1e+30)
    probs = low(jax.nn.softmax(scores, -1))
    attended = low(low_back(jnp.einsum('bhqk,bkhd->bqhd', probs, values, precision=HIGH))).reshape(batch, length, D)
    stream1 = stream0 + low_back(jnp.einsum('btd,ed->bte', attended, out_w, precision=HIGH))
    normed2 = low(rms_scale(stream1, gain_w[1]))
    gated = low_back(jnp.einsum('btd,fd->btf', normed2, gate_w, precision=HIGH))
    hidden = low(jax.nn.silu(gated[..., :FF]) * gated[..., FF:])
    stream2 = stream1 + low_back(jnp.einsum('btf,df->btd', hidden, down_w, precision=HIGH))
    normed3 = low(rms_scale(stream2, gain_w[2]))
    logits = low_back(jnp.einsum('btd,vd->btv', normed3, head_w, precision=HIGH))
    top = lax.optimization_barrier(jnp.max(logits, -1, keepdims=True))
    lse = jnp.log(lax.optimization_barrier(jnp.sum(jnp.exp(logits - top), -1))) + top[..., 0]
    picked = jnp.take_along_axis(logits, code_ids[..., None], -1)[..., 0]
    counted = jnp.arange(length)[None, :] < lengths[:, None]
    return jnp.sum(jnp.where(counted, lse - picked, 0.0))

def adam_update(weight, first, second, grad, rate, decay):
    first_new = BETA_ONE * first + (1.0 - BETA_ONE) * grad
    second_new = BETA_TWO * second + (1.0 - BETA_TWO) * grad * grad
    first_hat = first_new / (1.0 - BETA_ONE ** STEP)
    second_hat = second_new / (1.0 - BETA_TWO ** STEP)
    weight_new = weight - rate * (first_hat / (jnp.sqrt(second_hat) + ADAM_EPS) + decay * weight)
    return (weight_new, first_new, second_new)

def reference(class_ids, null_mask, code_ids, lengths, code_table, code_first, code_second, class_table, class_first, class_second, qkv_weight, qkv_first, qkv_second, out_weight, out_first, out_second, gate_up, gate_up_first, gate_up_second, down_weight, down_first, down_second, head_weight, head_first, head_second, norm_gains, gains_first, gains_second):
    masters = (code_table, class_table, qkv_weight, out_weight, gate_up, down_weight, head_weight, norm_gains)
    firsts = (code_first, class_first, qkv_first, out_first, gate_up_first, down_first, head_first, gains_first)
    seconds = (code_second, class_second, qkv_second, out_second, gate_up_second, down_second, head_second, gains_second)
    rates = (0.5, 0.5, 0.05, 0.05, 0.05, 0.05, 0.05, 0.5)
    decays = (0.1, 0.1, 0.1, 0.1, 0.1, 0.1, 0.1, 0.0)
    classes = jnp.where(null_mask == 1, CLASSES - 1, class_ids).astype(jnp.int32)
    counted = jnp.arange(SEQ)[None, :] < lengths[:, None]
    token_count = jnp.sum(counted.astype(jnp.float32))
    group = 16 if IMAGES % 16 == 0 else 1
    blocks = (classes.reshape(-1, group), code_ids.reshape(-1, group, SEQ), lengths.reshape(-1, group))

    def total(weights):
        lowered = tuple((low(w) for w in weights))

        def step_fn(carry, block):
            return (carry + jax.checkpoint(group_loss)(lowered, block[0], block[1], block[2]), None)
        summed, _ = lax.scan(step_fn, jnp.zeros((), jnp.float32), blocks)
        return summed
    loss_sum, pull = jax.vjp(total, masters)
    grads = pull(1.0 / token_count)[0]
    squares = jnp.zeros((), jnp.float32)
    for grad in grads:
        squares = squares + jnp.sum(grad * grad)
    grad_norm = jnp.sqrt(squares)
    factor = jnp.minimum(1.0, 1.0 / CLIP_INV / (grad_norm + 1e-06))
    results = [loss_sum, token_count, grad_norm]
    for index in range(8):
        results.extend(adam_update(masters[index], firsts[index], seconds[index], grads[index] * factor, rates[index], decays[index]))
    return tuple(results)
```

```python
import jax
import jax.numpy as jnp
from jax import lax
from jax.sharding import PartitionSpec as P

HEAD_DIM = 64
CLIP_INV = 500
STEP = 10
NORM_EPS = 1e-05
BETA_ONE = 0.5
BETA_TWO = 0.5
ADAM_EPS = 1e-08
BF = jnp.bfloat16
F32 = jnp.float32


def rotary_tables(length, width):
    half = width // 2
    freq = 10000.0 ** (-jnp.arange(half, dtype=F32) * 2.0 / width)
    angles = jnp.arange(length, dtype=F32)[:, None] * freq[None, :]
    cosine = jnp.concatenate([jnp.cos(angles), jnp.cos(angles)], -1)
    sine = jnp.concatenate([jnp.sin(angles), jnp.sin(angles)], -1)
    return (cosine, sine)


def rotate(values, cosine, sine):
    half = values.shape[-1] // 2
    swapped = jnp.concatenate([-values[..., half:], values[..., :half]], -1)
    return values * cosine[:, None, :] + swapped * sine[:, None, :]


def rotate_back(grads, cosine, sine):
    half = grads.shape[-1] // 2
    scaled = grads * sine[:, None, :]
    return grads * cosine[:, None, :] + jnp.concatenate(
        [scaled[..., half:], -scaled[..., :half]], -1
    )


def norm_forward(stream, gain):
    inverse = lax.rsqrt(jnp.mean(stream * stream, -1, keepdims=True) + NORM_EPS)
    return (stream * inverse * gain, inverse)


def norm_backward(stream, inverse, gain, grad_out):
    weighted = grad_out * gain
    inner = jnp.mean(weighted * stream, -1, keepdims=True)
    grad_in = inverse * weighted - stream * inverse * inverse * inverse * inner
    grad_gain = jnp.sum(grad_out * stream * inverse, axis=(0, 1))
    return (grad_in, grad_gain)


def attention_scores(queries, keys_rot):
    length = queries.shape[1]
    scores = jnp.einsum(
        "bqhd,bkhd->bhqk", queries, keys_rot, preferred_element_type=F32
    ) * HEAD_DIM ** (-0.5)
    causal = jnp.arange(length)[:, None] >= jnp.arange(length)[None, :]
    return jnp.where(causal, scores, -1e30)


def column_blocks(width, total):
    return [(at, min(width, total - at)) for at in range(0, total, width)]


def pack_rows(qkv, gate, out, down):
    width = qkv.shape[-1]
    parts = [qkv, gate, out]
    for at, size in column_blocks(width, down.shape[-1]):
        block = down[..., at : at + size]
        if size < width:
            pad = [(0, 0)] * (block.ndim - 1) + [(0, width - size)]
            block = jnp.pad(block, pad)
        parts.append(block)
    return jnp.concatenate(parts, -2)


def unpack_rows(packed, rows, hidden_width):
    width = packed.shape[-1]
    at, parts = 0, []
    for count in rows[:3]:
        parts.append(packed[..., at : at + count, :])
        at += count
    blocks = []
    for _, size in column_blocks(width, hidden_width):
        blocks.append(packed[..., at : at + rows[3], :size])
        at += rows[3]
    parts.append(jnp.concatenate(blocks, -1))
    return parts


def adam_update(weight, first, second, grad, rate, decay):
    first_new = BETA_ONE * first + (1.0 - BETA_ONE) * grad
    second_new = BETA_TWO * second + (1.0 - BETA_TWO) * grad * grad
    first_hat = first_new / (1.0 - BETA_ONE**STEP)
    second_hat = second_new / (1.0 - BETA_TWO**STEP)
    weight_new = weight - rate * (first_hat / (jnp.sqrt(second_hat) + ADAM_EPS) + decay * weight)
    return (weight_new, first_new, second_new)


def dot(subscripts, left, right):
    return jnp.einsum(subscripts, left, right, preferred_element_type=F32)


def local(*args):
    class_ids, null_mask, code_ids, lengths = args[:4]
    masters, firsts, seconds = args[4::3], args[5::3], args[6::3]
    code_table, class_table, qkv_weight, out_weight, gate_up, down_weight, head_weight, gains = (
        masters
    )
    rates = (0.5, 0.5, 0.05, 0.05, 0.05, 0.05, 0.05, 0.5)
    decays = (0.1, 0.1, 0.1, 0.1, 0.1, 0.1, 0.1, 0.0)
    n = lax.axis_size("fsdp")
    me = lax.axis_index("fsdp")
    batch, length = code_ids.shape
    width = qkv_weight.shape[1]
    hidden_width = down_weight.shape[1]
    table_rows, own_width = class_table.shape
    own_rows = code_table.shape[0]
    heads = width // HEAD_DIM
    rows = (qkv_weight.shape[0], gate_up.shape[0], out_weight.shape[0], down_weight.shape[0])

    classes = jnp.where(null_mask == 1, table_rows - 1, class_ids)
    facts = jnp.concatenate([code_ids, classes[:, None], lengths[:, None]], 1)
    facts = lax.all_gather(facts, "fsdp", axis=0, tiled=True)
    all_codes, all_classes, all_lengths = facts[:, :length], facts[:, length], facts[:, length + 1]
    images = n * batch
    tokens = images * length
    all_counted = (jnp.arange(length)[None, :] < all_lengths[:, None]).astype(F32)
    token_count = lax.psum(jnp.sum(all_counted), "rep")
    counted = (jnp.arange(length)[None, :] < lengths[:, None]).astype(F32)

    packed = pack_rows(
        qkv_weight.astype(BF), gate_up.astype(BF), out_weight.astype(BF), down_weight.astype(BF)
    )
    packed = lax.all_gather(packed, "fsdp", axis=0)
    parts = unpack_rows(packed, rows, hidden_width)
    qkv_w, gate_w, out_w, down_w = (p.reshape(-1, p.shape[-1]) for p in parts)
    gains32 = lax.all_gather(gains.astype(BF), "fsdp", axis=1, tiled=True).astype(F32)

    own_ids = jnp.arange(own_rows) + me * own_rows
    previous = jnp.concatenate(
        [jnp.full((images, 1), -1, all_codes.dtype), all_codes[:, :-1]], 1
    ).reshape(tokens)
    lookup = (previous[:, None] == own_ids[None, :]).astype(BF)
    rows_found = dot("tv,vd->td", lookup, code_table.astype(BF)).astype(BF)
    rows_found = rows_found.reshape(images, length, width)
    class_found = class_table.astype(BF)[all_classes]
    class_rows = lax.dynamic_update_slice(
        jnp.zeros((images, width), BF), class_found, (0, me * own_width)
    )
    first_spot = (jnp.arange(length) == 0)[None, :, None]
    rows_found = jnp.where(first_spot, class_rows[:, None, :], rows_found)
    stream0 = lax.psum_scatter(rows_found, "fsdp", scatter_dimension=0, tiled=True).astype(F32)

    normed1, inverse1 = norm_forward(stream0, gains32[0])
    normed1 = normed1.astype(BF)
    mixed = dot("btd,ed->bte", normed1, qkv_w)
    cosine, sine = rotary_tables(length, HEAD_DIM)
    split4 = (batch, length, heads, HEAD_DIM)
    queries = rotate(mixed[..., :width].reshape(split4), cosine, sine).astype(BF)
    keys_rot = rotate(mixed[..., width : 2 * width].reshape(split4), cosine, sine).astype(BF)
    values = mixed[..., 2 * width :].reshape(split4).astype(BF)
    scores = attention_scores(queries, keys_rot)
    top = jnp.max(scores, -1, keepdims=True)
    expo = jnp.exp(scores - top)
    probs32 = expo / jnp.sum(expo, -1, keepdims=True)
    probs = probs32.astype(BF)
    attended = dot("bhqk,bkhd->bqhd", probs, values).astype(BF).reshape(batch, length, width)
    stream1 = stream0 + dot("btd,ed->bte", attended, out_w)
    normed2, inverse2 = norm_forward(stream1, gains32[1])
    normed2 = normed2.astype(BF)
    gated = dot("btd,fd->btf", normed2, gate_w)
    gate_part = gated[..., :hidden_width]
    up_part = gated[..., hidden_width:]
    hidden = (jax.nn.silu(gate_part) * up_part).astype(BF)
    stream2 = stream1 + dot("btf,df->btd", hidden, down_w)
    normed3, inverse3 = norm_forward(stream2, gains32[2])
    normed3 = normed3.astype(BF)

    head_b = head_weight.astype(BF)
    normed3_all = lax.all_gather(normed3, "fsdp", axis=0, tiled=True).reshape(tokens, width)
    logits = dot("td,vd->tv", normed3_all, head_b)
    onehot = all_codes.reshape(tokens)[:, None] == own_ids[None, :]
    local_top = jnp.max(logits, -1)
    local_sum = jnp.sum(jnp.exp(logits - local_top[:, None]), -1)
    local_pick = jnp.sum(jnp.where(onehot, logits, 0.0), -1)
    stats = lax.all_gather(jnp.stack([local_top, local_sum, local_pick]), "fsdp", axis=0)
    ltop = jnp.max(stats[:, 0], 0)
    lse = jnp.log(jnp.sum(stats[:, 1] * jnp.exp(stats[:, 0] - ltop[None]), 0)) + ltop
    picked = jnp.sum(stats[:, 2], 0)
    loss_sum = lax.psum(jnp.sum(jnp.where(all_counted.reshape(tokens) > 0, lse - picked, 0.0)), "rep")
    weight_t = all_counted.reshape(tokens) * (1.0 / token_count)
    soft = jnp.exp(logits - lse[:, None])
    grad_logits = ((soft - onehot.astype(F32)) * weight_t[:, None]).astype(BF)
    grad_normed3 = dot("tv,vd->td", grad_logits, head_b).astype(BF).reshape(images, length, width)
    grad_normed3 = lax.psum_scatter(grad_normed3, "fsdp", scatter_dimension=0, tiled=True)
    grad_normed3 = grad_normed3.astype(F32)
    grad_head = dot("tv,td->vd", grad_logits, normed3_all)

    grad_stream2, gain_three = norm_backward(stream2, inverse3, gains32[2], grad_normed3)
    grad_branch = grad_stream2.astype(BF)
    grad_down = dot("btd,btf->df", grad_branch, hidden)
    grad_hidden = dot("btd,df->btf", grad_branch, down_w)
    sigma = jax.nn.sigmoid(gate_part)
    grad_gate = grad_hidden * up_part * sigma * (1.0 + gate_part * (1.0 - sigma))
    grad_up = grad_hidden * gate_part * sigma
    grad_gated = jnp.concatenate([grad_gate, grad_up], -1).astype(BF)
    grad_gate_up = dot("btf,btd->fd", grad_gated, normed2)
    grad_normed2 = dot("btf,fd->btd", grad_gated, gate_w)
    grad_middle, gain_two = norm_backward(stream1, inverse2, gains32[1], grad_normed2)
    grad_stream1 = grad_stream2 + grad_middle
    grad_attn = grad_stream1.astype(BF)
    grad_out = dot("bte,btd->ed", grad_attn, attended)
    grad_attended = dot("bte,ed->btd", grad_attn, out_w).astype(BF).reshape(split4)
    grad_probs = dot("bqhd,bkhd->bhqk", grad_attended, values)
    grad_values = dot("bhqk,bqhd->bkhd", probs, grad_attended)
    grad_scores = probs32 * (grad_probs - jnp.sum(probs32 * grad_probs, -1, keepdims=True))
    grad_scores = grad_scores.astype(BF)
    scale = HEAD_DIM ** (-0.5)
    grad_queries = dot("bhqk,bkhd->bqhd", grad_scores, keys_rot) * scale
    grad_keys = dot("bhqk,bqhd->bkhd", grad_scores, queries) * scale
    grad_mixed = jnp.concatenate(
        [
            rotate_back(grad_queries, cosine, sine).reshape(batch, length, width),
            rotate_back(grad_keys, cosine, sine).reshape(batch, length, width),
            grad_values.reshape(batch, length, width),
        ],
        -1,
    ).astype(BF)
    grad_qkv = dot("bte,btd->ed", grad_mixed, normed1)
    grad_normed1 = dot("bte,ed->btd", grad_mixed, qkv_w)
    grad_first, gain_one = norm_backward(stream0, inverse1, gains32[0], grad_normed1)
    grad_stream0 = grad_stream1 + grad_first

    blocks = [
        g.astype(BF).reshape(n, -1, g.shape[-1]) for g in (grad_qkv, grad_gate_up, grad_out, grad_down)
    ]
    layer_part = lax.psum_scatter(pack_rows(*blocks), "fsdp", scatter_dimension=0, tiled=False)
    rows_all = lax.all_gather(grad_stream0.astype(BF), "fsdp", axis=0, tiled=True)
    grad_codes = dot("tv,td->vd", lookup, rows_all.reshape(tokens, width))
    class_part = lax.dynamic_slice(rows_all[:, 0], (0, me * own_width), (images, own_width))
    class_spot = (all_classes[:, None] == jnp.arange(table_rows)[None, :]).astype(BF)
    grad_classes = dot("iv,id->vd", class_spot, class_part)
    summed = lax.psum(
        (grad_codes.astype(BF), grad_head.astype(BF), layer_part, grad_classes), "rep"
    )
    grad_codes, grad_head, layer_part, grad_classes = (s.astype(F32) for s in summed)
    grad_gains = lax.psum(jnp.stack([gain_one, gain_two, gain_three]), ("fsdp", "rep"))
    grad_gains = lax.dynamic_slice(grad_gains, (0, me * own_width), (3, own_width))
    grad_qkv, grad_gate_up, grad_out, grad_down = unpack_rows(layer_part, rows, hidden_width)
    reduced = (
        grad_codes, grad_classes, grad_qkv, grad_out, grad_gate_up, grad_down, grad_head, grad_gains
    )
    squares = jnp.zeros((), F32)
    for grad_piece in reduced:
        squares = squares + jnp.sum(grad_piece * grad_piece)
    grad_norm = jnp.sqrt(lax.psum(squares, "fsdp"))
    factor = jnp.minimum(1.0, 1.0 / CLIP_INV / (grad_norm + 1e-06))
    results = [loss_sum, token_count, grad_norm]
    for index in range(8):
        results.extend(
            adam_update(
                masters[index],
                firsts[index],
                seconds[index],
                reduced[index] * factor,
                rates[index],
                decays[index],
            )
        )
    return tuple(results)


def solution(mesh):
    split = P(("fsdp", "rep"))
    by_row, by_column = P("fsdp", None), P(None, "fsdp")
    weights = (by_row,) * 3 + (by_column,) * 3 + (by_row,) * 15 + (by_column,) * 3
    return jax.shard_map(
        local,
        mesh=mesh,
        in_specs=(split, split, P(("fsdp", "rep"), None), split) + weights,
        out_specs=(P(), P(), P()) + weights,
        check_vma=False,
    )
```

```python
import functools

import jax
import jax.numpy as jnp
from jax import lax
from jax.experimental import pallas as pl
from jax.experimental.pallas import tpu as pltpu
from jax.sharding import PartitionSpec as P

HEAD_DIM = 64
CLIP_INV = 500
STEP = 10
NORM_EPS = 1e-05
BETA_ONE = 0.5
BETA_TWO = 0.5
ADAM_EPS = 1e-08
BF = jnp.bfloat16
F32 = jnp.float32
MESH = pl.DeviceIdType.MESH


def rotary_tables(length, width):
    half = width // 2
    freq = 10000.0 ** (-jnp.arange(half, dtype=F32) * 2.0 / width)
    angles = jnp.arange(length, dtype=F32)[:, None] * freq[None, :]
    cosine = jnp.concatenate([jnp.cos(angles), jnp.cos(angles)], -1)
    sine = jnp.concatenate([jnp.sin(angles), jnp.sin(angles)], -1)
    return (cosine, sine)


def rotate(values, cosine, sine):
    half = values.shape[-1] // 2
    swapped = jnp.concatenate([-values[..., half:], values[..., :half]], -1)
    return values * cosine[:, None, :] + swapped * sine[:, None, :]


def rotate_back(grads, cosine, sine):
    half = grads.shape[-1] // 2
    scaled = grads * sine[:, None, :]
    return grads * cosine[:, None, :] + jnp.concatenate(
        [scaled[..., half:], -scaled[..., :half]], -1
    )


def norm_forward(stream, gain):
    inverse = lax.rsqrt(jnp.mean(stream * stream, -1, keepdims=True) + NORM_EPS)
    return (stream * inverse * gain, inverse)


def norm_backward(stream, inverse, gain, grad_out):
    weighted = grad_out * gain
    inner = jnp.mean(weighted * stream, -1, keepdims=True)
    grad_in = inverse * weighted - stream * inverse * inverse * inverse * inner
    grad_gain = jnp.sum(grad_out * stream * inverse, axis=(0, 1))
    return (grad_in, grad_gain)


def attention_scores(queries, keys_rot):
    length = queries.shape[1]
    scores = jnp.einsum(
        "bqhd,bkhd->bhqk", queries, keys_rot, preferred_element_type=F32
    ) * HEAD_DIM ** (-0.5)
    causal = jnp.arange(length)[:, None] >= jnp.arange(length)[None, :]
    return jnp.where(causal, scores, -1e30)


def column_blocks(width, total):
    return [(at, min(width, total - at)) for at in range(0, total, width)]


def pack_rows(qkv, gate, out, down):
    width = qkv.shape[-1]
    parts = [qkv, gate, out]
    for at, size in column_blocks(width, down.shape[-1]):
        block = down[..., at : at + size]
        if size < width:
            pad = [(0, 0)] * (block.ndim - 1) + [(0, width - size)]
            block = jnp.pad(block, pad)
        parts.append(block)
    return jnp.concatenate(parts, -2)


def unpack_rows(packed, rows, hidden_width):
    width = packed.shape[-1]
    at, parts = 0, []
    for count in rows[:3]:
        parts.append(packed[..., at : at + count, :])
        at += count
    blocks = []
    for _, size in column_blocks(width, hidden_width):
        blocks.append(packed[..., at : at + rows[3], :size])
        at += rows[3]
    parts.append(jnp.concatenate(blocks, -1))
    return parts


def geometry(n):
    chips = n // 2
    y_size = 1 << ((chips.bit_length() - 1) // 2)
    return chips // y_size, y_size


def where_am_i(z_size, y_size):
    me = lax.axis_index("fsdp")
    return me, me // (2 * y_size), (me // 2) % y_size, me % 2


def front_kernel(z_size, y_size, reps, own_width, parts, facts, code_b, class_b, *refs):
    count = len(parts)
    weights, refs = refs[:count], refs[count:]
    wholes, refs = refs[:count], refs[count:]
    (stream, facts_all, turned, acc, core_out, core_in, y_in, z_in,
     fact_sems, z_sems, y_sems, x_sems, c_sems, own_sems, rc_sems, ry_sems, rz_sems) = refs
    n = z_size * y_size * 2
    me, z, y, core = where_am_i(z_size, y_size)
    x = lax.axis_index("rep")
    length = stream.shape[0]
    width = stream.shape[1]
    own_rows = code_b.shape[0]

    def at(dz, dy, other=0):
        c = 1 - core if other else core
        return (lax.rem(z + dz, z_size) * y_size + lax.rem(y + dy, y_size)) * 2 + c

    barrier = pltpu.get_barrier_semaphore()
    for k in range(1, n):
        pl.semaphore_signal(barrier, inc=1, device_id=(lax.rem(me + k, n), x), device_id_type=MESH)
    for k in range(1, reps):
        pl.semaphore_signal(barrier, inc=1, device_id=(me, lax.rem(x + k, reps)), device_id_type=MESH)
    pl.semaphore_wait(barrier, n - 1 + reps - 1)

    def send(src, dst, sems, index, device):
        copy = pltpu.make_async_remote_copy(
            src_ref=src, dst_ref=dst, send_sem=sems.at[(0,) + index], recv_sem=sems.at[(1,) + index],
            device_id=device, device_id_type=MESH,
        )
        copy.start()

    def arrival(dst, sems, index):
        pltpu.make_async_copy(dst, dst, sems.at[(1,) + index]).wait()

    def departure(src, sems, index):
        pltpu.make_async_copy(src, src, sems.at[(0,) + index]).wait()

    for k in range(1, n):
        send(facts, facts_all.at[me], fact_sems, (k,), (lax.rem(me + k, n), x))
    facts_all[me] = facts[...]

    peers_z = [(dz, at(dz, 0)) for dz in range(1, z_size)]
    peers_y = [(dy, at(0, dy)) for dy in range(1, y_size)]
    spots = [(dz, dy) for dz in range(z_size) for dy in range(y_size)]
    for k, part in enumerate(parts):
        pltpu.make_async_copy(weights[k], wholes[k].at[me], own_sems.at[k]).start()

        @pl.when(x == part)
        def _():
            for dz, peer in peers_z:
                send(weights[k], wholes[k].at[me], z_sems, (k, dz), (peer, x))
            for dy, peer in peers_y:
                send(weights[k], wholes[k].at[me], y_sems, (k, 0, dy), (peer, x))

        send(weights[k], wholes[k].at[me], c_sems, (k, 0, 0), (at(0, 0, 1), x))

    def to_others(k, dz, dy):
        block = wholes[k].at[at(dz, dy)]
        for dx in range(1, reps):
            send(block, block, x_sems, (k, dz, dy, dx), (me, lax.rem(x + dx, reps)))
        send(block, block, c_sems, (k, dz, dy), (at(0, 0, 1), x))

    def after_z(dz):
        for k, part in enumerate(parts):

            @pl.when(x == part)
            def _():
                block = wholes[k].at[at(z_size - dz, 0)]
                arrival(block, z_sems, (k, dz))
                for dy, peer in peers_y:
                    send(block, block, y_sems, (k, z_size - dz, dy), (peer, x))
                to_others(k, z_size - dz, 0)

    def after_y(dz, dy):
        for k, part in enumerate(parts):

            @pl.when(x == part)
            def _():
                arrival(wholes[k].at[at(dz, y_size - dy)], y_sems, (k, dz, dy))
                to_others(k, dz, y_size - dy)

    def after_x(dz, dy):
        for k, part in enumerate(parts):

            @pl.when(x != part)
            def _():
                block = wholes[k].at[at(dz, dy)]
                arrival(block, x_sems, (k, dz, dy, lax.rem(x - part + reps, reps)))
                send(block, block, c_sems, (k, dz, dy), (at(0, 0, 1), x))

    for k in range(1, n):
        arrival(facts_all.at[lax.rem(me - k + n, n)], fact_sems, (k,))
    turned[...] = jnp.transpose(facts_all[...].reshape(n * 8, 128))
    lane = lax.broadcasted_iota(jnp.int32, (128, n * 8), 1)
    class_rows = class_b[...].astype(F32)
    class_iota = lax.broadcasted_iota(jnp.int32, class_rows.shape, 0).astype(F32)
    row_iota = lax.broadcasted_iota(jnp.int32, (length // 2, own_rows), 1) + me * own_rows
    row_iota = row_iota.astype(F32)

    def found(image, out):
        cls = jnp.sum(jnp.where(lane[:1] == image * 8 + 4, turned[:1, :], 0.0), -1, keepdims=True)
        row = jnp.sum(jnp.where(class_iota == cls, class_rows, 0.0), 0, keepdims=True)
        row = jnp.concatenate([row, jnp.zeros((1, width - row.shape[1]), F32)], -1)
        row = pltpu.roll(jnp.broadcast_to(row, (8, width)), me * own_width, 1)
        for half in range(2):
            ids = jnp.sum(jnp.where(lane == image * 8 + half, turned[...], 0.0), -1, keepdims=True)
            spot = jnp.where(row_iota == ids, 1.0, 0.0).astype(BF)
            rows = jnp.dot(spot, code_b[...], preferred_element_type=F32)
            out[pl.ds(half * (length // 2), length // 2)] = rows.astype(BF)
            if half == 0:
                first = lax.broadcasted_iota(jnp.int32, (16, width), 0) == 0
                head = jnp.where(first, jnp.concatenate([row, row], 0), rows[:16])
                out[pl.ds(0, 16)] = head.astype(BF)

    order = [(dz, dy) for dz in range(z_size - 1, -1, -1) for dy in range(y_size - 1, -1, -1)]
    for dz, dy in order:
        slot = dz * y_size + dy
        found(at(dz, dy, 1), core_out.at[slot])
        send(core_out.at[slot], core_in.at[slot], rc_sems, (slot,), (at(0, 0, 1), x))
        found(at(dz, dy), acc.at[slot])
    for dz, dy in order:
        slot = dz * y_size + dy
        arrival(core_in.at[slot], rc_sems, (slot,))
        acc[slot] = (acc[slot].astype(F32) + core_in[slot].astype(F32)).astype(BF)
        if dy:
            send(acc.at[slot], y_in.at[dz, dy], ry_sems, (dz, dy), (at(0, dy), x))
    for dz in range(1, z_size):
        after_z(dz)
    for dy in range(1, y_size):
        after_y(0, dy)
    for dz in range(z_size - 1, -1, -1):
        slot = dz * y_size
        total = acc[slot].astype(F32)
        for dy in range(1, y_size):
            arrival(y_in.at[dz, dy], ry_sems, (dz, dy))
            total = total + y_in[dz, dy].astype(F32)
        acc[slot] = total.astype(BF)
        if dz:
            send(acc.at[slot], z_in.at[dz], rz_sems, (dz,), (at(dz, 0), x))
    for dz in range(z_size - 1, 0, -1):
        for dy in range(1, y_size):
            after_y(dz, dy)
    total = acc[0].astype(F32)
    for dz in range(1, z_size):
        arrival(z_in.at[dz], rz_sems, (dz,))
        total = total + z_in[dz].astype(F32)
    stream[...] = total
    for dz, dy in spots[1:]:
        after_x(dz, dy)

    for k in range(1, n):
        departure(facts, fact_sems, (k,))
    for dz, dy in spots:
        slot = dz * y_size + dy
        departure(core_out.at[slot], rc_sems, (slot,))
        if dy:
            departure(acc.at[slot], ry_sems, (dz, dy))
        elif dz:
            departure(acc.at[slot], rz_sems, (dz,))
    for k, part in enumerate(parts):
        pltpu.make_async_copy(weights[k], wholes[k].at[me], own_sems.at[k]).wait()
        for dz, dy in spots:
            arrival(wholes[k].at[at(dz, dy, 1)], c_sems, (k, dz, dy))
            departure(weights[k], c_sems, (k, dz, dy))

        @pl.when(x == part)
        def _():
            for dz in range(1, z_size):
                departure(weights[k], z_sems, (k, dz))
            for dz, dy in spots:
                if dy:
                    departure(weights[k], y_sems, (k, dz, dy))
                if dz or dy:
                    for dx in range(1, reps):
                        departure(weights[k], x_sems, (k, dz, dy, dx))


def front(facts, code_b, class_b, weights, parts, own_width, length, reps, n):
    z_size, y_size = geometry(n)
    width = code_b.shape[1]
    count = len(weights)
    spots = z_size * y_size
    block = (length, width)
    vmem, hbm = pl.BlockSpec(memory_space=pltpu.VMEM), pl.BlockSpec(memory_space=pl.ANY)
    dma = pltpu.SemaphoreType.DMA
    outs = pl.pallas_call(
        functools.partial(front_kernel, z_size, y_size, reps, own_width, parts),
        out_shape=[jax.ShapeDtypeStruct((n,) + w.shape, w.dtype) for w in weights]
        + [jax.ShapeDtypeStruct(block, F32), jax.ShapeDtypeStruct((n, 8, 128), F32)],
        in_specs=[vmem] * 3 + [hbm] * count,
        out_specs=[hbm] * count + [vmem] * 2,
        scratch_shapes=[
            pltpu.VMEM((128, n * 8), F32),
            pltpu.VMEM((spots,) + block, BF),
            pltpu.VMEM((spots,) + block, BF),
            pltpu.VMEM((spots,) + block, BF),
            pltpu.VMEM((z_size, y_size) + block, BF),
            pltpu.VMEM((z_size,) + block, BF),
            dma((2, n)),
            dma((2, count, z_size)),
            dma((2, count, z_size, y_size)),
            dma((2, count, z_size, y_size, reps)),
            dma((2, count, z_size, y_size)),
            dma((count,)),
            dma((2, spots)),
            dma((2, z_size, y_size)),
            dma((2, z_size)),
        ],
        compiler_params=pltpu.CompilerParams(
            collective_id=0, has_side_effects=True, vmem_limit_bytes=60 * 2**20
        ),
        name="front",
    )(facts, code_b, class_b, *weights)
    return outs[:count], outs[count], outs[count + 1]


def adam_update(weight, first, second, grad, rate, decay):
    first_new = BETA_ONE * first + (1.0 - BETA_ONE) * grad
    second_new = BETA_TWO * second + (1.0 - BETA_TWO) * grad * grad
    first_hat = first_new / (1.0 - BETA_ONE**STEP)
    second_hat = second_new / (1.0 - BETA_TWO**STEP)
    weight_new = weight - rate * (first_hat / (jnp.sqrt(second_hat) + ADAM_EPS) + decay * weight)
    return (weight_new, first_new, second_new)


def dot(subscripts, left, right):
    return jnp.einsum(subscripts, left, right, preferred_element_type=F32)


def local(*args):
    class_ids, null_mask, code_ids, lengths = args[:4]
    masters, firsts, seconds = args[4::3], args[5::3], args[6::3]
    code_table, class_table, qkv_weight, out_weight, gate_up, down_weight, head_weight, gains = (
        masters
    )
    rates = (0.5, 0.5, 0.05, 0.05, 0.05, 0.05, 0.05, 0.5)
    decays = (0.1, 0.1, 0.1, 0.1, 0.1, 0.1, 0.1, 0.0)
    n = lax.axis_size("fsdp")
    me = lax.axis_index("fsdp")
    batch, length = code_ids.shape
    width = qkv_weight.shape[1]
    hidden_width = down_weight.shape[1]
    table_rows, own_width = class_table.shape
    own_rows = code_table.shape[0]
    heads = width // HEAD_DIM
    rows = (qkv_weight.shape[0], gate_up.shape[0], out_weight.shape[0], down_weight.shape[0])

    classes = jnp.where(null_mask == 1, table_rows - 1, class_ids)
    previous = jnp.concatenate([jnp.full((1, 1), -1, code_ids.dtype), code_ids[:, :-1]], 1)
    pair = jnp.stack([classes[0], lengths[0]])[None].astype(F32)
    own_gains = gains.astype(BF).astype(F32)
    facts = jnp.concatenate(
        [
            previous.astype(F32).reshape(2, -1),
            code_ids.astype(F32).reshape(2, -1),
            jnp.pad(pair, ((0, 0), (0, length // 2 - 2))),
            jnp.pad(own_gains, ((0, 0), (0, length // 2 - own_width))),
        ],
        0,
    )
    class_b = jnp.pad(class_table.astype(BF), ((0, -table_rows % 16), (0, 128 - own_width)))
    code_b = code_table.astype(BF)
    reps = lax.axis_size("rep")
    parts = tuple(k % reps for k in range(4))
    wholes, stream0, facts = front(
        facts,
        code_b,
        class_b,
        [w.astype(BF) for w in (gate_up, qkv_weight, out_weight, down_weight)],
        parts,
        own_width,
        length,
        reps,
        n,
    )
    gate_w, qkv_w, out_w, down_w = (w.reshape(-1, w.shape[-1]) for w in wholes)
    stream0 = stream0[None]
    images = n * batch
    tokens = images * length
    gains32 = facts[:, 5:8, :own_width].transpose(1, 0, 2).reshape(3, width)
    all_codes = facts[:, 2:4].reshape(images, length).astype(jnp.int32)
    previous = facts[:, 0:2].reshape(tokens).astype(jnp.int32)
    all_classes = facts[:, 4, 0].astype(jnp.int32)
    all_lengths = facts[:, 4, 1].astype(jnp.int32)
    all_counted = (jnp.arange(length)[None, :] < all_lengths[:, None]).astype(F32)
    token_count = lax.psum(jnp.sum(all_counted), "rep")
    own_ids = jnp.arange(own_rows) + me * own_rows
    lookup = (previous[:, None] == own_ids[None, :]).astype(BF)

    normed1, inverse1 = norm_forward(stream0, gains32[0])
    normed1 = normed1.astype(BF)
    mixed = dot("btd,ed->bte", normed1, qkv_w)
    cosine, sine = rotary_tables(length, HEAD_DIM)
    split4 = (batch, length, heads, HEAD_DIM)
    queries = rotate(mixed[..., :width].reshape(split4), cosine, sine).astype(BF)
    keys_rot = rotate(mixed[..., width : 2 * width].reshape(split4), cosine, sine).astype(BF)
    values = mixed[..., 2 * width :].reshape(split4).astype(BF)
    scores = attention_scores(queries, keys_rot)
    top = jnp.max(scores, -1, keepdims=True)
    expo = jnp.exp(scores - top)
    probs32 = expo / jnp.sum(expo, -1, keepdims=True)
    probs = probs32.astype(BF)
    attended = dot("bhqk,bkhd->bqhd", probs, values).astype(BF).reshape(batch, length, width)
    stream1 = stream0 + dot("btd,ed->bte", attended, out_w)
    normed2, inverse2 = norm_forward(stream1, gains32[1])
    normed2 = normed2.astype(BF)
    gated = dot("btd,fd->btf", normed2, gate_w)
    gate_part = gated[..., :hidden_width]
    up_part = gated[..., hidden_width:]
    hidden = (jax.nn.silu(gate_part) * up_part).astype(BF)
    stream2 = stream1 + dot("btf,df->btd", hidden, down_w)
    normed3, inverse3 = norm_forward(stream2, gains32[2])
    normed3 = normed3.astype(BF)

    head_b = head_weight.astype(BF)
    normed3_all = lax.all_gather(normed3, "fsdp", axis=0, tiled=True).reshape(tokens, width)
    logits = dot("td,vd->tv", normed3_all, head_b)
    onehot = all_codes.reshape(tokens)[:, None] == own_ids[None, :]
    local_top = jnp.max(logits, -1)
    local_sum = jnp.sum(jnp.exp(logits - local_top[:, None]), -1)
    local_pick = jnp.sum(jnp.where(onehot, logits, 0.0), -1)
    stats = lax.all_gather(jnp.stack([local_top, local_sum, local_pick]), "fsdp", axis=0)
    ltop = jnp.max(stats[:, 0], 0)
    lse = jnp.log(jnp.sum(stats[:, 1] * jnp.exp(stats[:, 0] - ltop[None]), 0)) + ltop
    picked = jnp.sum(stats[:, 2], 0)
    loss_sum = lax.psum(jnp.sum(jnp.where(all_counted.reshape(tokens) > 0, lse - picked, 0.0)), "rep")
    weight_t = all_counted.reshape(tokens) * (1.0 / token_count)
    soft = jnp.exp(logits - lse[:, None])
    grad_logits = ((soft - onehot.astype(F32)) * weight_t[:, None]).astype(BF)
    grad_normed3 = dot("tv,vd->td", grad_logits, head_b).astype(BF).reshape(images, length, width)
    grad_normed3 = lax.psum_scatter(grad_normed3, "fsdp", scatter_dimension=0, tiled=True)
    grad_normed3 = grad_normed3.astype(F32)
    grad_head = dot("tv,td->vd", grad_logits, normed3_all)

    grad_stream2, gain_three = norm_backward(stream2, inverse3, gains32[2], grad_normed3)
    grad_branch = grad_stream2.astype(BF)
    grad_down = dot("btd,btf->df", grad_branch, hidden)
    grad_hidden = dot("btd,df->btf", grad_branch, down_w)
    sigma = jax.nn.sigmoid(gate_part)
    grad_gate = grad_hidden * up_part * sigma * (1.0 + gate_part * (1.0 - sigma))
    grad_up = grad_hidden * gate_part * sigma
    grad_gated = jnp.concatenate([grad_gate, grad_up], -1).astype(BF)
    grad_gate_up = dot("btf,btd->fd", grad_gated, normed2)
    grad_normed2 = dot("btf,fd->btd", grad_gated, gate_w)
    grad_middle, gain_two = norm_backward(stream1, inverse2, gains32[1], grad_normed2)
    grad_stream1 = grad_stream2 + grad_middle
    grad_attn = grad_stream1.astype(BF)
    grad_out = dot("bte,btd->ed", grad_attn, attended)
    grad_attended = dot("bte,ed->btd", grad_attn, out_w).astype(BF).reshape(split4)
    grad_probs = dot("bqhd,bkhd->bhqk", grad_attended, values)
    grad_values = dot("bhqk,bqhd->bkhd", probs, grad_attended)
    grad_scores = probs32 * (grad_probs - jnp.sum(probs32 * grad_probs, -1, keepdims=True))
    grad_scores = grad_scores.astype(BF)
    scale = HEAD_DIM ** (-0.5)
    grad_queries = dot("bhqk,bkhd->bqhd", grad_scores, keys_rot) * scale
    grad_keys = dot("bhqk,bqhd->bkhd", grad_scores, queries) * scale
    grad_mixed = jnp.concatenate(
        [
            rotate_back(grad_queries, cosine, sine).reshape(batch, length, width),
            rotate_back(grad_keys, cosine, sine).reshape(batch, length, width),
            grad_values.reshape(batch, length, width),
        ],
        -1,
    ).astype(BF)
    grad_qkv = dot("bte,btd->ed", grad_mixed, normed1)
    grad_normed1 = dot("bte,ed->btd", grad_mixed, qkv_w)
    grad_first, gain_one = norm_backward(stream0, inverse1, gains32[0], grad_normed1)
    grad_stream0 = grad_stream1 + grad_first

    blocks = [
        g.astype(BF).reshape(n, -1, g.shape[-1]) for g in (grad_qkv, grad_gate_up, grad_out, grad_down)
    ]
    layer_part = lax.psum_scatter(pack_rows(*blocks), "fsdp", scatter_dimension=0, tiled=False)
    rows_all = lax.all_gather(grad_stream0.astype(BF), "fsdp", axis=0, tiled=True)
    grad_codes = dot("tv,td->vd", lookup, rows_all.reshape(tokens, width))
    class_part = lax.dynamic_slice(rows_all[:, 0], (0, me * own_width), (images, own_width))
    class_spot = (all_classes[:, None] == jnp.arange(table_rows)[None, :]).astype(BF)
    grad_classes = dot("iv,id->vd", class_spot, class_part)
    summed = lax.psum(
        (grad_codes.astype(BF), grad_head.astype(BF), layer_part, grad_classes), "rep"
    )
    grad_codes, grad_head, layer_part, grad_classes = (s.astype(F32) for s in summed)
    grad_gains = lax.psum(jnp.stack([gain_one, gain_two, gain_three]), ("fsdp", "rep"))
    grad_gains = lax.dynamic_slice(grad_gains, (0, me * own_width), (3, own_width))
    grad_qkv, grad_gate_up, grad_out, grad_down = unpack_rows(layer_part, rows, hidden_width)
    reduced = (
        grad_codes, grad_classes, grad_qkv, grad_out, grad_gate_up, grad_down, grad_head, grad_gains
    )
    squares = jnp.zeros((), F32)
    for grad_piece in reduced:
        squares = squares + jnp.sum(grad_piece * grad_piece)
    grad_norm = jnp.sqrt(lax.psum(squares, "fsdp"))
    factor = jnp.minimum(1.0, 1.0 / CLIP_INV / (grad_norm + 1e-06))
    results = [loss_sum, token_count, grad_norm]
    for index in range(8):
        results.extend(
            adam_update(
                masters[index],
                firsts[index],
                seconds[index],
                reduced[index] * factor,
                rates[index],
                decays[index],
            )
        )
    return tuple(results)


def solution(mesh):
    split = P(("fsdp", "rep"))
    by_row, by_column = P("fsdp", None), P(None, "fsdp")
    weights = (by_row,) * 3 + (by_column,) * 3 + (by_row,) * 15 + (by_column,) * 3
    return jax.shard_map(
        local,
        mesh=mesh,
        in_specs=(split, split, P(("fsdp", "rep"), None), split) + weights,
        out_specs=(P(), P(), P()) + weights,
        check_vma=False,
    )
```

```python
import functools
import math

import jax
import jax.numpy as jnp
from jax import lax
from jax.experimental import pallas as pl
from jax.experimental.pallas import tpu as pltpu
from jax.sharding import PartitionSpec as P

HEAD_DIM = 64
CLIP_INV = 500
STEP = 10
NORM_EPS = 1e-05
BETA_ONE = 0.5
BETA_TWO = 0.5
ADAM_EPS = 1e-08
BF = jnp.bfloat16
F32 = jnp.float32
MESH = pl.DeviceIdType.MESH


def rotary_tables(length, width):
    half = width // 2
    freq = 10000.0 ** (-jnp.arange(half, dtype=F32) * 2.0 / width)
    angles = jnp.arange(length, dtype=F32)[:, None] * freq[None, :]
    cosine = jnp.concatenate([jnp.cos(angles), jnp.cos(angles)], -1)
    sine = jnp.concatenate([jnp.sin(angles), jnp.sin(angles)], -1)
    return (cosine, sine)


def rotate(values, cosine, sine):
    half = values.shape[-1] // 2
    swapped = jnp.concatenate([-values[..., half:], values[..., :half]], -1)
    return values * cosine[:, None, :] + swapped * sine[:, None, :]


def rotate_back(grads, cosine, sine):
    half = grads.shape[-1] // 2
    scaled = grads * sine[:, None, :]
    return grads * cosine[:, None, :] + jnp.concatenate(
        [scaled[..., half:], -scaled[..., :half]], -1
    )


def norm_forward(stream, gain):
    inverse = lax.rsqrt(jnp.mean(stream * stream, -1, keepdims=True) + NORM_EPS)
    return (stream * inverse * gain, inverse)


def norm_backward(stream, inverse, gain, grad_out):
    weighted = grad_out * gain
    inner = jnp.mean(weighted * stream, -1, keepdims=True)
    grad_in = inverse * weighted - stream * inverse * inverse * inverse * inner
    grad_gain = jnp.sum(grad_out * stream * inverse, axis=(0, 1))
    return (grad_in, grad_gain)


def attention_scores(queries, keys_rot):
    length = queries.shape[1]
    scores = jnp.einsum(
        "bqhd,bkhd->bhqk", queries, keys_rot, preferred_element_type=F32
    ) * HEAD_DIM ** (-0.5)
    causal = jnp.arange(length)[:, None] >= jnp.arange(length)[None, :]
    return jnp.where(causal, scores, -1e30)


def column_blocks(width, total):
    return [(at, min(width, total - at)) for at in range(0, total, width)]


def pack_rows(qkv, gate, out, down):
    width = qkv.shape[-1]
    parts = [qkv, gate, out]
    for at, size in column_blocks(width, down.shape[-1]):
        block = down[..., at : at + size]
        if size < width:
            pad = [(0, 0)] * (block.ndim - 1) + [(0, width - size)]
            block = jnp.pad(block, pad)
        parts.append(block)
    return jnp.concatenate(parts, -2)


def unpack_rows(packed, rows, hidden_width):
    width = packed.shape[-1]
    at, parts = 0, []
    for count in rows[:3]:
        parts.append(packed[..., at : at + count, :])
        at += count
    blocks = []
    for _, size in column_blocks(width, hidden_width):
        blocks.append(packed[..., at : at + rows[3], :size])
        at += rows[3]
    parts.append(jnp.concatenate(blocks, -1))
    return parts


def geometry(n):
    chips = n // 2
    y_size = 1 << ((chips.bit_length() - 1) // 2)
    return chips // y_size, y_size


def where_am_i(z_size, y_size):
    me = lax.axis_index("fsdp")
    return me, me // (2 * y_size), (me // 2) % y_size, me % 2


def send(src, dst, sems, index, device):
    pltpu.make_async_remote_copy(
        src_ref=src, dst_ref=dst, send_sem=sems.at[(0,) + index], recv_sem=sems.at[(1,) + index],
        device_id=device, device_id_type=MESH,
    ).start()


def arrival(dst, sems, index):
    pltpu.make_async_copy(dst, dst, sems.at[(1,) + index]).wait()


def departure(src, sems, index):
    pltpu.make_async_copy(src, src, sems.at[(0,) + index]).wait()


def front_kernel(z_size, y_size, reps, own_width, parts, facts, code_b, class_b, *refs):
    count = len(parts)
    weights, refs = refs[:count], refs[count:]
    wholes, refs = refs[:count], refs[count:]
    (stream, facts_all, turned, acc, core_out, core_in, y_in, z_in,
     fact_sems, rep_sems, z_sems, y_sems, x_sems, c_sems, own_sems, rc_sems, ry_sems, rz_sems) = refs
    n = z_size * y_size * 2
    me, z, y, core = where_am_i(z_size, y_size)
    x = lax.axis_index("rep")
    length = stream.shape[0]
    width = stream.shape[1]
    own_rows = code_b.shape[0]

    def at(dz, dy, other=0):
        c = 1 - core if other else core
        return (lax.rem(z + dz, z_size) * y_size + lax.rem(y + dy, y_size)) * 2 + c

    barrier = pltpu.get_barrier_semaphore()
    for k in range(1, n):
        pl.semaphore_signal(barrier, inc=1, device_id=(lax.rem(me + k, n), x), device_id_type=MESH)
    for k in range(1, reps):
        pl.semaphore_signal(barrier, inc=1, device_id=(me, lax.rem(x + k, reps)), device_id_type=MESH)
    pl.semaphore_wait(barrier, n - 1 + reps - 1)

    for k in range(1, n):
        send(facts, facts_all.at[x, me], fact_sems, (k,), (lax.rem(me + k, n), x))
    facts_all[x, me] = facts[...]

    peers_z = [(dz, at(dz, 0)) for dz in range(1, z_size)]
    peers_y = [(dy, at(0, dy)) for dy in range(1, y_size)]
    spots = [(dz, dy) for dz in range(z_size) for dy in range(y_size)]
    for k, part in enumerate(parts):
        pltpu.make_async_copy(weights[k], wholes[k].at[me], own_sems.at[k]).start()

        @pl.when(x == part)
        def _():
            for dz, peer in peers_z:
                send(weights[k], wholes[k].at[me], z_sems, (k, dz), (peer, x))
            for dy, peer in peers_y:
                send(weights[k], wholes[k].at[me], y_sems, (k, 0, dy), (peer, x))

        send(weights[k], wholes[k].at[me], c_sems, (k, 0, 0), (at(0, 0, 1), x))

    def to_others(k, dz, dy):
        block = wholes[k].at[at(dz, dy)]
        for dx in range(1, reps):
            send(block, block, x_sems, (k, dz, dy, dx), (me, lax.rem(x + dx, reps)))
        send(block, block, c_sems, (k, dz, dy), (at(0, 0, 1), x))

    def after_z(dz):
        for k, part in enumerate(parts):

            @pl.when(x == part)
            def _():
                block = wholes[k].at[at(z_size - dz, 0)]
                arrival(block, z_sems, (k, dz))
                for dy, peer in peers_y:
                    send(block, block, y_sems, (k, z_size - dz, dy), (peer, x))
                to_others(k, z_size - dz, 0)

    def after_y(dz, dy):
        for k, part in enumerate(parts):

            @pl.when(x == part)
            def _():
                arrival(wholes[k].at[at(dz, y_size - dy)], y_sems, (k, dz, dy))
                to_others(k, dz, y_size - dy)

    def after_x(dz, dy):
        for k, part in enumerate(parts):

            @pl.when(x != part)
            def _():
                block = wholes[k].at[at(dz, dy)]
                arrival(block, x_sems, (k, dz, dy, lax.rem(x - part + reps, reps)))
                send(block, block, c_sems, (k, dz, dy), (at(0, 0, 1), x))

    for k in range(1, n):
        arrival(facts_all.at[x, lax.rem(me - k + n, n)], fact_sems, (k,))
    for k in range(1, reps):
        send(facts_all.at[x], facts_all.at[x], rep_sems, (k,), (me, lax.rem(x + k, reps)))
    turned[...] = jnp.transpose(facts_all[x].reshape(n * 8, 128))
    lane = lax.broadcasted_iota(jnp.int32, (128, n * 8), 1)
    class_rows = class_b[...].astype(F32)
    class_iota = lax.broadcasted_iota(jnp.int32, class_rows.shape, 0).astype(F32)
    row_iota = lax.broadcasted_iota(jnp.int32, (length // 2, own_rows), 1) + me * own_rows
    row_iota = row_iota.astype(F32)

    def found(image, out):
        cls = jnp.sum(jnp.where(lane[:1] == image * 8 + 4, turned[:1, :], 0.0), -1, keepdims=True)
        row = jnp.sum(jnp.where(class_iota == cls, class_rows, 0.0), 0, keepdims=True)
        row = jnp.concatenate([row, jnp.zeros((1, width - row.shape[1]), F32)], -1)
        row = pltpu.roll(jnp.broadcast_to(row, (8, width)), me * own_width, 1)
        for half in range(2):
            ids = jnp.sum(jnp.where(lane == image * 8 + half, turned[...], 0.0), -1, keepdims=True)
            spot = jnp.where(row_iota == ids, 1.0, 0.0).astype(BF)
            rows = jnp.dot(spot, code_b[...], preferred_element_type=F32)
            out[pl.ds(half * (length // 2), length // 2)] = rows.astype(BF)
            if half == 0:
                first = lax.broadcasted_iota(jnp.int32, (16, width), 0) == 0
                head = jnp.where(first, jnp.concatenate([row, row], 0), rows[:16])
                out[pl.ds(0, 16)] = head.astype(BF)

    order = [(dz, dy) for dz in range(z_size - 1, -1, -1) for dy in range(y_size - 1, -1, -1)]
    for dz, dy in order:
        slot = dz * y_size + dy
        found(at(dz, dy, 1), core_out.at[slot])
        send(core_out.at[slot], core_in.at[slot], rc_sems, (slot,), (at(0, 0, 1), x))
        found(at(dz, dy), acc.at[slot])
    for dz, dy in order:
        slot = dz * y_size + dy
        arrival(core_in.at[slot], rc_sems, (slot,))
        acc[slot] = (acc[slot].astype(F32) + core_in[slot].astype(F32)).astype(BF)
        if dy:
            send(acc.at[slot], y_in.at[dz, dy], ry_sems, (dz, dy), (at(0, dy), x))
    for dz in range(1, z_size):
        after_z(dz)
    for dy in range(1, y_size):
        after_y(0, dy)
    for dz in range(z_size - 1, -1, -1):
        slot = dz * y_size
        total = acc[slot].astype(F32)
        for dy in range(1, y_size):
            arrival(y_in.at[dz, dy], ry_sems, (dz, dy))
            total = total + y_in[dz, dy].astype(F32)
        acc[slot] = total.astype(BF)
        if dz:
            send(acc.at[slot], z_in.at[dz], rz_sems, (dz,), (at(dz, 0), x))
    for dz in range(z_size - 1, 0, -1):
        for dy in range(1, y_size):
            after_y(dz, dy)
    total = acc[0].astype(F32)
    for dz in range(1, z_size):
        arrival(z_in.at[dz], rz_sems, (dz,))
        total = total + z_in[dz].astype(F32)
    stream[...] = total
    for dz, dy in spots[1:]:
        after_x(dz, dy)

    for k in range(1, reps):
        arrival(facts_all.at[x], rep_sems, (k,))
        departure(facts_all.at[x], rep_sems, (k,))

    for k in range(1, n):
        departure(facts, fact_sems, (k,))
    for dz, dy in spots:
        slot = dz * y_size + dy
        departure(core_out.at[slot], rc_sems, (slot,))
        if dy:
            departure(acc.at[slot], ry_sems, (dz, dy))
        elif dz:
            departure(acc.at[slot], rz_sems, (dz,))
    for k, part in enumerate(parts):
        pltpu.make_async_copy(weights[k], wholes[k].at[me], own_sems.at[k]).wait()
        for dz, dy in spots:
            arrival(wholes[k].at[at(dz, dy, 1)], c_sems, (k, dz, dy))
            departure(weights[k], c_sems, (k, dz, dy))

        @pl.when(x == part)
        def _():
            for dz in range(1, z_size):
                departure(weights[k], z_sems, (k, dz))
            for dz, dy in spots:
                if dy:
                    departure(weights[k], y_sems, (k, dz, dy))
                if dz or dy:
                    for dx in range(1, reps):
                        departure(weights[k], x_sems, (k, dz, dy, dx))


def front(facts, code_b, class_b, weights, parts, own_width, length, reps, n):
    z_size, y_size = geometry(n)
    width = code_b.shape[1]
    count = len(weights)
    spots = z_size * y_size
    block = (length, width)
    vmem, hbm = pl.BlockSpec(memory_space=pltpu.VMEM), pl.BlockSpec(memory_space=pl.ANY)
    dma = pltpu.SemaphoreType.DMA
    outs = pl.pallas_call(
        functools.partial(front_kernel, z_size, y_size, reps, own_width, parts),
        out_shape=[jax.ShapeDtypeStruct((n,) + w.shape, w.dtype) for w in weights]
        + [jax.ShapeDtypeStruct(block, F32), jax.ShapeDtypeStruct((reps, n, 8, 128), F32)],
        in_specs=[vmem] * 3 + [hbm] * count,
        out_specs=[hbm] * count + [vmem] * 2,
        scratch_shapes=[
            pltpu.VMEM((128, n * 8), F32),
            pltpu.VMEM((spots,) + block, BF),
            pltpu.VMEM((spots,) + block, BF),
            pltpu.VMEM((spots,) + block, BF),
            pltpu.VMEM((z_size, y_size) + block, BF),
            pltpu.VMEM((z_size,) + block, BF),
            dma((2, n)),
            dma((2, reps)),
            dma((2, count, z_size)),
            dma((2, count, z_size, y_size)),
            dma((2, count, z_size, y_size, reps)),
            dma((2, count, z_size, y_size)),
            dma((count,)),
            dma((2, spots)),
            dma((2, z_size, y_size)),
            dma((2, z_size)),
        ],
        compiler_params=pltpu.CompilerParams(
            collective_id=0, has_side_effects=True, vmem_limit_bytes=60 * 2**20
        ),
        name="front",
    )(facts, code_b, class_b, *weights)
    return outs[:count], outs[count], outs[count + 1]


class Place:
    def __init__(self, z_size, y_size, reps):
        self.z_size, self.y_size, self.reps = z_size, y_size, reps
        self.n = z_size * y_size * 2
        self.me, self.z, self.y, self.core = where_am_i(z_size, y_size)
        self.x = lax.axis_index("rep")

    def at(self, dz, dy, other=0):
        c = 1 - self.core if other else self.core
        z, y = lax.rem(self.z + dz, self.z_size), lax.rem(self.y + dy, self.y_size)
        return (z * self.y_size + y) * 2 + c

    def plane(self, z, dy=0, other=0):
        c = 1 - self.core if other else self.core
        return (z * self.y_size + lax.rem(self.y + dy, self.y_size)) * 2 + c

    def twin(self):
        return (self.at(0, 0, 1), self.x)

    def greet(self, everyone):
        barrier = pltpu.get_barrier_semaphore()
        if everyone:
            group = [lax.rem(self.me + k, self.n) for k in range(1, self.n)]
        else:
            group = [self.at(dz, 0) for dz in range(1, self.z_size)]
            group += [self.at(0, dy) for dy in range(1, self.y_size)] + [self.at(0, 0, 1)]
        peers = [(p, self.x) for p in group]
        peers += [(self.me, lax.rem(self.x + k, self.reps)) for k in range(1, self.reps)]
        for peer in peers:
            pl.semaphore_signal(barrier, inc=1, device_id=peer, device_id_type=MESH)
        pl.semaphore_wait(barrier, len(peers))


class Spread:
    def __init__(self, place, whole, z_sems, y_sems, c_sems):
        self.p, self.whole = place, whole
        self.z_sems, self.y_sems, self.c_sems = z_sems, y_sems, c_sems

    def block(self, z, dy=0, other=0):
        return self.whole.at[self.p.plane(z, dy, other)]

    def pass_on(self, z, src, up, down):
        p = self.p
        dst = self.block(z)
        if up:

            @pl.when(p.z + 1 < p.z_size)
            def _():
                send(src, dst, self.z_sems, (0, z), (p.plane(p.z + 1), p.x))

        if down:

            @pl.when(p.z >= 1)
            def _():
                send(src, dst, self.z_sems, (1, z), (p.plane(p.z - 1), p.x))

        for dy in range(1, p.y_size):
            send(src, dst, self.y_sems, (z, dy), (p.at(0, dy), p.x))
        send(src, dst, self.c_sems, (z, 0), p.twin())

    def start(self, own):
        self.pass_on(self.p.z, own, True, True)

    def step_z(self, s):
        p = self.p

        @pl.when(p.z - s >= 0)
        def _():
            arrival(self.block(p.z - s), self.z_sems, (0, p.z - s))
            self.pass_on(p.z - s, self.block(p.z - s), True, False)

        @pl.when(p.z + s < p.z_size)
        def _():
            arrival(self.block(p.z + s), self.z_sems, (1, p.z + s))
            self.pass_on(p.z + s, self.block(p.z + s), False, True)

    def take_y(self, z):
        for dy in range(1, self.p.y_size):
            block = self.block(z, self.p.y_size - dy)
            arrival(block, self.y_sems, (z, dy))
            send(block, block, self.c_sems, (z, dy), self.p.twin())

    def take_twin(self, z):
        for dy in range(self.p.y_size):
            arrival(self.block(z, self.p.y_size - dy, 1), self.c_sems, (z, dy))

    def finish(self):
        p = self.p
        block = self.block(p.z)
        for z in range(p.z_size):

            @pl.when(jnp.logical_and(p.z + 1 < p.z_size, z <= p.z))
            def _():
                departure(block, self.z_sems, (0, z))

            @pl.when(jnp.logical_and(p.z >= 1, z >= p.z))
            def _():
                departure(block, self.z_sems, (1, z))

            for dy in range(p.y_size):
                departure(block, self.c_sems, (z, dy))
                if dy:
                    departure(block, self.y_sems, (z, dy))


def head_kernel(z_size, y_size, reps, normed3, head_b, facts, grad_normed3, grad_head, totals,
                whole, logits, grads, turned, marks, stats_in, lse_all, acc, core_out, core_in, y_in, z_in,
                loss_in, z_sems, y_sems, c_sems, st_sems, ls_sems, rc_sems, ry_sems, rz_sems, lo_sems):
    p = Place(z_size, y_size, reps)
    n, me, x = p.n, p.me, p.x
    length, width = normed3.shape
    half = length // 2
    own_rows = head_b.shape[0]
    p.greet(True)
    spread = Spread(p, whole, z_sems, y_sems, c_sems)
    spread.start(normed3)
    whole[me] = normed3[...]
    own_facts = facts.at[x]
    turned[...] = jnp.transpose(own_facts[...].reshape(n * 8, 128))
    lane = lax.broadcasted_iota(jnp.int32, (128, n * 8), 1)
    full_lane = lax.broadcasted_iota(jnp.int32, (length, n * 8), 1)
    column_iota = (lax.broadcasted_iota(jnp.int32, (length, own_rows), 1) + me * own_rows).astype(F32)
    token = lax.broadcasted_iota(jnp.int32, (length, 1), 0).astype(F32)
    every = facts[...].reshape(reps * n * 8, 128)
    row8 = lax.rem(lax.broadcasted_iota(jnp.int32, every.shape, 0), 8)
    spot = jnp.logical_and(row8 == 4, lax.broadcasted_iota(jnp.int32, every.shape, 1) == 1)
    token_count = jnp.sum(jnp.sum(jnp.where(spot, every, 0.0), 0, keepdims=True), 1, keepdims=True)
    inv_count = 1.0 / token_count

    def codes_of(image):
        parts = [
            jnp.sum(jnp.where(lane == image * 8 + 2 + h, turned[...], 0.0), -1, keepdims=True)
            for h in range(2)
        ]
        return jnp.concatenate(parts, 0)

    marks[...] = jnp.zeros_like(marks)

    def forward(image):
        out = lax.dot_general(
            whole[image], head_b[...], (((1,), (1,)), ((), ())), preferred_element_type=F32
        )
        logits[image] = out
        top = jnp.max(out, -1, keepdims=True)
        total = jnp.sum(jnp.exp(out - top), -1, keepdims=True)
        pick = jnp.sum(jnp.where(column_iota == codes_of(image), out, 0.0), -1, keepdims=True)
        old = marks[...]
        old = jnp.where(full_lane == image * 8, top, old)
        old = jnp.where(full_lane == image * 8 + 1, total, old)
        marks[...] = jnp.where(full_lane == image * 8 + 2, pick, old)

    def forward_column(z, first, last):
        def body(j, carry):
            forward(p.plane(z, lax.rem(y_size - j // 2, y_size), 0) + lax.rem(j, 2) * (1 - 2 * p.core))
            return carry

        lax.fori_loop(first * 2, last * 2, body, 0)

    def forward_y(z):
        spread.take_y(z)

    arrival(spread.block(p.z, 0, 1), c_sems, (p.z, 0))
    forward_column(p.z, 0, 1)

    def one(z, s):
        arrival(spread.block(z, 0, 1), c_sems, (z, 0))
        forward_column(z, 0, 1)

    def other(z):
        for dy in range(1, y_size):
            arrival(spread.block(z, y_size - dy, 1), c_sems, (z, dy))
        forward_column(z, 1, y_size)

    def both(s, act):
        if s == 0:
            act(p.z)
            return

        @pl.when(p.z - s >= 0)
        def _():
            act(p.z - s)

        @pl.when(p.z + s < z_size)
        def _():
            act(p.z + s)

    for s in range(1, z_size + 1):
        if s < z_size:
            spread.step_z(s)
        both(s - 1, spread.take_y)
        if s < z_size:
            both(s, lambda z: one(z, s))
        both(s - 1, other)

    tiles = jnp.transpose(marks[...]).reshape(n, 8, length)
    stats_in[1] = tiles
    for k in range(1, n):
        peer = lax.rem(me + k, n)
        send(stats_in.at[1, peer], stats_in.at[0, me], st_sems, (k,), (peer, x))
    stats_in[0, me] = stats_in[1, me]
    for k in range(1, n):
        arrival(stats_in.at[0, 0], st_sems, (k,))
    tops = stats_in[0, :, 0, :]
    sums = stats_in[0, :, 1, :]
    picks = stats_in[0, :, 2, :]
    top = jnp.max(tops, 0, keepdims=True)
    lse = jnp.log(jnp.sum(sums * jnp.exp(tops - top), 0, keepdims=True)) + top
    pick = jnp.sum(picks, 0, keepdims=True)
    here = own_facts[me]
    counted = lax.broadcasted_iota(jnp.int32, (1, length), 1).astype(F32) < here[4:5, 1:2]
    loss = jnp.where(counted, lse - pick, 0.0)
    lse_all[me] = jnp.concatenate([lse, loss, jnp.zeros((6, length), F32)], 0)
    for k in range(1, n):
        peer = lax.rem(me + k, n)
        send(lse_all.at[me], lse_all.at[me], ls_sems, (k,), (peer, x))
    for k in range(1, n):
        arrival(lse_all.at[0], ls_sems, (k,))
    table = lse_all[...].reshape(n * 8, length)
    row8 = lax.rem(lax.broadcasted_iota(jnp.int32, table.shape, 0), 8)
    group = jnp.sum(jnp.sum(jnp.where(row8 == 1, table, 0.0), 0, keepdims=True), 1, keepdims=True)
    loss_in[x] = jnp.broadcast_to(group, (8, 128))
    for k in range(1, reps):
        peer = (me, lax.rem(x + k, reps))
        send(loss_in.at[x], loss_in.at[x], lo_sems, (k,), peer)
    marks[...] = jnp.transpose(table)

    def backward(image, out):
        lse_t = jnp.sum(jnp.where(full_lane == image * 8, marks[...], 0.0), -1, keepdims=True)
        size = jnp.sum(jnp.where(lane[:8] == image * 8 + 4, turned[:8, :], 0.0), -1, keepdims=True)
        weight = jnp.where(token < size[1:2], inv_count, 0.0)
        hot = jnp.where(column_iota == codes_of(image), 1.0, 0.0)
        grad = ((jnp.exp(logits[image] - lse_t) - hot) * weight).astype(BF)
        grads[image] = grad
        out[...] = jnp.dot(grad, head_b[...], preferred_element_type=F32).astype(BF)

    last = z_size - 1

    def far(j):
        return last - j // y_size, lax.rem(j, y_size)

    def first_pass(j, carry):
        dz, dyy = far(j)
        dy = y_size - 1 - dyy
        slot = dz * y_size + dy
        backward(p.at(dz, dy, 1), core_out.at[slot])
        send(core_out.at[slot], core_in.at[slot], rc_sems, (slot,), p.twin())
        backward(p.at(dz, dy), acc.at[slot])
        return carry

    def twin_sum(slot):
        arrival(core_in.at[slot], rc_sems, (slot,))
        acc[slot] = (acc[slot].astype(F32) + core_in[slot].astype(F32)).astype(BF)

    def y_sum(dz):
        slot = dz * y_size
        total = acc[slot].astype(F32)
        for dy in range(1, y_size):
            arrival(y_in.at[dz, dy], ry_sems, (dz, dy))
            total = total + y_in[dz, dy].astype(F32)
        acc[slot] = total.astype(BF)

    def round_of(g, carry):
        dz = last - g

        def per_dy(i, c):
            return first_pass(g * y_size + i, c)

        lax.fori_loop(0, y_size, per_dy, 0)
        for dy in range(y_size - 1, -1, -1):
            slot = dz * y_size + dy
            twin_sum(slot)
            if dy:
                send(acc.at[slot], y_in.at[dz, dy], ry_sems, (dz, dy), (p.at(0, dy), x))

        @pl.when(g >= 1)
        def _():
            y_sum(dz + 1)
            send(acc.at[(dz + 1) * y_size], z_in.at[dz + 1], rz_sems, (dz + 1,), (p.at(dz + 1, 0), x))

        return carry

    lax.fori_loop(0, z_size, round_of, 0)

    blocks = 4
    rows = own_rows // blocks
    for r in range(blocks):

        def add(image, total):
            return total + lax.dot_general(
                grads[image, :, r * rows : (r + 1) * rows], whole[image],
                (((0,), (0,)), ((), ())), preferred_element_type=F32,
            )

        total = lax.fori_loop(0, n, add, jnp.zeros((rows, width), F32))
        grad_head[r * rows : (r + 1) * rows] = total.astype(BF)
    y_sum(0)
    total = acc[0].astype(F32)
    for dz in range(1, z_size):
        arrival(z_in.at[dz], rz_sems, (dz,))
        total = total + z_in[dz].astype(F32)
    grad_normed3[...] = total
    for k in range(1, reps):
        arrival(loss_in.at[0], lo_sems, (k,))
    loss_sum = loss_in[0]
    for k in range(1, reps):
        loss_sum = loss_sum + loss_in[k]
    totals[...] = jnp.where(
        lax.broadcasted_iota(jnp.int32, (8, 128), 0) == 0, loss_sum, token_count
    )

    spread.finish()
    for k in range(1, n):
        departure(stats_in.at[0, 0], st_sems, (k,))
        departure(lse_all.at[0], ls_sems, (k,))
    for k in range(1, reps):
        departure(loss_in.at[0], lo_sems, (k,))
    for dz in range(z_size):
        for dy in range(y_size):
            slot = dz * y_size + dy
            departure(core_out.at[slot], rc_sems, (slot,))
            if dy:
                departure(acc.at[slot], ry_sems, (dz, dy))
            elif dz:
                departure(acc.at[slot], rz_sems, (dz,))


def head_scratch(n, length, width, own_rows, reps):
    z_size, y_size = geometry(n)
    spots = z_size * y_size
    dma = pltpu.SemaphoreType.DMA
    buffers = [
        ((n, length, width), BF),
        ((n, length, own_rows), F32),
        ((n, length, own_rows), BF),
        ((128, n * 8), F32),
        ((length, n * 8), F32),
        ((2, n, 8, length), F32),
        ((n, 8, length), F32),
        ((spots, length, width), BF),
        ((spots, length, width), BF),
        ((spots, length, width), BF),
        ((z_size, y_size, length, width), BF),
        ((z_size, length, width), BF),
        ((reps, 8, 128), F32),
    ]
    sems = [
        dma((2, 2, z_size)), dma((2, z_size, y_size)), dma((2, z_size, y_size)),
        dma((2, n)), dma((2, n)), dma((2, spots)), dma((2, z_size, y_size)), dma((2, z_size)),
        dma((2, reps)),
    ]
    return buffers, sems


def size_of(buffers):
    return sum(math.prod(shape) * jnp.dtype(kind).itemsize for shape, kind in buffers)


def head_phase(normed3, head_b, facts, reps, n):
    z_size, y_size = geometry(n)
    length, width = normed3.shape
    buffers, sems = head_scratch(n, length, width, head_b.shape[0], reps)
    vmem = pl.BlockSpec(memory_space=pltpu.VMEM)
    return pl.pallas_call(
        functools.partial(head_kernel, z_size, y_size, reps),
        out_shape=[
            jax.ShapeDtypeStruct((length, width), F32),
            jax.ShapeDtypeStruct(head_b.shape, BF),
            jax.ShapeDtypeStruct((8, 128), F32),
        ],
        in_specs=[vmem] * 3,
        out_specs=[vmem] * 3,
        scratch_shapes=[pltpu.VMEM(shape, kind) for shape, kind in buffers] + sems,
        compiler_params=pltpu.CompilerParams(
            collective_id=1, has_side_effects=True, vmem_limit_bytes=60 * 2**20
        ),
        name="head",
    )(normed3, head_b, facts)


def tail_kernel(z_size, y_size, split, counts, grad_stream0, facts, *refs):
    count = len(split)
    grads, refs = refs[:count], refs[count:]
    sums, refs = refs[:count], refs[count:]
    code_sum, first_rows, refs = refs[0], refs[1], refs[2:]
    accs, refs = refs[:count], refs[count:]
    core_in, refs = refs[:count], refs[count:]
    x_in, refs = refs[:count], refs[count:]
    y_in, refs = refs[:count], refs[count:]
    z_in, refs = refs[:count], refs[count:]
    trade, refs = refs[:count], refs[count:]
    (whole, code_out, code_in, rows_out, z_sems, y_sems, c_sems, own_sems, rc_sems, rx_sems, ry_sems,
     rz_sems, tr_sems, co_sems, fr_sems) = refs
    p = Place(z_size, y_size, 2)
    n, me, x = p.n, p.me, p.x
    length, width = grad_stream0.shape
    own_rows = code_out.shape[0]
    spots = z_size * y_size
    p.greet(False)
    mate = (me, 1 - x)
    spread = Spread(p, whole, z_sems, y_sems, c_sems)
    spread.start(grad_stream0)
    whole[me] = grad_stream0[...]

    def slot_of(dz, dy):
        return dz * y_size + dy

    order = [(dz, dy) for dz in range(z_size - 1, -1, -1) for dy in range(y_size - 1, -1, -1)]
    for dz, dy in order:
        slot = slot_of(dz, dy)
        for k in range(count):
            send(grads[k].at[p.at(dz, dy, 1)], core_in[k].at[slot], rc_sems, (k, slot), p.twin())
            pltpu.make_async_copy(grads[k].at[p.at(dz, dy)], accs[k].at[slot], own_sems.at[k, slot]).start()

    def part(k, which):
        rows = counts[k] // 2
        return pl.ds(pl.multiple_of(which * rows, rows), rows)

    def ref_of(k, ref, which):
        return ref.at[part(k, which)] if split[k] else ref

    def send_y(k, dz, dy):
        slot = slot_of(dz, dy)
        send(ref_of(k, accs[k].at[slot], x), y_in[k].at[slot], ry_sems, (k, slot), (p.at(0, dy), x))

    for dz, dy in order:
        slot = slot_of(dz, dy)
        for k in range(count):
            pltpu.make_async_copy(grads[k].at[0], accs[k].at[slot], own_sems.at[k, slot]).wait()
            arrival(core_in[k].at[slot], rc_sems, (k, slot))
            accs[k][slot] = (accs[k][slot].astype(F32) + core_in[k][slot].astype(F32)).astype(BF)
            if split[k]:
                send(accs[k].at[slot, part(k, 1 - x)], x_in[k].at[slot], rx_sems, (k, slot), mate)
            elif dy:
                send_y(k, dz, dy)

    def take_x(dz):
        for dy in range(y_size - 1, -1, -1):
            slot = slot_of(dz, dy)
            for k in range(count):
                if split[k]:
                    arrival(x_in[k].at[slot], rx_sems, (k, slot))
                    mine = accs[k].at[slot, part(k, x)]
                    mine[...] = (mine[...].astype(F32) + x_in[k][slot].astype(F32)).astype(BF)
                    if dy:
                        send_y(k, dz, dy)

    def take_y(dz):
        for k in range(count):
            mine = ref_of(k, accs[k].at[slot_of(dz, 0)], x)
            total = mine[...].astype(F32)
            for dy in range(1, y_size):
                slot = slot_of(dz, dy)
                arrival(y_in[k].at[slot], ry_sems, (k, slot))
                total = total + y_in[k][slot].astype(F32)
            mine[...] = total.astype(BF)
            if dz:
                send(mine, z_in[k].at[dz], rz_sems, (k, dz), (p.at(dz, 0), x))

    spread.step_z(1)
    take_x(z_size - 1)
    spread.take_y(p.z)
    take_y(z_size - 1)

    def both(s, act):
        @pl.when(p.z - s >= 0)
        def _():
            act(p.z - s)

        @pl.when(p.z + s < z_size)
        def _():
            act(p.z + s)

    for s in range(2, z_size):
        dz = z_size - s
        spread.step_z(s)
        take_x(dz)
        both(s - 1, spread.take_y)
        take_y(dz)
    both(z_size - 1, spread.take_y)
    take_x(0)
    for z in range(z_size):
        spread.take_twin(z)

    blocks = 4
    rows = own_rows // blocks
    iota = lax.broadcasted_iota(jnp.int32, (rows, length // 2), 0) + me * own_rows

    def code_block(r, carry):
        base = (iota + r * rows).astype(F32)

        def add(image, total):
            ids = facts[x, image]
            hot = jnp.concatenate(
                [jnp.where(base == ids[h : h + 1, :], 1.0, 0.0) for h in range(2)], 1
            ).astype(BF)
            return total + jnp.dot(hot, whole[image], preferred_element_type=F32)

        total = lax.fori_loop(0, n, add, jnp.zeros((rows, width), F32))
        at = pl.ds(pl.multiple_of(r * rows, rows), rows)
        code_out[at] = total.astype(BF)
        send(code_out.at[at], code_in.at[at], co_sems, (r,), mate)
        return carry

    firsts = whole[:, 0:8, :].astype(F32)
    rows_out[x] = firsts
    send(rows_out.at[x], rows_out.at[x], fr_sems, (), mate)
    lax.fori_loop(0, blocks, code_block, 0)

    take_y(0)
    for k in range(count):
        mine = ref_of(k, accs[k].at[0], x)
        total = mine[...].astype(F32)
        for dz in range(1, z_size):
            arrival(z_in[k].at[dz], rz_sems, (k, dz))
            total = total + z_in[k][dz].astype(F32)
        ref_of(k, trade[k].at[0], x)[...] = total.astype(BF)
        source = ref_of(k, trade[k].at[0], x)
        target = source if split[k] else trade[k].at[1]
        if split[k]:
            target = trade[k].at[0, part(k, x)]
        send(source, target, tr_sems, (k,), mate)
    for k in range(count):
        if split[k]:
            arrival(trade[k].at[0, part(k, 1 - x)], tr_sems, (k,))
            sums[k][...] = trade[k][0].astype(F32)
        else:
            arrival(trade[k].at[1], tr_sems, (k,))
            sums[k][...] = trade[k][0].astype(F32) + trade[k][1].astype(F32)
    arrival(rows_out.at[1 - x], fr_sems, ())
    first_rows[...] = rows_out[...]
    for r in range(blocks):
        at = pl.ds(r * rows, rows)
        arrival(code_in.at[at], co_sems, (r,))
        code_sum[at] = code_out[at].astype(F32) + code_in[at].astype(F32)

    spread.finish()
    departure(rows_out.at[x], fr_sems, ())
    for r in range(blocks):
        departure(code_out.at[pl.ds(r * rows, rows)], co_sems, (r,))
    for k in range(count):
        departure(ref_of(k, trade[k].at[0], x), tr_sems, (k,))
        for dz in range(z_size):
            if dz:
                departure(z_in[k].at[dz], rz_sems, (k, dz))
            for dy in range(y_size):
                slot = slot_of(dz, dy)
                departure(core_in[k].at[slot], rc_sems, (k, slot))
                if split[k]:
                    departure(x_in[k].at[slot], rx_sems, (k, slot))
                if dy:
                    departure(y_in[k].at[slot], ry_sems, (k, slot))


def tail_scratch(n, length, width, own_rows, shapes, split):
    z_size, y_size = geometry(n)
    spots = z_size * y_size
    count = len(shapes)
    dma = pltpu.SemaphoreType.DMA
    halves = [(s[0] // 2, s[1]) if h else s for s, h in zip(shapes, split)]
    buffers = [((spots,) + s, BF) for s in shapes] * 2
    buffers += [((spots,) + s if h else (16, 128), BF) for s, h in zip(halves, split)]
    buffers += [((spots,) + s, BF) for s in halves]
    buffers += [((z_size,) + s, BF) for s in halves]
    buffers += [((2,) + s, BF) for s in shapes]
    buffers += [((n, length, width), BF), ((own_rows, width), BF), ((own_rows, width), BF),
                ((2, n, 8, width), F32)]
    sems = [
        dma((2, 2, z_size)), dma((2, z_size, y_size)), dma((2, z_size, y_size)),
        dma((count, spots)), dma((2, count, spots)), dma((2, count, spots)), dma((2, count, spots)),
        dma((2, count, z_size)), dma((2, count)), dma((2, 4)), dma((2,)),
    ]
    return buffers, sems


def tail_phase(grad_stream0, facts, grads, split, own_rows, n):
    z_size, y_size = geometry(n)
    length, width = grad_stream0.shape
    shapes = [g.shape[1:] for g in grads]
    buffers, sems = tail_scratch(n, length, width, own_rows, shapes, split)
    vmem, hbm = pl.BlockSpec(memory_space=pltpu.VMEM), pl.BlockSpec(memory_space=pl.ANY)
    outs = pl.pallas_call(
        functools.partial(tail_kernel, z_size, y_size, split, tuple(s[0] for s in shapes)),
        out_shape=[jax.ShapeDtypeStruct(s, F32) for s in shapes]
        + [jax.ShapeDtypeStruct((own_rows, width), F32), jax.ShapeDtypeStruct((2, n, 8, width), F32)],
        in_specs=[vmem] * 2 + [hbm] * len(grads),
        out_specs=[vmem] * (len(grads) + 2),
        scratch_shapes=[pltpu.VMEM(shape, kind) for shape, kind in buffers] + sems,
        compiler_params=pltpu.CompilerParams(
            collective_id=2, has_side_effects=True, vmem_limit_bytes=60 * 2**20
        ),
        name="tail",
    )(grad_stream0, facts, *grads)
    return outs[: len(grads)], outs[len(grads)], outs[len(grads) + 1]


def norm_kernel(n, squares, total, given, sems):
    me, x = lax.axis_index("fsdp"), lax.axis_index("rep")
    barrier = pltpu.get_barrier_semaphore()
    for k in range(1, n):
        pl.semaphore_signal(barrier, inc=1, device_id=(lax.rem(me + k, n), x), device_id_type=MESH)
    pl.semaphore_wait(barrier, n - 1)
    for k in range(1, n):
        send(squares, given.at[me], sems, (k,), (lax.rem(me + k, n), x))
    given[me] = squares[...]
    for k in range(1, n):
        arrival(given.at[0], sems, (k,))
    total[...] = jnp.sum(given[...], 0)
    for k in range(1, n):
        departure(given.at[0], sems, (k,))


def sum_over_fsdp(squares, n):
    vmem = pl.BlockSpec(memory_space=pltpu.VMEM)
    return pl.pallas_call(
        functools.partial(norm_kernel, n),
        out_shape=jax.ShapeDtypeStruct((8, 128), F32),
        in_specs=[vmem],
        out_specs=vmem,
        scratch_shapes=[pltpu.VMEM((n, 8, 128), F32), pltpu.SemaphoreType.DMA((2, n))],
        compiler_params=pltpu.CompilerParams(collective_id=3, has_side_effects=True),
        name="norm",
    )(jnp.broadcast_to(squares, (8, 128)))[0, 0]


def adam_update(weight, first, second, grad, rate, decay):
    first_new = BETA_ONE * first + (1.0 - BETA_ONE) * grad
    second_new = BETA_TWO * second + (1.0 - BETA_TWO) * grad * grad
    first_hat = first_new / (1.0 - BETA_ONE**STEP)
    second_hat = second_new / (1.0 - BETA_TWO**STEP)
    weight_new = weight - rate * (first_hat / (jnp.sqrt(second_hat) + ADAM_EPS) + decay * weight)
    return (weight_new, first_new, second_new)


def dot(subscripts, left, right):
    return jnp.einsum(subscripts, left, right, preferred_element_type=F32)


def local(*args):
    class_ids, null_mask, code_ids, lengths = args[:4]
    masters, firsts, seconds = args[4::3], args[5::3], args[6::3]
    code_table, class_table, qkv_weight, out_weight, gate_up, down_weight, head_weight, gains = (
        masters
    )
    rates = (0.5, 0.5, 0.05, 0.05, 0.05, 0.05, 0.05, 0.5)
    decays = (0.1, 0.1, 0.1, 0.1, 0.1, 0.1, 0.1, 0.0)
    n = lax.axis_size("fsdp")
    me = lax.axis_index("fsdp")
    batch, length = code_ids.shape
    width = qkv_weight.shape[1]
    hidden_width = down_weight.shape[1]
    table_rows, own_width = class_table.shape
    own_rows = code_table.shape[0]
    heads = width // HEAD_DIM
    rows = (qkv_weight.shape[0], gate_up.shape[0], out_weight.shape[0], down_weight.shape[0])

    classes = jnp.where(null_mask == 1, table_rows - 1, class_ids)
    previous = jnp.concatenate([jnp.full((1, 1), -1, code_ids.dtype), code_ids[:, :-1]], 1)
    pair = jnp.stack([classes[0], lengths[0]])[None].astype(F32)
    own_gains = gains.astype(BF).astype(F32)
    facts = jnp.concatenate(
        [
            previous.astype(F32).reshape(2, -1),
            code_ids.astype(F32).reshape(2, -1),
            jnp.pad(pair, ((0, 0), (0, length // 2 - 2))),
            jnp.pad(own_gains, ((0, 0), (0, length // 2 - own_width))),
        ],
        0,
    )
    class_b = jnp.pad(class_table.astype(BF), ((0, -table_rows % 16), (0, 128 - own_width)))
    code_b = code_table.astype(BF)
    reps = lax.axis_size("rep")
    parts = tuple(k % reps for k in range(4))
    wholes, stream0, facts = front(
        facts,
        code_b,
        class_b,
        [w.astype(BF) for w in (gate_up, qkv_weight, out_weight, down_weight)],
        parts,
        own_width,
        length,
        reps,
        n,
    )
    gate_w, qkv_w, out_w, down_w = (w.reshape(-1, w.shape[-1]) for w in wholes)
    stream0 = stream0[None]
    images = n * batch
    tokens = images * length
    every_fact, facts = facts, facts[lax.axis_index("rep")]
    gains32 = facts[:, 5:8, :own_width].transpose(1, 0, 2).reshape(3, width)
    all_codes = facts[:, 2:4].reshape(images, length).astype(jnp.int32)
    previous = facts[:, 0:2].reshape(tokens).astype(jnp.int32)
    all_classes = facts[:, 4, 0].astype(jnp.int32)
    all_lengths = facts[:, 4, 1].astype(jnp.int32)
    all_counted = (jnp.arange(length)[None, :] < all_lengths[:, None]).astype(F32)
    own_ids = jnp.arange(own_rows) + me * own_rows
    lookup = (previous[:, None] == own_ids[None, :]).astype(BF)

    normed1, inverse1 = norm_forward(stream0, gains32[0])
    normed1 = normed1.astype(BF)
    mixed = dot("btd,ed->bte", normed1, qkv_w)
    cosine, sine = rotary_tables(length, HEAD_DIM)
    split4 = (batch, length, heads, HEAD_DIM)
    queries = rotate(mixed[..., :width].reshape(split4), cosine, sine).astype(BF)
    keys_rot = rotate(mixed[..., width : 2 * width].reshape(split4), cosine, sine).astype(BF)
    values = mixed[..., 2 * width :].reshape(split4).astype(BF)
    scores = attention_scores(queries, keys_rot)
    top = jnp.max(scores, -1, keepdims=True)
    expo = jnp.exp(scores - top)
    probs32 = expo / jnp.sum(expo, -1, keepdims=True)
    probs = probs32.astype(BF)
    attended = dot("bhqk,bkhd->bqhd", probs, values).astype(BF).reshape(batch, length, width)
    stream1 = stream0 + dot("btd,ed->bte", attended, out_w)
    normed2, inverse2 = norm_forward(stream1, gains32[1])
    normed2 = normed2.astype(BF)
    gated = dot("btd,fd->btf", normed2, gate_w)
    gate_part = gated[..., :hidden_width]
    up_part = gated[..., hidden_width:]
    hidden = (jax.nn.silu(gate_part) * up_part).astype(BF)
    stream2 = stream1 + dot("btf,df->btd", hidden, down_w)
    normed3, inverse3 = norm_forward(stream2, gains32[2])
    normed3 = normed3.astype(BF)

    head_b = head_weight.astype(BF)
    in_kernel = reps == 2 and size_of(head_scratch(n, length, width, own_rows, reps)[0]) < 52 * 2**20
    if in_kernel:
        grad_normed3, grad_head, totals = head_phase(normed3[0], head_b, every_fact, reps, n)
        grad_normed3 = grad_normed3[None]
        loss_sum, token_count = totals[0, 0], totals[1, 0]
        grad_head = grad_head.astype(F32) + lax.ppermute(grad_head, "rep", [(0, 1), (1, 0)]).astype(F32)
    else:
        token_count = lax.psum(jnp.sum(all_counted), "rep")
        normed3_all = lax.all_gather(normed3, "fsdp", axis=0, tiled=True).reshape(tokens, width)
        logits = dot("td,vd->tv", normed3_all, head_b)
        onehot = all_codes.reshape(tokens)[:, None] == own_ids[None, :]
        local_top = jnp.max(logits, -1)
        local_sum = jnp.sum(jnp.exp(logits - local_top[:, None]), -1)
        local_pick = jnp.sum(jnp.where(onehot, logits, 0.0), -1)
        stats = lax.all_gather(jnp.stack([local_top, local_sum, local_pick]), "fsdp", axis=0)
        ltop = jnp.max(stats[:, 0], 0)
        lse = jnp.log(jnp.sum(stats[:, 1] * jnp.exp(stats[:, 0] - ltop[None]), 0)) + ltop
        picked = jnp.sum(stats[:, 2], 0)
        loss_sum = lax.psum(jnp.sum(jnp.where(all_counted.reshape(tokens) > 0, lse - picked, 0.0)), "rep")
        weight_t = all_counted.reshape(tokens) * (1.0 / token_count)
        soft = jnp.exp(logits - lse[:, None])
        grad_logits = ((soft - onehot.astype(F32)) * weight_t[:, None]).astype(BF)
        grad_normed3 = dot("tv,vd->td", grad_logits, head_b).astype(BF).reshape(images, length, width)
        grad_normed3 = lax.psum_scatter(grad_normed3, "fsdp", scatter_dimension=0, tiled=True)
        grad_normed3 = grad_normed3.astype(F32)
        grad_head = dot("tv,td->vd", grad_logits, normed3_all)

    grad_stream2, gain_three = norm_backward(stream2, inverse3, gains32[2], grad_normed3)
    grad_branch = grad_stream2.astype(BF)
    grad_down = dot("btd,btf->df", grad_branch, hidden)
    grad_hidden = dot("btd,df->btf", grad_branch, down_w)
    sigma = jax.nn.sigmoid(gate_part)
    grad_gate = grad_hidden * up_part * sigma * (1.0 + gate_part * (1.0 - sigma))
    grad_up = grad_hidden * gate_part * sigma
    grad_gated = jnp.concatenate([grad_gate, grad_up], -1).astype(BF)
    grad_gate_up = dot("btf,btd->fd", grad_gated, normed2)
    grad_normed2 = dot("btf,fd->btd", grad_gated, gate_w)
    grad_middle, gain_two = norm_backward(stream1, inverse2, gains32[1], grad_normed2)
    grad_stream1 = grad_stream2 + grad_middle
    grad_attn = grad_stream1.astype(BF)
    grad_out = dot("bte,btd->ed", grad_attn, attended)
    grad_attended = dot("bte,ed->btd", grad_attn, out_w).astype(BF).reshape(split4)
    grad_probs = dot("bqhd,bkhd->bhqk", grad_attended, values)
    grad_values = dot("bhqk,bqhd->bkhd", probs, grad_attended)
    grad_scores = probs32 * (grad_probs - jnp.sum(probs32 * grad_probs, -1, keepdims=True))
    grad_scores = grad_scores.astype(BF)
    scale = HEAD_DIM ** (-0.5)
    grad_queries = dot("bhqk,bkhd->bqhd", grad_scores, keys_rot) * scale
    grad_keys = dot("bhqk,bqhd->bkhd", grad_scores, queries) * scale
    grad_mixed = jnp.concatenate(
        [
            rotate_back(grad_queries, cosine, sine).reshape(batch, length, width),
            rotate_back(grad_keys, cosine, sine).reshape(batch, length, width),
            grad_values.reshape(batch, length, width),
        ],
        -1,
    ).astype(BF)
    grad_qkv = dot("bte,btd->ed", grad_mixed, normed1)
    grad_normed1 = dot("bte,ed->btd", grad_mixed, qkv_w)
    grad_first, gain_one = norm_backward(stream0, inverse1, gains32[0], grad_normed1)
    grad_stream0 = grad_stream1 + grad_first

    grad_gains = jnp.stack([gain_one, gain_two, gain_three])
    if in_kernel:
        gain_blocks = jnp.pad(
            grad_gains.reshape(3, n, own_width).transpose(1, 0, 2).astype(BF),
            ((0, 0), (0, 13), (0, 128 - own_width)),
        )
        blocks = [
            g.astype(BF).reshape(n, -1, g.shape[-1])
            for g in (grad_gate_up, grad_qkv, grad_out, grad_down)
        ]
        sums, grad_codes, first_rows = tail_phase(
            grad_stream0[0].astype(BF),
            every_fact,
            blocks + [gain_blocks],
            (True, False, False, False, False),
            own_rows,
            n,
        )
        grad_gate_up, grad_qkv, grad_out, grad_down, gain_part = sums
        grad_gains = gain_part[:3, :own_width]
        class_part = lax.dynamic_slice(
            first_rows[:, :, 0].reshape(-1, width), (0, me * own_width), (reps * n, own_width)
        )
        every_class = every_fact[:, :, 4, 0].reshape(-1).astype(jnp.int32)
        class_spot = (every_class[:, None] == jnp.arange(table_rows)[None, :]).astype(BF)
        grad_classes = dot("iv,id->vd", class_spot, class_part.astype(BF))
    else:
        blocks = [
            g.astype(BF).reshape(n, -1, g.shape[-1]) for g in (grad_qkv, grad_gate_up, grad_out, grad_down)
        ]
        layer_part = lax.psum_scatter(pack_rows(*blocks), "fsdp", scatter_dimension=0, tiled=False)
        rows_all = lax.all_gather(grad_stream0.astype(BF), "fsdp", axis=0, tiled=True)
        grad_codes = dot("tv,td->vd", lookup, rows_all.reshape(tokens, width))
        class_part = lax.dynamic_slice(rows_all[:, 0], (0, me * own_width), (images, own_width))
        class_spot = (all_classes[:, None] == jnp.arange(table_rows)[None, :]).astype(BF)
        grad_classes = dot("iv,id->vd", class_spot, class_part)
        summed = lax.psum(
            (grad_codes.astype(BF), grad_head.astype(BF), layer_part, grad_classes), "rep"
        )
        grad_codes, grad_head, layer_part, grad_classes = (s.astype(F32) for s in summed)
        grad_gains = lax.psum(grad_gains, ("fsdp", "rep"))
        grad_gains = lax.dynamic_slice(grad_gains, (0, me * own_width), (3, own_width))
        grad_qkv, grad_gate_up, grad_out, grad_down = unpack_rows(layer_part, rows, hidden_width)
    reduced = (
        grad_codes, grad_classes, grad_qkv, grad_out, grad_gate_up, grad_down, grad_head, grad_gains
    )
    squares = jnp.zeros((), F32)
    for grad_piece in reduced:
        squares = squares + jnp.sum(grad_piece * grad_piece)
    grad_norm = jnp.sqrt(sum_over_fsdp(squares, n))
    factor = jnp.minimum(1.0, 1.0 / CLIP_INV / (grad_norm + 1e-06))
    results = [loss_sum, token_count, grad_norm]
    for index in range(8):
        results.extend(
            adam_update(
                masters[index],
                firsts[index],
                seconds[index],
                reduced[index] * factor,
                rates[index],
                decays[index],
            )
        )
    return tuple(results)


def solution(mesh):
    split = P(("fsdp", "rep"))
    by_row, by_column = P("fsdp", None), P(None, "fsdp")
    weights = (by_row,) * 3 + (by_column,) * 3 + (by_row,) * 15 + (by_column,) * 3
    return jax.shard_map(
        local,
        mesh=mesh,
        in_specs=(split, split, P(("fsdp", "rep"), None), split) + weights,
        out_specs=(P(), P(), P()) + weights,
        check_vma=False,
    )
```

```python
import functools
import math

import jax
import jax.numpy as jnp
from jax import lax
from jax.experimental import pallas as pl
from jax.experimental.pallas import tpu as pltpu
from jax.sharding import PartitionSpec as P

HEAD_DIM = 64
CLIP_INV = 500
STEP = 10
NORM_EPS = 1e-05
BETA_ONE = 0.5
BETA_TWO = 0.5
ADAM_EPS = 1e-08
BF = jnp.bfloat16
F32 = jnp.float32
MESH = pl.DeviceIdType.MESH


def rotary_tables(length, width):
    half = width // 2
    freq = 10000.0 ** (-jnp.arange(half, dtype=F32) * 2.0 / width)
    angles = jnp.arange(length, dtype=F32)[:, None] * freq[None, :]
    cosine = jnp.concatenate([jnp.cos(angles), jnp.cos(angles)], -1)
    sine = jnp.concatenate([jnp.sin(angles), jnp.sin(angles)], -1)
    return (cosine, sine)


def rotate(values, cosine, sine):
    half = values.shape[-1] // 2
    swapped = jnp.concatenate([-values[..., half:], values[..., :half]], -1)
    return values * cosine[:, None, :] + swapped * sine[:, None, :]


def rotate_back(grads, cosine, sine):
    half = grads.shape[-1] // 2
    scaled = grads * sine[:, None, :]
    return grads * cosine[:, None, :] + jnp.concatenate(
        [scaled[..., half:], -scaled[..., :half]], -1
    )


def norm_forward(stream, gain):
    inverse = lax.rsqrt(jnp.mean(stream * stream, -1, keepdims=True) + NORM_EPS)
    return (stream * inverse * gain, inverse)


def norm_backward(stream, inverse, gain, grad_out):
    weighted = grad_out * gain
    inner = jnp.mean(weighted * stream, -1, keepdims=True)
    grad_in = inverse * weighted - stream * inverse * inverse * inverse * inner
    grad_gain = jnp.sum(grad_out * stream * inverse, axis=(0, 1))
    return (grad_in, grad_gain)


def attention_scores(queries, keys_rot):
    length = queries.shape[1]
    scores = jnp.einsum(
        "bqhd,bkhd->bhqk", queries, keys_rot, preferred_element_type=F32
    ) * HEAD_DIM ** (-0.5)
    causal = jnp.arange(length)[:, None] >= jnp.arange(length)[None, :]
    return jnp.where(causal, scores, -1e30)


def column_blocks(width, total):
    return [(at, min(width, total - at)) for at in range(0, total, width)]


def pack_rows(qkv, gate, out, down):
    width = qkv.shape[-1]
    parts = [qkv, gate, out]
    for at, size in column_blocks(width, down.shape[-1]):
        block = down[..., at : at + size]
        if size < width:
            pad = [(0, 0)] * (block.ndim - 1) + [(0, width - size)]
            block = jnp.pad(block, pad)
        parts.append(block)
    return jnp.concatenate(parts, -2)


def unpack_rows(packed, rows, hidden_width):
    width = packed.shape[-1]
    at, parts = 0, []
    for count in rows[:3]:
        parts.append(packed[..., at : at + count, :])
        at += count
    blocks = []
    for _, size in column_blocks(width, hidden_width):
        blocks.append(packed[..., at : at + rows[3], :size])
        at += rows[3]
    parts.append(jnp.concatenate(blocks, -1))
    return parts


def geometry(n):
    chips = n // 2
    y_size = 1 << ((chips.bit_length() - 1) // 2)
    return chips // y_size, y_size


def where_am_i(z_size, y_size):
    me = lax.axis_index("fsdp")
    return me, me // (2 * y_size), (me // 2) % y_size, me % 2


def send(src, dst, sems, index, device):
    pltpu.make_async_remote_copy(
        src_ref=src, dst_ref=dst, send_sem=sems.at[(0,) + index], recv_sem=sems.at[(1,) + index],
        device_id=device, device_id_type=MESH,
    ).start()


def arrival(dst, sems, index):
    pltpu.make_async_copy(dst, dst, sems.at[(1,) + index]).wait()


def departure(src, sems, index):
    pltpu.make_async_copy(src, src, sems.at[(0,) + index]).wait()


def weight_pieces(rows, reps):
    gate = rows[0]
    cut = gate * 15 // 16 // 16 * 16
    middle = cut // 2 // 16 * 16
    one = 1 % reps
    return (
        (2, 0, rows[2], 2 % reps),
        (0, cut, gate - cut, one),
        (0, 0, middle, 0),
        (3, 0, rows[3], 3 % reps),
        (0, middle, cut - middle, 0),
        (1, 0, rows[1], one),
    )


def front(facts, code_table, class_b, weights, own_width, length, reps, n):
    z_size, y_size = geometry(n)
    width = code_table.shape[1]
    count = len(weights)
    pieces = weight_pieces([w.shape[0] for w in weights], reps)
    many = len(pieces)
    spots = z_size * y_size
    block = (length, width)
    vmem, hbm = pl.BlockSpec(memory_space=pltpu.VMEM), pl.BlockSpec(memory_space=pl.ANY)
    dma = pltpu.SemaphoreType.DMA
    outs = pl.pallas_call(
        functools.partial(front_kernel, z_size, y_size, reps, own_width, pieces, count),
        out_shape=[jax.ShapeDtypeStruct((n,) + w.shape, BF) for w in weights]
        + [jax.ShapeDtypeStruct(block, F32), jax.ShapeDtypeStruct((reps, n, 8, 128), F32)],
        in_specs=[vmem] * (3 + count),
        out_specs=[hbm] * count + [vmem] * 2,
        scratch_shapes=[
            pltpu.VMEM(code_table.shape, BF),
            pltpu.VMEM((128, n * 8), F32),
            pltpu.VMEM((spots,) + block, BF),
            pltpu.VMEM((spots,) + block, BF),
            pltpu.VMEM((spots,) + block, BF),
            pltpu.VMEM((z_size, y_size) + block, BF),
            pltpu.VMEM((z_size,) + block, BF),
            dma((2, n)),
            dma((2, reps)),
            dma((2, many, 2, z_size)),
            dma((2, many, z_size, y_size)),
            dma((2, many, z_size, y_size, reps)),
            dma((2, many, z_size, y_size)),
            dma((count,)),
            dma((2, spots)),
            dma((2, z_size, y_size)),
            dma((2, z_size)),
        ]
        + [pltpu.VMEM(w.shape, BF) for w in weights],
        compiler_params=pltpu.CompilerParams(
            collective_id=0, has_side_effects=True, vmem_limit_bytes=60 * 2**20
        ),
        name="front",
    )(facts, code_table, class_b, *weights)
    return outs[:count], outs[count], outs[count + 1]


class Place:
    def __init__(self, z_size, y_size, reps):
        self.z_size, self.y_size, self.reps = z_size, y_size, reps
        self.n = z_size * y_size * 2
        self.me, self.z, self.y, self.core = where_am_i(z_size, y_size)
        self.x = lax.axis_index("rep")

    def at(self, dz, dy, other=0):
        c = 1 - self.core if other else self.core
        z, y = lax.rem(self.z + dz, self.z_size), lax.rem(self.y + dy, self.y_size)
        return (z * self.y_size + y) * 2 + c

    def plane(self, z, dy=0, other=0):
        c = 1 - self.core if other else self.core
        return (z * self.y_size + lax.rem(self.y + dy, self.y_size)) * 2 + c

    def twin(self):
        return (self.at(0, 0, 1), self.x)

    def greet(self, everyone):
        barrier = pltpu.get_barrier_semaphore()
        if everyone:
            group = [lax.rem(self.me + k, self.n) for k in range(1, self.n)]
        else:
            group = [self.at(dz, 0) for dz in range(1, self.z_size)]
            group += [self.at(0, dy) for dy in range(1, self.y_size)] + [self.at(0, 0, 1)]
        peers = [(p, self.x) for p in group]
        peers += [(self.me, lax.rem(self.x + k, self.reps)) for k in range(1, self.reps)]
        for peer in peers:
            pl.semaphore_signal(barrier, inc=1, device_id=peer, device_id_type=MESH)
        pl.semaphore_wait(barrier, len(peers))


class Spread:
    def __init__(self, place, whole, z_sems, y_sems, c_sems, x_sems=None, part=None, rows=None):
        self.p, self.whole, self.part, self.rows = place, whole, part, rows
        self.z_sems, self.y_sems, self.c_sems, self.x_sems = z_sems, y_sems, c_sems, x_sems

    def block(self, z, dy=0, other=0):
        block = self.whole.at[self.p.plane(z, dy, other)]
        return block if self.rows is None else block.at[pl.ds(*self.rows)]

    def in_part(self, act):
        if self.part is None:
            act()
        else:
            pl.when(self.p.x == self.part)(act)

    def hand_over(self, z, dy, src, dst):
        p = self.p
        if self.part is not None:
            for dx in range(1, p.reps):
                send(src, dst, self.x_sems, (z, dy, dx), (p.me, lax.rem(p.x + dx, p.reps)))
        send(src, dst, self.c_sems, (z, dy), p.twin())

    def pass_on(self, z, src, up, down):
        p = self.p
        dst = self.block(z)
        if up:

            @pl.when(p.z + 1 < p.z_size)
            def _():
                send(src, dst, self.z_sems, (0, z), (p.plane(p.z + 1), p.x))

        if down:

            @pl.when(p.z >= 1)
            def _():
                send(src, dst, self.z_sems, (1, z), (p.plane(p.z - 1), p.x))

        for dy in range(1, p.y_size):
            send(src, dst, self.y_sems, (z, dy), (p.at(0, dy), p.x))

    def start(self, own):
        self.in_part(lambda: self.pass_on(self.p.z, own, True, True))
        send(own, self.block(self.p.z), self.c_sems, (self.p.z, 0), self.p.twin())

    def near(self, s, act):
        p = self.p
        if s == 0:
            act(p.z)
            return

        @pl.when(p.z - s >= 0)
        def _():
            act(p.z - s)

        @pl.when(p.z + s < p.z_size)
        def _():
            act(p.z + s)

    def step_z(self, s):
        p = self.p

        def take(z, up):
            block = self.block(z)
            arrival(block, self.z_sems, (1 - int(up), z))
            self.pass_on(z, block, up, not up)
            self.hand_over(z, 0, block, block)

        def act():
            @pl.when(p.z - s >= 0)
            def _():
                take(p.z - s, True)

            @pl.when(p.z + s < p.z_size)
            def _():
                take(p.z + s, False)

        self.in_part(act)

    def step_y(self, s):
        def take(z):
            for dy in range(1, self.p.y_size):
                block = self.block(z, self.p.y_size - dy)
                arrival(block, self.y_sems, (z, dy))
                self.hand_over(z, dy, block, block)

        self.in_part(lambda: self.near(s, take))

    def step_x(self, s):
        p = self.p

        def take(z):
            for dy in range(0 if s else 1, p.y_size):
                block = self.block(z, p.y_size - dy)
                arrival(block, self.x_sems, (z, dy, lax.rem(p.x - self.part + p.reps, p.reps)))
                send(block, block, self.c_sems, (z, dy), p.twin())

        pl.when(p.x != self.part)(lambda: self.near(s, take))

    def take_twin(self, z):
        for dy in range(self.p.y_size):
            arrival(self.block(z, self.p.y_size - dy, 1), self.c_sems, (z, dy))

    def finish(self):
        p = self.p
        block = self.block(p.z)
        for z in range(p.z_size):
            for dy in range(p.y_size):
                departure(block, self.c_sems, (z, dy))

        def act():
            for z in range(p.z_size):

                @pl.when(jnp.logical_and(p.z + 1 < p.z_size, z <= p.z))
                def _():
                    departure(block, self.z_sems, (0, z))

                @pl.when(jnp.logical_and(p.z >= 1, z >= p.z))
                def _():
                    departure(block, self.z_sems, (1, z))

                for dy in range(1, p.y_size):
                    departure(block, self.y_sems, (z, dy))
                if self.part is None:
                    continue
                for dy in range(p.y_size):
                    for dx in range(1, p.reps):
                        if dy:
                            departure(block, self.x_sems, (z, dy, dx))
                        else:

                            @pl.when(z != p.z)
                            def _():
                                departure(block, self.x_sems, (z, dy, dx))

        self.in_part(act)


def front_kernel(z_size, y_size, reps, own_width, pieces, count, facts, code_table, class_b, *refs):
    masters, refs = refs[:count], refs[count:]
    wholes, refs = refs[:count], refs[count:]
    weights, refs = refs[-count:], refs[:-count]
    (stream, facts_all, code_b, turned, acc, core_out, core_in, y_in, z_in,
     fact_sems, rep_sems, z_sems, y_sems, x_sems, c_sems, own_sems, rc_sems, ry_sems, rz_sems) = refs
    p = Place(z_size, y_size, reps)
    n, me, x = p.n, p.me, p.x
    length, width = stream.shape
    own_rows = code_table.shape[0]
    p.greet(True)

    for k in range(1, n):
        send(facts, facts_all.at[x, me], fact_sems, (k,), (lax.rem(me + k, n), x))
    facts_all[x, me] = facts[...]
    for k in range(count):
        weights[k][...] = masters[k][...].astype(BF)
    spreads = []
    for i, (k, start, size, part) in enumerate(pieces):
        sems = [group.at[:, i] for group in (z_sems, y_sems, c_sems, x_sems)]
        spreads.append(Spread(p, wholes[k], *sems, part, (start, size)))
        spreads[i].start(weights[k].at[pl.ds(start, size)])
    for k in range(count):
        pltpu.make_async_copy(weights[k], wholes[k].at[me], own_sems.at[k]).start()
    code_b[...] = code_table[...].astype(BF)

    for k in range(1, n):
        arrival(facts_all.at[x, lax.rem(me - k + n, n)], fact_sems, (k,))
    for k in range(1, reps):
        send(facts_all.at[x], facts_all.at[x], rep_sems, (k,), (me, lax.rem(x + k, reps)))
    turned[...] = jnp.transpose(facts_all[x].reshape(n * 8, 128))
    lane = lax.broadcasted_iota(jnp.int32, (128, n * 8), 1)
    class_iota = lax.broadcasted_iota(jnp.int32, (16, class_b.shape[1]), 1).astype(F32)
    row_iota = lax.broadcasted_iota(jnp.int32, (length // 2, own_rows), 1) + me * own_rows
    row_iota = row_iota.astype(F32)

    def found(image, out):
        cls = jnp.sum(jnp.where(lane[:1] == image * 8 + 4, turned[:1, :], 0.0), -1, keepdims=True)
        spot = jnp.where(class_iota == cls, 1.0, 0.0).astype(BF)
        row = lax.dot_general(
            spot, class_b[...], (((1,), (1,)), ((), ())), preferred_element_type=F32
        )
        row = jnp.concatenate([row, jnp.zeros((16, width - row.shape[1]), F32)], -1)
        row = pltpu.roll(row, me * own_width, 1)
        for half in range(2):
            ids = jnp.sum(jnp.where(lane == image * 8 + half, turned[...], 0.0), -1, keepdims=True)
            spot = jnp.where(row_iota == ids, 1.0, 0.0).astype(BF)
            rows = jnp.dot(spot, code_b[...], preferred_element_type=F32)
            out[pl.ds(half * (length // 2), length // 2)] = rows.astype(BF)
            if half == 0:
                first = lax.broadcasted_iota(jnp.int32, (16, width), 0) == 0
                head = jnp.where(first, row, rows[:16])
                out[pl.ds(0, 16)] = head.astype(BF)

    def look_up(dz):
        def body(j, carry):
            dy = y_size - 1 - j
            slot = dz * y_size + dy
            found(p.at(dz, dy, 1), core_out.at[slot])
            send(core_out.at[slot], core_in.at[slot], rc_sems, (slot,), p.twin())
            found(p.at(dz, dy), acc.at[slot])
            return carry

        lax.fori_loop(0, y_size, body, 0)

    def twin_sum(dz):
        for dy in range(y_size - 1, -1, -1):
            slot = dz * y_size + dy
            arrival(core_in.at[slot], rc_sems, (slot,))
            acc[slot] = (acc[slot].astype(F32) + core_in[slot].astype(F32)).astype(BF)
            if dy:
                send(acc.at[slot], y_in.at[dz, dy], ry_sems, (dz, dy), (p.at(0, dy), x))

    def y_sum(dz):
        slot = dz * y_size
        total = acc[slot].astype(F32)
        for dy in range(1, y_size):
            arrival(y_in.at[dz, dy], ry_sems, (dz, dy))
            total = total + y_in[dz, dy].astype(F32)
        acc[slot] = total.astype(BF)
        if dz:
            send(acc.at[slot], z_in.at[dz], rz_sems, (dz,), (p.at(dz, 0), x))

    for s in range(1, z_size + 1):
        for spread in spreads:
            if s < z_size:
                spread.step_z(s)
        for spread in spreads:
            spread.step_y(s - 1)
        look_up(z_size - s)
        if s >= 2:
            twin_sum(z_size - s + 1)
        if s >= 3:
            y_sum(z_size - s + 2)
    twin_sum(0)
    for spread in spreads:
        spread.step_x(0)
    y_sum(1)
    for s in range(1, z_size - 1):
        for spread in spreads:
            spread.step_x(s)
    y_sum(0)
    total = acc[0].astype(F32)
    for dz in range(1, z_size):
        arrival(z_in.at[dz], rz_sems, (dz,))
        total = total + z_in[dz].astype(F32)
    stream[...] = total
    for spread in spreads:
        spread.step_x(z_size - 1)

    for k in range(1, reps):
        arrival(facts_all.at[x], rep_sems, (k,))
        departure(facts_all.at[x], rep_sems, (k,))
    for k in range(1, n):
        departure(facts, fact_sems, (k,))
    for dz in range(z_size):
        for dy in range(y_size):
            slot = dz * y_size + dy
            departure(core_out.at[slot], rc_sems, (slot,))
            if dy:
                departure(acc.at[slot], ry_sems, (dz, dy))
            elif dz:
                departure(acc.at[slot], rz_sems, (dz,))
    for k in range(count):
        pltpu.make_async_copy(weights[k], wholes[k].at[me], own_sems.at[k]).wait()
    for spread in spreads:
        for z in range(z_size):
            spread.take_twin(z)
        spread.finish()


def head_kernel(z_size, y_size, reps, normed3, head_weight, facts, grad_normed3, grad_head, totals,
                whole, logits, grads, turned, marks, stats_in, lse_all, acc, core_out, core_in, y_in, z_in,
                loss_in, head_b, z_sems, y_sems, c_sems, st_sems, ls_sems, rc_sems, ry_sems, rz_sems, lo_sems):
    p = Place(z_size, y_size, reps)
    n, me, x = p.n, p.me, p.x
    length, width = normed3.shape
    half = length // 2
    own_rows = head_weight.shape[0]
    p.greet(True)
    spread = Spread(p, whole, z_sems, y_sems, c_sems)
    spread.start(normed3)
    head_b[...] = head_weight[...].astype(BF)
    whole[me] = normed3[...]
    own_facts = facts.at[x]
    turned[...] = jnp.transpose(own_facts[...].reshape(n * 8, 128))
    lane = lax.broadcasted_iota(jnp.int32, (128, n * 8), 1)
    full_lane = lax.broadcasted_iota(jnp.int32, (length, n * 8), 1)
    column_iota = (lax.broadcasted_iota(jnp.int32, (length, own_rows), 1) + me * own_rows).astype(F32)
    token = lax.broadcasted_iota(jnp.int32, (length, 1), 0).astype(F32)
    every = facts[...].reshape(reps * n * 8, 128)
    row8 = lax.rem(lax.broadcasted_iota(jnp.int32, every.shape, 0), 8)
    spot = jnp.logical_and(row8 == 4, lax.broadcasted_iota(jnp.int32, every.shape, 1) == 1)
    token_count = jnp.sum(jnp.sum(jnp.where(spot, every, 0.0), 0, keepdims=True), 1, keepdims=True)
    inv_count = 1.0 / token_count

    def codes_of(image):
        parts = [
            jnp.sum(jnp.where(lane == image * 8 + 2 + h, turned[...], 0.0), -1, keepdims=True)
            for h in range(2)
        ]
        return jnp.concatenate(parts, 0)

    marks[...] = jnp.zeros_like(marks)

    def forward(image):
        out = lax.dot_general(
            whole[image], head_b[...], (((1,), (1,)), ((), ())), preferred_element_type=F32
        )
        logits[image] = out
        top = jnp.max(out, -1, keepdims=True)
        total = jnp.sum(jnp.exp(out - top), -1, keepdims=True)
        pick = jnp.sum(jnp.where(column_iota == codes_of(image), out, 0.0), -1, keepdims=True)
        old = marks[...]
        old = jnp.where(full_lane == image * 8, top, old)
        old = jnp.where(full_lane == image * 8 + 1, total, old)
        marks[...] = jnp.where(full_lane == image * 8 + 2, pick, old)

    def forward_column(z, first, last):
        def body(j, carry):
            forward(p.plane(z, lax.rem(y_size - j // 2, y_size), 0) + lax.rem(j, 2) * (1 - 2 * p.core))
            return carry

        lax.fori_loop(first * 2, last * 2, body, 0)

    arrival(spread.block(p.z, 0, 1), c_sems, (p.z, 0))
    forward_column(p.z, 0, 1)

    def one(z, s):
        arrival(spread.block(z, 0, 1), c_sems, (z, 0))
        forward_column(z, 0, 1)

    def other(z):
        for dy in range(1, y_size):
            arrival(spread.block(z, y_size - dy, 1), c_sems, (z, dy))
        forward_column(z, 1, y_size)

    def both(s, act):
        if s == 0:
            act(p.z)
            return

        @pl.when(p.z - s >= 0)
        def _():
            act(p.z - s)

        @pl.when(p.z + s < z_size)
        def _():
            act(p.z + s)

    for s in range(1, z_size + 1):
        if s < z_size:
            spread.step_z(s)
        spread.step_y(s - 1)
        if s < z_size:
            both(s, lambda z: one(z, s))
        both(s - 1, other)

    tiles = jnp.transpose(marks[...]).reshape(n, 8, length)
    stats_in[1] = tiles
    for k in range(1, n):
        peer = lax.rem(me + k, n)
        send(stats_in.at[1, peer], stats_in.at[0, me], st_sems, (k,), (peer, x))
    stats_in[0, me] = stats_in[1, me]
    for k in range(1, n):
        arrival(stats_in.at[0, 0], st_sems, (k,))
    tops = stats_in[0, :, 0, :]
    sums = stats_in[0, :, 1, :]
    picks = stats_in[0, :, 2, :]
    top = jnp.max(tops, 0, keepdims=True)
    lse = jnp.log(jnp.sum(sums * jnp.exp(tops - top), 0, keepdims=True)) + top
    pick = jnp.sum(picks, 0, keepdims=True)
    here = own_facts[me]
    counted = lax.broadcasted_iota(jnp.int32, (1, length), 1).astype(F32) < here[4:5, 1:2]
    loss = jnp.where(counted, lse - pick, 0.0)
    lse_all[me] = jnp.concatenate([lse, loss, jnp.zeros((6, length), F32)], 0)
    for k in range(1, n):
        peer = lax.rem(me + k, n)
        send(lse_all.at[me], lse_all.at[me], ls_sems, (k,), (peer, x))
    for k in range(1, n):
        arrival(lse_all.at[0], ls_sems, (k,))
    table = lse_all[...].reshape(n * 8, length)
    row8 = lax.rem(lax.broadcasted_iota(jnp.int32, table.shape, 0), 8)
    group = jnp.sum(jnp.sum(jnp.where(row8 == 1, table, 0.0), 0, keepdims=True), 1, keepdims=True)
    loss_in[x] = jnp.broadcast_to(group, (8, 128))
    for k in range(1, reps):
        peer = (me, lax.rem(x + k, reps))
        send(loss_in.at[x], loss_in.at[x], lo_sems, (k,), peer)
    marks[...] = jnp.transpose(table)

    def backward(image, out):
        lse_t = jnp.sum(jnp.where(full_lane == image * 8, marks[...], 0.0), -1, keepdims=True)
        size = jnp.sum(jnp.where(lane[:8] == image * 8 + 4, turned[:8, :], 0.0), -1, keepdims=True)
        weight = jnp.where(token < size[1:2], inv_count, 0.0)
        hot = jnp.where(column_iota == codes_of(image), 1.0, 0.0)
        grad = ((jnp.exp(logits[image] - lse_t) - hot) * weight).astype(BF)
        grads[image] = grad
        out[...] = jnp.dot(grad, head_b[...], preferred_element_type=F32).astype(BF)

    last = z_size - 1

    def far(j):
        return last - j // y_size, lax.rem(j, y_size)

    def first_pass(j, carry):
        dz, dyy = far(j)
        dy = y_size - 1 - dyy
        slot = dz * y_size + dy
        backward(p.at(dz, dy, 1), core_out.at[slot])
        send(core_out.at[slot], core_in.at[slot], rc_sems, (slot,), p.twin())
        backward(p.at(dz, dy), acc.at[slot])
        return carry

    def twin_sum(slot):
        arrival(core_in.at[slot], rc_sems, (slot,))
        acc[slot] = (acc[slot].astype(F32) + core_in[slot].astype(F32)).astype(BF)

    def y_sum(dz):
        slot = dz * y_size
        total = acc[slot].astype(F32)
        for dy in range(1, y_size):
            arrival(y_in.at[dz, dy], ry_sems, (dz, dy))
            total = total + y_in[dz, dy].astype(F32)
        acc[slot] = total.astype(BF)

    def round_of(g, carry):
        dz = last - g

        def per_dy(i, c):
            return first_pass(g * y_size + i, c)

        lax.fori_loop(0, y_size, per_dy, 0)
        for dy in range(y_size - 1, -1, -1):
            slot = dz * y_size + dy
            twin_sum(slot)
            if dy:
                send(acc.at[slot], y_in.at[dz, dy], ry_sems, (dz, dy), (p.at(0, dy), x))

        @pl.when(g >= 1)
        def _():
            y_sum(dz + 1)
            send(acc.at[(dz + 1) * y_size], z_in.at[dz + 1], rz_sems, (dz + 1,), (p.at(dz + 1, 0), x))

        return carry

    lax.fori_loop(0, z_size, round_of, 0)

    blocks = 4
    rows = own_rows // blocks
    for r in range(blocks):

        def add(image, total):
            return total + lax.dot_general(
                grads[image, :, r * rows : (r + 1) * rows], whole[image],
                (((0,), (0,)), ((), ())), preferred_element_type=F32,
            )

        total = lax.fori_loop(0, n, add, jnp.zeros((rows, width), F32))
        grad_head[r * rows : (r + 1) * rows] = total.astype(BF)
    y_sum(0)
    total = acc[0].astype(F32)
    for dz in range(1, z_size):
        arrival(z_in.at[dz], rz_sems, (dz,))
        total = total + z_in[dz].astype(F32)
    grad_normed3[...] = total
    for k in range(1, reps):
        arrival(loss_in.at[0], lo_sems, (k,))
    loss_sum = loss_in[0]
    for k in range(1, reps):
        loss_sum = loss_sum + loss_in[k]
    totals[...] = jnp.where(
        lax.broadcasted_iota(jnp.int32, (8, 128), 0) == 0, loss_sum, token_count
    )

    spread.finish()
    for k in range(1, n):
        departure(stats_in.at[0, 0], st_sems, (k,))
        departure(lse_all.at[0], ls_sems, (k,))
    for k in range(1, reps):
        departure(loss_in.at[0], lo_sems, (k,))
    for dz in range(z_size):
        for dy in range(y_size):
            slot = dz * y_size + dy
            departure(core_out.at[slot], rc_sems, (slot,))
            if dy:
                departure(acc.at[slot], ry_sems, (dz, dy))
            elif dz:
                departure(acc.at[slot], rz_sems, (dz,))


def head_scratch(n, length, width, own_rows, reps):
    z_size, y_size = geometry(n)
    spots = z_size * y_size
    dma = pltpu.SemaphoreType.DMA
    buffers = [
        ((n, length, width), BF),
        ((n, length, own_rows), F32),
        ((n, length, own_rows), BF),
        ((128, n * 8), F32),
        ((length, n * 8), F32),
        ((2, n, 8, length), F32),
        ((n, 8, length), F32),
        ((spots, length, width), BF),
        ((spots, length, width), BF),
        ((spots, length, width), BF),
        ((z_size, y_size, length, width), BF),
        ((z_size, length, width), BF),
        ((reps, 8, 128), F32),
        ((own_rows, width), BF),
    ]
    sems = [
        dma((2, 2, z_size)), dma((2, z_size, y_size)), dma((2, z_size, y_size)),
        dma((2, n)), dma((2, n)), dma((2, spots)), dma((2, z_size, y_size)), dma((2, z_size)),
        dma((2, reps)),
    ]
    return buffers, sems


def size_of(buffers):
    return sum(math.prod(shape) * jnp.dtype(kind).itemsize for shape, kind in buffers)


def head_phase(normed3, head_weight, facts, reps, n):
    z_size, y_size = geometry(n)
    length, width = normed3.shape
    buffers, sems = head_scratch(n, length, width, head_weight.shape[0], reps)
    vmem = pl.BlockSpec(memory_space=pltpu.VMEM)
    return pl.pallas_call(
        functools.partial(head_kernel, z_size, y_size, reps),
        out_shape=[
            jax.ShapeDtypeStruct((length, width), F32),
            jax.ShapeDtypeStruct(head_weight.shape, BF),
            jax.ShapeDtypeStruct((8, 128), F32),
        ],
        in_specs=[vmem] * 3,
        out_specs=[vmem] * 3,
        scratch_shapes=[pltpu.VMEM(shape, kind) for shape, kind in buffers] + sems,
        compiler_params=pltpu.CompilerParams(
            collective_id=1, has_side_effects=True, vmem_limit_bytes=60 * 2**20
        ),
        name="head",
    )(normed3, head_weight, facts)


def tail_kernel(z_size, y_size, own_width, split, counts, grad_stream0, facts, head_one, head_two, *refs):
    count = len(split)
    grads, refs = refs[:count], refs[count:]
    sums, refs = refs[:count], refs[count:]
    code_sum, class_sum, squares, refs = refs[0], refs[1], refs[2], refs[3:]
    accs, refs = refs[:count], refs[count:]
    core_in, refs = refs[:count], refs[count:]
    x_in, refs = refs[:count], refs[count:]
    y_in, refs = refs[:count], refs[count:]
    z_in, refs = refs[:count], refs[count:]
    trade, refs = refs[:count], refs[count:]
    (whole, code_out, code_in, rows_out, given, z_sems, y_sems, c_sems, own_sems, rc_sems, rx_sems,
     ry_sems, rz_sems, tr_sems, co_sems, fr_sems, sq_sems) = refs
    p = Place(z_size, y_size, 2)
    n, me, x = p.n, p.me, p.x
    length, width = grad_stream0.shape
    own_rows = code_out.shape[0]
    p.greet(True)
    mate = (me, 1 - x)
    spread = Spread(p, whole, z_sems, y_sems, c_sems)
    spread.start(grad_stream0)
    whole[me] = grad_stream0[...]

    def slot_of(dz, dy):
        return dz * y_size + dy

    order = [(dz, dy) for dz in range(z_size - 1, -1, -1) for dy in range(y_size - 1, -1, -1)]
    halved = [k for k in range(count) if split[k]]
    plain = [k for k in range(count) if not split[k]]
    for kinds in (halved, plain):
        for dz, dy in order:
            slot = slot_of(dz, dy)
            for k in kinds:
                send(grads[k].at[p.at(dz, dy, 1)], core_in[k].at[slot], rc_sems, (k, slot), p.twin())
                pltpu.make_async_copy(
                    grads[k].at[p.at(dz, dy)], accs[k].at[slot], own_sems.at[k, slot]
                ).start()

    def part(k, which):
        rows = counts[k] // 2
        return pl.ds(pl.multiple_of(which * rows, rows), rows)

    def ref_of(k, ref, which):
        return ref.at[part(k, which)] if split[k] else ref

    def twin_sums(kinds, dz):
        def body(dy, carry):
            slot = slot_of(dz, dy)
            for k in kinds:
                pltpu.make_async_copy(grads[k].at[0], accs[k].at[slot], own_sems.at[k, slot]).wait()
                arrival(core_in[k].at[slot], rc_sems, (k, slot))
                accs[k][slot] = (accs[k][slot].astype(F32) + core_in[k][slot].astype(F32)).astype(BF)
                if split[k]:
                    send(accs[k].at[slot, part(k, 1 - x)], x_in[k].at[slot], rx_sems, (k, slot), mate)
            return carry

        lax.fori_loop(0, y_size, body, 0)

    def send_y(kinds, dz):
        for dy in range(1, y_size):
            slot = slot_of(dz, dy)
            for k in kinds:
                source = ref_of(k, accs[k].at[slot], x)
                send(source, y_in[k].at[slot], ry_sems, (k, slot), (p.at(0, dy), x))

    def take_x(dz):
        def body(dy, carry):
            slot = slot_of(dz, dy)
            for k in halved:
                arrival(x_in[k].at[slot], rx_sems, (k, slot))
                mine = accs[k].at[slot, part(k, x)]
                mine[...] = (mine[...].astype(F32) + x_in[k][slot].astype(F32)).astype(BF)
            return carry

        lax.fori_loop(0, y_size, body, 0)
        send_y(halved, dz)

    def take_y(kinds, dz):
        for k in kinds:
            mine = ref_of(k, accs[k].at[slot_of(dz, 0)], x)
            total = mine[...].astype(F32)
            for dy in range(1, y_size):
                slot = slot_of(dz, dy)
                arrival(y_in[k].at[slot], ry_sems, (k, slot))
                total = total + y_in[k][slot].astype(F32)
            mine[...] = total.astype(BF)
            if dz:
                send(mine, z_in[k].at[dz], rz_sems, (k, dz), (p.at(dz, 0), x))

    def square(value):
        return jnp.sum(jnp.sum(value * value, 0, keepdims=True), 1, keepdims=True)

    for s in range(1, z_size):
        twin_sums(halved, z_size - s)
        if s == z_size - 1:
            twin_sums(halved, 0)
        spread.step_z(s)
        spread.step_y(s - 1)
        twin_sums(plain, z_size - s)
    send_y(plain, z_size - 1)
    twin_sums(plain, 0)
    take_x(z_size - 1)
    spread.step_y(z_size - 1)
    send_y(plain, z_size - 2)
    take_x(z_size - 2)
    for z in range(z_size):
        spread.take_twin(z)

    rows_out[x] = whole[:, 0:8, :].astype(F32)
    send(rows_out.at[x], rows_out.at[x], fr_sems, (), mate)

    blocks = 4
    rows = own_rows // blocks
    iota = lax.broadcasted_iota(jnp.int32, (rows, length // 2), 0) + me * own_rows

    def code_block(r, carry):
        base = (iota + r * rows).astype(F32)

        def add(image, total):
            ids = facts[x, image]
            hot = jnp.concatenate(
                [jnp.where(base == ids[h : h + 1, :], 1.0, 0.0) for h in range(2)], 1
            ).astype(BF)
            return total + jnp.dot(hot, whole[image], preferred_element_type=F32)

        total = lax.fori_loop(0, n, add, jnp.zeros((rows, width), F32))
        at = pl.ds(pl.multiple_of(r * rows, rows), rows)
        code_out[at] = total.astype(BF)
        send(code_out.at[at], code_in.at[at], co_sems, (r,), mate)
        return carry

    lax.fori_loop(0, blocks // 2, code_block, 0)
    take_y(plain, z_size - 1)
    for dz in range(z_size - 3, -1, -1):
        send_y(plain, dz)
        take_x(dz)
    take_y(halved, z_size - 1)
    lax.fori_loop(blocks // 2, blocks, code_block, 0)
    for dz in range(z_size - 2, -1, -1):
        take_y(plain, dz)
        take_y(halved, dz)

    total_squares = square(head_one[...].astype(F32) + head_two[...].astype(F32))

    arrival(rows_out.at[1 - x], fr_sems, ())
    firsts = rows_out[:, :, 0, :].reshape(2 * n, width)
    shift = lax.rem(width - me * own_width, width)
    firsts = pltpu.roll(firsts, shift, 1)[:, :128]
    firsts = jnp.where(lax.broadcasted_iota(jnp.int32, firsts.shape, 1) < own_width, firsts, 0.0)
    classes = facts[:, :, 4, :].reshape(2 * n, 128)[:, 0:1]
    class_iota = lax.broadcasted_iota(jnp.int32, (2 * n, class_sum.shape[1]), 1).astype(F32)
    hot = jnp.where(class_iota == classes, 1.0, 0.0).astype(BF)
    class_grad = lax.dot_general(
        firsts.astype(BF), hot, (((0,), (0,)), ((), ())), preferred_element_type=F32
    )
    class_sum[...] = class_grad
    total_squares = total_squares + square(class_grad)

    for k in range(count):
        mine = ref_of(k, accs[k].at[0], x)
        total = mine[...].astype(F32)
        for dz in range(1, z_size):
            arrival(z_in[k].at[dz], rz_sems, (k, dz))
            total = total + z_in[k][dz].astype(F32)
        source = ref_of(k, trade[k].at[0], x)
        source[...] = total.astype(BF)
        target = trade[k].at[0, part(k, x)] if split[k] else trade[k].at[1]
        send(source, target, tr_sems, (k,), mate)
    for r in range(blocks):
        at = pl.ds(r * rows, rows)
        arrival(code_in.at[at], co_sems, (r,))
        total = code_out[at].astype(F32) + code_in[at].astype(F32)
        code_sum[at] = total
        total_squares = total_squares + square(total)
    for k in range(count):
        if split[k]:
            arrival(trade[k].at[0, part(k, 1 - x)], tr_sems, (k,))
            total = trade[k][0].astype(F32)
        else:
            arrival(trade[k].at[1], tr_sems, (k,))
            total = trade[k][0].astype(F32) + trade[k][1].astype(F32)
        sums[k][...] = total
        total_squares = total_squares + square(total)

    given[me] = jnp.broadcast_to(total_squares, (8, 128))
    for k in range(1, n):
        send(given.at[me], given.at[me], sq_sems, (k,), (lax.rem(me + k, n), x))

    spread.finish()
    departure(rows_out.at[x], fr_sems, ())
    for r in range(blocks):
        departure(code_out.at[pl.ds(r * rows, rows)], co_sems, (r,))
    for k in range(count):
        departure(ref_of(k, trade[k].at[0], x), tr_sems, (k,))
        for dz in range(z_size):
            if dz:
                departure(z_in[k].at[dz], rz_sems, (k, dz))
            for dy in range(y_size):
                slot = slot_of(dz, dy)
                departure(core_in[k].at[slot], rc_sems, (k, slot))
                if split[k]:
                    departure(x_in[k].at[slot], rx_sems, (k, slot))
                if dy:
                    departure(y_in[k].at[slot], ry_sems, (k, slot))
    for k in range(1, n):
        arrival(given.at[0], sq_sems, (k,))
    squares[...] = jnp.sum(given[...], 0)
    for k in range(1, n):
        departure(given.at[0], sq_sems, (k,))


def tail_scratch(n, length, width, own_rows, shapes, split):
    z_size, y_size = geometry(n)
    spots = z_size * y_size
    count = len(shapes)
    dma = pltpu.SemaphoreType.DMA
    halves = [(s[0] // 2, s[1]) if h else s for s, h in zip(shapes, split)]
    buffers = [((spots,) + s, BF) for s in shapes] * 2
    buffers += [((spots,) + s if h else (16, 128), BF) for s, h in zip(halves, split)]
    buffers += [((spots,) + s, BF) for s in halves]
    buffers += [((z_size,) + s, BF) for s in halves]
    buffers += [((2,) + s, BF) for s in shapes]
    buffers += [((n, length, width), BF), ((own_rows, width), BF), ((own_rows, width), BF),
                ((2, n, 8, width), F32), ((n, 8, 128), F32)]
    sems = [
        dma((2, 2, z_size)), dma((2, z_size, y_size)), dma((2, z_size, y_size)),
        dma((count, spots)), dma((2, count, spots)), dma((2, count, spots)), dma((2, count, spots)),
        dma((2, count, z_size)), dma((2, count)), dma((2, 4)), dma((2,)), dma((2, n)),
    ]
    return buffers, sems


def tail_phase(grad_stream0, facts, heads, grads, split, class_rows, own_width, n):
    z_size, y_size = geometry(n)
    length, width = grad_stream0.shape
    own_rows = heads[0].shape[0]
    shapes = [g.shape[1:] for g in grads]
    buffers, sems = tail_scratch(n, length, width, own_rows, shapes, split)
    vmem, hbm = pl.BlockSpec(memory_space=pltpu.VMEM), pl.BlockSpec(memory_space=pl.ANY)
    counts = tuple(s[0] for s in shapes)
    outs = pl.pallas_call(
        functools.partial(tail_kernel, z_size, y_size, own_width, split, counts),
        out_shape=[jax.ShapeDtypeStruct(s, F32) for s in shapes]
        + [
            jax.ShapeDtypeStruct((own_rows, width), F32),
            jax.ShapeDtypeStruct((128, class_rows), F32),
            jax.ShapeDtypeStruct((8, 128), F32),
        ],
        in_specs=[vmem] * 4 + [hbm] * len(grads),
        out_specs=[vmem] * (len(grads) + 3),
        scratch_shapes=[pltpu.VMEM(shape, kind) for shape, kind in buffers] + sems,
        compiler_params=pltpu.CompilerParams(
            collective_id=2, has_side_effects=True, vmem_limit_bytes=60 * 2**20
        ),
        name="tail",
    )(grad_stream0, facts, *heads, *grads)
    return outs[: len(grads)], outs[len(grads)], outs[len(grads) + 1], outs[len(grads) + 2][0, 0]


def adam_update(weight, first, second, grad, rate, decay):
    first_new = BETA_ONE * first + (1.0 - BETA_ONE) * grad
    second_new = BETA_TWO * second + (1.0 - BETA_TWO) * grad * grad
    first_hat = first_new / (1.0 - BETA_ONE**STEP)
    second_hat = second_new / (1.0 - BETA_TWO**STEP)
    weight_new = weight - rate * (first_hat / (jnp.sqrt(second_hat) + ADAM_EPS) + decay * weight)
    return (weight_new, first_new, second_new)


def dot(subscripts, left, right):
    return jnp.einsum(subscripts, left, right, preferred_element_type=F32)


def local(*args):
    class_ids, null_mask, code_ids, lengths = args[:4]
    masters, firsts, seconds = args[4::3], args[5::3], args[6::3]
    code_table, class_table, qkv_weight, out_weight, gate_up, down_weight, head_weight, gains = (
        masters
    )
    rates = (0.5, 0.5, 0.05, 0.05, 0.05, 0.05, 0.05, 0.5)
    decays = (0.1, 0.1, 0.1, 0.1, 0.1, 0.1, 0.1, 0.0)
    n = lax.axis_size("fsdp")
    me = lax.axis_index("fsdp")
    batch, length = code_ids.shape
    width = qkv_weight.shape[1]
    hidden_width = down_weight.shape[1]
    table_rows, own_width = class_table.shape
    own_rows = code_table.shape[0]
    heads = width // HEAD_DIM
    rows = (qkv_weight.shape[0], gate_up.shape[0], out_weight.shape[0], down_weight.shape[0])

    classes = jnp.where(null_mask == 1, table_rows - 1, class_ids)
    previous = jnp.concatenate([jnp.full((1, 1), -1, code_ids.dtype), code_ids[:, :-1]], 1)
    pair = jnp.stack([classes[0], lengths[0]])[None].astype(F32)
    own_gains = gains.astype(BF).astype(F32)
    facts = jnp.concatenate(
        [
            previous.astype(F32).reshape(2, -1),
            code_ids.astype(F32).reshape(2, -1),
            jnp.pad(pair, ((0, 0), (0, length // 2 - 2))),
            jnp.pad(own_gains, ((0, 0), (0, length // 2 - own_width))),
        ],
        0,
    )
    class_b = jnp.pad(class_table.T.astype(BF), ((0, 128 - own_width), (0, -table_rows % 128)))
    reps = lax.axis_size("rep")
    wholes, stream0, facts = front(
        facts,
        code_table,
        class_b,
        [gate_up, qkv_weight, out_weight, down_weight],
        own_width,
        length,
        reps,
        n,
    )
    gate_w, qkv_w, out_w, down_w = (w.reshape(-1, w.shape[-1]) for w in wholes)
    stream0 = stream0[None]
    images = n * batch
    tokens = images * length
    every_fact, facts = facts, facts[lax.axis_index("rep")]
    gains32 = facts[:, 5:8, :own_width].transpose(1, 0, 2).reshape(3, width)
    all_codes = facts[:, 2:4].reshape(images, length).astype(jnp.int32)
    previous = facts[:, 0:2].reshape(tokens).astype(jnp.int32)
    all_classes = facts[:, 4, 0].astype(jnp.int32)
    all_lengths = facts[:, 4, 1].astype(jnp.int32)
    all_counted = (jnp.arange(length)[None, :] < all_lengths[:, None]).astype(F32)
    own_ids = jnp.arange(own_rows) + me * own_rows
    lookup = (previous[:, None] == own_ids[None, :]).astype(BF)

    normed1, inverse1 = norm_forward(stream0, gains32[0])
    normed1 = normed1.astype(BF)
    mixed = dot("btd,ed->bte", normed1, qkv_w)
    cosine, sine = rotary_tables(length, HEAD_DIM)
    split4 = (batch, length, heads, HEAD_DIM)
    queries = rotate(mixed[..., :width].reshape(split4), cosine, sine).astype(BF)
    keys_rot = rotate(mixed[..., width : 2 * width].reshape(split4), cosine, sine).astype(BF)
    values = mixed[..., 2 * width :].reshape(split4).astype(BF)
    scores = attention_scores(queries, keys_rot)
    top = jnp.max(scores, -1, keepdims=True)
    expo = jnp.exp(scores - top)
    probs32 = expo / jnp.sum(expo, -1, keepdims=True)
    probs = probs32.astype(BF)
    attended = dot("bhqk,bkhd->bqhd", probs, values).astype(BF).reshape(batch, length, width)
    stream1 = stream0 + dot("btd,ed->bte", attended, out_w)
    normed2, inverse2 = norm_forward(stream1, gains32[1])
    normed2 = normed2.astype(BF)
    gated = dot("btd,fd->btf", normed2, gate_w)
    gate_part = gated[..., :hidden_width]
    up_part = gated[..., hidden_width:]
    hidden = (jax.nn.silu(gate_part) * up_part).astype(BF)
    stream2 = stream1 + dot("btf,df->btd", hidden, down_w)
    normed3, inverse3 = norm_forward(stream2, gains32[2])
    normed3 = normed3.astype(BF)

    head_b = head_weight.astype(BF)
    in_kernel = reps == 2 and size_of(head_scratch(n, length, width, own_rows, reps)[0]) < 52 * 2**20
    if in_kernel:
        grad_normed3, grad_head, totals = head_phase(normed3[0], head_weight, every_fact, reps, n)
        grad_normed3 = grad_normed3[None]
        loss_sum, token_count = totals[0, 0], totals[1, 0]
        head_pair = (grad_head, lax.ppermute(grad_head, "rep", [(0, 1), (1, 0)]))
        grad_head = head_pair[0].astype(F32) + head_pair[1].astype(F32)
    else:
        token_count = lax.psum(jnp.sum(all_counted), "rep")
        normed3_all = lax.all_gather(normed3, "fsdp", axis=0, tiled=True).reshape(tokens, width)
        logits = dot("td,vd->tv", normed3_all, head_b)
        onehot = all_codes.reshape(tokens)[:, None] == own_ids[None, :]
        local_top = jnp.max(logits, -1)
        local_sum = jnp.sum(jnp.exp(logits - local_top[:, None]), -1)
        local_pick = jnp.sum(jnp.where(onehot, logits, 0.0), -1)
        stats = lax.all_gather(jnp.stack([local_top, local_sum, local_pick]), "fsdp", axis=0)
        ltop = jnp.max(stats[:, 0], 0)
        lse = jnp.log(jnp.sum(stats[:, 1] * jnp.exp(stats[:, 0] - ltop[None]), 0)) + ltop
        picked = jnp.sum(stats[:, 2], 0)
        loss_sum = lax.psum(jnp.sum(jnp.where(all_counted.reshape(tokens) > 0, lse - picked, 0.0)), "rep")
        weight_t = all_counted.reshape(tokens) * (1.0 / token_count)
        soft = jnp.exp(logits - lse[:, None])
        grad_logits = ((soft - onehot.astype(F32)) * weight_t[:, None]).astype(BF)
        grad_normed3 = dot("tv,vd->td", grad_logits, head_b).astype(BF).reshape(images, length, width)
        grad_normed3 = lax.psum_scatter(grad_normed3, "fsdp", scatter_dimension=0, tiled=True)
        grad_normed3 = grad_normed3.astype(F32)
        grad_head = dot("tv,td->vd", grad_logits, normed3_all)

    grad_stream2, gain_three = norm_backward(stream2, inverse3, gains32[2], grad_normed3)
    grad_branch = grad_stream2.astype(BF)
    grad_down = dot("btd,btf->df", grad_branch, hidden)
    grad_hidden = dot("btd,df->btf", grad_branch, down_w)
    sigma = jax.nn.sigmoid(gate_part)
    grad_gate = grad_hidden * up_part * sigma * (1.0 + gate_part * (1.0 - sigma))
    grad_up = grad_hidden * gate_part * sigma
    grad_gated = jnp.concatenate([grad_gate, grad_up], -1).astype(BF)
    grad_gate_up = dot("btf,btd->fd", grad_gated, normed2)
    grad_normed2 = dot("btf,fd->btd", grad_gated, gate_w)
    grad_middle, gain_two = norm_backward(stream1, inverse2, gains32[1], grad_normed2)
    grad_stream1 = grad_stream2 + grad_middle
    grad_attn = grad_stream1.astype(BF)
    grad_out = dot("bte,btd->ed", grad_attn, attended)
    grad_attended = dot("bte,ed->btd", grad_attn, out_w).astype(BF).reshape(split4)
    grad_probs = dot("bqhd,bkhd->bhqk", grad_attended, values)
    grad_values = dot("bhqk,bqhd->bkhd", probs, grad_attended)
    grad_scores = probs32 * (grad_probs - jnp.sum(probs32 * grad_probs, -1, keepdims=True))
    grad_scores = grad_scores.astype(BF)
    scale = HEAD_DIM ** (-0.5)
    grad_queries = dot("bhqk,bkhd->bqhd", grad_scores, keys_rot) * scale
    grad_keys = dot("bhqk,bqhd->bkhd", grad_scores, queries) * scale
    grad_mixed = jnp.concatenate(
        [
            rotate_back(grad_queries, cosine, sine).reshape(batch, length, width),
            rotate_back(grad_keys, cosine, sine).reshape(batch, length, width),
            grad_values.reshape(batch, length, width),
        ],
        -1,
    ).astype(BF)
    grad_qkv = dot("bte,btd->ed", grad_mixed, normed1)
    grad_normed1 = dot("bte,ed->btd", grad_mixed, qkv_w)
    grad_first, gain_one = norm_backward(stream0, inverse1, gains32[0], grad_normed1)
    grad_stream0 = grad_stream1 + grad_first

    grad_gains = jnp.stack([gain_one, gain_two, gain_three])
    if in_kernel:
        gain_blocks = jnp.pad(
            grad_gains.reshape(3, n, own_width).transpose(1, 0, 2).astype(BF),
            ((0, 0), (0, 13), (0, 128 - own_width)),
        )
        blocks = [
            g.astype(BF).reshape(n, -1, g.shape[-1])
            for g in (grad_gate_up, grad_qkv, grad_out, grad_down)
        ]
        sums, grad_codes, grad_classes, squares = tail_phase(
            grad_stream0[0].astype(BF),
            every_fact,
            head_pair,
            blocks + [gain_blocks],
            (True, False, False, False, False),
            table_rows + -table_rows % 128,
            own_width,
            n,
        )
        grad_gate_up, grad_qkv, grad_out, grad_down, gain_part = sums
        grad_gains = gain_part[:3, :own_width]
        grad_classes = grad_classes[:own_width, :table_rows].T
    else:
        blocks = [
            g.astype(BF).reshape(n, -1, g.shape[-1]) for g in (grad_qkv, grad_gate_up, grad_out, grad_down)
        ]
        layer_part = lax.psum_scatter(pack_rows(*blocks), "fsdp", scatter_dimension=0, tiled=False)
        rows_all = lax.all_gather(grad_stream0.astype(BF), "fsdp", axis=0, tiled=True)
        grad_codes = dot("tv,td->vd", lookup, rows_all.reshape(tokens, width))
        class_part = lax.dynamic_slice(rows_all[:, 0], (0, me * own_width), (images, own_width))
        class_spot = (all_classes[:, None] == jnp.arange(table_rows)[None, :]).astype(BF)
        grad_classes = dot("iv,id->vd", class_spot, class_part)
        summed = lax.psum(
            (grad_codes.astype(BF), grad_head.astype(BF), layer_part, grad_classes), "rep"
        )
        grad_codes, grad_head, layer_part, grad_classes = (s.astype(F32) for s in summed)
        grad_gains = lax.psum(grad_gains, ("fsdp", "rep"))
        grad_gains = lax.dynamic_slice(grad_gains, (0, me * own_width), (3, own_width))
        grad_qkv, grad_gate_up, grad_out, grad_down = unpack_rows(layer_part, rows, hidden_width)
    reduced = (
        grad_codes, grad_classes, grad_qkv, grad_out, grad_gate_up, grad_down, grad_head, grad_gains
    )
    if not in_kernel:
        squares = lax.psum(sum(jnp.sum(piece * piece) for piece in reduced), "fsdp")
    grad_norm = jnp.sqrt(squares)
    factor = jnp.minimum(1.0, 1.0 / CLIP_INV / (grad_norm + 1e-06))
    results = [loss_sum, token_count, grad_norm]
    for index in range(8):
        results.extend(
            adam_update(
                masters[index],
                firsts[index],
                seconds[index],
                reduced[index] * factor,
                rates[index],
                decays[index],
            )
        )
    return tuple(results)


def solution(mesh):
    split = P(("fsdp", "rep"))
    by_row, by_column = P("fsdp", None), P(None, "fsdp")
    weights = (by_row,) * 3 + (by_column,) * 3 + (by_row,) * 15 + (by_column,) * 3
    return jax.shard_map(
        local,
        mesh=mesh,
        in_specs=(split, split, P(("fsdp", "rep"), None), split) + weights,
        out_specs=(P(), P(), P()) + weights,
        check_vma=False,
    )
```

```python
import functools
import math

import jax
import jax.numpy as jnp
from jax import lax
from jax.experimental import pallas as pl
from jax.experimental.pallas import tpu as pltpu
from jax.sharding import PartitionSpec as P

HEAD_DIM = 64
CLIP_INV = 500
STEP = 10
NORM_EPS = 1e-05
BETA_ONE = 0.5
BETA_TWO = 0.5
ADAM_EPS = 1e-08
BF = jnp.bfloat16
F32 = jnp.float32
MESH = pl.DeviceIdType.MESH


def rotary_tables(length, width):
    half = width // 2
    freq = 10000.0 ** (-jnp.arange(half, dtype=F32) * 2.0 / width)
    angles = jnp.arange(length, dtype=F32)[:, None] * freq[None, :]
    cosine = jnp.concatenate([jnp.cos(angles), jnp.cos(angles)], -1)
    sine = jnp.concatenate([jnp.sin(angles), jnp.sin(angles)], -1)
    return (cosine, sine)


def rotate_back(grads, cosine, sine):
    half = grads.shape[-1] // 2
    scaled = grads * sine[:, None, :]
    return grads * cosine[:, None, :] + jnp.concatenate(
        [scaled[..., half:], -scaled[..., :half]], -1
    )


def norm_backward(stream, inverse, gain, grad_out):
    weighted = grad_out * gain
    inner = jnp.mean(weighted * stream, -1, keepdims=True)
    grad_in = inverse * weighted - stream * inverse * inverse * inverse * inner
    grad_gain = jnp.sum(grad_out * stream * inverse, axis=(0, 1))
    return (grad_in, grad_gain)


def attention_scores(queries, keys_rot):
    length = queries.shape[1]
    scores = jnp.einsum(
        "bqhd,bkhd->bhqk", queries, keys_rot, preferred_element_type=F32
    ) * HEAD_DIM ** (-0.5)
    causal = jnp.arange(length)[:, None] >= jnp.arange(length)[None, :]
    return jnp.where(causal, scores, -1e30)


def column_blocks(width, total):
    return [(at, min(width, total - at)) for at in range(0, total, width)]


def pack_rows(qkv, gate, out, down):
    width = qkv.shape[-1]
    parts = [qkv, gate, out]
    for at, size in column_blocks(width, down.shape[-1]):
        block = down[..., at : at + size]
        if size < width:
            pad = [(0, 0)] * (block.ndim - 1) + [(0, width - size)]
            block = jnp.pad(block, pad)
        parts.append(block)
    return jnp.concatenate(parts, -2)


def unpack_rows(packed, rows, hidden_width):
    width = packed.shape[-1]
    at, parts = 0, []
    for count in rows[:3]:
        parts.append(packed[..., at : at + count, :])
        at += count
    blocks = []
    for _, size in column_blocks(width, hidden_width):
        blocks.append(packed[..., at : at + rows[3], :size])
        at += rows[3]
    parts.append(jnp.concatenate(blocks, -1))
    return parts


def geometry(n):
    chips = n // 2
    y_size = 1 << ((chips.bit_length() - 1) // 2)
    return chips // y_size, y_size


def where_am_i(z_size, y_size):
    me = lax.axis_index("fsdp")
    return me, me // (2 * y_size), (me // 2) % y_size, me % 2


def send(src, dst, sems, index, device):
    pltpu.make_async_remote_copy(
        src_ref=src, dst_ref=dst, send_sem=sems.at[(0,) + index], recv_sem=sems.at[(1,) + index],
        device_id=device, device_id_type=MESH,
    ).start()


def arrival(dst, sems, index):
    pltpu.make_async_copy(dst, dst, sems.at[(1,) + index]).wait()


def departure(src, sems, index):
    pltpu.make_async_copy(src, src, sems.at[(0,) + index]).wait()


def weight_pieces(rows, reps):
    gate = rows[0]
    cut = gate * 15 // 16 // 16 * 16
    middle = cut // 2 // 16 * 16
    one = 1 % reps
    return (
        (2, 0, rows[2], 2 % reps),
        (0, cut, gate - cut, one),
        (0, 0, middle, 0),
        (3, 0, rows[3], 3 % reps),
        (0, middle, cut - middle, 0),
        (1, 0, rows[1], one),
    )


def front(facts, code_table, class_b, weights, own_width, length, reps, n):
    z_size, y_size = geometry(n)
    width = code_table.shape[1]
    count = len(weights)
    pieces = weight_pieces([w.shape[0] for w in weights], reps)
    many = len(pieces)
    spots = z_size * y_size
    block = (length, width)
    vmem, hbm = pl.BlockSpec(memory_space=pltpu.VMEM), pl.BlockSpec(memory_space=pl.ANY)
    dma = pltpu.SemaphoreType.DMA
    outs = pl.pallas_call(
        functools.partial(front_kernel, z_size, y_size, reps, own_width, pieces, count),
        out_shape=[jax.ShapeDtypeStruct((n,) + w.shape, BF) for w in weights]
        + [jax.ShapeDtypeStruct(block, F32), jax.ShapeDtypeStruct((reps, n, 8, 128), F32)],
        in_specs=[vmem] * (3 + count),
        out_specs=[hbm] * count + [vmem] * 2,
        scratch_shapes=[
            pltpu.VMEM(code_table.shape, BF),
            pltpu.VMEM((128, n * 8), F32),
            pltpu.VMEM((spots,) + block, BF),
            pltpu.VMEM((spots,) + block, BF),
            pltpu.VMEM((spots,) + block, BF),
            pltpu.VMEM((z_size, y_size) + block, BF),
            pltpu.VMEM((z_size,) + block, BF),
            dma((2, n)),
            dma((2, reps)),
            dma((2, many, 2, z_size)),
            dma((2, many, z_size, y_size)),
            dma((2, many, z_size, y_size, reps)),
            dma((2, many, z_size, y_size)),
            dma((count,)),
            dma((2, spots)),
            dma((2, z_size, y_size)),
            dma((2, z_size)),
        ]
        + [pltpu.VMEM(w.shape, BF) for w in weights],
        compiler_params=pltpu.CompilerParams(
            collective_id=0, has_side_effects=True, vmem_limit_bytes=60 * 2**20
        ),
        name="front",
    )(facts, code_table, class_b, *weights)
    return outs[:count], outs[count], outs[count + 1]


class Place:
    def __init__(self, z_size, y_size, reps):
        self.z_size, self.y_size, self.reps = z_size, y_size, reps
        self.n = z_size * y_size * 2
        self.me, self.z, self.y, self.core = where_am_i(z_size, y_size)
        self.x = lax.axis_index("rep")

    def at(self, dz, dy, other=0):
        c = 1 - self.core if other else self.core
        z, y = lax.rem(self.z + dz, self.z_size), lax.rem(self.y + dy, self.y_size)
        return (z * self.y_size + y) * 2 + c

    def plane(self, z, dy=0, other=0):
        c = 1 - self.core if other else self.core
        return (z * self.y_size + lax.rem(self.y + dy, self.y_size)) * 2 + c

    def twin(self):
        return (self.at(0, 0, 1), self.x)

    def greet(self, everyone):
        barrier = pltpu.get_barrier_semaphore()
        if everyone:
            group = [lax.rem(self.me + k, self.n) for k in range(1, self.n)]
        else:
            group = [self.at(dz, 0) for dz in range(1, self.z_size)]
            group += [self.at(0, dy) for dy in range(1, self.y_size)] + [self.at(0, 0, 1)]
        peers = [(p, self.x) for p in group]
        peers += [(self.me, lax.rem(self.x + k, self.reps)) for k in range(1, self.reps)]
        for peer in peers:
            pl.semaphore_signal(barrier, inc=1, device_id=peer, device_id_type=MESH)
        pl.semaphore_wait(barrier, len(peers))


class Spread:
    def __init__(self, place, whole, z_sems, y_sems, c_sems, x_sems=None, part=None, rows=None):
        self.p, self.whole, self.part, self.rows = place, whole, part, rows
        self.z_sems, self.y_sems, self.c_sems, self.x_sems = z_sems, y_sems, c_sems, x_sems

    def block(self, z, dy=0, other=0):
        block = self.whole.at[self.p.plane(z, dy, other)]
        return block if self.rows is None else block.at[pl.ds(*self.rows)]

    def in_part(self, act):
        if self.part is None:
            act()
        else:
            pl.when(self.p.x == self.part)(act)

    def hand_over(self, z, dy, src, dst):
        p = self.p
        if self.part is not None:
            for dx in range(1, p.reps):
                send(src, dst, self.x_sems, (z, dy, dx), (p.me, lax.rem(p.x + dx, p.reps)))
        send(src, dst, self.c_sems, (z, dy), p.twin())

    def pass_on(self, z, src, up, down):
        p = self.p
        dst = self.block(z)
        if up:

            @pl.when(p.z + 1 < p.z_size)
            def _():
                send(src, dst, self.z_sems, (0, z), (p.plane(p.z + 1), p.x))

        if down:

            @pl.when(p.z >= 1)
            def _():
                send(src, dst, self.z_sems, (1, z), (p.plane(p.z - 1), p.x))

        for dy in range(1, p.y_size):
            send(src, dst, self.y_sems, (z, dy), (p.at(0, dy), p.x))

    def start(self, own):
        self.in_part(lambda: self.pass_on(self.p.z, own, True, True))
        send(own, self.block(self.p.z), self.c_sems, (self.p.z, 0), self.p.twin())

    def near(self, s, act):
        p = self.p
        if s == 0:
            act(p.z)
            return

        @pl.when(p.z - s >= 0)
        def _():
            act(p.z - s)

        @pl.when(p.z + s < p.z_size)
        def _():
            act(p.z + s)

    def step_z(self, s):
        p = self.p

        def take(z, up):
            block = self.block(z)
            arrival(block, self.z_sems, (1 - int(up), z))
            self.pass_on(z, block, up, not up)
            self.hand_over(z, 0, block, block)

        def act():
            @pl.when(p.z - s >= 0)
            def _():
                take(p.z - s, True)

            @pl.when(p.z + s < p.z_size)
            def _():
                take(p.z + s, False)

        self.in_part(act)

    def step_y(self, s):
        def take(z):
            for dy in range(1, self.p.y_size):
                block = self.block(z, self.p.y_size - dy)
                arrival(block, self.y_sems, (z, dy))
                self.hand_over(z, dy, block, block)

        self.in_part(lambda: self.near(s, take))

    def step_x(self, s):
        p = self.p

        def take(z):
            for dy in range(0 if s else 1, p.y_size):
                block = self.block(z, p.y_size - dy)
                arrival(block, self.x_sems, (z, dy, lax.rem(p.x - self.part + p.reps, p.reps)))
                send(block, block, self.c_sems, (z, dy), p.twin())

        pl.when(p.x != self.part)(lambda: self.near(s, take))

    def take_twin(self, z):
        for dy in range(self.p.y_size):
            arrival(self.block(z, self.p.y_size - dy, 1), self.c_sems, (z, dy))

    def finish(self):
        p = self.p
        block = self.block(p.z)
        for z in range(p.z_size):
            for dy in range(p.y_size):
                departure(block, self.c_sems, (z, dy))

        def act():
            for z in range(p.z_size):

                @pl.when(jnp.logical_and(p.z + 1 < p.z_size, z <= p.z))
                def _():
                    departure(block, self.z_sems, (0, z))

                @pl.when(jnp.logical_and(p.z >= 1, z >= p.z))
                def _():
                    departure(block, self.z_sems, (1, z))

                for dy in range(1, p.y_size):
                    departure(block, self.y_sems, (z, dy))
                if self.part is None:
                    continue
                for dy in range(p.y_size):
                    for dx in range(1, p.reps):
                        if dy:
                            departure(block, self.x_sems, (z, dy, dx))
                        else:

                            @pl.when(z != p.z)
                            def _():
                                departure(block, self.x_sems, (z, dy, dx))

        self.in_part(act)


def front_kernel(z_size, y_size, reps, own_width, pieces, count, facts, code_table, class_b, *refs):
    masters, refs = refs[:count], refs[count:]
    wholes, refs = refs[:count], refs[count:]
    weights, refs = refs[-count:], refs[:-count]
    (stream, facts_all, code_b, turned, acc, core_out, core_in, y_in, z_in,
     fact_sems, rep_sems, z_sems, y_sems, x_sems, c_sems, own_sems, rc_sems, ry_sems, rz_sems) = refs
    p = Place(z_size, y_size, reps)
    n, me, x = p.n, p.me, p.x
    length, width = stream.shape
    own_rows = code_table.shape[0]
    p.greet(True)

    for k in range(1, n):
        send(facts, facts_all.at[x, me], fact_sems, (k,), (lax.rem(me + k, n), x))
    facts_all[x, me] = facts[...]
    for k in range(count):
        weights[k][...] = masters[k][...].astype(BF)
    spreads = []
    for i, (k, start, size, part) in enumerate(pieces):
        sems = [group.at[:, i] for group in (z_sems, y_sems, c_sems, x_sems)]
        spreads.append(Spread(p, wholes[k], *sems, part, (start, size)))
        spreads[i].start(weights[k].at[pl.ds(start, size)])
    for k in range(count):
        pltpu.make_async_copy(weights[k], wholes[k].at[me], own_sems.at[k]).start()
    code_b[...] = code_table[...].astype(BF)

    for k in range(1, n):
        arrival(facts_all.at[x, lax.rem(me - k + n, n)], fact_sems, (k,))
    for k in range(1, reps):
        send(facts_all.at[x], facts_all.at[x], rep_sems, (k,), (me, lax.rem(x + k, reps)))
    turned[...] = jnp.transpose(facts_all[x].reshape(n * 8, 128))
    lane = lax.broadcasted_iota(jnp.int32, (128, n * 8), 1)
    class_iota = lax.broadcasted_iota(jnp.int32, (16, class_b.shape[1]), 1).astype(F32)
    row_iota = lax.broadcasted_iota(jnp.int32, (length // 2, own_rows), 1) + me * own_rows
    row_iota = row_iota.astype(F32)

    def found(image, out):
        cls = jnp.sum(jnp.where(lane[:1] == image * 8 + 4, turned[:1, :], 0.0), -1, keepdims=True)
        spot = jnp.where(class_iota == cls, 1.0, 0.0).astype(BF)
        row = lax.dot_general(
            spot, class_b[...], (((1,), (1,)), ((), ())), preferred_element_type=F32
        )
        row = jnp.concatenate([row, jnp.zeros((16, width - row.shape[1]), F32)], -1)
        row = pltpu.roll(row, me * own_width, 1)
        for half in range(2):
            ids = jnp.sum(jnp.where(lane == image * 8 + half, turned[...], 0.0), -1, keepdims=True)
            spot = jnp.where(row_iota == ids, 1.0, 0.0).astype(BF)
            rows = jnp.dot(spot, code_b[...], preferred_element_type=F32)
            out[pl.ds(half * (length // 2), length // 2)] = rows.astype(BF)
            if half == 0:
                first = lax.broadcasted_iota(jnp.int32, (16, width), 0) == 0
                head = jnp.where(first, row, rows[:16])
                out[pl.ds(0, 16)] = head.astype(BF)

    def look_up(dz):
        def body(j, carry):
            dy = y_size - 1 - j
            slot = dz * y_size + dy
            found(p.at(dz, dy, 1), core_out.at[slot])
            send(core_out.at[slot], core_in.at[slot], rc_sems, (slot,), p.twin())
            found(p.at(dz, dy), acc.at[slot])
            return carry

        lax.fori_loop(0, y_size, body, 0)

    def twin_sum(dz):
        for dy in range(y_size - 1, -1, -1):
            slot = dz * y_size + dy
            arrival(core_in.at[slot], rc_sems, (slot,))
            acc[slot] = (acc[slot].astype(F32) + core_in[slot].astype(F32)).astype(BF)
            if dy:
                send(acc.at[slot], y_in.at[dz, dy], ry_sems, (dz, dy), (p.at(0, dy), x))

    def y_sum(dz):
        slot = dz * y_size
        total = acc[slot].astype(F32)
        for dy in range(1, y_size):
            arrival(y_in.at[dz, dy], ry_sems, (dz, dy))
            total = total + y_in[dz, dy].astype(F32)
        acc[slot] = total.astype(BF)
        if dz:
            send(acc.at[slot], z_in.at[dz], rz_sems, (dz,), (p.at(dz, 0), x))

    for s in range(1, z_size + 1):
        for spread in spreads:
            if s < z_size:
                spread.step_z(s)
        for spread in spreads:
            spread.step_y(s - 1)
        look_up(z_size - s)
        if s >= 2:
            twin_sum(z_size - s + 1)
        if s >= 3:
            y_sum(z_size - s + 2)
    twin_sum(0)
    for spread in spreads:
        spread.step_x(0)
    y_sum(1)
    for s in range(1, z_size - 1):
        for spread in spreads:
            spread.step_x(s)
    y_sum(0)
    total = acc[0].astype(F32)
    for dz in range(1, z_size):
        arrival(z_in.at[dz], rz_sems, (dz,))
        total = total + z_in[dz].astype(F32)
    stream[...] = total
    for spread in spreads:
        spread.step_x(z_size - 1)

    for k in range(1, reps):
        arrival(facts_all.at[x], rep_sems, (k,))
        departure(facts_all.at[x], rep_sems, (k,))
    for k in range(1, n):
        departure(facts, fact_sems, (k,))
    for dz in range(z_size):
        for dy in range(y_size):
            slot = dz * y_size + dy
            departure(core_out.at[slot], rc_sems, (slot,))
            if dy:
                departure(acc.at[slot], ry_sems, (dz, dy))
            elif dz:
                departure(acc.at[slot], rz_sems, (dz,))
    for k in range(count):
        pltpu.make_async_copy(weights[k], wholes[k].at[me], own_sems.at[k]).wait()
    for spread in spreads:
        for z in range(z_size):
            spread.take_twin(z)
        spread.finish()


def head_kernel(z_size, y_size, reps, normed3, head_weight, facts, grad_normed3, grad_head, totals,
                whole, logits, grads, turned, marks, stats_in, lse_all, acc, core_out, core_in, y_in, z_in,
                loss_in, head_b, z_sems, y_sems, c_sems, st_sems, ls_sems, rc_sems, ry_sems, rz_sems, lo_sems):
    p = Place(z_size, y_size, reps)
    n, me, x = p.n, p.me, p.x
    length, width = normed3.shape
    half = length // 2
    own_rows = head_weight.shape[0]
    p.greet(True)
    spread = Spread(p, whole, z_sems, y_sems, c_sems)
    spread.start(normed3)
    head_b[...] = head_weight[...].astype(BF)
    whole[me] = normed3[...]
    own_facts = facts.at[x]
    turned[...] = jnp.transpose(own_facts[...].reshape(n * 8, 128))
    lane = lax.broadcasted_iota(jnp.int32, (128, n * 8), 1)
    full_lane = lax.broadcasted_iota(jnp.int32, (length, n * 8), 1)
    column_iota = (lax.broadcasted_iota(jnp.int32, (length, own_rows), 1) + me * own_rows).astype(F32)
    token = lax.broadcasted_iota(jnp.int32, (length, 1), 0).astype(F32)
    every = facts[...].reshape(reps * n * 8, 128)
    row8 = lax.rem(lax.broadcasted_iota(jnp.int32, every.shape, 0), 8)
    spot = jnp.logical_and(row8 == 4, lax.broadcasted_iota(jnp.int32, every.shape, 1) == 1)
    token_count = jnp.sum(jnp.sum(jnp.where(spot, every, 0.0), 0, keepdims=True), 1, keepdims=True)
    inv_count = 1.0 / token_count

    def codes_of(image):
        parts = [
            jnp.sum(jnp.where(lane == image * 8 + 2 + h, turned[...], 0.0), -1, keepdims=True)
            for h in range(2)
        ]
        return jnp.concatenate(parts, 0)

    marks[...] = jnp.zeros_like(marks)

    def forward(image):
        out = lax.dot_general(
            whole[image], head_b[...], (((1,), (1,)), ((), ())), preferred_element_type=F32
        )
        logits[image] = out
        top = jnp.max(out, -1, keepdims=True)
        total = jnp.sum(jnp.exp(out - top), -1, keepdims=True)
        pick = jnp.sum(jnp.where(column_iota == codes_of(image), out, 0.0), -1, keepdims=True)
        old = marks[...]
        old = jnp.where(full_lane == image * 8, top, old)
        old = jnp.where(full_lane == image * 8 + 1, total, old)
        marks[...] = jnp.where(full_lane == image * 8 + 2, pick, old)

    def forward_column(z, first, last):
        def body(j, carry):
            forward(p.plane(z, lax.rem(y_size - j // 2, y_size), 0) + lax.rem(j, 2) * (1 - 2 * p.core))
            return carry

        lax.fori_loop(first * 2, last * 2, body, 0)

    arrival(spread.block(p.z, 0, 1), c_sems, (p.z, 0))
    forward_column(p.z, 0, 1)

    def one(z, s):
        arrival(spread.block(z, 0, 1), c_sems, (z, 0))
        forward_column(z, 0, 1)

    def other(z):
        for dy in range(1, y_size):
            arrival(spread.block(z, y_size - dy, 1), c_sems, (z, dy))
        forward_column(z, 1, y_size)

    def both(s, act):
        if s == 0:
            act(p.z)
            return

        @pl.when(p.z - s >= 0)
        def _():
            act(p.z - s)

        @pl.when(p.z + s < z_size)
        def _():
            act(p.z + s)

    for s in range(1, z_size + 1):
        if s < z_size:
            spread.step_z(s)
        spread.step_y(s - 1)
        if s < z_size:
            both(s, lambda z: one(z, s))
        both(s - 1, other)

    tiles = jnp.transpose(marks[...]).reshape(n, 8, length)
    stats_in[1] = tiles
    for k in range(1, n):
        peer = lax.rem(me + k, n)
        send(stats_in.at[1, peer], stats_in.at[0, me], st_sems, (k,), (peer, x))
    stats_in[0, me] = stats_in[1, me]
    for k in range(1, n):
        arrival(stats_in.at[0, 0], st_sems, (k,))
    tops = stats_in[0, :, 0, :]
    sums = stats_in[0, :, 1, :]
    picks = stats_in[0, :, 2, :]
    top = jnp.max(tops, 0, keepdims=True)
    lse = jnp.log(jnp.sum(sums * jnp.exp(tops - top), 0, keepdims=True)) + top
    pick = jnp.sum(picks, 0, keepdims=True)
    here = own_facts[me]
    counted = lax.broadcasted_iota(jnp.int32, (1, length), 1).astype(F32) < here[4:5, 1:2]
    loss = jnp.where(counted, lse - pick, 0.0)
    lse_all[me] = jnp.concatenate([lse, loss, jnp.zeros((6, length), F32)], 0)
    for k in range(1, n):
        peer = lax.rem(me + k, n)
        send(lse_all.at[me], lse_all.at[me], ls_sems, (k,), (peer, x))
    for k in range(1, n):
        arrival(lse_all.at[0], ls_sems, (k,))
    table = lse_all[...].reshape(n * 8, length)
    row8 = lax.rem(lax.broadcasted_iota(jnp.int32, table.shape, 0), 8)
    group = jnp.sum(jnp.sum(jnp.where(row8 == 1, table, 0.0), 0, keepdims=True), 1, keepdims=True)
    loss_in[x] = jnp.broadcast_to(group, (8, 128))
    for k in range(1, reps):
        peer = (me, lax.rem(x + k, reps))
        send(loss_in.at[x], loss_in.at[x], lo_sems, (k,), peer)
    marks[...] = jnp.transpose(table)

    def backward(image, out):
        lse_t = jnp.sum(jnp.where(full_lane == image * 8, marks[...], 0.0), -1, keepdims=True)
        size = jnp.sum(jnp.where(lane[:8] == image * 8 + 4, turned[:8, :], 0.0), -1, keepdims=True)
        weight = jnp.where(token < size[1:2], inv_count, 0.0)
        hot = jnp.where(column_iota == codes_of(image), 1.0, 0.0)
        grad = ((jnp.exp(logits[image] - lse_t) - hot) * weight).astype(BF)
        grads[image] = grad
        out[...] = jnp.dot(grad, head_b[...], preferred_element_type=F32).astype(BF)

    last = z_size - 1

    def far(j):
        return last - j // y_size, lax.rem(j, y_size)

    def first_pass(j, carry):
        dz, dyy = far(j)
        dy = y_size - 1 - dyy
        slot = dz * y_size + dy
        backward(p.at(dz, dy, 1), core_out.at[slot])
        send(core_out.at[slot], core_in.at[slot], rc_sems, (slot,), p.twin())
        backward(p.at(dz, dy), acc.at[slot])
        return carry

    def twin_sum(slot):
        arrival(core_in.at[slot], rc_sems, (slot,))
        acc[slot] = (acc[slot].astype(F32) + core_in[slot].astype(F32)).astype(BF)

    def y_sum(dz):
        slot = dz * y_size
        total = acc[slot].astype(F32)
        for dy in range(1, y_size):
            arrival(y_in.at[dz, dy], ry_sems, (dz, dy))
            total = total + y_in[dz, dy].astype(F32)
        acc[slot] = total.astype(BF)

    def round_of(g, carry):
        dz = last - g

        def per_dy(i, c):
            return first_pass(g * y_size + i, c)

        lax.fori_loop(0, y_size, per_dy, 0)
        for dy in range(y_size - 1, -1, -1):
            slot = dz * y_size + dy
            twin_sum(slot)
            if dy:
                send(acc.at[slot], y_in.at[dz, dy], ry_sems, (dz, dy), (p.at(0, dy), x))

        @pl.when(g >= 1)
        def _():
            y_sum(dz + 1)
            send(acc.at[(dz + 1) * y_size], z_in.at[dz + 1], rz_sems, (dz + 1,), (p.at(dz + 1, 0), x))

        return carry

    lax.fori_loop(0, z_size, round_of, 0)

    blocks = 4
    rows = own_rows // blocks
    for r in range(blocks):

        def add(image, total):
            return total + lax.dot_general(
                grads[image, :, r * rows : (r + 1) * rows], whole[image],
                (((0,), (0,)), ((), ())), preferred_element_type=F32,
            )

        total = lax.fori_loop(0, n, add, jnp.zeros((rows, width), F32))
        grad_head[r * rows : (r + 1) * rows] = total.astype(BF)
    y_sum(0)
    total = acc[0].astype(F32)
    for dz in range(1, z_size):
        arrival(z_in.at[dz], rz_sems, (dz,))
        total = total + z_in[dz].astype(F32)
    grad_normed3[...] = total
    for k in range(1, reps):
        arrival(loss_in.at[0], lo_sems, (k,))
    loss_sum = loss_in[0]
    for k in range(1, reps):
        loss_sum = loss_sum + loss_in[k]
    totals[...] = jnp.where(
        lax.broadcasted_iota(jnp.int32, (8, 128), 0) == 0, loss_sum, token_count
    )

    spread.finish()
    for k in range(1, n):
        departure(stats_in.at[0, 0], st_sems, (k,))
        departure(lse_all.at[0], ls_sems, (k,))
    for k in range(1, reps):
        departure(loss_in.at[0], lo_sems, (k,))
    for dz in range(z_size):
        for dy in range(y_size):
            slot = dz * y_size + dy
            departure(core_out.at[slot], rc_sems, (slot,))
            if dy:
                departure(acc.at[slot], ry_sems, (dz, dy))
            elif dz:
                departure(acc.at[slot], rz_sems, (dz,))


def head_scratch(n, length, width, own_rows, reps):
    z_size, y_size = geometry(n)
    spots = z_size * y_size
    dma = pltpu.SemaphoreType.DMA
    buffers = [
        ((n, length, width), BF),
        ((n, length, own_rows), F32),
        ((n, length, own_rows), BF),
        ((128, n * 8), F32),
        ((length, n * 8), F32),
        ((2, n, 8, length), F32),
        ((n, 8, length), F32),
        ((spots, length, width), BF),
        ((spots, length, width), BF),
        ((spots, length, width), BF),
        ((z_size, y_size, length, width), BF),
        ((z_size, length, width), BF),
        ((reps, 8, 128), F32),
        ((own_rows, width), BF),
    ]
    sems = [
        dma((2, 2, z_size)), dma((2, z_size, y_size)), dma((2, z_size, y_size)),
        dma((2, n)), dma((2, n)), dma((2, spots)), dma((2, z_size, y_size)), dma((2, z_size)),
        dma((2, reps)),
    ]
    return buffers, sems


def size_of(buffers):
    return sum(math.prod(shape) * jnp.dtype(kind).itemsize for shape, kind in buffers)


def head_phase(normed3, head_weight, facts, reps, n):
    z_size, y_size = geometry(n)
    length, width = normed3.shape
    buffers, sems = head_scratch(n, length, width, head_weight.shape[0], reps)
    vmem = pl.BlockSpec(memory_space=pltpu.VMEM)
    return pl.pallas_call(
        functools.partial(head_kernel, z_size, y_size, reps),
        out_shape=[
            jax.ShapeDtypeStruct((length, width), F32),
            jax.ShapeDtypeStruct(head_weight.shape, BF),
            jax.ShapeDtypeStruct((8, 128), F32),
        ],
        in_specs=[vmem] * 3,
        out_specs=[vmem] * 3,
        scratch_shapes=[pltpu.VMEM(shape, kind) for shape, kind in buffers] + sems,
        compiler_params=pltpu.CompilerParams(
            collective_id=1, has_side_effects=True, vmem_limit_bytes=60 * 2**20
        ),
        name="head",
    )(normed3, head_weight, facts)


def tail_kernel(z_size, y_size, own_width, split, counts, queries, keys, values, grad_attended, turn,
                qkv_w, stream0, normed1, grad_stream1, gains, facts, head_one, head_two, *refs):
    count = len(split)
    early = count - 2
    qkv_at, gain_at = early, early + 1
    grads, refs = refs[:early], refs[early:]
    sums, refs = refs[:count], refs[count:]
    code_sum, class_sum, squares, refs = refs[0], refs[1], refs[2], refs[3:]
    accs, refs = refs[:count], refs[count:]
    core_in, refs = refs[:count], refs[count:]
    x_in, refs = refs[:count], refs[count:]
    y_in, refs = refs[:count], refs[count:]
    z_in, refs = refs[:count], refs[count:]
    trade, refs = refs[:count], refs[count:]
    (whole, code_out, code_in, rows_out, given, grad_mixed, grad_qkv, gain_blocks, grad_stream0, z_sems, y_sems, c_sems, own_sems, rc_sems, rx_sems,
     ry_sems, rz_sems, tr_sems, co_sems, fr_sems, sq_sems) = refs
    p = Place(z_size, y_size, 2)
    n, me, x = p.n, p.me, p.x
    length, width = stream0.shape
    own_rows = code_out.shape[0]
    p.greet(True)
    mate = (me, 1 - x)
    spread = Spread(p, whole, z_sems, y_sems, c_sems)

    def slot_of(dz, dy):
        return dz * y_size + dy

    order = [(dz, dy) for dz in range(z_size - 1, -1, -1) for dy in range(y_size - 1, -1, -1)]
    halved = [k for k in range(early) if split[k]]
    plain = [k for k in range(early) if not split[k]]
    late = [qkv_at, gain_at]

    def block_of(k, f):
        if k == qkv_at:
            rows = counts[k]
            return grad_qkv.at[pl.ds(pl.multiple_of(f * rows, rows), rows)]
        return gain_blocks.at[f] if k == gain_at else grads[k].at[f]

    def to_twin(kinds):
        for dz, dy in order:
            slot = slot_of(dz, dy)
            for k in kinds:
                send(block_of(k, p.at(dz, dy, 1)), core_in[k].at[slot], rc_sems, (k, slot), p.twin())
                pltpu.make_async_copy(
                    block_of(k, p.at(dz, dy)), accs[k].at[slot], own_sems.at[k, slot]
                ).start()

    to_twin(halved)
    to_twin(plain)

    def part(k, which):
        rows = counts[k] // 2
        return pl.ds(pl.multiple_of(which * rows, rows), rows)

    def ref_of(k, ref, which):
        return ref.at[part(k, which)] if split[k] else ref

    def twin_sums(kinds, dz):
        def body(dy, carry):
            slot = slot_of(dz, dy)
            for k in kinds:
                pltpu.make_async_copy(accs[k].at[slot], accs[k].at[slot], own_sems.at[k, slot]).wait()
                arrival(core_in[k].at[slot], rc_sems, (k, slot))
                accs[k][slot] = (accs[k][slot].astype(F32) + core_in[k][slot].astype(F32)).astype(BF)
                if split[k]:
                    send(accs[k].at[slot, part(k, 1 - x)], x_in[k].at[slot], rx_sems, (k, slot), mate)
            return carry

        lax.fori_loop(0, y_size, body, 0)

    def send_y(kinds, dz):
        for dy in range(1, y_size):
            slot = slot_of(dz, dy)
            for k in kinds:
                source = ref_of(k, accs[k].at[slot], x)
                send(source, y_in[k].at[slot], ry_sems, (k, slot), (p.at(0, dy), x))

    def take_x(dz):
        def body(dy, carry):
            slot = slot_of(dz, dy)
            for k in halved:
                arrival(x_in[k].at[slot], rx_sems, (k, slot))
                mine = accs[k].at[slot, part(k, x)]
                mine[...] = (mine[...].astype(F32) + x_in[k][slot].astype(F32)).astype(BF)
            return carry

        lax.fori_loop(0, y_size, body, 0)
        send_y(halved, dz)

    def take_y(kinds, dz):
        for k in kinds:
            mine = ref_of(k, accs[k].at[slot_of(dz, 0)], x)
            total = mine[...].astype(F32)
            for dy in range(1, y_size):
                slot = slot_of(dz, dy)
                arrival(y_in[k].at[slot], ry_sems, (k, slot))
                total = total + y_in[k][slot].astype(F32)
            mine[...] = total.astype(BF)
            if dz:
                send(mine, z_in[k].at[dz], rz_sems, (k, dz), (p.at(dz, 0), x))

    def square(value):
        return jnp.sum(jnp.sum(value * value, 0, keepdims=True), 1, keepdims=True)

    lane = lax.broadcasted_iota(jnp.int32, (length, 128), 1)
    low = lax.rem(lane, HEAD_DIM) < HEAD_DIM // 2
    scale = HEAD_DIM ** (-0.5)

    def turn_back(grad):
        scaled = grad * turn[1]
        other = jnp.where(
            low, pltpu.roll(scaled, 128 - HEAD_DIM // 2, 1), -pltpu.roll(scaled, HEAD_DIM // 2, 1)
        )
        return grad * turn[0] + other

    def pair(j, carry):
        at = pl.ds(pl.multiple_of(j * 128, 128), 128)
        q, k, v, grad = queries[:, at], keys[:, at], values[:, at], grad_attended[:, at]
        q_two, grad_two = both_heads(q), both_heads(grad)
        probs = attention_probs(q_two, k)
        grad_probs = product(grad_two, v, BY_LANES)
        inner = jnp.sum(probs * grad_probs, -1, keepdims=True)
        grad_scores = (probs * (grad_probs - inner)).astype(BF)
        grad_v = product(probs.astype(BF), grad_two, BY_ROWS)
        grad_q = one_row(jnp.dot(grad_scores, k, preferred_element_type=F32))
        grad_k = product(grad_scores, q_two, BY_ROWS)
        grad_mixed[:, at] = turn_back(grad_q * scale).astype(BF)
        base = pl.multiple_of(j * 128, 128)
        grad_mixed[:, pl.ds(width + base, 128)] = turn_back(grad_k * scale).astype(BF)
        grad_mixed[:, pl.ds(2 * width + base, 128)] = grad_v.astype(BF)
        return carry

    def settle(kinds):
        for k in kinds:
            mine = ref_of(k, accs[k].at[0], x)
            total = mine[...].astype(F32)
            for dz in range(1, z_size):
                arrival(z_in[k].at[dz], rz_sems, (k, dz))
                total = total + z_in[k][dz].astype(F32)
            source = ref_of(k, trade[k].at[0], x)
            source[...] = total.astype(BF)
            target = trade[k].at[0, part(k, x)] if split[k] else trade[k].at[1]
            send(source, target, tr_sems, (k,), mate)

    def collect(kinds):
        summed = jnp.zeros((1, 1), F32)
        for k in kinds:
            if split[k]:
                arrival(trade[k].at[0, part(k, 1 - x)], tr_sems, (k,))
                total = trade[k][0].astype(F32)
            else:
                arrival(trade[k].at[1], tr_sems, (k,))
                total = trade[k][0].astype(F32) + trade[k][1].astype(F32)
            sums[k][...] = total
            summed = summed + square(total)
        return summed

    pairs = width // 128
    for s in range(z_size):
        dz = z_size - 1 - s
        lax.fori_loop(s * pairs // z_size, (s + 1) * pairs // z_size, pair, 0)
        twin_sums(halved, dz)
        twin_sums(plain, dz)
        send_y(plain, dz)

    grad_out = jnp.dot(grad_mixed[...], qkv_w[...], preferred_element_type=F32)
    stream = stream0[...]
    inverse = lax.rsqrt(jnp.mean(stream * stream, -1, keepdims=True) + NORM_EPS)
    weighted = grad_out * gains[3:4, :]
    inner = jnp.mean(weighted * stream, -1, keepdims=True)
    grad_first = inverse * weighted - stream * (inverse * inverse * inverse) * inner
    grad_stream0[...] = (grad_stream1[...] + grad_first).astype(BF)
    spread.start(grad_stream0)
    whole[me] = grad_stream0[...]
    gain_one = jnp.sum(grad_out * stream * inverse, 0, keepdims=True)
    third = grad_qkv.shape[0] // 6
    for r in range(6):
        at = pl.ds(r * third, third)
        grad_qkv[at, :] = product(grad_mixed[:, r * third : (r + 1) * third], normed1[...], BY_ROWS).astype(BF)
    row = lax.broadcasted_iota(jnp.int32, (16, width), 0)
    spare = jnp.concatenate([gains[...], gains[...]], 0)
    all_gains = jnp.where(row == 0, gain_one, jnp.where(row < 3, spare, 0.0))

    def gain_block(f, carry):
        turned = pltpu.roll(all_gains, lax.rem(width - f * own_width, width), 1)[:, :128]
        own = lax.broadcasted_iota(jnp.int32, turned.shape, 1) < own_width
        gain_blocks[f] = jnp.where(own, turned, 0.0).astype(BF)
        return carry

    lax.fori_loop(0, n, gain_block, 0)
    to_twin(late)
    for s in range(1, z_size):
        spread.step_z(s)
        spread.step_y(s - 1)
        twin_sums(late, z_size - s)
        take_y(plain, z_size - s)
    twin_sums(late, 0)
    spread.step_y(z_size - 1)
    for dz in range(z_size - 1, -1, -1):
        take_x(dz)
        send_y(late, dz)
    take_y(plain, 0)
    for z in range(z_size):
        spread.take_twin(z)

    rows_out[x] = whole[:, 0:8, :].astype(F32)
    send(rows_out.at[x], rows_out.at[x], fr_sems, (), mate)

    blocks = 4
    rows = own_rows // blocks
    iota = lax.broadcasted_iota(jnp.int32, (rows, length // 2), 0) + me * own_rows

    def code_block(r, carry):
        base = (iota + r * rows).astype(F32)

        def add(image, total):
            ids = facts[x, image]
            hot = jnp.concatenate(
                [jnp.where(base == ids[h : h + 1, :], 1.0, 0.0) for h in range(2)], 1
            ).astype(BF)
            return total + jnp.dot(hot, whole[image], preferred_element_type=F32)

        total = lax.fori_loop(0, n, add, jnp.zeros((rows, width), F32))
        at = pl.ds(pl.multiple_of(r * rows, rows), rows)
        code_out[at] = total.astype(BF)
        send(code_out.at[at], code_in.at[at], co_sems, (r,), mate)
        return carry

    for r in range(z_size):
        lax.fori_loop(r * blocks // z_size, (r + 1) * blocks // z_size, code_block, 0)
        take_y(halved, z_size - 1 - r)
        take_y(late, z_size - 1 - r)
    settle(halved + plain)

    total_squares = square(head_one[...].astype(F32) + head_two[...].astype(F32))

    arrival(rows_out.at[1 - x], fr_sems, ())
    firsts = rows_out[:, :, 0, :].reshape(2 * n, width)
    shift = lax.rem(width - me * own_width, width)
    firsts = pltpu.roll(firsts, shift, 1)[:, :128]
    firsts = jnp.where(lax.broadcasted_iota(jnp.int32, firsts.shape, 1) < own_width, firsts, 0.0)
    classes = facts[:, :, 4, :].reshape(2 * n, 128)[:, 0:1]
    class_iota = lax.broadcasted_iota(jnp.int32, (2 * n, class_sum.shape[1]), 1).astype(F32)
    hot = jnp.where(class_iota == classes, 1.0, 0.0).astype(BF)
    class_grad = lax.dot_general(
        firsts.astype(BF), hot, (((0,), (0,)), ((), ())), preferred_element_type=F32
    )
    class_sum[...] = class_grad
    total_squares = total_squares + square(class_grad)

    total_squares = total_squares + collect(halved + plain)
    settle(late)
    for r in range(blocks):
        at = pl.ds(r * rows, rows)
        arrival(code_in.at[at], co_sems, (r,))
        total = code_out[at].astype(F32) + code_in[at].astype(F32)
        code_sum[at] = total
        total_squares = total_squares + square(total)
    total_squares = total_squares + collect(late)

    given[me] = jnp.broadcast_to(total_squares, (8, 128))
    for k in range(1, n):
        send(given.at[me], given.at[me], sq_sems, (k,), (lax.rem(me + k, n), x))

    spread.finish()
    departure(rows_out.at[x], fr_sems, ())
    for r in range(blocks):
        departure(code_out.at[pl.ds(r * rows, rows)], co_sems, (r,))
    for k in range(count):
        departure(ref_of(k, trade[k].at[0], x), tr_sems, (k,))
        for dz in range(z_size):
            if dz:
                departure(z_in[k].at[dz], rz_sems, (k, dz))
            for dy in range(y_size):
                slot = slot_of(dz, dy)
                departure(core_in[k].at[slot], rc_sems, (k, slot))
                if split[k]:
                    departure(x_in[k].at[slot], rx_sems, (k, slot))
                if dy:
                    departure(y_in[k].at[slot], ry_sems, (k, slot))
    for k in range(1, n):
        arrival(given.at[0], sq_sems, (k,))
    squares[...] = jnp.sum(given[...], 0)
    for k in range(1, n):
        departure(given.at[0], sq_sems, (k,))


def tail_scratch(n, length, width, own_rows, shapes, split):
    z_size, y_size = geometry(n)
    spots = z_size * y_size
    count = len(shapes)
    dma = pltpu.SemaphoreType.DMA
    halves = [(s[0] // 2, s[1]) if h else s for s, h in zip(shapes, split)]
    buffers = [((spots,) + s, BF) for s in shapes] * 2
    buffers += [((spots,) + s if h else (16, 128), BF) for s, h in zip(halves, split)]
    buffers += [((spots,) + s, BF) for s in halves]
    buffers += [((z_size,) + s, BF) for s in halves]
    buffers += [((2,) + s, BF) for s in shapes]
    buffers += [((n, length, width), BF), ((own_rows, width), BF), ((own_rows, width), BF),
                ((2, n, 8, width), F32), ((n, 8, 128), F32), ((length, 3 * width), BF),
                ((3 * width, width), BF), ((n, 16, 128), BF), ((length, width), BF)]
    sems = [
        dma((2, 2, z_size)), dma((2, z_size, y_size)), dma((2, z_size, y_size)),
        dma((count, spots)), dma((2, count, spots)), dma((2, count, spots)), dma((2, count, spots)),
        dma((2, count, z_size)), dma((2, count)), dma((2, 4)), dma((2,)), dma((2, n)),
    ]
    return buffers, sems


def tail_phase(layer, facts, heads, grads, late, split, class_rows, own_width, n):
    z_size, y_size = geometry(n)
    length, width = layer[0].shape
    own_rows = heads[0].shape[0]
    shapes = [g.shape[1:] for g in grads] + late
    buffers, sems = tail_scratch(n, length, width, own_rows, shapes, split)
    vmem, hbm = pl.BlockSpec(memory_space=pltpu.VMEM), pl.BlockSpec(memory_space=pl.ANY)
    counts = tuple(s[0] for s in shapes)
    outs = pl.pallas_call(
        functools.partial(tail_kernel, z_size, y_size, own_width, split, counts),
        out_shape=[jax.ShapeDtypeStruct(s, F32) for s in shapes]
        + [
            jax.ShapeDtypeStruct((own_rows, width), F32),
            jax.ShapeDtypeStruct((128, class_rows), F32),
            jax.ShapeDtypeStruct((8, 128), F32),
        ],
        in_specs=[vmem] * (len(layer) + 3) + [hbm] * len(grads),
        out_specs=[vmem] * (len(shapes) + 3),
        scratch_shapes=[pltpu.VMEM(shape, kind) for shape, kind in buffers] + sems,
        compiler_params=pltpu.CompilerParams(
            collective_id=2, has_side_effects=True, vmem_limit_bytes=60 * 2**20
        ),
        name="tail",
    )(*layer, facts, *heads, *grads)
    many = len(shapes)
    return outs[:many], outs[many], outs[many + 1], outs[many + 2][0, 0]


BY_ROWS = (((0,), (0,)), ((), ()))
BY_LANES = (((1,), (1,)), ((), ()))


def product(left, right, dims):
    return lax.dot_general(left, right, dims, preferred_element_type=F32)


def both_heads(pair):
    lane = lax.broadcasted_iota(jnp.int32, pair.shape, 1)
    zero = jnp.zeros_like(pair)
    first, second = jnp.where(lane < HEAD_DIM, pair, zero), jnp.where(lane < HEAD_DIM, zero, pair)
    return jnp.concatenate([first, second], 0)


def one_row(two):
    length = two.shape[0] // 2
    lane = lax.broadcasted_iota(jnp.int32, (length, 128), 1)
    return jnp.where(lane < HEAD_DIM, two[:length], two[length:])


def attention_probs(q_two, k):
    length = k.shape[0]
    query = lax.rem(lax.broadcasted_iota(jnp.int32, (2 * length, length), 0), length)
    causal = query >= lax.broadcasted_iota(jnp.int32, (2 * length, length), 1)
    scores = jnp.where(causal, product(q_two, k, BY_LANES) * HEAD_DIM ** (-0.5), -1e30)
    expo = jnp.exp(scores - jnp.max(scores, -1, keepdims=True))
    return expo / jnp.sum(expo, -1, keepdims=True)


def layer_kernel(stream0, gains, turn, qkv_hbm, out_hbm, gate_hbm, down_hbm,
                 normed1, queries, keys, values, attended, stream1, normed2, gated, hidden, stream2, normed3,
                 qkv_w, out_w, gate_w, down_w, sems):
    moves = [
        pltpu.make_async_copy(src, dst, sems.at[i])
        for i, (src, dst) in enumerate(
            ((qkv_hbm, qkv_w), (out_hbm, out_w), (gate_hbm, gate_w), (down_hbm, down_w))
        )
    ]
    for move in moves:
        move.start()
    length, width = stream0.shape
    hidden_width = hidden.shape[1]

    def rms(stream, row):
        inverse = lax.rsqrt(jnp.mean(stream * stream, -1, keepdims=True) + NORM_EPS)
        return (stream * inverse * gains[row : row + 1, :]).astype(BF)

    normed1[...] = rms(stream0[...], 0)
    lane = lax.broadcasted_iota(jnp.int32, (length, 128), 1)
    low = lax.rem(lane, HEAD_DIM) < HEAD_DIM // 2

    def turned(part):
        other = jnp.where(
            low, -pltpu.roll(part, 128 - HEAD_DIM // 2, 1), pltpu.roll(part, HEAD_DIM // 2, 1)
        )
        return (part * turn[0] + other * turn[1]).astype(BF)

    moves[0].wait()

    def pair(j, carry):
        base = pl.multiple_of(j * 128, 128)
        at = pl.ds(base, 128)
        x = normed1[...]
        q = turned(product(x, qkv_w[at, :], BY_LANES))
        k = turned(product(x, qkv_w[pl.ds(width + base, 128), :], BY_LANES))
        v = product(x, qkv_w[pl.ds(2 * width + base, 128), :], BY_LANES).astype(BF)
        queries[:, at], keys[:, at], values[:, at] = q, k, v
        probs = attention_probs(both_heads(q), k).astype(BF)
        attended[:, at] = one_row(jnp.dot(probs, v, preferred_element_type=F32)).astype(BF)
        return carry

    lax.fori_loop(0, width // 128, pair, 0)
    moves[1].wait()
    stream1[...] = stream0[...] + product(attended[...], out_w[...], BY_LANES)
    normed2[...] = rms(stream1[...], 1)
    moves[2].wait()
    step = 512
    for at in range(0, hidden_width, step):
        gate = product(normed2[...], gate_w[at : at + step, :], BY_LANES)
        up = product(normed2[...], gate_w[hidden_width + at : hidden_width + at + step, :], BY_LANES)
        gated[:, at : at + step] = gate
        gated[:, hidden_width + at : hidden_width + at + step] = up
        hidden[:, at : at + step] = (gate * (1.0 / (1.0 + jnp.exp(-gate))) * up).astype(BF)
    moves[3].wait()
    stream2[...] = stream1[...] + product(hidden[...], down_w[...], BY_LANES)
    normed3[...] = rms(stream2[...], 2)


def layer_forward(stream0, gains, turn, qkv_w, out_w, gate_w, down_w):
    length, width = stream0.shape
    hidden_width = down_w.shape[1]
    vmem, hbm = pl.BlockSpec(memory_space=pltpu.VMEM), pl.BlockSpec(memory_space=pl.ANY)
    half, full = jax.ShapeDtypeStruct((length, width), BF), jax.ShapeDtypeStruct((length, width), F32)
    outs = [half] * 5 + [full, half, jax.ShapeDtypeStruct((length, 2 * hidden_width), F32)]
    outs += [jax.ShapeDtypeStruct((length, hidden_width), BF), full, half]
    return pl.pallas_call(
        layer_kernel,
        out_shape=outs,
        in_specs=[vmem] * 3 + [hbm] * 4,
        out_specs=[vmem] * len(outs),
        scratch_shapes=[pltpu.VMEM(w.shape, BF) for w in (qkv_w, out_w, gate_w, down_w)]
        + [pltpu.SemaphoreType.DMA((4,))],
        compiler_params=pltpu.CompilerParams(vmem_limit_bytes=56 * 2**20),
        name="layer",
    )(stream0, gains, turn, qkv_w, out_w, gate_w, down_w)


def adam_update(weight, first, second, grad, rate, decay):
    first_new = BETA_ONE * first + (1.0 - BETA_ONE) * grad
    second_new = BETA_TWO * second + (1.0 - BETA_TWO) * grad * grad
    first_hat = first_new / (1.0 - BETA_ONE**STEP)
    second_hat = second_new / (1.0 - BETA_TWO**STEP)
    weight_new = weight - rate * (first_hat / (jnp.sqrt(second_hat) + ADAM_EPS) + decay * weight)
    return (weight_new, first_new, second_new)


def dot(subscripts, left, right):
    return jnp.einsum(subscripts, left, right, preferred_element_type=F32)


def local(*args):
    class_ids, null_mask, code_ids, lengths = args[:4]
    masters, firsts, seconds = args[4::3], args[5::3], args[6::3]
    code_table, class_table, qkv_weight, out_weight, gate_up, down_weight, head_weight, gains = (
        masters
    )
    rates = (0.5, 0.5, 0.05, 0.05, 0.05, 0.05, 0.05, 0.5)
    decays = (0.1, 0.1, 0.1, 0.1, 0.1, 0.1, 0.1, 0.0)
    n = lax.axis_size("fsdp")
    me = lax.axis_index("fsdp")
    batch, length = code_ids.shape
    width = qkv_weight.shape[1]
    hidden_width = down_weight.shape[1]
    table_rows, own_width = class_table.shape
    own_rows = code_table.shape[0]
    heads = width // HEAD_DIM
    rows = (qkv_weight.shape[0], gate_up.shape[0], out_weight.shape[0], down_weight.shape[0])

    classes = jnp.where(null_mask == 1, table_rows - 1, class_ids)
    previous = jnp.concatenate([jnp.full((1, 1), -1, code_ids.dtype), code_ids[:, :-1]], 1)
    pair = jnp.stack([classes[0], lengths[0]])[None].astype(F32)
    own_gains = gains.astype(BF).astype(F32)
    facts = jnp.concatenate(
        [
            previous.astype(F32).reshape(2, -1),
            code_ids.astype(F32).reshape(2, -1),
            jnp.pad(pair, ((0, 0), (0, length // 2 - 2))),
            jnp.pad(own_gains, ((0, 0), (0, length // 2 - own_width))),
        ],
        0,
    )
    class_b = jnp.pad(class_table.T.astype(BF), ((0, 128 - own_width), (0, -table_rows % 128)))
    reps = lax.axis_size("rep")
    wholes, stream0, facts = front(
        facts,
        code_table,
        class_b,
        [gate_up, qkv_weight, out_weight, down_weight],
        own_width,
        length,
        reps,
        n,
    )
    gate_w, qkv_w, out_w, down_w = (w.reshape(-1, w.shape[-1]) for w in wholes)
    stream0 = stream0[None]
    images = n * batch
    tokens = images * length
    every_fact, facts = facts, facts[lax.axis_index("rep")]
    gains32 = facts[:, 5:8, :own_width].transpose(1, 0, 2).reshape(3, width)
    all_codes = facts[:, 2:4].reshape(images, length).astype(jnp.int32)
    previous = facts[:, 0:2].reshape(tokens).astype(jnp.int32)
    all_classes = facts[:, 4, 0].astype(jnp.int32)
    all_lengths = facts[:, 4, 1].astype(jnp.int32)
    all_counted = (jnp.arange(length)[None, :] < all_lengths[:, None]).astype(F32)
    own_ids = jnp.arange(own_rows) + me * own_rows
    lookup = (previous[:, None] == own_ids[None, :]).astype(BF)

    cosine, sine = rotary_tables(length, HEAD_DIM)
    turn = jnp.stack([jnp.concatenate([t, t], -1) for t in (cosine, sine)])
    split4 = (batch, length, heads, HEAD_DIM)
    kept = layer_forward(
        stream0[0], jnp.pad(gains32, ((0, 5), (0, 0))), turn, qkv_w, out_w, gate_w, down_w
    )
    (normed1, queries, keys_rot, values, attended, stream1, normed2, gated, hidden, stream2, normed3) = (
        t[None] for t in kept
    )
    gate_part = gated[..., :hidden_width]
    up_part = gated[..., hidden_width:]
    inverse1, inverse2, inverse3 = (
        lax.rsqrt(jnp.mean(t * t, -1, keepdims=True) + NORM_EPS) for t in (stream0, stream1, stream2)
    )

    head_b = head_weight.astype(BF)
    in_kernel = reps == 2 and size_of(head_scratch(n, length, width, own_rows, reps)[0]) < 52 * 2**20
    if in_kernel:
        grad_normed3, grad_head, totals = head_phase(normed3[0], head_weight, every_fact, reps, n)
        grad_normed3 = grad_normed3[None]
        loss_sum, token_count = totals[0, 0], totals[1, 0]
        head_pair = (grad_head, lax.ppermute(grad_head, "rep", [(0, 1), (1, 0)]))
        grad_head = head_pair[0].astype(F32) + head_pair[1].astype(F32)
    else:
        token_count = lax.psum(jnp.sum(all_counted), "rep")
        normed3_all = lax.all_gather(normed3, "fsdp", axis=0, tiled=True).reshape(tokens, width)
        logits = dot("td,vd->tv", normed3_all, head_b)
        onehot = all_codes.reshape(tokens)[:, None] == own_ids[None, :]
        local_top = jnp.max(logits, -1)
        local_sum = jnp.sum(jnp.exp(logits - local_top[:, None]), -1)
        local_pick = jnp.sum(jnp.where(onehot, logits, 0.0), -1)
        stats = lax.all_gather(jnp.stack([local_top, local_sum, local_pick]), "fsdp", axis=0)
        ltop = jnp.max(stats[:, 0], 0)
        lse = jnp.log(jnp.sum(stats[:, 1] * jnp.exp(stats[:, 0] - ltop[None]), 0)) + ltop
        picked = jnp.sum(stats[:, 2], 0)
        loss_sum = lax.psum(jnp.sum(jnp.where(all_counted.reshape(tokens) > 0, lse - picked, 0.0)), "rep")
        weight_t = all_counted.reshape(tokens) * (1.0 / token_count)
        soft = jnp.exp(logits - lse[:, None])
        grad_logits = ((soft - onehot.astype(F32)) * weight_t[:, None]).astype(BF)
        grad_normed3 = dot("tv,vd->td", grad_logits, head_b).astype(BF).reshape(images, length, width)
        grad_normed3 = lax.psum_scatter(grad_normed3, "fsdp", scatter_dimension=0, tiled=True)
        grad_normed3 = grad_normed3.astype(F32)
        grad_head = dot("tv,td->vd", grad_logits, normed3_all)

    grad_stream2, gain_three = norm_backward(stream2, inverse3, gains32[2], grad_normed3)
    grad_branch = grad_stream2.astype(BF)
    grad_down = dot("btd,btf->df", grad_branch, hidden)
    grad_hidden = dot("btd,df->btf", grad_branch, down_w)
    sigma = jax.nn.sigmoid(gate_part)
    grad_gate = grad_hidden * up_part * sigma * (1.0 + gate_part * (1.0 - sigma))
    grad_up = grad_hidden * gate_part * sigma
    grad_gated = jnp.concatenate([grad_gate, grad_up], -1).astype(BF)
    grad_gate_up = dot("btf,btd->fd", grad_gated, normed2)
    grad_normed2 = dot("btf,fd->btd", grad_gated, gate_w)
    grad_middle, gain_two = norm_backward(stream1, inverse2, gains32[1], grad_normed2)
    grad_stream1 = grad_stream2 + grad_middle
    grad_attn = grad_stream1.astype(BF)
    grad_out = dot("bte,btd->ed", grad_attn, attended)
    grad_attended = dot("bte,ed->btd", grad_attn, out_w).astype(BF)
    if in_kernel:
        flat = [t[0] for t in (queries, keys_rot, values, grad_attended)]
        no_gain = jnp.zeros((width,), F32)
        gain_rows = jnp.stack([no_gain, gain_two, gain_three, gains32[0]] + [no_gain] * 4)
        layer = flat + [turn, qkv_w, stream0[0], normed1[0], grad_stream1[0], gain_rows]
        blocks = [
            g.astype(BF).reshape(n, -1, g.shape[-1]) for g in (grad_gate_up, grad_out, grad_down)
        ]
        sums, grad_codes, grad_classes, squares = tail_phase(
            layer,
            every_fact,
            head_pair,
            blocks,
            [qkv_weight.shape, (16, 128)],
            (True, False, False, False, False),
            table_rows + -table_rows % 128,
            own_width,
            n,
        )
        grad_gate_up, grad_out, grad_down, grad_qkv, gain_part = sums
        grad_gains = gain_part[:3, :own_width]
        grad_classes = grad_classes[:own_width, :table_rows].T
    else:
        queries, keys_rot, values, grad_attended = (
            t.reshape(split4) for t in (queries, keys_rot, values, grad_attended)
        )
        probs32 = jax.nn.softmax(attention_scores(queries, keys_rot), -1)
        probs = probs32.astype(BF)
        grad_probs = dot("bqhd,bkhd->bhqk", grad_attended, values)
        grad_values = dot("bhqk,bqhd->bkhd", probs, grad_attended)
        grad_scores = probs32 * (grad_probs - jnp.sum(probs32 * grad_probs, -1, keepdims=True))
        grad_scores = grad_scores.astype(BF)
        scale = HEAD_DIM ** (-0.5)
        grad_queries = dot("bhqk,bkhd->bqhd", grad_scores, keys_rot) * scale
        grad_keys = dot("bhqk,bqhd->bkhd", grad_scores, queries) * scale
        grad_mixed = jnp.concatenate(
            [
                rotate_back(grad_queries, cosine, sine).reshape(batch, length, width),
                rotate_back(grad_keys, cosine, sine).reshape(batch, length, width),
                grad_values.reshape(batch, length, width),
            ],
            -1,
        ).astype(BF)
        grad_qkv = dot("bte,btd->ed", grad_mixed, normed1)
        grad_normed1 = dot("bte,ed->btd", grad_mixed, qkv_w)
        grad_first, gain_one = norm_backward(stream0, inverse1, gains32[0], grad_normed1)
        grad_stream0 = grad_stream1 + grad_first

        grad_gains = jnp.stack([gain_one, gain_two, gain_three])
        blocks = [
            g.astype(BF).reshape(n, -1, g.shape[-1]) for g in (grad_qkv, grad_gate_up, grad_out, grad_down)
        ]
        layer_part = lax.psum_scatter(pack_rows(*blocks), "fsdp", scatter_dimension=0, tiled=False)
        rows_all = lax.all_gather(grad_stream0.astype(BF), "fsdp", axis=0, tiled=True)
        grad_codes = dot("tv,td->vd", lookup, rows_all.reshape(tokens, width))
        class_part = lax.dynamic_slice(rows_all[:, 0], (0, me * own_width), (images, own_width))
        class_spot = (all_classes[:, None] == jnp.arange(table_rows)[None, :]).astype(BF)
        grad_classes = dot("iv,id->vd", class_spot, class_part)
        summed = lax.psum(
            (grad_codes.astype(BF), grad_head.astype(BF), layer_part, grad_classes), "rep"
        )
        grad_codes, grad_head, layer_part, grad_classes = (s.astype(F32) for s in summed)
        grad_gains = lax.psum(grad_gains, ("fsdp", "rep"))
        grad_gains = lax.dynamic_slice(grad_gains, (0, me * own_width), (3, own_width))
        grad_qkv, grad_gate_up, grad_out, grad_down = unpack_rows(layer_part, rows, hidden_width)
    reduced = (
        grad_codes, grad_classes, grad_qkv, grad_out, grad_gate_up, grad_down, grad_head, grad_gains
    )
    if not in_kernel:
        squares = lax.psum(sum(jnp.sum(piece * piece) for piece in reduced), "fsdp")
    grad_norm = jnp.sqrt(squares)
    factor = jnp.minimum(1.0, 1.0 / CLIP_INV / (grad_norm + 1e-06))
    results = [loss_sum, token_count, grad_norm]
    for index in range(8):
        results.extend(
            adam_update(
                masters[index],
                firsts[index],
                seconds[index],
                reduced[index] * factor,
                rates[index],
                decays[index],
            )
        )
    return tuple(results)


def solution(mesh):
    split = P(("fsdp", "rep"))
    by_row, by_column = P("fsdp", None), P(None, "fsdp")
    weights = (by_row,) * 3 + (by_column,) * 3 + (by_row,) * 15 + (by_column,) * 3
    return jax.shard_map(
        local,
        mesh=mesh,
        in_specs=(split, split, P(("fsdp", "rep"), None), split) + weights,
        out_specs=(P(), P(), P()) + weights,
        check_vma=False,
    )
```

```python
import functools
import math

import jax
import jax.numpy as jnp
from jax import lax
from jax.experimental import pallas as pl
from jax.experimental.pallas import tpu as pltpu
from jax.sharding import PartitionSpec as P

HEAD_DIM = 64
CLIP_INV = 500
STEP = 10
NORM_EPS = 1e-05
BETA_ONE = 0.5
BETA_TWO = 0.5
ADAM_EPS = 1e-08
BF = jnp.bfloat16
F32 = jnp.float32
MESH = pl.DeviceIdType.MESH


def rotary_tables(length, width):
    half = width // 2
    freq = 10000.0 ** (-jnp.arange(half, dtype=F32) * 2.0 / width)
    angles = jnp.arange(length, dtype=F32)[:, None] * freq[None, :]
    cosine = jnp.concatenate([jnp.cos(angles), jnp.cos(angles)], -1)
    sine = jnp.concatenate([jnp.sin(angles), jnp.sin(angles)], -1)
    return (cosine, sine)


def rotate_back(grads, cosine, sine):
    half = grads.shape[-1] // 2
    scaled = grads * sine[:, None, :]
    return grads * cosine[:, None, :] + jnp.concatenate(
        [scaled[..., half:], -scaled[..., :half]], -1
    )


def norm_backward(stream, inverse, gain, grad_out):
    weighted = grad_out * gain
    inner = jnp.mean(weighted * stream, -1, keepdims=True)
    grad_in = inverse * weighted - stream * inverse * inverse * inverse * inner
    grad_gain = jnp.sum(grad_out * stream * inverse, axis=(0, 1))
    return (grad_in, grad_gain)


def attention_scores(queries, keys_rot):
    length = queries.shape[1]
    scores = jnp.einsum(
        "bqhd,bkhd->bhqk", queries, keys_rot, preferred_element_type=F32
    ) * HEAD_DIM ** (-0.5)
    causal = jnp.arange(length)[:, None] >= jnp.arange(length)[None, :]
    return jnp.where(causal, scores, -1e30)


def column_blocks(width, total):
    return [(at, min(width, total - at)) for at in range(0, total, width)]


def pack_rows(qkv, gate, out, down):
    width = qkv.shape[-1]
    parts = [qkv, gate, out]
    for at, size in column_blocks(width, down.shape[-1]):
        block = down[..., at : at + size]
        if size < width:
            pad = [(0, 0)] * (block.ndim - 1) + [(0, width - size)]
            block = jnp.pad(block, pad)
        parts.append(block)
    return jnp.concatenate(parts, -2)


def unpack_rows(packed, rows, hidden_width):
    width = packed.shape[-1]
    at, parts = 0, []
    for count in rows[:3]:
        parts.append(packed[..., at : at + count, :])
        at += count
    blocks = []
    for _, size in column_blocks(width, hidden_width):
        blocks.append(packed[..., at : at + rows[3], :size])
        at += rows[3]
    parts.append(jnp.concatenate(blocks, -1))
    return parts


def geometry(n):
    chips = n // 2
    y_size = 1 << ((chips.bit_length() - 1) // 2)
    return chips // y_size, y_size


def where_am_i(z_size, y_size):
    me = lax.axis_index("fsdp")
    return me, me // (2 * y_size), (me // 2) % y_size, me % 2


def send(src, dst, sems, index, device):
    pltpu.make_async_remote_copy(
        src_ref=src, dst_ref=dst, send_sem=sems.at[(0,) + index], recv_sem=sems.at[(1,) + index],
        device_id=device, device_id_type=MESH,
    ).start()


def arrival(dst, sems, index):
    pltpu.make_async_copy(dst, dst, sems.at[(1,) + index]).wait()


def departure(src, sems, index):
    pltpu.make_async_copy(src, src, sems.at[(0,) + index]).wait()


def weight_pieces(rows, reps):
    gate = rows[0]
    cut = gate * 15 // 16 // 16 * 16
    middle = cut // 2 // 16 * 16
    one = 1 % reps
    return (
        (2, 0, rows[2], 2 % reps),
        (0, cut, gate - cut, one),
        (0, 0, middle, 0),
        (3, 0, rows[3], 3 % reps),
        (0, middle, cut - middle, 0),
        (1, 0, rows[1], one),
    )


def front(facts, code_table, class_b, weights, own_width, length, reps, n):
    z_size, y_size = geometry(n)
    width = code_table.shape[1]
    count = len(weights)
    pieces = weight_pieces([w.shape[0] for w in weights], reps)
    many = len(pieces)
    spots = z_size * y_size
    block = (length, width)
    vmem, hbm = pl.BlockSpec(memory_space=pltpu.VMEM), pl.BlockSpec(memory_space=pl.ANY)
    dma = pltpu.SemaphoreType.DMA
    outs = pl.pallas_call(
        functools.partial(front_kernel, z_size, y_size, reps, own_width, pieces, count),
        out_shape=[jax.ShapeDtypeStruct((n,) + w.shape, BF) for w in weights]
        + [jax.ShapeDtypeStruct(block, F32), jax.ShapeDtypeStruct((reps, n, 8, 128), F32)],
        in_specs=[vmem] * (3 + count),
        out_specs=[hbm] * count + [vmem] * 2,
        scratch_shapes=[
            pltpu.VMEM(code_table.shape, BF),
            pltpu.VMEM((128, n * 8), F32),
            pltpu.VMEM((spots,) + block, BF),
            pltpu.VMEM((spots,) + block, BF),
            pltpu.VMEM((spots,) + block, BF),
            pltpu.VMEM((z_size, y_size) + block, BF),
            pltpu.VMEM((z_size,) + block, BF),
            dma((2, n)),
            dma((2, reps)),
            dma((2, many, 2, z_size)),
            dma((2, many, z_size, y_size)),
            dma((2, many, z_size, y_size, reps)),
            dma((2, many, z_size, y_size)),
            dma((count,)),
            dma((2, spots)),
            dma((2, z_size, y_size)),
            dma((2, z_size)),
        ]
        + [pltpu.VMEM(w.shape, BF) for w in weights],
        compiler_params=pltpu.CompilerParams(
            collective_id=0, has_side_effects=True, vmem_limit_bytes=60 * 2**20
        ),
        name="front",
    )(facts, code_table, class_b, *weights)
    return outs[:count], outs[count], outs[count + 1]


class Place:
    def __init__(self, z_size, y_size, reps):
        self.z_size, self.y_size, self.reps = z_size, y_size, reps
        self.n = z_size * y_size * 2
        self.me, self.z, self.y, self.core = where_am_i(z_size, y_size)
        self.x = lax.axis_index("rep")

    def at(self, dz, dy, other=0):
        c = 1 - self.core if other else self.core
        z, y = lax.rem(self.z + dz, self.z_size), lax.rem(self.y + dy, self.y_size)
        return (z * self.y_size + y) * 2 + c

    def plane(self, z, dy=0, other=0):
        c = 1 - self.core if other else self.core
        return (z * self.y_size + lax.rem(self.y + dy, self.y_size)) * 2 + c

    def twin(self):
        return (self.at(0, 0, 1), self.x)

    def greet(self, everyone):
        barrier = pltpu.get_barrier_semaphore()
        if everyone:
            group = [lax.rem(self.me + k, self.n) for k in range(1, self.n)]
        else:
            group = [self.at(dz, 0) for dz in range(1, self.z_size)]
            group += [self.at(0, dy) for dy in range(1, self.y_size)] + [self.at(0, 0, 1)]
        peers = [(p, self.x) for p in group]
        peers += [(self.me, lax.rem(self.x + k, self.reps)) for k in range(1, self.reps)]
        for peer in peers:
            pl.semaphore_signal(barrier, inc=1, device_id=peer, device_id_type=MESH)
        pl.semaphore_wait(barrier, len(peers))


class Spread:
    def __init__(self, place, whole, z_sems, y_sems, c_sems, x_sems=None, part=None, rows=None):
        self.p, self.whole, self.part, self.rows = place, whole, part, rows
        self.z_sems, self.y_sems, self.c_sems, self.x_sems = z_sems, y_sems, c_sems, x_sems

    def block(self, z, dy=0, other=0):
        block = self.whole.at[self.p.plane(z, dy, other)]
        return block if self.rows is None else block.at[pl.ds(*self.rows)]

    def in_part(self, act):
        if self.part is None:
            act()
        else:
            pl.when(self.p.x == self.part)(act)

    def hand_over(self, z, dy, src, dst):
        p = self.p
        if self.part is not None:
            for dx in range(1, p.reps):
                send(src, dst, self.x_sems, (z, dy, dx), (p.me, lax.rem(p.x + dx, p.reps)))
        send(src, dst, self.c_sems, (z, dy), p.twin())

    def pass_on(self, z, src, up, down):
        p = self.p
        dst = self.block(z)
        if up:

            @pl.when(p.z + 1 < p.z_size)
            def _():
                send(src, dst, self.z_sems, (0, z), (p.plane(p.z + 1), p.x))

        if down:

            @pl.when(p.z >= 1)
            def _():
                send(src, dst, self.z_sems, (1, z), (p.plane(p.z - 1), p.x))

        for dy in range(1, p.y_size):
            send(src, dst, self.y_sems, (z, dy), (p.at(0, dy), p.x))

    def start(self, own):
        self.in_part(lambda: self.pass_on(self.p.z, own, True, True))
        send(own, self.block(self.p.z), self.c_sems, (self.p.z, 0), self.p.twin())

    def near(self, s, act):
        p = self.p
        if s == 0:
            act(p.z)
            return

        @pl.when(p.z - s >= 0)
        def _():
            act(p.z - s)

        @pl.when(p.z + s < p.z_size)
        def _():
            act(p.z + s)

    def step_z(self, s):
        p = self.p

        def take(z, up):
            block = self.block(z)
            arrival(block, self.z_sems, (1 - int(up), z))
            self.pass_on(z, block, up, not up)
            self.hand_over(z, 0, block, block)

        def act():
            @pl.when(p.z - s >= 0)
            def _():
                take(p.z - s, True)

            @pl.when(p.z + s < p.z_size)
            def _():
                take(p.z + s, False)

        self.in_part(act)

    def step_y(self, s):
        def take(z):
            for dy in range(1, self.p.y_size):
                block = self.block(z, self.p.y_size - dy)
                arrival(block, self.y_sems, (z, dy))
                self.hand_over(z, dy, block, block)

        self.in_part(lambda: self.near(s, take))

    def step_x(self, s):
        p = self.p

        def take(z):
            for dy in range(0 if s else 1, p.y_size):
                block = self.block(z, p.y_size - dy)
                arrival(block, self.x_sems, (z, dy, lax.rem(p.x - self.part + p.reps, p.reps)))
                send(block, block, self.c_sems, (z, dy), p.twin())

        pl.when(p.x != self.part)(lambda: self.near(s, take))

    def take_twin(self, z):
        for dy in range(self.p.y_size):
            arrival(self.block(z, self.p.y_size - dy, 1), self.c_sems, (z, dy))

    def finish(self):
        p = self.p
        block = self.block(p.z)
        for z in range(p.z_size):
            for dy in range(p.y_size):
                departure(block, self.c_sems, (z, dy))

        def act():
            for z in range(p.z_size):

                @pl.when(jnp.logical_and(p.z + 1 < p.z_size, z <= p.z))
                def _():
                    departure(block, self.z_sems, (0, z))

                @pl.when(jnp.logical_and(p.z >= 1, z >= p.z))
                def _():
                    departure(block, self.z_sems, (1, z))

                for dy in range(1, p.y_size):
                    departure(block, self.y_sems, (z, dy))
                if self.part is None:
                    continue
                for dy in range(p.y_size):
                    for dx in range(1, p.reps):
                        if dy:
                            departure(block, self.x_sems, (z, dy, dx))
                        else:

                            @pl.when(z != p.z)
                            def _():
                                departure(block, self.x_sems, (z, dy, dx))

        self.in_part(act)


def front_kernel(z_size, y_size, reps, own_width, pieces, count, facts, code_table, class_b, *refs):
    masters, refs = refs[:count], refs[count:]
    wholes, refs = refs[:count], refs[count:]
    weights, refs = refs[-count:], refs[:-count]
    (stream, facts_all, code_b, turned, acc, core_out, core_in, y_in, z_in,
     fact_sems, rep_sems, z_sems, y_sems, x_sems, c_sems, own_sems, rc_sems, ry_sems, rz_sems) = refs
    p = Place(z_size, y_size, reps)
    n, me, x = p.n, p.me, p.x
    length, width = stream.shape
    own_rows = code_table.shape[0]
    p.greet(True)

    for k in range(1, n):
        send(facts, facts_all.at[x, me], fact_sems, (k,), (lax.rem(me + k, n), x))
    facts_all[x, me] = facts[...]
    for k in range(count):
        weights[k][...] = masters[k][...].astype(BF)
    spreads = []
    for i, (k, start, size, part) in enumerate(pieces):
        sems = [group.at[:, i] for group in (z_sems, y_sems, c_sems, x_sems)]
        spreads.append(Spread(p, wholes[k], *sems, part, (start, size)))
        spreads[i].start(weights[k].at[pl.ds(start, size)])
    for k in range(count):
        pltpu.make_async_copy(weights[k], wholes[k].at[me], own_sems.at[k]).start()
    code_b[...] = code_table[...].astype(BF)

    for k in range(1, n):
        arrival(facts_all.at[x, lax.rem(me - k + n, n)], fact_sems, (k,))
    for k in range(1, reps):
        send(facts_all.at[x], facts_all.at[x], rep_sems, (k,), (me, lax.rem(x + k, reps)))
    turned[...] = jnp.transpose(facts_all[x].reshape(n * 8, 128))
    lane = lax.broadcasted_iota(jnp.int32, (128, n * 8), 1)
    class_iota = lax.broadcasted_iota(jnp.int32, (16, class_b.shape[1]), 1).astype(F32)
    row_iota = lax.broadcasted_iota(jnp.int32, (length // 2, own_rows), 1) + me * own_rows
    row_iota = row_iota.astype(F32)

    def found(image, out):
        cls = jnp.sum(jnp.where(lane[:1] == image * 8 + 4, turned[:1, :], 0.0), -1, keepdims=True)
        spot = jnp.where(class_iota == cls, 1.0, 0.0).astype(BF)
        row = lax.dot_general(
            spot, class_b[...], (((1,), (1,)), ((), ())), preferred_element_type=F32
        )
        row = jnp.concatenate([row, jnp.zeros((16, width - row.shape[1]), F32)], -1)
        row = pltpu.roll(row, me * own_width, 1)
        for half in range(2):
            ids = jnp.sum(jnp.where(lane == image * 8 + half, turned[...], 0.0), -1, keepdims=True)
            spot = jnp.where(row_iota == ids, 1.0, 0.0).astype(BF)
            rows = jnp.dot(spot, code_b[...], preferred_element_type=F32)
            out[pl.ds(half * (length // 2), length // 2)] = rows.astype(BF)
            if half == 0:
                first = lax.broadcasted_iota(jnp.int32, (16, width), 0) == 0
                head = jnp.where(first, row, rows[:16])
                out[pl.ds(0, 16)] = head.astype(BF)

    def look_up(dz):
        def body(j, carry):
            dy = y_size - 1 - j
            slot = dz * y_size + dy
            found(p.at(dz, dy, 1), core_out.at[slot])
            send(core_out.at[slot], core_in.at[slot], rc_sems, (slot,), p.twin())
            found(p.at(dz, dy), acc.at[slot])
            return carry

        lax.fori_loop(0, y_size, body, 0)

    def twin_sum(dz):
        for dy in range(y_size - 1, -1, -1):
            slot = dz * y_size + dy
            arrival(core_in.at[slot], rc_sems, (slot,))
            acc[slot] = (acc[slot].astype(F32) + core_in[slot].astype(F32)).astype(BF)
            if dy:
                send(acc.at[slot], y_in.at[dz, dy], ry_sems, (dz, dy), (p.at(0, dy), x))

    def y_sum(dz):
        slot = dz * y_size
        total = acc[slot].astype(F32)
        for dy in range(1, y_size):
            arrival(y_in.at[dz, dy], ry_sems, (dz, dy))
            total = total + y_in[dz, dy].astype(F32)
        acc[slot] = total.astype(BF)
        if dz:
            send(acc.at[slot], z_in.at[dz], rz_sems, (dz,), (p.at(dz, 0), x))

    for s in range(1, z_size + 1):
        for spread in spreads:
            if s < z_size:
                spread.step_z(s)
        for spread in spreads:
            spread.step_y(s - 1)
        look_up(z_size - s)
        if s >= 2:
            twin_sum(z_size - s + 1)
        if s >= 3:
            y_sum(z_size - s + 2)
    twin_sum(0)
    for spread in spreads:
        spread.step_x(0)
    y_sum(1)
    for s in range(1, z_size - 1):
        for spread in spreads:
            spread.step_x(s)
    y_sum(0)
    total = acc[0].astype(F32)
    for dz in range(1, z_size):
        arrival(z_in.at[dz], rz_sems, (dz,))
        total = total + z_in[dz].astype(F32)
    stream[...] = total
    for spread in spreads:
        spread.step_x(z_size - 1)

    for k in range(1, reps):
        arrival(facts_all.at[x], rep_sems, (k,))
        departure(facts_all.at[x], rep_sems, (k,))
    for k in range(1, n):
        departure(facts, fact_sems, (k,))
    for dz in range(z_size):
        for dy in range(y_size):
            slot = dz * y_size + dy
            departure(core_out.at[slot], rc_sems, (slot,))
            if dy:
                departure(acc.at[slot], ry_sems, (dz, dy))
            elif dz:
                departure(acc.at[slot], rz_sems, (dz,))
    for k in range(count):
        pltpu.make_async_copy(weights[k], wholes[k].at[me], own_sems.at[k]).wait()
    for spread in spreads:
        for z in range(z_size):
            spread.take_twin(z)
        spread.finish()


def head_kernel(z_size, y_size, reps, normed3, head_weight, facts, grad_normed3, grad_head, totals,
                whole, logits, grads, turned, marks, stats_in, lse_all, acc, core_out, core_in, y_in, z_in,
                loss_in, head_b, z_sems, y_sems, c_sems, st_sems, ls_sems, rc_sems, ry_sems, rz_sems, lo_sems):
    p = Place(z_size, y_size, reps)
    n, me, x = p.n, p.me, p.x
    length, width = normed3.shape
    half = length // 2
    own_rows = head_weight.shape[0]
    p.greet(True)
    spread = Spread(p, whole, z_sems, y_sems, c_sems)
    spread.start(normed3)
    head_b[...] = head_weight[...].astype(BF)
    whole[me] = normed3[...]
    own_facts = facts.at[x]
    turned[...] = jnp.transpose(own_facts[...].reshape(n * 8, 128))
    lane = lax.broadcasted_iota(jnp.int32, (128, n * 8), 1)
    full_lane = lax.broadcasted_iota(jnp.int32, (length, n * 8), 1)
    column_iota = (lax.broadcasted_iota(jnp.int32, (length, own_rows), 1) + me * own_rows).astype(F32)
    token = lax.broadcasted_iota(jnp.int32, (length, 1), 0).astype(F32)
    every = facts[...].reshape(reps * n * 8, 128)
    row8 = lax.rem(lax.broadcasted_iota(jnp.int32, every.shape, 0), 8)
    spot = jnp.logical_and(row8 == 4, lax.broadcasted_iota(jnp.int32, every.shape, 1) == 1)
    token_count = jnp.sum(jnp.sum(jnp.where(spot, every, 0.0), 0, keepdims=True), 1, keepdims=True)
    inv_count = 1.0 / token_count

    def codes_of(image):
        parts = [
            jnp.sum(jnp.where(lane == image * 8 + 2 + h, turned[...], 0.0), -1, keepdims=True)
            for h in range(2)
        ]
        return jnp.concatenate(parts, 0)

    marks[...] = jnp.zeros_like(marks)

    def forward(image):
        out = lax.dot_general(
            whole[image], head_b[...], (((1,), (1,)), ((), ())), preferred_element_type=F32
        )
        logits[image] = out
        top = jnp.max(out, -1, keepdims=True)
        total = jnp.sum(jnp.exp(out - top), -1, keepdims=True)
        pick = jnp.sum(jnp.where(column_iota == codes_of(image), out, 0.0), -1, keepdims=True)
        old = marks[...]
        old = jnp.where(full_lane == image * 8, top, old)
        old = jnp.where(full_lane == image * 8 + 1, total, old)
        marks[...] = jnp.where(full_lane == image * 8 + 2, pick, old)

    def forward_column(z, first, last):
        def body(j, carry):
            forward(p.plane(z, lax.rem(y_size - j // 2, y_size), 0) + lax.rem(j, 2) * (1 - 2 * p.core))
            return carry

        lax.fori_loop(first * 2, last * 2, body, 0)

    arrival(spread.block(p.z, 0, 1), c_sems, (p.z, 0))
    forward_column(p.z, 0, 1)

    def one(z, s):
        arrival(spread.block(z, 0, 1), c_sems, (z, 0))
        forward_column(z, 0, 1)

    def other(z):
        for dy in range(1, y_size):
            arrival(spread.block(z, y_size - dy, 1), c_sems, (z, dy))
        forward_column(z, 1, y_size)

    def both(s, act):
        if s == 0:
            act(p.z)
            return

        @pl.when(p.z - s >= 0)
        def _():
            act(p.z - s)

        @pl.when(p.z + s < z_size)
        def _():
            act(p.z + s)

    for s in range(1, z_size + 1):
        if s < z_size:
            spread.step_z(s)
        spread.step_y(s - 1)
        if s < z_size:
            both(s, lambda z: one(z, s))
        both(s - 1, other)

    tiles = jnp.transpose(marks[...]).reshape(n, 8, length)
    stats_in[1] = tiles
    for k in range(1, n):
        peer = lax.rem(me + k, n)
        send(stats_in.at[1, peer], stats_in.at[0, me], st_sems, (k,), (peer, x))
    stats_in[0, me] = stats_in[1, me]
    for k in range(1, n):
        arrival(stats_in.at[0, 0], st_sems, (k,))
    tops = stats_in[0, :, 0, :]
    sums = stats_in[0, :, 1, :]
    picks = stats_in[0, :, 2, :]
    top = jnp.max(tops, 0, keepdims=True)
    lse = jnp.log(jnp.sum(sums * jnp.exp(tops - top), 0, keepdims=True)) + top
    pick = jnp.sum(picks, 0, keepdims=True)
    here = own_facts[me]
    counted = lax.broadcasted_iota(jnp.int32, (1, length), 1).astype(F32) < here[4:5, 1:2]
    loss = jnp.where(counted, lse - pick, 0.0)
    lse_all[me] = jnp.concatenate([lse, loss, jnp.zeros((6, length), F32)], 0)
    for k in range(1, n):
        peer = lax.rem(me + k, n)
        send(lse_all.at[me], lse_all.at[me], ls_sems, (k,), (peer, x))
    for k in range(1, n):
        arrival(lse_all.at[0], ls_sems, (k,))
    table = lse_all[...].reshape(n * 8, length)
    row8 = lax.rem(lax.broadcasted_iota(jnp.int32, table.shape, 0), 8)
    group = jnp.sum(jnp.sum(jnp.where(row8 == 1, table, 0.0), 0, keepdims=True), 1, keepdims=True)
    loss_in[x] = jnp.broadcast_to(group, (8, 128))
    for k in range(1, reps):
        peer = (me, lax.rem(x + k, reps))
        send(loss_in.at[x], loss_in.at[x], lo_sems, (k,), peer)
    marks[...] = jnp.transpose(table)

    def backward(image, out):
        lse_t = jnp.sum(jnp.where(full_lane == image * 8, marks[...], 0.0), -1, keepdims=True)
        size = jnp.sum(jnp.where(lane[:8] == image * 8 + 4, turned[:8, :], 0.0), -1, keepdims=True)
        weight = jnp.where(token < size[1:2], inv_count, 0.0)
        hot = jnp.where(column_iota == codes_of(image), 1.0, 0.0)
        grad = ((jnp.exp(logits[image] - lse_t) - hot) * weight).astype(BF)
        grads[image] = grad
        out[...] = jnp.dot(grad, head_b[...], preferred_element_type=F32).astype(BF)

    last = z_size - 1

    def far(j):
        return last - j // y_size, lax.rem(j, y_size)

    def first_pass(j, carry):
        dz, dyy = far(j)
        dy = y_size - 1 - dyy
        slot = dz * y_size + dy
        backward(p.at(dz, dy, 1), core_out.at[slot])
        send(core_out.at[slot], core_in.at[slot], rc_sems, (slot,), p.twin())
        backward(p.at(dz, dy), acc.at[slot])
        return carry

    def twin_sum(slot):
        arrival(core_in.at[slot], rc_sems, (slot,))
        acc[slot] = (acc[slot].astype(F32) + core_in[slot].astype(F32)).astype(BF)

    def y_sum(dz):
        slot = dz * y_size
        total = acc[slot].astype(F32)
        for dy in range(1, y_size):
            arrival(y_in.at[dz, dy], ry_sems, (dz, dy))
            total = total + y_in[dz, dy].astype(F32)
        acc[slot] = total.astype(BF)

    def round_of(g, carry):
        dz = last - g

        def per_dy(i, c):
            return first_pass(g * y_size + i, c)

        lax.fori_loop(0, y_size, per_dy, 0)
        for dy in range(y_size - 1, -1, -1):
            slot = dz * y_size + dy
            twin_sum(slot)
            if dy:
                send(acc.at[slot], y_in.at[dz, dy], ry_sems, (dz, dy), (p.at(0, dy), x))

        @pl.when(g >= 1)
        def _():
            y_sum(dz + 1)
            send(acc.at[(dz + 1) * y_size], z_in.at[dz + 1], rz_sems, (dz + 1,), (p.at(dz + 1, 0), x))

        return carry

    lax.fori_loop(0, z_size, round_of, 0)

    blocks = 4
    rows = own_rows // blocks
    for r in range(blocks):

        def add(image, total):
            return total + lax.dot_general(
                grads[image, :, r * rows : (r + 1) * rows], whole[image],
                (((0,), (0,)), ((), ())), preferred_element_type=F32,
            )

        total = lax.fori_loop(0, n, add, jnp.zeros((rows, width), F32))
        grad_head[r * rows : (r + 1) * rows] = total.astype(BF)
    y_sum(0)
    total = acc[0].astype(F32)
    for dz in range(1, z_size):
        arrival(z_in.at[dz], rz_sems, (dz,))
        total = total + z_in[dz].astype(F32)
    grad_normed3[...] = total
    for k in range(1, reps):
        arrival(loss_in.at[0], lo_sems, (k,))
    loss_sum = loss_in[0]
    for k in range(1, reps):
        loss_sum = loss_sum + loss_in[k]
    totals[...] = jnp.where(
        lax.broadcasted_iota(jnp.int32, (8, 128), 0) == 0, loss_sum, token_count
    )

    spread.finish()
    for k in range(1, n):
        departure(stats_in.at[0, 0], st_sems, (k,))
        departure(lse_all.at[0], ls_sems, (k,))
    for k in range(1, reps):
        departure(loss_in.at[0], lo_sems, (k,))
    for dz in range(z_size):
        for dy in range(y_size):
            slot = dz * y_size + dy
            departure(core_out.at[slot], rc_sems, (slot,))
            if dy:
                departure(acc.at[slot], ry_sems, (dz, dy))
            elif dz:
                departure(acc.at[slot], rz_sems, (dz,))


def head_scratch(n, length, width, own_rows, reps):
    z_size, y_size = geometry(n)
    spots = z_size * y_size
    dma = pltpu.SemaphoreType.DMA
    buffers = [
        ((n, length, width), BF),
        ((n, length, own_rows), F32),
        ((n, length, own_rows), BF),
        ((128, n * 8), F32),
        ((length, n * 8), F32),
        ((2, n, 8, length), F32),
        ((n, 8, length), F32),
        ((spots, length, width), BF),
        ((spots, length, width), BF),
        ((spots, length, width), BF),
        ((z_size, y_size, length, width), BF),
        ((z_size, length, width), BF),
        ((reps, 8, 128), F32),
        ((own_rows, width), BF),
    ]
    sems = [
        dma((2, 2, z_size)), dma((2, z_size, y_size)), dma((2, z_size, y_size)),
        dma((2, n)), dma((2, n)), dma((2, spots)), dma((2, z_size, y_size)), dma((2, z_size)),
        dma((2, reps)),
    ]
    return buffers, sems


def size_of(buffers):
    return sum(math.prod(shape) * jnp.dtype(kind).itemsize for shape, kind in buffers)


def head_phase(normed3, head_weight, facts, reps, n):
    z_size, y_size = geometry(n)
    length, width = normed3.shape
    buffers, sems = head_scratch(n, length, width, head_weight.shape[0], reps)
    vmem = pl.BlockSpec(memory_space=pltpu.VMEM)
    return pl.pallas_call(
        functools.partial(head_kernel, z_size, y_size, reps),
        out_shape=[
            jax.ShapeDtypeStruct((length, width), F32),
            jax.ShapeDtypeStruct(head_weight.shape, BF),
            jax.ShapeDtypeStruct((8, 128), F32),
        ],
        in_specs=[vmem] * 3,
        out_specs=[vmem] * 3,
        scratch_shapes=[pltpu.VMEM(shape, kind) for shape, kind in buffers] + sems,
        compiler_params=pltpu.CompilerParams(
            collective_id=1, has_side_effects=True, vmem_limit_bytes=60 * 2**20
        ),
        name="head",
    )(normed3, head_weight, facts)


def tail_kernel(z_size, y_size, own_width, split, counts, queries, keys, values, attended, normed1, normed2,
                stream0, stream1, stream2, grad_normed3, turn, gains, facts, head_one, *refs):
    count = len(split)
    weights, refs = refs[: count - 1], refs[count - 1 :]
    sums, refs = refs[:count], refs[count:]
    code_out, code_in, class_sum, head_two, squares, refs = *refs[:5], refs[5:]
    grads, refs = refs[:count], refs[count:]
    core_in, refs = refs[:count], refs[count:]
    x_in, refs = refs[:count], refs[count:]
    y_in, refs = refs[:count], refs[count:]
    z_in, refs = refs[:count], refs[count:]
    trade, refs = refs[:count], refs[count:]
    (whole, rows_out, given, grad_mixed, grad_gated, hidden, grad_stream1, grad_attended, grad_stream0,
     z_sems, y_sems, c_sems, own_sems, rc_sems, rx_sems,
     ry_sems, rz_sems, tr_sems, co_sems, fr_sems, hd_sems, sq_sems) = refs
    p = Place(z_size, y_size, 2)
    n, me, x = p.n, p.me, p.x
    length, width = stream0.shape
    hidden_width = hidden.shape[1]
    own_rows = code_out.shape[0]
    gate_at, out_at, down_at, qkv_at, gain_at = range(5)
    late = [qkv_at, gain_at]
    halved = [k for k in (down_at, gate_at, out_at) if split[k]]
    plain = [k for k in (down_at, gate_at, out_at) if not split[k]]
    for k in range(count - 1):
        pltpu.make_async_copy(weights[k], grads[k], own_sems.at[k]).start()
    p.greet(True)
    mate = (me, 1 - x)
    spread = Spread(p, whole, z_sems, y_sems, c_sems)
    send(head_one, head_two, hd_sems, (), mate)

    def weight(k):
        pltpu.make_async_copy(weights[k], grads[k], own_sems.at[k]).wait()

    def slot_of(dz, dy):
        return dz * y_size + dy

    order = [(dz, dy) for dz in range(z_size - 1, -1, -1) for dy in range(y_size - 1, -1, -1)]

    def block_of(k, f):
        rows = counts[k]
        return grads[k].at[pl.ds(pl.multiple_of(f * rows, rows), rows)]

    def to_twin(kinds):
        for dz, dy in order:
            slot = slot_of(dz, dy)
            for k in kinds:
                send(block_of(k, p.at(dz, dy, 1)), core_in[k].at[slot], rc_sems, (k, slot), p.twin())

    def half_of(k, ref, which):
        columns = sums[k].shape[1] // 2
        return ref.at[:, pl.ds(pl.multiple_of(which * columns, columns), columns)]

    def ref_of(k, ref, which):
        return half_of(k, ref, which) if split[k] else ref

    def twin_sums(kinds, dz):
        def body(dy, carry):
            slot = slot_of(dz, dy)
            for k in kinds:
                arrival(core_in[k].at[slot], rc_sems, (k, slot))
                own = block_of(k, p.at(dz, dy))[...].astype(F32)
                core_in[k][slot] = (own + core_in[k][slot].astype(F32)).astype(BF)
                if split[k]:
                    send(half_of(k, core_in[k].at[slot], 1 - x), x_in[k].at[slot], rx_sems, (k, slot), mate)
            return carry

        lax.fori_loop(0, y_size, body, 0)

    def y_slot(dz, dy):
        return dz * (y_size - 1) + dy - 1

    def send_y(kinds, dz):
        for dy in range(1, y_size):
            for k in kinds:
                source = ref_of(k, core_in[k].at[slot_of(dz, dy)], x)
                at = y_slot(dz, dy)
                send(source, y_in[k].at[at], ry_sems, (k, at), (p.at(0, dy), x))

    def take_x(dz):
        def body(dy, carry):
            slot = slot_of(dz, dy)
            for k in halved:
                arrival(x_in[k].at[slot], rx_sems, (k, slot))
                mine = half_of(k, core_in[k].at[slot], x)
                mine[...] = (mine[...].astype(F32) + x_in[k][slot].astype(F32)).astype(BF)
            return carry

        lax.fori_loop(0, y_size, body, 0)
        send_y(halved, dz)

    def take_y(kinds, dz):
        for k in kinds:
            mine = ref_of(k, core_in[k].at[slot_of(dz, 0)], x)
            total = mine[...].astype(F32)
            for dy in range(1, y_size):
                at = y_slot(dz, dy)
                arrival(y_in[k].at[at], ry_sems, (k, at))
                total = total + y_in[k][at].astype(F32)
            mine[...] = total.astype(BF)
            if dz:
                send(mine, z_in[k].at[dz - 1], rz_sems, (k, dz - 1), (p.at(dz, 0), x))

    def settle(kinds):
        for k in kinds:
            mine = ref_of(k, core_in[k].at[0], x)
            total = mine[...].astype(F32)
            for dz in range(1, z_size):
                arrival(z_in[k].at[dz - 1], rz_sems, (k, dz - 1))
                total = total + z_in[k][dz - 1].astype(F32)
            source = ref_of(k, trade[k].at[0], x)
            source[...] = total.astype(BF)
            target = source if split[k] else trade[k].at[1]
            send(source, target, tr_sems, (k,), mate)

    def collect(kinds):
        summed = jnp.zeros((1, 1), F32)
        for k in kinds:
            if split[k]:
                arrival(half_of(k, trade[k].at[0], 1 - x), tr_sems, (k,))
                total = trade[k][0].astype(F32)
            else:
                arrival(trade[k].at[1], tr_sems, (k,))
                total = trade[k][0].astype(F32) + trade[k][1].astype(F32)
            sums[k][...] = total
            summed = summed + square(total)
        return summed

    def square(value):
        return jnp.sum(jnp.sum(value * value, 0, keepdims=True), 1, keepdims=True)

    def norm_back(stream, row, grad_out):
        inverse = lax.rsqrt(jnp.mean(stream * stream, -1, keepdims=True) + NORM_EPS)
        weighted = grad_out * gains[row : row + 1, :]
        inner = jnp.mean(weighted * stream, -1, keepdims=True)
        grad = inverse * weighted - stream * (inverse * inverse * inverse) * inner
        return grad, jnp.sum(grad_out * stream * inverse, 0, keepdims=True)

    grad_stream2, gain_three = norm_back(stream2[...], 2, grad_normed3[...])
    grad_stream1[...] = grad_stream2
    grad_stream0[...] = grad_stream2.astype(BF)
    weight(gate_at)
    weight(down_at)
    step = 512
    for at in range(0, hidden_width, step):
        gate = product(normed2[...], grads[gate_at][at : at + step, :], BY_LANES)
        up = product(normed2[...], grads[gate_at][hidden_width + at : hidden_width + at + step, :], BY_LANES)
        back = jnp.dot(grad_stream0[...], grads[down_at][:, at : at + step], preferred_element_type=F32)
        sigma = 1.0 / (1.0 + jnp.exp(-gate))
        hidden[:, at : at + step] = (gate * sigma * up).astype(BF)
        grad_gated[:, at : at + step] = (back * up * sigma * (1.0 + gate * (1.0 - sigma))).astype(BF)
        grad_gated[:, hidden_width + at : hidden_width + at + step] = (back * gate * sigma).astype(BF)
    for at in range(0, hidden_width, step):
        grads[down_at][:, at : at + step] = product(
            grad_stream0[...], hidden[:, at : at + step], BY_ROWS
        ).astype(BF)
    to_twin([down_at])
    grad_normed2 = jnp.dot(grad_gated[...], grads[gate_at][...], preferred_element_type=F32)
    for at in range(0, 2 * hidden_width, step):
        grads[gate_at][at : at + step, :] = product(
            grad_gated[:, at : at + step], normed2[...], BY_ROWS
        ).astype(BF)
    to_twin([gate_at])
    grad_middle, gain_two = norm_back(stream1[...], 1, grad_normed2)
    grad_stream1[...] = grad_stream1[...] + grad_middle
    grad_stream0[...] = grad_stream1[...].astype(BF)
    weight(out_at)
    grad_attended[...] = jnp.dot(
        grad_stream0[...], grads[out_at][...], preferred_element_type=F32
    ).astype(BF)
    grads[out_at][...] = product(grad_stream0[...], attended[...], BY_ROWS).astype(BF)
    to_twin([out_at])

    lane = lax.broadcasted_iota(jnp.int32, (length, 128), 1)
    low = lax.rem(lane, HEAD_DIM) < HEAD_DIM // 2
    scale = HEAD_DIM ** (-0.5)

    def turn_back(grad):
        scaled = grad * turn[1]
        other = jnp.where(
            low, pltpu.roll(scaled, 128 - HEAD_DIM // 2, 1), -pltpu.roll(scaled, HEAD_DIM // 2, 1)
        )
        return grad * turn[0] + other

    def pair(j, carry):
        base = pl.multiple_of(j * 128, 128)
        at = pl.ds(base, 128)
        q, k, v, grad = queries[:, at], keys[:, at], values[:, at], grad_attended[:, at]
        q_two, grad_two = both_heads(q), both_heads(grad)
        probs = attention_probs(q_two, k)
        grad_probs = product(grad_two, v, BY_LANES)
        inner = jnp.sum(probs * grad_probs, -1, keepdims=True)
        grad_scores = (probs * (grad_probs - inner)).astype(BF)
        grad_v = product(probs.astype(BF), grad_two, BY_ROWS)
        grad_q = one_row(jnp.dot(grad_scores, k, preferred_element_type=F32))
        grad_k = product(grad_scores, q_two, BY_ROWS)
        grad_mixed[:, at] = turn_back(grad_q * scale).astype(BF)
        grad_mixed[:, pl.ds(width + base, 128)] = turn_back(grad_k * scale).astype(BF)
        grad_mixed[:, pl.ds(2 * width + base, 128)] = grad_v.astype(BF)
        return carry

    pairs = width // 128
    for s in range(z_size):
        dz = z_size - 1 - s
        twin_sums(halved, dz)
        twin_sums(plain, dz)
        send_y(plain, dz)
        lax.fori_loop(s * pairs // z_size, (s + 1) * pairs // z_size, pair, 0)

    weight(qkv_at)
    grad_normed1 = jnp.dot(grad_mixed[...], grads[qkv_at][...], preferred_element_type=F32)
    grad_first, gain_one = norm_back(stream0[...], 0, grad_normed1)
    grad_stream0[...] = (grad_stream1[...] + grad_first).astype(BF)
    spread.start(grad_stream0)
    whole[me] = grad_stream0[...]
    step = 3 * width // 6
    for at in range(0, 3 * width, step):
        grads[qkv_at][at : at + step, :] = product(
            grad_mixed[:, at : at + step], normed1[...], BY_ROWS
        ).astype(BF)
    row = lax.broadcasted_iota(jnp.int32, (16, width), 0)
    all_gains = jnp.where(row == 2, gain_three, 0.0)
    all_gains = jnp.where(row == 0, gain_one, jnp.where(row == 1, gain_two, all_gains))

    def gain_block(f, carry):
        turned = pltpu.roll(all_gains, lax.rem(width - f * own_width, width), 1)[:, :128]
        own = lax.broadcasted_iota(jnp.int32, turned.shape, 1) < own_width
        block_of(gain_at, f)[...] = jnp.where(own, turned, 0.0).astype(BF)
        return carry

    lax.fori_loop(0, n, gain_block, 0)
    to_twin(late)
    for s in range(1, z_size):
        spread.step_z(s)
        spread.step_y(s - 1)
        twin_sums(late, z_size - s)
        take_y(plain, z_size - s)
    twin_sums(late, 0)
    spread.step_y(z_size - 1)
    for dz in range(z_size - 1, -1, -1):
        take_x(dz)
        send_y(late, dz)
    take_y(plain, 0)
    for z in range(z_size):
        spread.take_twin(z)

    rows_out[x] = whole[:, 0:16, :].astype(F32)[:, 0, :]
    send(rows_out.at[x], rows_out.at[x], fr_sems, (), mate)

    blocks = 4
    rows = own_rows // blocks
    iota = lax.broadcasted_iota(jnp.int32, (rows, length // 2), 0) + me * own_rows

    def code_block(r, carry):
        base = (iota + r * rows).astype(F32)

        def add(image, total):
            ids = facts[x, image]
            hot = jnp.concatenate(
                [jnp.where(base == ids[h : h + 1, :], 1.0, 0.0) for h in range(2)], 1
            ).astype(BF)
            return total + jnp.dot(hot, whole[image], preferred_element_type=F32)

        total = lax.fori_loop(0, n, add, jnp.zeros((rows, width), F32))
        at = pl.ds(pl.multiple_of(r * rows, rows), rows)
        code_out[at] = total.astype(BF)
        send(code_out.at[at], code_in.at[at], co_sems, (r,), mate)
        return carry

    for r in range(z_size):
        lax.fori_loop(r * blocks // z_size, (r + 1) * blocks // z_size, code_block, 0)
        take_y(halved, z_size - 1 - r)
        take_y(late, z_size - 1 - r)
    settle(plain + halved)

    arrival(head_two, hd_sems, ())
    total_squares = square(head_one[...].astype(F32) + head_two[...].astype(F32))

    arrival(rows_out.at[1 - x], fr_sems, ())
    firsts = rows_out[...].reshape(2 * n, width)
    shift = lax.rem(width - me * own_width, width)
    firsts = pltpu.roll(firsts, shift, 1)[:, :128]
    firsts = jnp.where(lax.broadcasted_iota(jnp.int32, firsts.shape, 1) < own_width, firsts, 0.0)
    classes = facts[:, :, 4, :].reshape(2 * n, 128)[:, 0:1]
    class_iota = lax.broadcasted_iota(jnp.int32, (2 * n, class_sum.shape[1]), 1).astype(F32)
    hot = jnp.where(class_iota == classes, 1.0, 0.0).astype(BF)
    class_grad = product(firsts.astype(BF), hot, BY_ROWS)
    class_sum[...] = class_grad
    total_squares = total_squares + square(class_grad)

    total_squares = total_squares + collect(plain + halved)
    settle(late)
    for r in range(blocks):
        at = pl.ds(r * rows, rows)
        arrival(code_in.at[at], co_sems, (r,))
        total_squares = total_squares + square(code_out[at].astype(F32) + code_in[at].astype(F32))
    total_squares = total_squares + collect(late)

    given[me] = jnp.broadcast_to(total_squares, (8, 128))
    for k in range(1, n):
        send(given.at[me], given.at[me], sq_sems, (k,), (lax.rem(me + k, n), x))

    spread.finish()
    departure(head_one, hd_sems, ())
    departure(rows_out.at[x], fr_sems, ())
    for r in range(blocks):
        departure(code_out.at[pl.ds(r * rows, rows)], co_sems, (r,))
    for k in range(count):
        departure(ref_of(k, trade[k].at[0], x), tr_sems, (k,))
        for dz in range(z_size):
            if dz:
                departure(z_in[k].at[dz - 1], rz_sems, (k, dz - 1))
            for dy in range(y_size):
                slot = slot_of(dz, dy)
                departure(core_in[k].at[slot], rc_sems, (k, slot))
                if split[k]:
                    departure(x_in[k].at[slot], rx_sems, (k, slot))
                if dy:
                    departure(y_in[k].at[y_slot(dz, dy)], ry_sems, (k, y_slot(dz, dy)))
    for k in range(1, n):
        arrival(given.at[0], sq_sems, (k,))
    squares[...] = jnp.sum(given[...], 0)
    for k in range(1, n):
        departure(given.at[0], sq_sems, (k,))


def tail_phase(layer, facts, head_one, weights, split, class_rows, own_width, n):
    z_size, y_size = geometry(n)
    length, width = layer[0].shape
    hidden_width = weights[2].shape[1]
    own_rows = head_one.shape[0]
    shapes = [(w.shape[0] // n, w.shape[1]) for w in weights] + [(16, 128)]
    count, spots = len(shapes), z_size * y_size
    halves = [(s[0], s[1] // 2) if h else s for s, h in zip(shapes, split)]
    dma = pltpu.SemaphoreType.DMA
    buffers = [((n * s[0], s[1]), BF) for s in shapes]
    buffers += [((spots,) + s, BF) for s in shapes]
    buffers += [((spots,) + s if h else (16, 128), BF) for s, h in zip(halves, split)]
    buffers += [((z_size * (y_size - 1),) + s, BF) for s in halves]
    buffers += [((z_size - 1,) + s, BF) for s in halves]
    buffers += [((2,) + s, BF) for s in shapes]
    buffers += [((n, length, width), BF), ((2, n, width), F32), ((n, 8, 128), F32),
                ((length, 3 * width), BF), ((length, 2 * hidden_width), BF), ((length, hidden_width), BF),
                ((length, width), F32), ((length, width), BF), ((length, width), BF)]
    sems = [
        dma((2, 2, z_size)), dma((2, z_size, y_size)), dma((2, z_size, y_size)),
        dma((count,)), dma((2, count, spots)), dma((2, count, spots)), dma((2, count, spots)),
        dma((2, count, z_size)), dma((2, count)), dma((2, 4)), dma((2,)), dma((2,)), dma((2, n)),
    ]
    vmem, hbm = pl.BlockSpec(memory_space=pltpu.VMEM), pl.BlockSpec(memory_space=pl.ANY)
    counts = tuple(s[0] for s in shapes)
    half = jax.ShapeDtypeStruct((own_rows, width), BF)
    outs = pl.pallas_call(
        functools.partial(tail_kernel, z_size, y_size, own_width, split, counts),
        out_shape=[jax.ShapeDtypeStruct(s, F32) for s in shapes]
        + [half, half, jax.ShapeDtypeStruct((128, class_rows), F32), half,
           jax.ShapeDtypeStruct((8, 128), F32)],
        in_specs=[vmem] * (len(layer) + 2) + [hbm] * len(weights),
        out_specs=[vmem] * (count + 5),
        scratch_shapes=[pltpu.VMEM(shape, kind) for shape, kind in buffers] + sems,
        compiler_params=pltpu.CompilerParams(
            collective_id=2, has_side_effects=True, vmem_limit_bytes=60 * 2**20
        ),
        name="tail",
    )(*layer, facts, head_one, *weights)
    code_one, code_two, class_sum, head_two, squares = outs[count:]
    return outs[:count], (code_one, code_two), class_sum, head_two, squares[0, 0]


BY_ROWS = (((0,), (0,)), ((), ()))
BY_LANES = (((1,), (1,)), ((), ()))


def product(left, right, dims):
    return lax.dot_general(left, right, dims, preferred_element_type=F32)


def both_heads(pair):
    lane = lax.broadcasted_iota(jnp.int32, pair.shape, 1)
    zero = jnp.zeros_like(pair)
    first, second = jnp.where(lane < HEAD_DIM, pair, zero), jnp.where(lane < HEAD_DIM, zero, pair)
    return jnp.concatenate([first, second], 0)


def one_row(two):
    length = two.shape[0] // 2
    lane = lax.broadcasted_iota(jnp.int32, (length, 128), 1)
    return jnp.where(lane < HEAD_DIM, two[:length], two[length:])


def attention_probs(q_two, k):
    length = k.shape[0]
    query = lax.rem(lax.broadcasted_iota(jnp.int32, (2 * length, length), 0), length)
    causal = query >= lax.broadcasted_iota(jnp.int32, (2 * length, length), 1)
    scores = jnp.where(causal, product(q_two, k, BY_LANES) * HEAD_DIM ** (-0.5), -1e30)
    expo = jnp.exp(scores - jnp.max(scores, -1, keepdims=True))
    return expo / jnp.sum(expo, -1, keepdims=True)


def layer_kernel(stream0, gains, turn, qkv_hbm, out_hbm, gate_hbm, down_hbm,
                 normed1, queries, keys, values, attended, stream1, normed2, stream2, normed3,
                 hidden, qkv_w, out_w, gate_w, down_w, sems):
    moves = [
        pltpu.make_async_copy(src, dst, sems.at[i])
        for i, (src, dst) in enumerate(
            ((qkv_hbm, qkv_w), (out_hbm, out_w), (gate_hbm, gate_w), (down_hbm, down_w))
        )
    ]
    for move in moves:
        move.start()
    length, width = stream0.shape
    hidden_width = hidden.shape[1]

    def rms(stream, row):
        inverse = lax.rsqrt(jnp.mean(stream * stream, -1, keepdims=True) + NORM_EPS)
        return (stream * inverse * gains[row : row + 1, :]).astype(BF)

    normed1[...] = rms(stream0[...], 0)
    lane = lax.broadcasted_iota(jnp.int32, (length, 128), 1)
    low = lax.rem(lane, HEAD_DIM) < HEAD_DIM // 2

    def turned(part):
        other = jnp.where(
            low, -pltpu.roll(part, 128 - HEAD_DIM // 2, 1), pltpu.roll(part, HEAD_DIM // 2, 1)
        )
        return (part * turn[0] + other * turn[1]).astype(BF)

    moves[0].wait()

    def pair(j, carry):
        base = pl.multiple_of(j * 128, 128)
        at = pl.ds(base, 128)
        x = normed1[...]
        q = turned(product(x, qkv_w[at, :], BY_LANES))
        k = turned(product(x, qkv_w[pl.ds(width + base, 128), :], BY_LANES))
        v = product(x, qkv_w[pl.ds(2 * width + base, 128), :], BY_LANES).astype(BF)
        queries[:, at], keys[:, at], values[:, at] = q, k, v
        probs = attention_probs(both_heads(q), k).astype(BF)
        attended[:, at] = one_row(jnp.dot(probs, v, preferred_element_type=F32)).astype(BF)
        return carry

    lax.fori_loop(0, width // 128, pair, 0)
    moves[1].wait()
    stream1[...] = stream0[...] + product(attended[...], out_w[...], BY_LANES)
    normed2[...] = rms(stream1[...], 1)
    moves[2].wait()
    step = 512
    for at in range(0, hidden_width, step):
        gate = product(normed2[...], gate_w[at : at + step, :], BY_LANES)
        up = product(normed2[...], gate_w[hidden_width + at : hidden_width + at + step, :], BY_LANES)
        hidden[:, at : at + step] = (gate * (1.0 / (1.0 + jnp.exp(-gate))) * up).astype(BF)
    moves[3].wait()
    stream2[...] = stream1[...] + product(hidden[...], down_w[...], BY_LANES)
    normed3[...] = rms(stream2[...], 2)


def layer_forward(stream0, gains, turn, qkv_w, out_w, gate_w, down_w):
    length, width = stream0.shape
    hidden_width = down_w.shape[1]
    vmem, hbm = pl.BlockSpec(memory_space=pltpu.VMEM), pl.BlockSpec(memory_space=pl.ANY)
    half, full = jax.ShapeDtypeStruct((length, width), BF), jax.ShapeDtypeStruct((length, width), F32)
    outs = [half] * 5 + [full, half, full, half]
    return pl.pallas_call(
        layer_kernel,
        out_shape=outs,
        in_specs=[vmem] * 3 + [hbm] * 4,
        out_specs=[vmem] * len(outs),
        scratch_shapes=[pltpu.VMEM((length, hidden_width), BF)]
        + [pltpu.VMEM(w.shape, BF) for w in (qkv_w, out_w, gate_w, down_w)]
        + [pltpu.SemaphoreType.DMA((4,))],
        compiler_params=pltpu.CompilerParams(vmem_limit_bytes=56 * 2**20),
        name="layer",
    )(stream0, gains, turn, qkv_w, out_w, gate_w, down_w)


def adam_update(weight, first, second, grad, rate, decay):
    first_new = BETA_ONE * first + (1.0 - BETA_ONE) * grad
    second_new = BETA_TWO * second + (1.0 - BETA_TWO) * grad * grad
    first_hat = first_new / (1.0 - BETA_ONE**STEP)
    second_hat = second_new / (1.0 - BETA_TWO**STEP)
    weight_new = weight - rate * (first_hat / (jnp.sqrt(second_hat) + ADAM_EPS) + decay * weight)
    return (weight_new, first_new, second_new)


def dot(subscripts, left, right):
    return jnp.einsum(subscripts, left, right, preferred_element_type=F32)


def local(*args):
    class_ids, null_mask, code_ids, lengths = args[:4]
    masters, firsts, seconds = args[4::3], args[5::3], args[6::3]
    code_table, class_table, qkv_weight, out_weight, gate_up, down_weight, head_weight, gains = (
        masters
    )
    rates = (0.5, 0.5, 0.05, 0.05, 0.05, 0.05, 0.05, 0.5)
    decays = (0.1, 0.1, 0.1, 0.1, 0.1, 0.1, 0.1, 0.0)
    n = lax.axis_size("fsdp")
    me = lax.axis_index("fsdp")
    batch, length = code_ids.shape
    width = qkv_weight.shape[1]
    hidden_width = down_weight.shape[1]
    table_rows, own_width = class_table.shape
    own_rows = code_table.shape[0]
    heads = width // HEAD_DIM
    rows = (qkv_weight.shape[0], gate_up.shape[0], out_weight.shape[0], down_weight.shape[0])

    classes = jnp.where(null_mask == 1, table_rows - 1, class_ids)
    previous = jnp.concatenate([jnp.full((1, 1), -1, code_ids.dtype), code_ids[:, :-1]], 1)
    pair = jnp.stack([classes[0], lengths[0]])[None].astype(F32)
    own_gains = gains.astype(BF).astype(F32)
    facts = jnp.concatenate(
        [
            previous.astype(F32).reshape(2, -1),
            code_ids.astype(F32).reshape(2, -1),
            jnp.pad(pair, ((0, 0), (0, length // 2 - 2))),
            jnp.pad(own_gains, ((0, 0), (0, length // 2 - own_width))),
        ],
        0,
    )
    class_b = jnp.pad(class_table.T.astype(BF), ((0, 128 - own_width), (0, -table_rows % 128)))
    reps = lax.axis_size("rep")
    wholes, stream0, facts = front(
        facts,
        code_table,
        class_b,
        [gate_up, qkv_weight, out_weight, down_weight],
        own_width,
        length,
        reps,
        n,
    )
    gate_w, qkv_w, out_w, down_w = (w.reshape(-1, w.shape[-1]) for w in wholes)
    stream0 = stream0[None]
    images = n * batch
    tokens = images * length
    every_fact, facts = facts, facts[lax.axis_index("rep")]
    gains32 = facts[:, 5:8, :own_width].transpose(1, 0, 2).reshape(3, width)
    all_codes = facts[:, 2:4].reshape(images, length).astype(jnp.int32)
    previous = facts[:, 0:2].reshape(tokens).astype(jnp.int32)
    all_classes = facts[:, 4, 0].astype(jnp.int32)
    all_lengths = facts[:, 4, 1].astype(jnp.int32)
    all_counted = (jnp.arange(length)[None, :] < all_lengths[:, None]).astype(F32)
    own_ids = jnp.arange(own_rows) + me * own_rows
    lookup = (previous[:, None] == own_ids[None, :]).astype(BF)

    cosine, sine = rotary_tables(length, HEAD_DIM)
    turn = jnp.stack([jnp.concatenate([t, t], -1) for t in (cosine, sine)])
    split4 = (batch, length, heads, HEAD_DIM)
    gain_rows = jnp.pad(gains32, ((0, 5), (0, 0)))
    kept = layer_forward(
        stream0[0], gain_rows, turn, qkv_w, out_w, gate_w, down_w
    )
    (normed1, queries, keys_rot, values, attended, stream1, normed2, stream2, normed3) = (
        t[None] for t in kept
    )
    head_b = head_weight.astype(BF)
    in_kernel = reps == 2 and size_of(head_scratch(n, length, width, own_rows, reps)[0]) < 52 * 2**20
    if in_kernel:
        grad_normed3, grad_head, totals = head_phase(normed3[0], head_weight, every_fact, reps, n)
        loss_sum, token_count = totals[0, 0], totals[1, 0]
    else:
        token_count = lax.psum(jnp.sum(all_counted), "rep")
        normed3_all = lax.all_gather(normed3, "fsdp", axis=0, tiled=True).reshape(tokens, width)
        logits = dot("td,vd->tv", normed3_all, head_b)
        onehot = all_codes.reshape(tokens)[:, None] == own_ids[None, :]
        local_top = jnp.max(logits, -1)
        local_sum = jnp.sum(jnp.exp(logits - local_top[:, None]), -1)
        local_pick = jnp.sum(jnp.where(onehot, logits, 0.0), -1)
        stats = lax.all_gather(jnp.stack([local_top, local_sum, local_pick]), "fsdp", axis=0)
        ltop = jnp.max(stats[:, 0], 0)
        lse = jnp.log(jnp.sum(stats[:, 1] * jnp.exp(stats[:, 0] - ltop[None]), 0)) + ltop
        picked = jnp.sum(stats[:, 2], 0)
        loss_sum = lax.psum(jnp.sum(jnp.where(all_counted.reshape(tokens) > 0, lse - picked, 0.0)), "rep")
        weight_t = all_counted.reshape(tokens) * (1.0 / token_count)
        soft = jnp.exp(logits - lse[:, None])
        grad_logits = ((soft - onehot.astype(F32)) * weight_t[:, None]).astype(BF)
        grad_normed3 = dot("tv,vd->td", grad_logits, head_b).astype(BF).reshape(images, length, width)
        grad_normed3 = lax.psum_scatter(grad_normed3, "fsdp", scatter_dimension=0, tiled=True)
        grad_normed3 = grad_normed3.astype(F32)
        grad_head = dot("tv,td->vd", grad_logits, normed3_all)

    if in_kernel:
        kinds = (queries, keys_rot, values, attended, normed1, normed2, stream0, stream1, stream2)
        layer = [t[0] for t in kinds] + [grad_normed3, turn, gain_rows]
        sums, codes, grad_classes, head_two, squares = tail_phase(
            layer,
            every_fact,
            grad_head,
            [gate_w, out_w, down_w, qkv_w],
            (True, True, False, False, False),
            table_rows + -table_rows % 128,
            own_width,
            n,
        )
        grad_codes, grad_head = (
            one.astype(F32) + two.astype(F32) for one, two in (codes, (grad_head, head_two))
        )
        grad_gate_up, grad_out, grad_down, grad_qkv, gain_part = sums
        grad_gains = gain_part[:3, :own_width]
        grad_classes = grad_classes[:own_width, :table_rows].T
    else:
        gated = dot("btd,fd->btf", normed2, gate_w)
        gate_part = gated[..., :hidden_width]
        up_part = gated[..., hidden_width:]
        hidden = (jax.nn.silu(gate_part) * up_part).astype(BF)
        inverse1, inverse2, inverse3 = (
            lax.rsqrt(jnp.mean(t * t, -1, keepdims=True) + NORM_EPS) for t in (stream0, stream1, stream2)
        )
        grad_stream2, gain_three = norm_backward(stream2, inverse3, gains32[2], grad_normed3)
        grad_branch = grad_stream2.astype(BF)
        grad_down = dot("btd,btf->df", grad_branch, hidden)
        grad_hidden = dot("btd,df->btf", grad_branch, down_w)
        sigma = jax.nn.sigmoid(gate_part)
        grad_gate = grad_hidden * up_part * sigma * (1.0 + gate_part * (1.0 - sigma))
        grad_up = grad_hidden * gate_part * sigma
        grad_gated = jnp.concatenate([grad_gate, grad_up], -1).astype(BF)
        grad_gate_up = dot("btf,btd->fd", grad_gated, normed2)
        grad_normed2 = dot("btf,fd->btd", grad_gated, gate_w)
        grad_middle, gain_two = norm_backward(stream1, inverse2, gains32[1], grad_normed2)
        grad_stream1 = grad_stream2 + grad_middle
        grad_attn = grad_stream1.astype(BF)
        grad_out = dot("bte,btd->ed", grad_attn, attended)
        grad_attended = dot("bte,ed->btd", grad_attn, out_w).astype(BF)
        queries, keys_rot, values, grad_attended = (
            t.reshape(split4) for t in (queries, keys_rot, values, grad_attended)
        )
        probs32 = jax.nn.softmax(attention_scores(queries, keys_rot), -1)
        probs = probs32.astype(BF)
        grad_probs = dot("bqhd,bkhd->bhqk", grad_attended, values)
        grad_values = dot("bhqk,bqhd->bkhd", probs, grad_attended)
        grad_scores = probs32 * (grad_probs - jnp.sum(probs32 * grad_probs, -1, keepdims=True))
        grad_scores = grad_scores.astype(BF)
        scale = HEAD_DIM ** (-0.5)
        grad_queries = dot("bhqk,bkhd->bqhd", grad_scores, keys_rot) * scale
        grad_keys = dot("bhqk,bqhd->bkhd", grad_scores, queries) * scale
        grad_mixed = jnp.concatenate(
            [
                rotate_back(grad_queries, cosine, sine).reshape(batch, length, width),
                rotate_back(grad_keys, cosine, sine).reshape(batch, length, width),
                grad_values.reshape(batch, length, width),
            ],
            -1,
        ).astype(BF)
        grad_qkv = dot("bte,btd->ed", grad_mixed, normed1)
        grad_normed1 = dot("bte,ed->btd", grad_mixed, qkv_w)
        grad_first, gain_one = norm_backward(stream0, inverse1, gains32[0], grad_normed1)
        grad_stream0 = grad_stream1 + grad_first

        grad_gains = jnp.stack([gain_one, gain_two, gain_three])
        blocks = [
            g.astype(BF).reshape(n, -1, g.shape[-1]) for g in (grad_qkv, grad_gate_up, grad_out, grad_down)
        ]
        layer_part = lax.psum_scatter(pack_rows(*blocks), "fsdp", scatter_dimension=0, tiled=False)
        rows_all = lax.all_gather(grad_stream0.astype(BF), "fsdp", axis=0, tiled=True)
        grad_codes = dot("tv,td->vd", lookup, rows_all.reshape(tokens, width))
        class_part = lax.dynamic_slice(rows_all[:, 0], (0, me * own_width), (images, own_width))
        class_spot = (all_classes[:, None] == jnp.arange(table_rows)[None, :]).astype(BF)
        grad_classes = dot("iv,id->vd", class_spot, class_part)
        summed = lax.psum(
            (grad_codes.astype(BF), grad_head.astype(BF), layer_part, grad_classes), "rep"
        )
        grad_codes, grad_head, layer_part, grad_classes = (s.astype(F32) for s in summed)
        grad_gains = lax.psum(grad_gains, ("fsdp", "rep"))
        grad_gains = lax.dynamic_slice(grad_gains, (0, me * own_width), (3, own_width))
        grad_qkv, grad_gate_up, grad_out, grad_down = unpack_rows(layer_part, rows, hidden_width)
    reduced = (
        grad_codes, grad_classes, grad_qkv, grad_out, grad_gate_up, grad_down, grad_head, grad_gains
    )
    if not in_kernel:
        squares = lax.psum(sum(jnp.sum(piece * piece) for piece in reduced), "fsdp")
    grad_norm = jnp.sqrt(squares)
    factor = jnp.minimum(1.0, 1.0 / CLIP_INV / (grad_norm + 1e-06))
    results = [loss_sum, token_count, grad_norm]
    for index in range(8):
        results.extend(
            adam_update(
                masters[index],
                firsts[index],
                seconds[index],
                reduced[index] * factor,
                rates[index],
                decays[index],
            )
        )
    return tuple(results)


def solution(mesh):
    split = P(("fsdp", "rep"))
    by_row, by_column = P("fsdp", None), P(None, "fsdp")
    weights = (by_row,) * 3 + (by_column,) * 3 + (by_row,) * 15 + (by_column,) * 3
    return jax.shard_map(
        local,
        mesh=mesh,
        in_specs=(split, split, P(("fsdp", "rep"), None), split) + weights,
        out_specs=(P(), P(), P()) + weights,
        check_vma=False,
    )
```

```python
import functools
import math

import jax
import jax.numpy as jnp
from jax import lax
from jax.experimental import pallas as pl
from jax.experimental.pallas import tpu as pltpu
from jax.sharding import PartitionSpec as P

HEAD_DIM = 64
CLIP_INV = 500
STEP = 10
NORM_EPS = 1e-05
BETA_ONE = 0.5
BETA_TWO = 0.5
ADAM_EPS = 1e-08
BF = jnp.bfloat16
F32 = jnp.float32
MESH = pl.DeviceIdType.MESH


def rotary_tables(length, width):
    half = width // 2
    freq = 10000.0 ** (-jnp.arange(half, dtype=F32) * 2.0 / width)
    angles = jnp.arange(length, dtype=F32)[:, None] * freq[None, :]
    cosine = jnp.concatenate([jnp.cos(angles), jnp.cos(angles)], -1)
    sine = jnp.concatenate([jnp.sin(angles), jnp.sin(angles)], -1)
    return (cosine, sine)


def rotate_back(grads, cosine, sine):
    half = grads.shape[-1] // 2
    scaled = grads * sine[:, None, :]
    return grads * cosine[:, None, :] + jnp.concatenate(
        [scaled[..., half:], -scaled[..., :half]], -1
    )


def norm_backward(stream, inverse, gain, grad_out):
    weighted = grad_out * gain
    inner = jnp.mean(weighted * stream, -1, keepdims=True)
    grad_in = inverse * weighted - stream * inverse * inverse * inverse * inner
    grad_gain = jnp.sum(grad_out * stream * inverse, axis=(0, 1))
    return (grad_in, grad_gain)


def attention_scores(queries, keys_rot):
    length = queries.shape[1]
    scores = jnp.einsum(
        "bqhd,bkhd->bhqk", queries, keys_rot, preferred_element_type=F32
    ) * HEAD_DIM ** (-0.5)
    causal = jnp.arange(length)[:, None] >= jnp.arange(length)[None, :]
    return jnp.where(causal, scores, -1e30)


def column_blocks(width, total):
    return [(at, min(width, total - at)) for at in range(0, total, width)]


def pack_rows(qkv, gate, out, down):
    width = qkv.shape[-1]
    parts = [qkv, gate, out]
    for at, size in column_blocks(width, down.shape[-1]):
        block = down[..., at : at + size]
        if size < width:
            pad = [(0, 0)] * (block.ndim - 1) + [(0, width - size)]
            block = jnp.pad(block, pad)
        parts.append(block)
    return jnp.concatenate(parts, -2)


def unpack_rows(packed, rows, hidden_width):
    width = packed.shape[-1]
    at, parts = 0, []
    for count in rows[:3]:
        parts.append(packed[..., at : at + count, :])
        at += count
    blocks = []
    for _, size in column_blocks(width, hidden_width):
        blocks.append(packed[..., at : at + rows[3], :size])
        at += rows[3]
    parts.append(jnp.concatenate(blocks, -1))
    return parts


def geometry(n):
    chips = n // 2
    y_size = 1 << ((chips.bit_length() - 1) // 2)
    return chips // y_size, y_size


def where_am_i(z_size, y_size):
    me = lax.axis_index("fsdp")
    return me, me // (2 * y_size), (me // 2) % y_size, me % 2


def send(src, dst, sems, index, device):
    pltpu.make_async_remote_copy(
        src_ref=src, dst_ref=dst, send_sem=sems.at[(0,) + index], recv_sem=sems.at[(1,) + index],
        device_id=device, device_id_type=MESH,
    ).start()


def arrival(dst, sems, index):
    pltpu.make_async_copy(dst, dst, sems.at[(1,) + index]).wait()


def departure(src, sems, index):
    pltpu.make_async_copy(src, src, sems.at[(0,) + index]).wait()


def weight_pieces(rows, reps):
    gate = rows[0]
    cut = gate * 15 // 16 // 16 * 16
    middle = cut // 2 // 16 * 16
    one = 1 % reps
    return (
        (2, 0, rows[2], 2 % reps),
        (0, cut, gate - cut, one),
        (0, 0, middle, 0),
        (3, 0, rows[3], 3 % reps),
        (0, middle, cut - middle, 0),
        (1, 0, rows[1], one),
    )


def front(facts, code_table, class_b, weights, own_width, length, reps, n):
    z_size, y_size = geometry(n)
    width = code_table.shape[1]
    count = len(weights)
    pieces = weight_pieces([w.shape[0] for w in weights], reps)
    many = len(pieces)
    spots = z_size * y_size
    block = (length, width)
    vmem, hbm = pl.BlockSpec(memory_space=pltpu.VMEM), pl.BlockSpec(memory_space=pl.ANY)
    dma = pltpu.SemaphoreType.DMA
    outs = pl.pallas_call(
        functools.partial(front_kernel, z_size, y_size, reps, own_width, pieces, count),
        out_shape=[jax.ShapeDtypeStruct((n,) + w.shape, BF) for w in weights]
        + [jax.ShapeDtypeStruct(block, F32), jax.ShapeDtypeStruct((reps, n, 8, 128), F32)],
        in_specs=[vmem] * (3 + count),
        out_specs=[hbm] * count + [vmem] * 2,
        scratch_shapes=[
            pltpu.VMEM(code_table.shape, BF),
            pltpu.VMEM((128, n * 8), F32),
            pltpu.VMEM((spots,) + block, BF),
            pltpu.VMEM((spots,) + block, BF),
            pltpu.VMEM((spots,) + block, BF),
            pltpu.VMEM((z_size, y_size) + block, BF),
            pltpu.VMEM((z_size,) + block, BF),
            dma((2, n)),
            dma((2, reps)),
            dma((2, many, 2, z_size)),
            dma((2, many, z_size, y_size)),
            dma((2, many, z_size, y_size, reps)),
            dma((2, many, z_size, y_size)),
            dma((count,)),
            dma((2, spots)),
            dma((2, z_size, y_size)),
            dma((2, z_size)),
        ]
        + [pltpu.VMEM(w.shape, BF) for w in weights],
        compiler_params=pltpu.CompilerParams(
            collective_id=0, has_side_effects=True, vmem_limit_bytes=60 * 2**20
        ),
        name="front",
    )(facts, code_table, class_b, *weights)
    return outs[:count], outs[count], outs[count + 1]


class Place:
    def __init__(self, z_size, y_size, reps):
        self.z_size, self.y_size, self.reps = z_size, y_size, reps
        self.n = z_size * y_size * 2
        self.me, self.z, self.y, self.core = where_am_i(z_size, y_size)
        self.x = lax.axis_index("rep")

    def at(self, dz, dy, other=0):
        c = 1 - self.core if other else self.core
        z, y = lax.rem(self.z + dz, self.z_size), lax.rem(self.y + dy, self.y_size)
        return (z * self.y_size + y) * 2 + c

    def plane(self, z, dy=0, other=0):
        c = 1 - self.core if other else self.core
        return (z * self.y_size + lax.rem(self.y + dy, self.y_size)) * 2 + c

    def twin(self):
        return (self.at(0, 0, 1), self.x)

    def greet(self, everyone):
        barrier = pltpu.get_barrier_semaphore()
        if everyone:
            group = [lax.rem(self.me + k, self.n) for k in range(1, self.n)]
        else:
            group = [self.at(dz, 0) for dz in range(1, self.z_size)]
            group += [self.at(0, dy) for dy in range(1, self.y_size)] + [self.at(0, 0, 1)]
        peers = [(p, self.x) for p in group]
        peers += [(self.me, lax.rem(self.x + k, self.reps)) for k in range(1, self.reps)]
        for peer in peers:
            pl.semaphore_signal(barrier, inc=1, device_id=peer, device_id_type=MESH)
        pl.semaphore_wait(barrier, len(peers))


class Spread:
    def __init__(self, place, whole, z_sems, y_sems, c_sems, x_sems=None, part=None, rows=None):
        self.p, self.whole, self.part, self.rows = place, whole, part, rows
        self.z_sems, self.y_sems, self.c_sems, self.x_sems = z_sems, y_sems, c_sems, x_sems

    def block(self, z, dy=0, other=0):
        block = self.whole.at[self.p.plane(z, dy, other)]
        return block if self.rows is None else block.at[pl.ds(*self.rows)]

    def in_part(self, act):
        if self.part is None:
            act()
        else:
            pl.when(self.p.x == self.part)(act)

    def hand_over(self, z, dy, src, dst):
        p = self.p
        if self.part is not None:
            for dx in range(1, p.reps):
                send(src, dst, self.x_sems, (z, dy, dx), (p.me, lax.rem(p.x + dx, p.reps)))
        send(src, dst, self.c_sems, (z, dy), p.twin())

    def pass_on(self, z, src, up, down):
        p = self.p
        dst = self.block(z)
        if up:

            @pl.when(p.z + 1 < p.z_size)
            def _():
                send(src, dst, self.z_sems, (0, z), (p.plane(p.z + 1), p.x))

        if down:

            @pl.when(p.z >= 1)
            def _():
                send(src, dst, self.z_sems, (1, z), (p.plane(p.z - 1), p.x))

        for dy in range(1, p.y_size):
            send(src, dst, self.y_sems, (z, dy), (p.at(0, dy), p.x))

    def start(self, own):
        self.in_part(lambda: self.pass_on(self.p.z, own, True, True))
        send(own, self.block(self.p.z), self.c_sems, (self.p.z, 0), self.p.twin())

    def near(self, s, act):
        p = self.p
        if s == 0:
            act(p.z)
            return

        @pl.when(p.z - s >= 0)
        def _():
            act(p.z - s)

        @pl.when(p.z + s < p.z_size)
        def _():
            act(p.z + s)

    def step_z(self, s):
        p = self.p

        def take(z, up):
            block = self.block(z)
            arrival(block, self.z_sems, (1 - int(up), z))
            self.pass_on(z, block, up, not up)
            self.hand_over(z, 0, block, block)

        def act():
            @pl.when(p.z - s >= 0)
            def _():
                take(p.z - s, True)

            @pl.when(p.z + s < p.z_size)
            def _():
                take(p.z + s, False)

        self.in_part(act)

    def step_y(self, s):
        def take(z):
            for dy in range(1, self.p.y_size):
                block = self.block(z, self.p.y_size - dy)
                arrival(block, self.y_sems, (z, dy))
                self.hand_over(z, dy, block, block)

        self.in_part(lambda: self.near(s, take))

    def step_x(self, s):
        p = self.p

        def take(z):
            for dy in range(0 if s else 1, p.y_size):
                block = self.block(z, p.y_size - dy)
                arrival(block, self.x_sems, (z, dy, lax.rem(p.x - self.part + p.reps, p.reps)))
                send(block, block, self.c_sems, (z, dy), p.twin())

        pl.when(p.x != self.part)(lambda: self.near(s, take))

    def take_twin(self, z):
        for dy in range(self.p.y_size):
            arrival(self.block(z, self.p.y_size - dy, 1), self.c_sems, (z, dy))

    def finish(self):
        p = self.p
        block = self.block(p.z)
        for z in range(p.z_size):
            for dy in range(p.y_size):
                departure(block, self.c_sems, (z, dy))

        def act():
            for z in range(p.z_size):

                @pl.when(jnp.logical_and(p.z + 1 < p.z_size, z <= p.z))
                def _():
                    departure(block, self.z_sems, (0, z))

                @pl.when(jnp.logical_and(p.z >= 1, z >= p.z))
                def _():
                    departure(block, self.z_sems, (1, z))

                for dy in range(1, p.y_size):
                    departure(block, self.y_sems, (z, dy))
                if self.part is None:
                    continue
                for dy in range(p.y_size):
                    for dx in range(1, p.reps):
                        if dy:
                            departure(block, self.x_sems, (z, dy, dx))
                        else:

                            @pl.when(z != p.z)
                            def _():
                                departure(block, self.x_sems, (z, dy, dx))

        self.in_part(act)


def front_kernel(z_size, y_size, reps, own_width, pieces, count, facts, code_table, class_b, *refs):
    masters, refs = refs[:count], refs[count:]
    wholes, refs = refs[:count], refs[count:]
    weights, refs = refs[-count:], refs[:-count]
    (stream, facts_all, code_b, turned, acc, core_out, core_in, y_in, z_in,
     fact_sems, rep_sems, z_sems, y_sems, x_sems, c_sems, own_sems, rc_sems, ry_sems, rz_sems) = refs
    p = Place(z_size, y_size, reps)
    n, me, x = p.n, p.me, p.x
    length, width = stream.shape
    own_rows = code_table.shape[0]
    p.greet(True)

    for k in range(1, n):
        send(facts, facts_all.at[x, me], fact_sems, (k,), (lax.rem(me + k, n), x))
    facts_all[x, me] = facts[...]
    for k in range(count):
        weights[k][...] = masters[k][...].astype(BF)
    spreads = []
    for i, (k, start, size, part) in enumerate(pieces):
        sems = [group.at[:, i] for group in (z_sems, y_sems, c_sems, x_sems)]
        spreads.append(Spread(p, wholes[k], *sems, part, (start, size)))
        spreads[i].start(weights[k].at[pl.ds(start, size)])
    for k in range(count):
        pltpu.make_async_copy(weights[k], wholes[k].at[me], own_sems.at[k]).start()
    code_b[...] = code_table[...].astype(BF)

    for k in range(1, n):
        arrival(facts_all.at[x, lax.rem(me - k + n, n)], fact_sems, (k,))
    for k in range(1, reps):
        send(facts_all.at[x], facts_all.at[x], rep_sems, (k,), (me, lax.rem(x + k, reps)))
    turned[...] = jnp.transpose(facts_all[x].reshape(n * 8, 128))
    lane = lax.broadcasted_iota(jnp.int32, (128, n * 8), 1)
    class_iota = lax.broadcasted_iota(jnp.int32, (16, class_b.shape[1]), 1).astype(F32)
    row_iota = lax.broadcasted_iota(jnp.int32, (length // 2, own_rows), 1) + me * own_rows
    row_iota = row_iota.astype(F32)

    def found(image, out):
        cls = jnp.sum(jnp.where(lane[:1] == image * 8 + 4, turned[:1, :], 0.0), -1, keepdims=True)
        spot = jnp.where(class_iota == cls, 1.0, 0.0).astype(BF)
        row = lax.dot_general(
            spot, class_b[...], (((1,), (1,)), ((), ())), preferred_element_type=F32
        )
        row = jnp.concatenate([row, jnp.zeros((16, width - row.shape[1]), F32)], -1)
        row = pltpu.roll(row, me * own_width, 1)
        for half in range(2):
            ids = jnp.sum(jnp.where(lane == image * 8 + half, turned[...], 0.0), -1, keepdims=True)
            spot = jnp.where(row_iota == ids, 1.0, 0.0).astype(BF)
            rows = jnp.dot(spot, code_b[...], preferred_element_type=F32)
            out[pl.ds(half * (length // 2), length // 2)] = rows.astype(BF)
            if half == 0:
                first = lax.broadcasted_iota(jnp.int32, (16, width), 0) == 0
                head = jnp.where(first, row, rows[:16])
                out[pl.ds(0, 16)] = head.astype(BF)

    def look_up(dz):
        def body(j, carry):
            dy = y_size - 1 - j
            slot = dz * y_size + dy
            found(p.at(dz, dy, 1), core_out.at[slot])
            send(core_out.at[slot], core_in.at[slot], rc_sems, (slot,), p.twin())
            found(p.at(dz, dy), acc.at[slot])
            return carry

        lax.fori_loop(0, y_size, body, 0)

    def twin_sum(dz):
        for dy in range(y_size - 1, -1, -1):
            slot = dz * y_size + dy
            arrival(core_in.at[slot], rc_sems, (slot,))
            acc[slot] = (acc[slot].astype(F32) + core_in[slot].astype(F32)).astype(BF)
            if dy:
                send(acc.at[slot], y_in.at[dz, dy], ry_sems, (dz, dy), (p.at(0, dy), x))

    def y_sum(dz):
        slot = dz * y_size
        total = acc[slot].astype(F32)
        for dy in range(1, y_size):
            arrival(y_in.at[dz, dy], ry_sems, (dz, dy))
            total = total + y_in[dz, dy].astype(F32)
        acc[slot] = total.astype(BF)
        if dz:
            send(acc.at[slot], z_in.at[dz], rz_sems, (dz,), (p.at(dz, 0), x))

    for s in range(1, z_size + 1):
        for spread in spreads:
            if s < z_size:
                spread.step_z(s)
        for spread in spreads:
            spread.step_y(s - 1)
        look_up(z_size - s)
        if s >= 2:
            twin_sum(z_size - s + 1)
        if s >= 3:
            y_sum(z_size - s + 2)
    twin_sum(0)
    for spread in spreads:
        spread.step_x(0)
    y_sum(1)
    for s in range(1, z_size - 1):
        for spread in spreads:
            spread.step_x(s)
    y_sum(0)
    total = acc[0].astype(F32)
    for dz in range(1, z_size):
        arrival(z_in.at[dz], rz_sems, (dz,))
        total = total + z_in[dz].astype(F32)
    stream[...] = total
    for spread in spreads:
        spread.step_x(z_size - 1)

    for k in range(1, reps):
        arrival(facts_all.at[x], rep_sems, (k,))
        departure(facts_all.at[x], rep_sems, (k,))
    for k in range(1, n):
        departure(facts, fact_sems, (k,))
    for dz in range(z_size):
        for dy in range(y_size):
            slot = dz * y_size + dy
            departure(core_out.at[slot], rc_sems, (slot,))
            if dy:
                departure(acc.at[slot], ry_sems, (dz, dy))
            elif dz:
                departure(acc.at[slot], rz_sems, (dz,))
    for k in range(count):
        pltpu.make_async_copy(weights[k], wholes[k].at[me], own_sems.at[k]).wait()
    for spread in spreads:
        for z in range(z_size):
            spread.take_twin(z)
        spread.finish()


def head_kernel(z_size, y_size, reps, normed3, head_weight, facts, grad_normed3, grad_head, totals,
                whole, logits, grads, turned, marks, stats_in, lse_all, acc, core_out, core_in, y_in, z_in,
                loss_in, head_b, z_sems, y_sems, c_sems, st_sems, ls_sems, rc_sems, ry_sems, rz_sems, lo_sems):
    p = Place(z_size, y_size, reps)
    n, me, x = p.n, p.me, p.x
    length, width = normed3.shape
    half = length // 2
    own_rows = head_weight.shape[0]
    p.greet(True)
    spread = Spread(p, whole, z_sems, y_sems, c_sems)
    spread.start(normed3)
    head_b[...] = head_weight[...].astype(BF)
    whole[me] = normed3[...]
    own_facts = facts.at[x]
    turned[...] = jnp.transpose(own_facts[...].reshape(n * 8, 128))
    lane = lax.broadcasted_iota(jnp.int32, (128, n * 8), 1)
    full_lane = lax.broadcasted_iota(jnp.int32, (length, n * 8), 1)
    column_iota = (lax.broadcasted_iota(jnp.int32, (length, own_rows), 1) + me * own_rows).astype(F32)
    token = lax.broadcasted_iota(jnp.int32, (length, 1), 0).astype(F32)
    every = facts[...].reshape(reps * n * 8, 128)
    row8 = lax.rem(lax.broadcasted_iota(jnp.int32, every.shape, 0), 8)
    spot = jnp.logical_and(row8 == 4, lax.broadcasted_iota(jnp.int32, every.shape, 1) == 1)
    token_count = jnp.sum(jnp.sum(jnp.where(spot, every, 0.0), 0, keepdims=True), 1, keepdims=True)
    inv_count = 1.0 / token_count

    def codes_of(image):
        parts = [
            jnp.sum(jnp.where(lane == image * 8 + 2 + h, turned[...], 0.0), -1, keepdims=True)
            for h in range(2)
        ]
        return jnp.concatenate(parts, 0)

    marks[...] = jnp.zeros_like(marks)

    def forward(image):
        out = lax.dot_general(
            whole[image], head_b[...], (((1,), (1,)), ((), ())), preferred_element_type=F32
        )
        logits[image] = out
        top = jnp.max(out, -1, keepdims=True)
        total = jnp.sum(jnp.exp(out - top), -1, keepdims=True)
        pick = jnp.sum(jnp.where(column_iota == codes_of(image), out, 0.0), -1, keepdims=True)
        old = marks[...]
        old = jnp.where(full_lane == image * 8, top, old)
        old = jnp.where(full_lane == image * 8 + 1, total, old)
        marks[...] = jnp.where(full_lane == image * 8 + 2, pick, old)

    def forward_column(z, first, last):
        def body(j, carry):
            forward(p.plane(z, lax.rem(y_size - j // 2, y_size), 0) + lax.rem(j, 2) * (1 - 2 * p.core))
            return carry

        lax.fori_loop(first * 2, last * 2, body, 0)

    arrival(spread.block(p.z, 0, 1), c_sems, (p.z, 0))
    forward_column(p.z, 0, 1)

    def one(z, s):
        arrival(spread.block(z, 0, 1), c_sems, (z, 0))
        forward_column(z, 0, 1)

    def other(z):
        for dy in range(1, y_size):
            arrival(spread.block(z, y_size - dy, 1), c_sems, (z, dy))
        forward_column(z, 1, y_size)

    def both(s, act):
        if s == 0:
            act(p.z)
            return

        @pl.when(p.z - s >= 0)
        def _():
            act(p.z - s)

        @pl.when(p.z + s < z_size)
        def _():
            act(p.z + s)

    for s in range(1, z_size + 1):
        if s < z_size:
            spread.step_z(s)
        spread.step_y(s - 1)
        if s < z_size:
            both(s, lambda z: one(z, s))
        both(s - 1, other)

    tiles = jnp.transpose(marks[...]).reshape(n, 8, length)
    stats_in[1] = tiles
    for k in range(1, n):
        peer = lax.rem(me + k, n)
        send(stats_in.at[1, peer], stats_in.at[0, me], st_sems, (k,), (peer, x))
    stats_in[0, me] = stats_in[1, me]
    for k in range(1, n):
        arrival(stats_in.at[0, 0], st_sems, (k,))
    tops = stats_in[0, :, 0, :]
    sums = stats_in[0, :, 1, :]
    picks = stats_in[0, :, 2, :]
    top = jnp.max(tops, 0, keepdims=True)
    lse = jnp.log(jnp.sum(sums * jnp.exp(tops - top), 0, keepdims=True)) + top
    pick = jnp.sum(picks, 0, keepdims=True)
    here = own_facts[me]
    counted = lax.broadcasted_iota(jnp.int32, (1, length), 1).astype(F32) < here[4:5, 1:2]
    loss = jnp.where(counted, lse - pick, 0.0)
    lse_all[me] = jnp.concatenate([lse, loss, jnp.zeros((6, length), F32)], 0)
    for k in range(1, n):
        peer = lax.rem(me + k, n)
        send(lse_all.at[me], lse_all.at[me], ls_sems, (k,), (peer, x))
    for k in range(1, n):
        arrival(lse_all.at[0], ls_sems, (k,))
    table = lse_all[...].reshape(n * 8, length)
    row8 = lax.rem(lax.broadcasted_iota(jnp.int32, table.shape, 0), 8)
    group = jnp.sum(jnp.sum(jnp.where(row8 == 1, table, 0.0), 0, keepdims=True), 1, keepdims=True)
    loss_in[x] = jnp.broadcast_to(group, (8, 128))
    for k in range(1, reps):
        peer = (me, lax.rem(x + k, reps))
        send(loss_in.at[x], loss_in.at[x], lo_sems, (k,), peer)
    marks[...] = jnp.transpose(table)

    def backward(image, out):
        lse_t = jnp.sum(jnp.where(full_lane == image * 8, marks[...], 0.0), -1, keepdims=True)
        size = jnp.sum(jnp.where(lane[:8] == image * 8 + 4, turned[:8, :], 0.0), -1, keepdims=True)
        weight = jnp.where(token < size[1:2], inv_count, 0.0)
        hot = jnp.where(column_iota == codes_of(image), 1.0, 0.0)
        grad = ((jnp.exp(logits[image] - lse_t) - hot) * weight).astype(BF)
        grads[image] = grad
        out[...] = jnp.dot(grad, head_b[...], preferred_element_type=F32).astype(BF)

    last = z_size - 1

    def for_twin(dz, dy):
        slot = dz * y_size + dy
        backward(p.at(dz, dy, 1), core_out.at[slot])
        send(core_out.at[slot], core_in.at[slot], rc_sems, (slot,), p.twin())

    def twin_sum(slot):
        arrival(core_in.at[slot], rc_sems, (slot,))
        acc[slot] = (acc[slot].astype(F32) + core_in[slot].astype(F32)).astype(BF)

    def y_sum(dz):
        slot = dz * y_size
        total = acc[slot].astype(F32)
        for dy in range(1, y_size):
            arrival(y_in.at[dz, dy], ry_sems, (dz, dy))
            total = total + y_in[dz, dy].astype(F32)
        acc[slot] = total.astype(BF)

    def round_of(g, carry):
        dz, near = last - g, last - g + 1

        @pl.when(g < z_size)
        def _():
            for dy in range(1, y_size):
                for_twin(dz, dy)
                backward(p.at(dz, dy), acc.at[dz * y_size + dy])

        @pl.when(g >= 1)
        def _():
            for_twin(near, 0)

        @pl.when(g < z_size)
        def _():
            for dy in range(1, y_size):
                slot = dz * y_size + dy
                twin_sum(slot)
                send(acc.at[slot], y_in.at[dz, dy], ry_sems, (dz, dy), (p.at(0, dy), x))

        @pl.when(g >= 1)
        def _():
            slot = near * y_size
            backward(p.at(near, 0), acc.at[slot])
            twin_sum(slot)

            @pl.when(near >= 1)
            def _():
                y_sum(near)
                send(acc.at[slot], z_in.at[near], rz_sems, (near,), (p.at(near, 0), x))

        return carry

    lax.fori_loop(0, z_size + 1, round_of, 0)

    blocks = 4
    rows = own_rows // blocks
    for r in range(blocks):

        def add(image, total):
            return total + lax.dot_general(
                grads[image, :, r * rows : (r + 1) * rows], whole[image],
                (((0,), (0,)), ((), ())), preferred_element_type=F32,
            )

        total = lax.fori_loop(0, n, add, jnp.zeros((rows, width), F32), unroll=4)
        grad_head[r * rows : (r + 1) * rows] = total.astype(BF)
    y_sum(0)
    total = acc[0].astype(F32)
    for dz in range(1, z_size):
        arrival(z_in.at[dz], rz_sems, (dz,))
        total = total + z_in[dz].astype(F32)
    grad_normed3[...] = total
    for k in range(1, reps):
        arrival(loss_in.at[0], lo_sems, (k,))
    loss_sum = loss_in[0]
    for k in range(1, reps):
        loss_sum = loss_sum + loss_in[k]
    totals[...] = jnp.where(
        lax.broadcasted_iota(jnp.int32, (8, 128), 0) == 0, loss_sum, token_count
    )

    spread.finish()
    for k in range(1, n):
        departure(stats_in.at[0, 0], st_sems, (k,))
        departure(lse_all.at[0], ls_sems, (k,))
    for k in range(1, reps):
        departure(loss_in.at[0], lo_sems, (k,))
    for dz in range(z_size):
        for dy in range(y_size):
            slot = dz * y_size + dy
            departure(core_out.at[slot], rc_sems, (slot,))
            if dy:
                departure(acc.at[slot], ry_sems, (dz, dy))
            elif dz:
                departure(acc.at[slot], rz_sems, (dz,))


def head_scratch(n, length, width, own_rows, reps):
    z_size, y_size = geometry(n)
    spots = z_size * y_size
    dma = pltpu.SemaphoreType.DMA
    buffers = [
        ((n, length, width), BF),
        ((n, length, own_rows), F32),
        ((n, length, own_rows), BF),
        ((128, n * 8), F32),
        ((length, n * 8), F32),
        ((2, n, 8, length), F32),
        ((n, 8, length), F32),
        ((spots, length, width), BF),
        ((spots, length, width), BF),
        ((spots, length, width), BF),
        ((z_size, y_size, length, width), BF),
        ((z_size, length, width), BF),
        ((reps, 8, 128), F32),
        ((own_rows, width), BF),
    ]
    sems = [
        dma((2, 2, z_size)), dma((2, z_size, y_size)), dma((2, z_size, y_size)),
        dma((2, n)), dma((2, n)), dma((2, spots)), dma((2, z_size, y_size)), dma((2, z_size)),
        dma((2, reps)),
    ]
    return buffers, sems


def size_of(buffers):
    return sum(math.prod(shape) * jnp.dtype(kind).itemsize for shape, kind in buffers)


def head_phase(normed3, head_weight, facts, reps, n):
    z_size, y_size = geometry(n)
    length, width = normed3.shape
    buffers, sems = head_scratch(n, length, width, head_weight.shape[0], reps)
    vmem = pl.BlockSpec(memory_space=pltpu.VMEM)
    return pl.pallas_call(
        functools.partial(head_kernel, z_size, y_size, reps),
        out_shape=[
            jax.ShapeDtypeStruct((length, width), F32),
            jax.ShapeDtypeStruct(head_weight.shape, BF),
            jax.ShapeDtypeStruct((8, 128), F32),
        ],
        in_specs=[vmem] * 3,
        out_specs=[vmem] * 3,
        scratch_shapes=[pltpu.VMEM(shape, kind) for shape, kind in buffers] + sems,
        compiler_params=pltpu.CompilerParams(
            collective_id=1, has_side_effects=True, vmem_limit_bytes=60 * 2**20
        ),
        name="head",
    )(normed3, head_weight, facts)


def tail_kernel(z_size, y_size, own_width, split, counts, queries, keys, values, attended, normed1, normed2,
                stream0, stream1, stream2, grad_normed3, turn, gains, facts, head_one, *refs):
    count = len(split)
    weights, refs = refs[: count - 1], refs[count - 1 :]
    sums, refs = refs[:count], refs[count:]
    code_out, code_in, class_sum, head_two, squares, refs = *refs[:5], refs[5:]
    grads, refs = refs[:count], refs[count:]
    core_in, refs = refs[:count], refs[count:]
    x_in, refs = refs[:count], refs[count:]
    y_in, refs = refs[:count], refs[count:]
    z_in, refs = refs[:count], refs[count:]
    trade, refs = refs[:count], refs[count:]
    (whole, rows_out, given, grad_mixed, grad_gated, hidden, grad_stream1, grad_attended, grad_stream0,
     z_sems, y_sems, c_sems, own_sems, rc_sems, rx_sems,
     ry_sems, rz_sems, tr_sems, co_sems, fr_sems, hd_sems, sq_sems) = refs
    p = Place(z_size, y_size, 2)
    n, me, x = p.n, p.me, p.x
    length, width = stream0.shape
    hidden_width = hidden.shape[1]
    own_rows = code_out.shape[0]
    gate_at, out_at, down_at, qkv_at, gain_at = range(5)
    late = [qkv_at, gain_at]
    halved = [k for k in (down_at, gate_at, out_at) if split[k]]
    plain = [k for k in (down_at, gate_at, out_at) if not split[k]]
    for k in range(count - 1):
        pltpu.make_async_copy(weights[k], grads[k], own_sems.at[k]).start()
    p.greet(True)
    mate = (me, 1 - x)
    spread = Spread(p, whole, z_sems, y_sems, c_sems)
    send(head_one, head_two, hd_sems, (), mate)

    def weight(k):
        pltpu.make_async_copy(weights[k], grads[k], own_sems.at[k]).wait()

    def slot_of(dz, dy):
        return dz * y_size + dy

    order = [(dz, dy) for dz in range(z_size - 1, -1, -1) for dy in range(y_size - 1, -1, -1)]

    def block_of(k, f):
        rows = counts[k]
        return grads[k].at[pl.ds(pl.multiple_of(f * rows, rows), rows)]

    def to_twin(kinds):
        for dz, dy in order:
            slot = slot_of(dz, dy)
            for k in kinds:
                send(block_of(k, p.at(dz, dy, 1)), core_in[k].at[slot], rc_sems, (k, slot), p.twin())

    def half_of(k, ref, which):
        columns = sums[k].shape[1] // 2
        return ref.at[:, pl.ds(pl.multiple_of(which * columns, columns), columns)]

    def ref_of(k, ref, which):
        return half_of(k, ref, which) if split[k] else ref

    def twin_sums(kinds, dz):
        def body(dy, carry):
            slot = slot_of(dz, dy)
            for k in kinds:
                arrival(core_in[k].at[slot], rc_sems, (k, slot))
                own = block_of(k, p.at(dz, dy))[...].astype(F32)
                core_in[k][slot] = (own + core_in[k][slot].astype(F32)).astype(BF)
                if split[k]:
                    send(half_of(k, core_in[k].at[slot], 1 - x), x_in[k].at[slot], rx_sems, (k, slot), mate)
            return carry

        lax.fori_loop(0, y_size, body, 0)

    def y_slot(dz, dy):
        return dz * (y_size - 1) + dy - 1

    def send_y(kinds, dz):
        for dy in range(1, y_size):
            for k in kinds:
                source = ref_of(k, core_in[k].at[slot_of(dz, dy)], x)
                at = y_slot(dz, dy)
                send(source, y_in[k].at[at], ry_sems, (k, at), (p.at(0, dy), x))

    def take_x(dz):
        def body(dy, carry):
            slot = slot_of(dz, dy)
            for k in halved:
                arrival(x_in[k].at[slot], rx_sems, (k, slot))
                mine = half_of(k, core_in[k].at[slot], x)
                mine[...] = (mine[...].astype(F32) + x_in[k][slot].astype(F32)).astype(BF)
            return carry

        lax.fori_loop(0, y_size, body, 0)
        send_y(halved, dz)

    def take_y(kinds, dz):
        for k in kinds:
            mine = ref_of(k, core_in[k].at[slot_of(dz, 0)], x)
            total = mine[...].astype(F32)
            for dy in range(1, y_size):
                at = y_slot(dz, dy)
                arrival(y_in[k].at[at], ry_sems, (k, at))
                total = total + y_in[k][at].astype(F32)
            mine[...] = total.astype(BF)
            if dz:
                send(mine, z_in[k].at[dz - 1], rz_sems, (k, dz - 1), (p.at(dz, 0), x))

    def settle(kinds):
        for k in kinds:
            mine = ref_of(k, core_in[k].at[0], x)
            total = mine[...].astype(F32)
            for dz in range(1, z_size):
                arrival(z_in[k].at[dz - 1], rz_sems, (k, dz - 1))
                total = total + z_in[k][dz - 1].astype(F32)
            source = ref_of(k, trade[k].at[0], x)
            source[...] = total.astype(BF)
            target = source if split[k] else trade[k].at[1]
            send(source, target, tr_sems, (k,), mate)

    def collect(kinds):
        summed = jnp.zeros((1, 1), F32)
        for k in kinds:
            if split[k]:
                arrival(half_of(k, trade[k].at[0], 1 - x), tr_sems, (k,))
                total = trade[k][0].astype(F32)
            else:
                arrival(trade[k].at[1], tr_sems, (k,))
                total = trade[k][0].astype(F32) + trade[k][1].astype(F32)
            sums[k][...] = total
            summed = summed + square(total)
        return summed

    def square(value):
        return jnp.sum(jnp.sum(value * value, 0, keepdims=True), 1, keepdims=True)

    def norm_back(stream, row, grad_out):
        inverse = lax.rsqrt(jnp.mean(stream * stream, -1, keepdims=True) + NORM_EPS)
        weighted = grad_out * gains[row : row + 1, :]
        inner = jnp.mean(weighted * stream, -1, keepdims=True)
        grad = inverse * weighted - stream * (inverse * inverse * inverse) * inner
        return grad, jnp.sum(grad_out * stream * inverse, 0, keepdims=True)

    grad_stream2, gain_three = norm_back(stream2[...], 2, grad_normed3[...])
    grad_stream1[...] = grad_stream2
    grad_stream0[...] = grad_stream2.astype(BF)
    weight(gate_at)
    weight(down_at)
    step = 512
    for at in range(0, hidden_width, step):
        gate = product(normed2[...], grads[gate_at][at : at + step, :], BY_LANES)
        up = product(normed2[...], grads[gate_at][hidden_width + at : hidden_width + at + step, :], BY_LANES)
        back = jnp.dot(grad_stream0[...], grads[down_at][:, at : at + step], preferred_element_type=F32)
        sigma = 1.0 / (1.0 + jnp.exp(-gate))
        hidden[:, at : at + step] = (gate * sigma * up).astype(BF)
        grad_gated[:, at : at + step] = (back * up * sigma * (1.0 + gate * (1.0 - sigma))).astype(BF)
        grad_gated[:, hidden_width + at : hidden_width + at + step] = (back * gate * sigma).astype(BF)
    for at in range(0, hidden_width, step):
        grads[down_at][:, at : at + step] = product(
            grad_stream0[...], hidden[:, at : at + step], BY_ROWS
        ).astype(BF)
    to_twin([down_at])
    grad_normed2 = jnp.dot(grad_gated[...], grads[gate_at][...], preferred_element_type=F32)
    for at in range(0, 2 * hidden_width, step):
        grads[gate_at][at : at + step, :] = product(
            grad_gated[:, at : at + step], normed2[...], BY_ROWS
        ).astype(BF)
    to_twin([gate_at])
    grad_middle, gain_two = norm_back(stream1[...], 1, grad_normed2)
    grad_stream1[...] = grad_stream1[...] + grad_middle
    grad_stream0[...] = grad_stream1[...].astype(BF)
    weight(out_at)
    grad_attended[...] = jnp.dot(
        grad_stream0[...], grads[out_at][...], preferred_element_type=F32
    ).astype(BF)
    grads[out_at][...] = product(grad_stream0[...], attended[...], BY_ROWS).astype(BF)
    to_twin([out_at])

    lane = lax.broadcasted_iota(jnp.int32, (length, 128), 1)
    low = lax.rem(lane, HEAD_DIM) < HEAD_DIM // 2
    scale = HEAD_DIM ** (-0.5)

    def turn_back(grad):
        scaled = grad * turn[1]
        other = jnp.where(
            low, pltpu.roll(scaled, 128 - HEAD_DIM // 2, 1), -pltpu.roll(scaled, HEAD_DIM // 2, 1)
        )
        return grad * turn[0] + other

    def pair(j, carry):
        base = pl.multiple_of(j * 128, 128)
        at = pl.ds(base, 128)
        q, k, v, grad = queries[:, at], keys[:, at], values[:, at], grad_attended[:, at]
        q_two, grad_two = both_heads(q), both_heads(grad)
        probs = attention_probs(q_two, k)
        grad_probs = product(grad_two, v, BY_LANES)
        inner = jnp.sum(probs * grad_probs, -1, keepdims=True)
        grad_scores = (probs * (grad_probs - inner)).astype(BF)
        grad_v = product(probs.astype(BF), grad_two, BY_ROWS)
        grad_q = one_row(jnp.dot(grad_scores, k, preferred_element_type=F32))
        grad_k = product(grad_scores, q_two, BY_ROWS)
        grad_mixed[:, at] = turn_back(grad_q * scale).astype(BF)
        grad_mixed[:, pl.ds(width + base, 128)] = turn_back(grad_k * scale).astype(BF)
        grad_mixed[:, pl.ds(2 * width + base, 128)] = grad_v.astype(BF)
        return carry

    pairs = width // 128
    for s in range(z_size):
        dz = z_size - 1 - s
        twin_sums(halved, dz)
        twin_sums(plain, dz)
        send_y(plain, dz)
        lax.fori_loop(s * pairs // z_size, (s + 1) * pairs // z_size, pair, 0)

    weight(qkv_at)
    grad_normed1 = jnp.dot(grad_mixed[...], grads[qkv_at][...], preferred_element_type=F32)
    grad_first, gain_one = norm_back(stream0[...], 0, grad_normed1)
    grad_stream0[...] = (grad_stream1[...] + grad_first).astype(BF)
    spread.start(grad_stream0)
    whole[me] = grad_stream0[...]
    step = 3 * width // 6
    for at in range(0, 3 * width, step):
        grads[qkv_at][at : at + step, :] = product(
            grad_mixed[:, at : at + step], normed1[...], BY_ROWS
        ).astype(BF)
    row = lax.broadcasted_iota(jnp.int32, (16, width), 0)
    all_gains = jnp.where(row == 2, gain_three, 0.0)
    all_gains = jnp.where(row == 0, gain_one, jnp.where(row == 1, gain_two, all_gains))

    def gain_block(f, carry):
        turned = pltpu.roll(all_gains, lax.rem(width - f * own_width, width), 1)[:, :128]
        own = lax.broadcasted_iota(jnp.int32, turned.shape, 1) < own_width
        block_of(gain_at, f)[...] = jnp.where(own, turned, 0.0).astype(BF)
        return carry

    lax.fori_loop(0, n, gain_block, 0)
    to_twin(late)
    for s in range(1, z_size):
        spread.step_z(s)
        spread.step_y(s - 1)
        twin_sums(late, z_size - s)
        take_y(plain, z_size - s)
    twin_sums(late, 0)
    spread.step_y(z_size - 1)
    for dz in range(z_size - 1, -1, -1):
        take_x(dz)
        send_y(late, dz)
    take_y(plain, 0)
    for z in range(z_size):
        spread.take_twin(z)

    rows_out[x] = whole[:, 0:16, :].astype(F32)[:, 0, :]
    send(rows_out.at[x], rows_out.at[x], fr_sems, (), mate)

    blocks = 4
    rows = own_rows // blocks
    iota = lax.broadcasted_iota(jnp.int32, (rows, length // 2), 0) + me * own_rows

    def code_block(r, carry):
        base = (iota + r * rows).astype(F32)

        def add(image, total):
            ids = facts[x, image]
            hot = jnp.concatenate(
                [jnp.where(base == ids[h : h + 1, :], 1.0, 0.0) for h in range(2)], 1
            ).astype(BF)
            return total + jnp.dot(hot, whole[image], preferred_element_type=F32)

        total = lax.fori_loop(0, n, add, jnp.zeros((rows, width), F32), unroll=4)
        at = pl.ds(pl.multiple_of(r * rows, rows), rows)
        code_out[at] = total.astype(BF)
        send(code_out.at[at], code_in.at[at], co_sems, (r,), mate)
        return carry

    for r in range(z_size):
        lax.fori_loop(r * blocks // z_size, (r + 1) * blocks // z_size, code_block, 0)
        take_y(halved, z_size - 1 - r)
        take_y(late, z_size - 1 - r)
    settle(plain + halved)

    arrival(head_two, hd_sems, ())
    total_squares = square(head_one[...].astype(F32) + head_two[...].astype(F32))

    arrival(rows_out.at[1 - x], fr_sems, ())
    firsts = rows_out[...].reshape(2 * n, width)
    shift = lax.rem(width - me * own_width, width)
    firsts = pltpu.roll(firsts, shift, 1)[:, :128]
    firsts = jnp.where(lax.broadcasted_iota(jnp.int32, firsts.shape, 1) < own_width, firsts, 0.0)
    classes = facts[:, :, 4, :].reshape(2 * n, 128)[:, 0:1]
    class_iota = lax.broadcasted_iota(jnp.int32, (2 * n, class_sum.shape[1]), 1).astype(F32)
    hot = jnp.where(class_iota == classes, 1.0, 0.0).astype(BF)
    class_grad = product(firsts.astype(BF), hot, BY_ROWS)
    class_sum[...] = class_grad
    total_squares = total_squares + square(class_grad)

    total_squares = total_squares + collect(plain + halved)
    settle(late)
    for r in range(blocks):
        at = pl.ds(r * rows, rows)
        arrival(code_in.at[at], co_sems, (r,))
        total_squares = total_squares + square(code_out[at].astype(F32) + code_in[at].astype(F32))
    total_squares = total_squares + collect(late)

    given[me] = jnp.broadcast_to(total_squares, (8, 128))
    for k in range(1, n):
        send(given.at[me], given.at[me], sq_sems, (k,), (lax.rem(me + k, n), x))

    spread.finish()
    departure(head_one, hd_sems, ())
    departure(rows_out.at[x], fr_sems, ())
    for r in range(blocks):
        departure(code_out.at[pl.ds(r * rows, rows)], co_sems, (r,))
    for k in range(count):
        departure(ref_of(k, trade[k].at[0], x), tr_sems, (k,))
        for dz in range(z_size):
            if dz:
                departure(z_in[k].at[dz - 1], rz_sems, (k, dz - 1))
            for dy in range(y_size):
                slot = slot_of(dz, dy)
                departure(core_in[k].at[slot], rc_sems, (k, slot))
                if split[k]:
                    departure(x_in[k].at[slot], rx_sems, (k, slot))
                if dy:
                    departure(y_in[k].at[y_slot(dz, dy)], ry_sems, (k, y_slot(dz, dy)))
    for k in range(1, n):
        arrival(given.at[0], sq_sems, (k,))
    squares[...] = jnp.sum(given[...], 0)
    for k in range(1, n):
        departure(given.at[0], sq_sems, (k,))


def tail_phase(layer, facts, head_one, weights, split, class_rows, own_width, n):
    z_size, y_size = geometry(n)
    length, width = layer[0].shape
    hidden_width = weights[2].shape[1]
    own_rows = head_one.shape[0]
    shapes = [(w.shape[0] // n, w.shape[1]) for w in weights] + [(16, 128)]
    count, spots = len(shapes), z_size * y_size
    halves = [(s[0], s[1] // 2) if h else s for s, h in zip(shapes, split)]
    dma = pltpu.SemaphoreType.DMA
    buffers = [((n * s[0], s[1]), BF) for s in shapes]
    buffers += [((spots,) + s, BF) for s in shapes]
    buffers += [((spots,) + s if h else (16, 128), BF) for s, h in zip(halves, split)]
    buffers += [((z_size * (y_size - 1),) + s, BF) for s in halves]
    buffers += [((z_size - 1,) + s, BF) for s in halves]
    buffers += [((2,) + s, BF) for s in shapes]
    buffers += [((n, length, width), BF), ((2, n, width), F32), ((n, 8, 128), F32),
                ((length, 3 * width), BF), ((length, 2 * hidden_width), BF), ((length, hidden_width), BF),
                ((length, width), F32), ((length, width), BF), ((length, width), BF)]
    sems = [
        dma((2, 2, z_size)), dma((2, z_size, y_size)), dma((2, z_size, y_size)),
        dma((count,)), dma((2, count, spots)), dma((2, count, spots)), dma((2, count, spots)),
        dma((2, count, z_size)), dma((2, count)), dma((2, 4)), dma((2,)), dma((2,)), dma((2, n)),
    ]
    vmem, hbm = pl.BlockSpec(memory_space=pltpu.VMEM), pl.BlockSpec(memory_space=pl.ANY)
    counts = tuple(s[0] for s in shapes)
    half = jax.ShapeDtypeStruct((own_rows, width), BF)
    outs = pl.pallas_call(
        functools.partial(tail_kernel, z_size, y_size, own_width, split, counts),
        out_shape=[jax.ShapeDtypeStruct(s, F32) for s in shapes]
        + [half, half, jax.ShapeDtypeStruct((128, class_rows), F32), half,
           jax.ShapeDtypeStruct((8, 128), F32)],
        in_specs=[vmem] * (len(layer) + 2) + [hbm] * len(weights),
        out_specs=[vmem] * (count + 5),
        scratch_shapes=[pltpu.VMEM(shape, kind) for shape, kind in buffers] + sems,
        compiler_params=pltpu.CompilerParams(
            collective_id=2, has_side_effects=True, vmem_limit_bytes=60 * 2**20
        ),
        name="tail",
    )(*layer, facts, head_one, *weights)
    code_one, code_two, class_sum, head_two, squares = outs[count:]
    return outs[:count], (code_one, code_two), class_sum, head_two, squares[0, 0]


BY_ROWS = (((0,), (0,)), ((), ()))
BY_LANES = (((1,), (1,)), ((), ()))


def product(left, right, dims):
    return lax.dot_general(left, right, dims, preferred_element_type=F32)


def both_heads(pair):
    lane = lax.broadcasted_iota(jnp.int32, pair.shape, 1)
    zero = jnp.zeros_like(pair)
    first, second = jnp.where(lane < HEAD_DIM, pair, zero), jnp.where(lane < HEAD_DIM, zero, pair)
    return jnp.concatenate([first, second], 0)


def one_row(two):
    length = two.shape[0] // 2
    lane = lax.broadcasted_iota(jnp.int32, (length, 128), 1)
    return jnp.where(lane < HEAD_DIM, two[:length], two[length:])


def attention_probs(q_two, k):
    length = k.shape[0]
    query = lax.rem(lax.broadcasted_iota(jnp.int32, (2 * length, length), 0), length)
    causal = query >= lax.broadcasted_iota(jnp.int32, (2 * length, length), 1)
    scores = jnp.where(causal, product(q_two, k, BY_LANES) * HEAD_DIM ** (-0.5), -1e30)
    expo = jnp.exp(scores - jnp.max(scores, -1, keepdims=True))
    return expo / jnp.sum(expo, -1, keepdims=True)


def layer_kernel(stream0, gains, turn, qkv_hbm, out_hbm, gate_hbm, down_hbm,
                 normed1, queries, keys, values, attended, stream1, normed2, stream2, normed3,
                 hidden, qkv_w, out_w, gate_w, down_w, sems):
    moves = [
        pltpu.make_async_copy(src, dst, sems.at[i])
        for i, (src, dst) in enumerate(
            ((qkv_hbm, qkv_w), (out_hbm, out_w), (gate_hbm, gate_w), (down_hbm, down_w))
        )
    ]
    for move in moves:
        move.start()
    length, width = stream0.shape
    hidden_width = hidden.shape[1]

    def rms(stream, row):
        inverse = lax.rsqrt(jnp.mean(stream * stream, -1, keepdims=True) + NORM_EPS)
        return (stream * inverse * gains[row : row + 1, :]).astype(BF)

    normed1[...] = rms(stream0[...], 0)
    lane = lax.broadcasted_iota(jnp.int32, (length, 128), 1)
    low = lax.rem(lane, HEAD_DIM) < HEAD_DIM // 2

    def turned(part):
        other = jnp.where(
            low, -pltpu.roll(part, 128 - HEAD_DIM // 2, 1), pltpu.roll(part, HEAD_DIM // 2, 1)
        )
        return (part * turn[0] + other * turn[1]).astype(BF)

    moves[0].wait()

    def pair(j, carry):
        base = pl.multiple_of(j * 128, 128)
        at = pl.ds(base, 128)
        x = normed1[...]
        q = turned(product(x, qkv_w[at, :], BY_LANES))
        k = turned(product(x, qkv_w[pl.ds(width + base, 128), :], BY_LANES))
        v = product(x, qkv_w[pl.ds(2 * width + base, 128), :], BY_LANES).astype(BF)
        queries[:, at], keys[:, at], values[:, at] = q, k, v
        probs = attention_probs(both_heads(q), k).astype(BF)
        attended[:, at] = one_row(jnp.dot(probs, v, preferred_element_type=F32)).astype(BF)
        return carry

    lax.fori_loop(0, width // 128, pair, 0)
    moves[1].wait()
    stream1[...] = stream0[...] + product(attended[...], out_w[...], BY_LANES)
    normed2[...] = rms(stream1[...], 1)
    moves[2].wait()
    step = 512
    for at in range(0, hidden_width, step):
        gate = product(normed2[...], gate_w[at : at + step, :], BY_LANES)
        up = product(normed2[...], gate_w[hidden_width + at : hidden_width + at + step, :], BY_LANES)
        hidden[:, at : at + step] = (gate * (1.0 / (1.0 + jnp.exp(-gate))) * up).astype(BF)
    moves[3].wait()
    stream2[...] = stream1[...] + product(hidden[...], down_w[...], BY_LANES)
    normed3[...] = rms(stream2[...], 2)


def layer_forward(stream0, gains, turn, qkv_w, out_w, gate_w, down_w):
    length, width = stream0.shape
    hidden_width = down_w.shape[1]
    vmem, hbm = pl.BlockSpec(memory_space=pltpu.VMEM), pl.BlockSpec(memory_space=pl.ANY)
    half, full = jax.ShapeDtypeStruct((length, width), BF), jax.ShapeDtypeStruct((length, width), F32)
    outs = [half] * 5 + [full, half, full, half]
    return pl.pallas_call(
        layer_kernel,
        out_shape=outs,
        in_specs=[vmem] * 3 + [hbm] * 4,
        out_specs=[vmem] * len(outs),
        scratch_shapes=[pltpu.VMEM((length, hidden_width), BF)]
        + [pltpu.VMEM(w.shape, BF) for w in (qkv_w, out_w, gate_w, down_w)]
        + [pltpu.SemaphoreType.DMA((4,))],
        compiler_params=pltpu.CompilerParams(vmem_limit_bytes=56 * 2**20),
        name="layer",
    )(stream0, gains, turn, qkv_w, out_w, gate_w, down_w)


def adam_update(weight, first, second, grad, rate, decay):
    first_new = BETA_ONE * first + (1.0 - BETA_ONE) * grad
    second_new = BETA_TWO * second + (1.0 - BETA_TWO) * grad * grad
    first_hat = first_new / (1.0 - BETA_ONE**STEP)
    second_hat = second_new / (1.0 - BETA_TWO**STEP)
    weight_new = weight - rate * (first_hat / (jnp.sqrt(second_hat) + ADAM_EPS) + decay * weight)
    return (weight_new, first_new, second_new)


def dot(subscripts, left, right):
    return jnp.einsum(subscripts, left, right, preferred_element_type=F32)


def local(*args):
    class_ids, null_mask, code_ids, lengths = args[:4]
    masters, firsts, seconds = args[4::3], args[5::3], args[6::3]
    code_table, class_table, qkv_weight, out_weight, gate_up, down_weight, head_weight, gains = (
        masters
    )
    rates = (0.5, 0.5, 0.05, 0.05, 0.05, 0.05, 0.05, 0.5)
    decays = (0.1, 0.1, 0.1, 0.1, 0.1, 0.1, 0.1, 0.0)
    n = lax.axis_size("fsdp")
    me = lax.axis_index("fsdp")
    batch, length = code_ids.shape
    width = qkv_weight.shape[1]
    hidden_width = down_weight.shape[1]
    table_rows, own_width = class_table.shape
    own_rows = code_table.shape[0]
    heads = width // HEAD_DIM
    rows = (qkv_weight.shape[0], gate_up.shape[0], out_weight.shape[0], down_weight.shape[0])

    classes = jnp.where(null_mask == 1, table_rows - 1, class_ids)
    previous = jnp.concatenate([jnp.full((1, 1), -1, code_ids.dtype), code_ids[:, :-1]], 1)
    pair = jnp.stack([classes[0], lengths[0]])[None].astype(F32)
    own_gains = gains.astype(BF).astype(F32)
    facts = jnp.concatenate(
        [
            previous.astype(F32).reshape(2, -1),
            code_ids.astype(F32).reshape(2, -1),
            jnp.pad(pair, ((0, 0), (0, length // 2 - 2))),
            jnp.pad(own_gains, ((0, 0), (0, length // 2 - own_width))),
        ],
        0,
    )
    class_b = jnp.pad(class_table.T.astype(BF), ((0, 128 - own_width), (0, -table_rows % 128)))
    reps = lax.axis_size("rep")
    wholes, stream0, facts = front(
        facts,
        code_table,
        class_b,
        [gate_up, qkv_weight, out_weight, down_weight],
        own_width,
        length,
        reps,
        n,
    )
    gate_w, qkv_w, out_w, down_w = (w.reshape(-1, w.shape[-1]) for w in wholes)
    stream0 = stream0[None]
    images = n * batch
    tokens = images * length
    every_fact, facts = facts, facts[lax.axis_index("rep")]
    gains32 = facts[:, 5:8, :own_width].transpose(1, 0, 2).reshape(3, width)
    all_codes = facts[:, 2:4].reshape(images, length).astype(jnp.int32)
    previous = facts[:, 0:2].reshape(tokens).astype(jnp.int32)
    all_classes = facts[:, 4, 0].astype(jnp.int32)
    all_lengths = facts[:, 4, 1].astype(jnp.int32)
    all_counted = (jnp.arange(length)[None, :] < all_lengths[:, None]).astype(F32)
    own_ids = jnp.arange(own_rows) + me * own_rows
    lookup = (previous[:, None] == own_ids[None, :]).astype(BF)

    cosine, sine = rotary_tables(length, HEAD_DIM)
    turn = jnp.stack([jnp.concatenate([t, t], -1) for t in (cosine, sine)])
    split4 = (batch, length, heads, HEAD_DIM)
    gain_rows = jnp.pad(gains32, ((0, 5), (0, 0)))
    kept = layer_forward(
        stream0[0], gain_rows, turn, qkv_w, out_w, gate_w, down_w
    )
    (normed1, queries, keys_rot, values, attended, stream1, normed2, stream2, normed3) = (
        t[None] for t in kept
    )
    head_b = head_weight.astype(BF)
    in_kernel = reps == 2 and size_of(head_scratch(n, length, width, own_rows, reps)[0]) < 52 * 2**20
    if in_kernel:
        grad_normed3, grad_head, totals = head_phase(normed3[0], head_weight, every_fact, reps, n)
        loss_sum, token_count = totals[0, 0], totals[1, 0]
    else:
        token_count = lax.psum(jnp.sum(all_counted), "rep")
        normed3_all = lax.all_gather(normed3, "fsdp", axis=0, tiled=True).reshape(tokens, width)
        logits = dot("td,vd->tv", normed3_all, head_b)
        onehot = all_codes.reshape(tokens)[:, None] == own_ids[None, :]
        local_top = jnp.max(logits, -1)
        local_sum = jnp.sum(jnp.exp(logits - local_top[:, None]), -1)
        local_pick = jnp.sum(jnp.where(onehot, logits, 0.0), -1)
        stats = lax.all_gather(jnp.stack([local_top, local_sum, local_pick]), "fsdp", axis=0)
        ltop = jnp.max(stats[:, 0], 0)
        lse = jnp.log(jnp.sum(stats[:, 1] * jnp.exp(stats[:, 0] - ltop[None]), 0)) + ltop
        picked = jnp.sum(stats[:, 2], 0)
        loss_sum = lax.psum(jnp.sum(jnp.where(all_counted.reshape(tokens) > 0, lse - picked, 0.0)), "rep")
        weight_t = all_counted.reshape(tokens) * (1.0 / token_count)
        soft = jnp.exp(logits - lse[:, None])
        grad_logits = ((soft - onehot.astype(F32)) * weight_t[:, None]).astype(BF)
        grad_normed3 = dot("tv,vd->td", grad_logits, head_b).astype(BF).reshape(images, length, width)
        grad_normed3 = lax.psum_scatter(grad_normed3, "fsdp", scatter_dimension=0, tiled=True)
        grad_normed3 = grad_normed3.astype(F32)
        grad_head = dot("tv,td->vd", grad_logits, normed3_all)

    if in_kernel:
        kinds = (queries, keys_rot, values, attended, normed1, normed2, stream0, stream1, stream2)
        layer = [t[0] for t in kinds] + [grad_normed3, turn, gain_rows]
        sums, codes, grad_classes, head_two, squares = tail_phase(
            layer,
            every_fact,
            grad_head,
            [gate_w, out_w, down_w, qkv_w],
            (True, True, False, False, False),
            table_rows + -table_rows % 128,
            own_width,
            n,
        )
        grad_codes, grad_head = (
            one.astype(F32) + two.astype(F32) for one, two in (codes, (grad_head, head_two))
        )
        grad_gate_up, grad_out, grad_down, grad_qkv, gain_part = sums
        grad_gains = gain_part[:3, :own_width]
        grad_classes = grad_classes[:own_width, :table_rows].T
    else:
        gated = dot("btd,fd->btf", normed2, gate_w)
        gate_part = gated[..., :hidden_width]
        up_part = gated[..., hidden_width:]
        hidden = (jax.nn.silu(gate_part) * up_part).astype(BF)
        inverse1, inverse2, inverse3 = (
            lax.rsqrt(jnp.mean(t * t, -1, keepdims=True) + NORM_EPS) for t in (stream0, stream1, stream2)
        )
        grad_stream2, gain_three = norm_backward(stream2, inverse3, gains32[2], grad_normed3)
        grad_branch = grad_stream2.astype(BF)
        grad_down = dot("btd,btf->df", grad_branch, hidden)
        grad_hidden = dot("btd,df->btf", grad_branch, down_w)
        sigma = jax.nn.sigmoid(gate_part)
        grad_gate = grad_hidden * up_part * sigma * (1.0 + gate_part * (1.0 - sigma))
        grad_up = grad_hidden * gate_part * sigma
        grad_gated = jnp.concatenate([grad_gate, grad_up], -1).astype(BF)
        grad_gate_up = dot("btf,btd->fd", grad_gated, normed2)
        grad_normed2 = dot("btf,fd->btd", grad_gated, gate_w)
        grad_middle, gain_two = norm_backward(stream1, inverse2, gains32[1], grad_normed2)
        grad_stream1 = grad_stream2 + grad_middle
        grad_attn = grad_stream1.astype(BF)
        grad_out = dot("bte,btd->ed", grad_attn, attended)
        grad_attended = dot("bte,ed->btd", grad_attn, out_w).astype(BF)
        queries, keys_rot, values, grad_attended = (
            t.reshape(split4) for t in (queries, keys_rot, values, grad_attended)
        )
        probs32 = jax.nn.softmax(attention_scores(queries, keys_rot), -1)
        probs = probs32.astype(BF)
        grad_probs = dot("bqhd,bkhd->bhqk", grad_attended, values)
        grad_values = dot("bhqk,bqhd->bkhd", probs, grad_attended)
        grad_scores = probs32 * (grad_probs - jnp.sum(probs32 * grad_probs, -1, keepdims=True))
        grad_scores = grad_scores.astype(BF)
        scale = HEAD_DIM ** (-0.5)
        grad_queries = dot("bhqk,bkhd->bqhd", grad_scores, keys_rot) * scale
        grad_keys = dot("bhqk,bqhd->bkhd", grad_scores, queries) * scale
        grad_mixed = jnp.concatenate(
            [
                rotate_back(grad_queries, cosine, sine).reshape(batch, length, width),
                rotate_back(grad_keys, cosine, sine).reshape(batch, length, width),
                grad_values.reshape(batch, length, width),
            ],
            -1,
        ).astype(BF)
        grad_qkv = dot("bte,btd->ed", grad_mixed, normed1)
        grad_normed1 = dot("bte,ed->btd", grad_mixed, qkv_w)
        grad_first, gain_one = norm_backward(stream0, inverse1, gains32[0], grad_normed1)
        grad_stream0 = grad_stream1 + grad_first

        grad_gains = jnp.stack([gain_one, gain_two, gain_three])
        blocks = [
            g.astype(BF).reshape(n, -1, g.shape[-1]) for g in (grad_qkv, grad_gate_up, grad_out, grad_down)
        ]
        layer_part = lax.psum_scatter(pack_rows(*blocks), "fsdp", scatter_dimension=0, tiled=False)
        rows_all = lax.all_gather(grad_stream0.astype(BF), "fsdp", axis=0, tiled=True)
        grad_codes = dot("tv,td->vd", lookup, rows_all.reshape(tokens, width))
        class_part = lax.dynamic_slice(rows_all[:, 0], (0, me * own_width), (images, own_width))
        class_spot = (all_classes[:, None] == jnp.arange(table_rows)[None, :]).astype(BF)
        grad_classes = dot("iv,id->vd", class_spot, class_part)
        summed = lax.psum(
            (grad_codes.astype(BF), grad_head.astype(BF), layer_part, grad_classes), "rep"
        )
        grad_codes, grad_head, layer_part, grad_classes = (s.astype(F32) for s in summed)
        grad_gains = lax.psum(grad_gains, ("fsdp", "rep"))
        grad_gains = lax.dynamic_slice(grad_gains, (0, me * own_width), (3, own_width))
        grad_qkv, grad_gate_up, grad_out, grad_down = unpack_rows(layer_part, rows, hidden_width)
    reduced = (
        grad_codes, grad_classes, grad_qkv, grad_out, grad_gate_up, grad_down, grad_head, grad_gains
    )
    if not in_kernel:
        squares = lax.psum(sum(jnp.sum(piece * piece) for piece in reduced), "fsdp")
    grad_norm = jnp.sqrt(squares)
    factor = jnp.minimum(1.0, 1.0 / CLIP_INV / (grad_norm + 1e-06))
    results = [loss_sum, token_count, grad_norm]
    for index in range(8):
        results.extend(
            adam_update(
                masters[index],
                firsts[index],
                seconds[index],
                reduced[index] * factor,
                rates[index],
                decays[index],
            )
        )
    return tuple(results)


def solution(mesh):
    split = P(("fsdp", "rep"))
    by_row, by_column = P("fsdp", None), P(None, "fsdp")
    weights = (by_row,) * 3 + (by_column,) * 3 + (by_row,) * 15 + (by_column,) * 3
    return jax.shard_map(
        local,
        mesh=mesh,
        in_specs=(split, split, P(("fsdp", "rep"), None), split) + weights,
        out_specs=(P(), P(), P()) + weights,
        check_vma=False,
    )
```

```python
import functools
import math

import jax
import jax.numpy as jnp
from jax import lax
from jax.experimental import pallas as pl
from jax.experimental.pallas import tpu as pltpu
from jax.sharding import PartitionSpec as P

HEAD_DIM = 64
CLIP_INV = 500
STEP = 10
NORM_EPS = 1e-05
BETA_ONE = 0.5
BETA_TWO = 0.5
ADAM_EPS = 1e-08
BF = jnp.bfloat16
F32 = jnp.float32
MESH = pl.DeviceIdType.MESH


def rotary_tables(length, width):
    half = width // 2
    freq = 10000.0 ** (-jnp.arange(half, dtype=F32) * 2.0 / width)
    angles = jnp.arange(length, dtype=F32)[:, None] * freq[None, :]
    cosine = jnp.concatenate([jnp.cos(angles), jnp.cos(angles)], -1)
    sine = jnp.concatenate([jnp.sin(angles), jnp.sin(angles)], -1)
    return (cosine, sine)


def rotate_back(grads, cosine, sine):
    half = grads.shape[-1] // 2
    scaled = grads * sine[:, None, :]
    return grads * cosine[:, None, :] + jnp.concatenate(
        [scaled[..., half:], -scaled[..., :half]], -1
    )


def norm_backward(stream, inverse, gain, grad_out):
    weighted = grad_out * gain
    inner = jnp.mean(weighted * stream, -1, keepdims=True)
    grad_in = inverse * weighted - stream * inverse * inverse * inverse * inner
    grad_gain = jnp.sum(grad_out * stream * inverse, axis=(0, 1))
    return (grad_in, grad_gain)


def attention_scores(queries, keys_rot):
    length = queries.shape[1]
    scores = jnp.einsum(
        "bqhd,bkhd->bhqk", queries, keys_rot, preferred_element_type=F32
    ) * HEAD_DIM ** (-0.5)
    causal = jnp.arange(length)[:, None] >= jnp.arange(length)[None, :]
    return jnp.where(causal, scores, -1e30)


def column_blocks(width, total):
    return [(at, min(width, total - at)) for at in range(0, total, width)]


def pack_rows(qkv, gate, out, down):
    width = qkv.shape[-1]
    parts = [qkv, gate, out]
    for at, size in column_blocks(width, down.shape[-1]):
        block = down[..., at : at + size]
        if size < width:
            pad = [(0, 0)] * (block.ndim - 1) + [(0, width - size)]
            block = jnp.pad(block, pad)
        parts.append(block)
    return jnp.concatenate(parts, -2)


def unpack_rows(packed, rows, hidden_width):
    width = packed.shape[-1]
    at, parts = 0, []
    for count in rows[:3]:
        parts.append(packed[..., at : at + count, :])
        at += count
    blocks = []
    for _, size in column_blocks(width, hidden_width):
        blocks.append(packed[..., at : at + rows[3], :size])
        at += rows[3]
    parts.append(jnp.concatenate(blocks, -1))
    return parts


def geometry(n):
    chips = n // 2
    y_size = 1 << ((chips.bit_length() - 1) // 2)
    return chips // y_size, y_size


def where_am_i(z_size, y_size):
    me = lax.axis_index("fsdp")
    return me, me // (2 * y_size), (me // 2) % y_size, me % 2


def send(src, dst, sems, index, device):
    pltpu.make_async_remote_copy(
        src_ref=src, dst_ref=dst, send_sem=sems.at[(0,) + index], recv_sem=sems.at[(1,) + index],
        device_id=device, device_id_type=MESH,
    ).start()


def arrival(dst, sems, index):
    pltpu.make_async_copy(dst, dst, sems.at[(1,) + index]).wait()


def departure(src, sems, index):
    pltpu.make_async_copy(src, src, sems.at[(0,) + index]).wait()


def weight_pieces(rows, reps):
    gate = rows[0]
    cut = gate * 15 // 16 // 16 * 16
    middle = cut // 2 // 16 * 16
    one = 1 % reps
    return (
        (2, 0, rows[2], 2 % reps),
        (0, cut, gate - cut, one),
        (0, 0, middle, 0),
        (3, 0, rows[3], 3 % reps),
        (0, middle, cut - middle, 0),
        (1, 0, rows[1], one),
    )


def front(facts, code_table, class_b, weights, own_width, length, reps, n):
    z_size, y_size = geometry(n)
    width = code_table.shape[1]
    count = len(weights)
    pieces = weight_pieces([w.shape[0] for w in weights], reps)
    many = len(pieces)
    spots = z_size * y_size
    block = (length, width)
    vmem, hbm = pl.BlockSpec(memory_space=pltpu.VMEM), pl.BlockSpec(memory_space=pl.ANY)
    dma = pltpu.SemaphoreType.DMA
    outs = pl.pallas_call(
        functools.partial(front_kernel, z_size, y_size, reps, own_width, pieces, count),
        out_shape=[jax.ShapeDtypeStruct((n,) + w.shape, BF) for w in weights]
        + [jax.ShapeDtypeStruct(block, F32), jax.ShapeDtypeStruct((reps, n, 8, 128), F32)],
        in_specs=[vmem] * (3 + count),
        out_specs=[hbm] * count + [vmem] * 2,
        scratch_shapes=[
            pltpu.VMEM(code_table.shape, BF),
            pltpu.VMEM((128, n * 8), F32),
            pltpu.VMEM((spots,) + block, BF),
            pltpu.VMEM((spots,) + block, BF),
            pltpu.VMEM((spots,) + block, BF),
            pltpu.VMEM((z_size, y_size) + block, BF),
            pltpu.VMEM((z_size,) + block, BF),
            dma((2, n)),
            dma((2, reps)),
            dma((2, many, 2, z_size)),
            dma((2, many, z_size, y_size)),
            dma((2, many, z_size, y_size, reps)),
            dma((2, many, z_size, y_size)),
            dma((count,)),
            dma((2, spots)),
            dma((2, z_size, y_size)),
            dma((2, z_size)),
        ]
        + [pltpu.VMEM(w.shape, BF) for w in weights],
        compiler_params=pltpu.CompilerParams(
            collective_id=0, has_side_effects=True, vmem_limit_bytes=60 * 2**20
        ),
        name="front",
    )(facts, code_table, class_b, *weights)
    return outs[:count], outs[count], outs[count + 1]


class Place:
    def __init__(self, z_size, y_size, reps):
        self.z_size, self.y_size, self.reps = z_size, y_size, reps
        self.n = z_size * y_size * 2
        self.me, self.z, self.y, self.core = where_am_i(z_size, y_size)
        self.x = lax.axis_index("rep")

    def at(self, dz, dy, other=0):
        c = 1 - self.core if other else self.core
        z, y = lax.rem(self.z + dz, self.z_size), lax.rem(self.y + dy, self.y_size)
        return (z * self.y_size + y) * 2 + c

    def plane(self, z, dy=0, other=0):
        c = 1 - self.core if other else self.core
        return (z * self.y_size + lax.rem(self.y + dy, self.y_size)) * 2 + c

    def twin(self):
        return (self.at(0, 0, 1), self.x)

    def greet(self, everyone):
        barrier = pltpu.get_barrier_semaphore()
        if everyone:
            group = [lax.rem(self.me + k, self.n) for k in range(1, self.n)]
        else:
            group = [self.at(dz, 0) for dz in range(1, self.z_size)]
            group += [self.at(0, dy) for dy in range(1, self.y_size)] + [self.at(0, 0, 1)]
        peers = [(p, self.x) for p in group]
        peers += [(self.me, lax.rem(self.x + k, self.reps)) for k in range(1, self.reps)]
        for peer in peers:
            pl.semaphore_signal(barrier, inc=1, device_id=peer, device_id_type=MESH)
        pl.semaphore_wait(barrier, len(peers))


class Spread:
    def __init__(self, place, whole, z_sems, y_sems, c_sems, x_sems=None, part=None, rows=None):
        self.p, self.whole, self.part, self.rows = place, whole, part, rows
        self.z_sems, self.y_sems, self.c_sems, self.x_sems = z_sems, y_sems, c_sems, x_sems

    def block(self, z, dy=0, other=0):
        block = self.whole.at[self.p.plane(z, dy, other)]
        return block if self.rows is None else block.at[pl.ds(*self.rows)]

    def in_part(self, act):
        if self.part is None:
            act()
        else:
            pl.when(self.p.x == self.part)(act)

    def hand_over(self, z, dy, src, dst):
        p = self.p
        if self.part is not None:
            for dx in range(1, p.reps):
                send(src, dst, self.x_sems, (z, dy, dx), (p.me, lax.rem(p.x + dx, p.reps)))
        send(src, dst, self.c_sems, (z, dy), p.twin())

    def pass_on(self, z, src, up, down):
        p = self.p
        dst = self.block(z)
        if up:

            @pl.when(p.z + 1 < p.z_size)
            def _():
                send(src, dst, self.z_sems, (0, z), (p.plane(p.z + 1), p.x))

        if down:

            @pl.when(p.z >= 1)
            def _():
                send(src, dst, self.z_sems, (1, z), (p.plane(p.z - 1), p.x))

        for dy in range(1, p.y_size):
            send(src, dst, self.y_sems, (z, dy), (p.at(0, dy), p.x))

    def start(self, own):
        self.in_part(lambda: self.pass_on(self.p.z, own, True, True))
        send(own, self.block(self.p.z), self.c_sems, (self.p.z, 0), self.p.twin())

    def near(self, s, act):
        p = self.p
        if s == 0:
            act(p.z)
            return

        @pl.when(p.z - s >= 0)
        def _():
            act(p.z - s)

        @pl.when(p.z + s < p.z_size)
        def _():
            act(p.z + s)

    def step_z(self, s):
        p = self.p

        def take(z, up):
            block = self.block(z)
            arrival(block, self.z_sems, (1 - int(up), z))
            self.pass_on(z, block, up, not up)
            self.hand_over(z, 0, block, block)

        def act():
            @pl.when(p.z - s >= 0)
            def _():
                take(p.z - s, True)

            @pl.when(p.z + s < p.z_size)
            def _():
                take(p.z + s, False)

        self.in_part(act)

    def step_y(self, s):
        def take(z):
            for dy in range(1, self.p.y_size):
                block = self.block(z, self.p.y_size - dy)
                arrival(block, self.y_sems, (z, dy))
                self.hand_over(z, dy, block, block)

        self.in_part(lambda: self.near(s, take))

    def step_x(self, s):
        p = self.p

        def take(z):
            for dy in range(0 if s else 1, p.y_size):
                block = self.block(z, p.y_size - dy)
                arrival(block, self.x_sems, (z, dy, lax.rem(p.x - self.part + p.reps, p.reps)))
                send(block, block, self.c_sems, (z, dy), p.twin())

        pl.when(p.x != self.part)(lambda: self.near(s, take))

    def take_twin(self, z):
        for dy in range(self.p.y_size):
            arrival(self.block(z, self.p.y_size - dy, 1), self.c_sems, (z, dy))

    def finish(self):
        p = self.p
        block = self.block(p.z)
        for z in range(p.z_size):
            for dy in range(p.y_size):
                departure(block, self.c_sems, (z, dy))

        def act():
            for z in range(p.z_size):

                @pl.when(jnp.logical_and(p.z + 1 < p.z_size, z <= p.z))
                def _():
                    departure(block, self.z_sems, (0, z))

                @pl.when(jnp.logical_and(p.z >= 1, z >= p.z))
                def _():
                    departure(block, self.z_sems, (1, z))

                for dy in range(1, p.y_size):
                    departure(block, self.y_sems, (z, dy))
                if self.part is None:
                    continue
                for dy in range(p.y_size):
                    for dx in range(1, p.reps):
                        if dy:
                            departure(block, self.x_sems, (z, dy, dx))
                        else:

                            @pl.when(z != p.z)
                            def _():
                                departure(block, self.x_sems, (z, dy, dx))

        self.in_part(act)


def front_kernel(z_size, y_size, reps, own_width, pieces, count, facts, code_table, class_b, *refs):
    masters, refs = refs[:count], refs[count:]
    wholes, refs = refs[:count], refs[count:]
    weights, refs = refs[-count:], refs[:-count]
    (stream, facts_all, code_b, turned, acc, core_out, core_in, y_in, z_in,
     fact_sems, rep_sems, z_sems, y_sems, x_sems, c_sems, own_sems, rc_sems, ry_sems, rz_sems) = refs
    p = Place(z_size, y_size, reps)
    n, me, x = p.n, p.me, p.x
    length, width = stream.shape
    own_rows = code_table.shape[0]
    p.greet(True)

    for k in range(1, n):
        send(facts, facts_all.at[x, me], fact_sems, (k,), (lax.rem(me + k, n), x))
    facts_all[x, me] = facts[...]
    for k in range(count):
        weights[k][...] = masters[k][...].astype(BF)
    spreads = []
    for i, (k, start, size, part) in enumerate(pieces):
        sems = [group.at[:, i] for group in (z_sems, y_sems, c_sems, x_sems)]
        spreads.append(Spread(p, wholes[k], *sems, part, (start, size)))
        spreads[i].start(weights[k].at[pl.ds(start, size)])
    for k in range(count):
        pltpu.make_async_copy(weights[k], wholes[k].at[me], own_sems.at[k]).start()
    code_b[...] = code_table[...].astype(BF)

    for k in range(1, n):
        arrival(facts_all.at[x, lax.rem(me - k + n, n)], fact_sems, (k,))
    for k in range(1, reps):
        send(facts_all.at[x], facts_all.at[x], rep_sems, (k,), (me, lax.rem(x + k, reps)))
    turned[...] = jnp.transpose(facts_all[x].reshape(n * 8, 128))
    lane = lax.broadcasted_iota(jnp.int32, (128, n * 8), 1)
    class_iota = lax.broadcasted_iota(jnp.int32, (16, class_b.shape[1]), 1).astype(F32)
    row_iota = lax.broadcasted_iota(jnp.int32, (length // 2, own_rows), 1) + me * own_rows
    row_iota = row_iota.astype(F32)

    def found(image, out):
        cls = jnp.sum(jnp.where(lane[:1] == image * 8 + 4, turned[:1, :], 0.0), -1, keepdims=True)
        spot = jnp.where(class_iota == cls, 1.0, 0.0).astype(BF)
        row = lax.dot_general(
            spot, class_b[...], (((1,), (1,)), ((), ())), preferred_element_type=F32
        )
        row = jnp.concatenate([row, jnp.zeros((16, width - row.shape[1]), F32)], -1)
        row = pltpu.roll(row, me * own_width, 1)
        for half in range(2):
            ids = jnp.sum(jnp.where(lane == image * 8 + half, turned[...], 0.0), -1, keepdims=True)
            spot = jnp.where(row_iota == ids, 1.0, 0.0).astype(BF)
            rows = jnp.dot(spot, code_b[...], preferred_element_type=F32)
            out[pl.ds(half * (length // 2), length // 2)] = rows.astype(BF)
            if half == 0:
                first = lax.broadcasted_iota(jnp.int32, (16, width), 0) == 0
                head = jnp.where(first, row, rows[:16])
                out[pl.ds(0, 16)] = head.astype(BF)

    def look_up(dz):
        def body(j, carry):
            dy = y_size - 1 - j
            slot = dz * y_size + dy
            found(p.at(dz, dy, 1), core_out.at[slot])
            send(core_out.at[slot], core_in.at[slot], rc_sems, (slot,), p.twin())
            found(p.at(dz, dy), acc.at[slot])
            return carry

        lax.fori_loop(0, y_size, body, 0)

    def twin_sum(dz):
        for dy in range(y_size - 1, -1, -1):
            slot = dz * y_size + dy
            arrival(core_in.at[slot], rc_sems, (slot,))
            acc[slot] = (acc[slot].astype(F32) + core_in[slot].astype(F32)).astype(BF)
            if dy:
                send(acc.at[slot], y_in.at[dz, dy], ry_sems, (dz, dy), (p.at(0, dy), x))

    def y_sum(dz):
        slot = dz * y_size
        total = acc[slot].astype(F32)
        for dy in range(1, y_size):
            arrival(y_in.at[dz, dy], ry_sems, (dz, dy))
            total = total + y_in[dz, dy].astype(F32)
        acc[slot] = total.astype(BF)
        if dz:
            send(acc.at[slot], z_in.at[dz], rz_sems, (dz,), (p.at(dz, 0), x))

    for s in range(1, z_size + 1):
        for spread in spreads:
            if s < z_size:
                spread.step_z(s)
        for spread in spreads:
            spread.step_y(s - 1)
        look_up(z_size - s)
        if s >= 2:
            twin_sum(z_size - s + 1)
        if s >= 3:
            y_sum(z_size - s + 2)
    twin_sum(0)
    for spread in spreads:
        spread.step_x(0)
    y_sum(1)
    for s in range(1, z_size - 1):
        for spread in spreads:
            spread.step_x(s)
    y_sum(0)
    total = acc[0].astype(F32)
    for dz in range(1, z_size):
        arrival(z_in.at[dz], rz_sems, (dz,))
        total = total + z_in[dz].astype(F32)
    stream[...] = total
    for spread in spreads:
        spread.step_x(z_size - 1)

    for k in range(1, reps):
        arrival(facts_all.at[x], rep_sems, (k,))
        departure(facts_all.at[x], rep_sems, (k,))
    for k in range(1, n):
        departure(facts, fact_sems, (k,))
    for dz in range(z_size):
        for dy in range(y_size):
            slot = dz * y_size + dy
            departure(core_out.at[slot], rc_sems, (slot,))
            if dy:
                departure(acc.at[slot], ry_sems, (dz, dy))
            elif dz:
                departure(acc.at[slot], rz_sems, (dz,))
    for k in range(count):
        pltpu.make_async_copy(weights[k], wholes[k].at[me], own_sems.at[k]).wait()
    for spread in spreads:
        for z in range(z_size):
            spread.take_twin(z)
        spread.finish()


def head_kernel(z_size, y_size, reps, normed3, head_weight, facts, grad_normed3, grad_head, totals,
                whole, logits, grads, turned, marks, stats_in, lse_all, acc, core_out, core_in, y_in, z_in,
                loss_in, head_b, z_sems, y_sems, c_sems, st_sems, ls_sems, rc_sems, ry_sems, rz_sems, lo_sems):
    p = Place(z_size, y_size, reps)
    n, me, x = p.n, p.me, p.x
    length, width = normed3.shape
    half = length // 2
    own_rows = head_weight.shape[0]
    p.greet(True)
    spread = Spread(p, whole, z_sems, y_sems, c_sems)
    spread.start(normed3)
    head_b[...] = head_weight[...].astype(BF)
    whole[me] = normed3[...]
    own_facts = facts.at[x]
    turned[...] = jnp.transpose(own_facts[...].reshape(n * 8, 128))
    lane = lax.broadcasted_iota(jnp.int32, (128, n * 8), 1)
    full_lane = lax.broadcasted_iota(jnp.int32, (length, n * 8), 1)
    column_iota = (lax.broadcasted_iota(jnp.int32, (length, own_rows), 1) + me * own_rows).astype(F32)
    token = lax.broadcasted_iota(jnp.int32, (length, 1), 0).astype(F32)
    every = facts[...].reshape(reps * n * 8, 128)
    row8 = lax.rem(lax.broadcasted_iota(jnp.int32, every.shape, 0), 8)
    spot = jnp.logical_and(row8 == 4, lax.broadcasted_iota(jnp.int32, every.shape, 1) == 1)
    token_count = jnp.sum(jnp.sum(jnp.where(spot, every, 0.0), 0, keepdims=True), 1, keepdims=True)
    inv_count = 1.0 / token_count

    def codes_of(image):
        parts = [
            jnp.sum(jnp.where(lane == image * 8 + 2 + h, turned[...], 0.0), -1, keepdims=True)
            for h in range(2)
        ]
        return jnp.concatenate(parts, 0)

    marks[...] = jnp.zeros_like(marks)

    def forward(image):
        out = lax.dot_general(
            whole[image], head_b[...], (((1,), (1,)), ((), ())), preferred_element_type=F32
        )
        logits[image] = out
        top = jnp.max(out, -1, keepdims=True)
        total = jnp.sum(jnp.exp(out - top), -1, keepdims=True)
        pick = jnp.sum(jnp.where(column_iota == codes_of(image), out, 0.0), -1, keepdims=True)
        old = marks[...]
        old = jnp.where(full_lane == image * 8, top, old)
        old = jnp.where(full_lane == image * 8 + 1, total, old)
        marks[...] = jnp.where(full_lane == image * 8 + 2, pick, old)

    def forward_column(z, first, last):
        def body(j, carry):
            forward(p.plane(z, lax.rem(y_size - j // 2, y_size), 0) + lax.rem(j, 2) * (1 - 2 * p.core))
            return carry

        lax.fori_loop(first * 2, last * 2, body, 0)

    arrival(spread.block(p.z, 0, 1), c_sems, (p.z, 0))
    forward_column(p.z, 0, 1)

    def one(z, s):
        arrival(spread.block(z, 0, 1), c_sems, (z, 0))
        forward_column(z, 0, 1)

    def other(z):
        for dy in range(1, y_size):
            arrival(spread.block(z, y_size - dy, 1), c_sems, (z, dy))
        forward_column(z, 1, y_size)

    def both(s, act):
        if s == 0:
            act(p.z)
            return

        @pl.when(p.z - s >= 0)
        def _():
            act(p.z - s)

        @pl.when(p.z + s < z_size)
        def _():
            act(p.z + s)

    for s in range(1, z_size + 1):
        if s < z_size:
            spread.step_z(s)
        spread.step_y(s - 1)
        if s < z_size:
            both(s, lambda z: one(z, s))
        both(s - 1, other)

    tiles = jnp.transpose(marks[...]).reshape(n, 8, length)
    stats_in[1] = tiles
    for k in range(1, n):
        peer = lax.rem(me + k, n)
        send(stats_in.at[1, peer], stats_in.at[0, me], st_sems, (k,), (peer, x))
    stats_in[0, me] = stats_in[1, me]
    for k in range(1, n):
        arrival(stats_in.at[0, 0], st_sems, (k,))
    tops = stats_in[0, :, 0, :]
    sums = stats_in[0, :, 1, :]
    picks = stats_in[0, :, 2, :]
    top = jnp.max(tops, 0, keepdims=True)
    lse = jnp.log(jnp.sum(sums * jnp.exp(tops - top), 0, keepdims=True)) + top
    pick = jnp.sum(picks, 0, keepdims=True)
    here = own_facts[me]
    counted = lax.broadcasted_iota(jnp.int32, (1, length), 1).astype(F32) < here[4:5, 1:2]
    loss = jnp.where(counted, lse - pick, 0.0)
    lse_all[me] = jnp.concatenate([lse, loss, jnp.zeros((6, length), F32)], 0)
    for k in range(1, n):
        peer = lax.rem(me + k, n)
        send(lse_all.at[me], lse_all.at[me], ls_sems, (k,), (peer, x))
    for k in range(1, n):
        arrival(lse_all.at[0], ls_sems, (k,))
    table = lse_all[...].reshape(n * 8, length)
    row8 = lax.rem(lax.broadcasted_iota(jnp.int32, table.shape, 0), 8)
    group = jnp.sum(jnp.sum(jnp.where(row8 == 1, table, 0.0), 0, keepdims=True), 1, keepdims=True)
    loss_in[x] = jnp.broadcast_to(group, (8, 128))
    for k in range(1, reps):
        peer = (me, lax.rem(x + k, reps))
        send(loss_in.at[x], loss_in.at[x], lo_sems, (k,), peer)
    marks[...] = jnp.transpose(table)

    def backward(image, out):
        lse_t = jnp.sum(jnp.where(full_lane == image * 8, marks[...], 0.0), -1, keepdims=True)
        size = jnp.sum(jnp.where(lane[:8] == image * 8 + 4, turned[:8, :], 0.0), -1, keepdims=True)
        weight = jnp.where(token < size[1:2], inv_count, 0.0)
        hot = jnp.where(column_iota == codes_of(image), 1.0, 0.0)
        grad = ((jnp.exp(logits[image] - lse_t) - hot) * weight).astype(BF)
        grads[image] = grad
        out[...] = jnp.dot(grad, head_b[...], preferred_element_type=F32).astype(BF)

    last = z_size - 1

    def for_twin(dz, dy):
        slot = dz * y_size + dy
        backward(p.at(dz, dy, 1), core_out.at[slot])
        send(core_out.at[slot], core_in.at[slot], rc_sems, (slot,), p.twin())

    def twin_sum(slot):
        arrival(core_in.at[slot], rc_sems, (slot,))
        acc[slot] = (acc[slot].astype(F32) + core_in[slot].astype(F32)).astype(BF)

    def y_sum(dz):
        slot = dz * y_size
        total = acc[slot].astype(F32)
        for dy in range(1, y_size):
            arrival(y_in.at[dz, dy], ry_sems, (dz, dy))
            total = total + y_in[dz, dy].astype(F32)
        acc[slot] = total.astype(BF)

    def round_of(g, carry):
        dz, near = last - g, last - g + 1

        @pl.when(g < z_size)
        def _():
            for dy in range(1, y_size):
                for_twin(dz, dy)
                backward(p.at(dz, dy), acc.at[dz * y_size + dy])

        @pl.when(g >= 1)
        def _():
            for_twin(near, 0)

        @pl.when(g < z_size)
        def _():
            for dy in range(1, y_size):
                slot = dz * y_size + dy
                twin_sum(slot)
                send(acc.at[slot], y_in.at[dz, dy], ry_sems, (dz, dy), (p.at(0, dy), x))

        @pl.when(g >= 1)
        def _():
            slot = near * y_size
            backward(p.at(near, 0), acc.at[slot])
            twin_sum(slot)

            @pl.when(near >= 1)
            def _():
                y_sum(near)
                send(acc.at[slot], z_in.at[near], rz_sems, (near,), (p.at(near, 0), x))

        return carry

    lax.fori_loop(0, z_size + 1, round_of, 0)

    blocks = 4
    rows = own_rows // blocks
    for r in range(blocks):

        def add(image, total):
            return total + lax.dot_general(
                grads[image, :, r * rows : (r + 1) * rows], whole[image],
                (((0,), (0,)), ((), ())), preferred_element_type=F32,
            )

        total = lax.fori_loop(0, n, add, jnp.zeros((rows, width), F32), unroll=4)
        grad_head[r * rows : (r + 1) * rows] = total.astype(BF)
    y_sum(0)
    total = acc[0].astype(F32)
    for dz in range(1, z_size):
        arrival(z_in.at[dz], rz_sems, (dz,))
        total = total + z_in[dz].astype(F32)
    grad_normed3[...] = total
    for k in range(1, reps):
        arrival(loss_in.at[0], lo_sems, (k,))
    loss_sum = loss_in[0]
    for k in range(1, reps):
        loss_sum = loss_sum + loss_in[k]
    totals[...] = jnp.where(
        lax.broadcasted_iota(jnp.int32, (8, 128), 0) == 0, loss_sum, token_count
    )

    spread.finish()
    for k in range(1, n):
        departure(stats_in.at[0, 0], st_sems, (k,))
        departure(lse_all.at[0], ls_sems, (k,))
    for k in range(1, reps):
        departure(loss_in.at[0], lo_sems, (k,))
    for dz in range(z_size):
        for dy in range(y_size):
            slot = dz * y_size + dy
            departure(core_out.at[slot], rc_sems, (slot,))
            if dy:
                departure(acc.at[slot], ry_sems, (dz, dy))
            elif dz:
                departure(acc.at[slot], rz_sems, (dz,))


def head_scratch(n, length, width, own_rows, reps):
    z_size, y_size = geometry(n)
    spots = z_size * y_size
    dma = pltpu.SemaphoreType.DMA
    buffers = [
        ((n, length, width), BF),
        ((n, length, own_rows), F32),
        ((n, length, own_rows), BF),
        ((128, n * 8), F32),
        ((length, n * 8), F32),
        ((2, n, 8, length), F32),
        ((n, 8, length), F32),
        ((spots, length, width), BF),
        ((spots, length, width), BF),
        ((spots, length, width), BF),
        ((z_size, y_size, length, width), BF),
        ((z_size, length, width), BF),
        ((reps, 8, 128), F32),
        ((own_rows, width), BF),
    ]
    sems = [
        dma((2, 2, z_size)), dma((2, z_size, y_size)), dma((2, z_size, y_size)),
        dma((2, n)), dma((2, n)), dma((2, spots)), dma((2, z_size, y_size)), dma((2, z_size)),
        dma((2, reps)),
    ]
    return buffers, sems


def size_of(buffers):
    return sum(math.prod(shape) * jnp.dtype(kind).itemsize for shape, kind in buffers)


def head_phase(normed3, head_weight, facts, reps, n):
    z_size, y_size = geometry(n)
    length, width = normed3.shape
    buffers, sems = head_scratch(n, length, width, head_weight.shape[0], reps)
    vmem = pl.BlockSpec(memory_space=pltpu.VMEM)
    return pl.pallas_call(
        functools.partial(head_kernel, z_size, y_size, reps),
        out_shape=[
            jax.ShapeDtypeStruct((length, width), F32),
            jax.ShapeDtypeStruct(head_weight.shape, BF),
            jax.ShapeDtypeStruct((8, 128), F32),
        ],
        in_specs=[vmem] * 3,
        out_specs=[vmem] * 3,
        scratch_shapes=[pltpu.VMEM(shape, kind) for shape, kind in buffers] + sems,
        compiler_params=pltpu.CompilerParams(
            collective_id=1, has_side_effects=True, vmem_limit_bytes=60 * 2**20
        ),
        name="head",
    )(normed3, head_weight, facts)


def tail_kernel(z_size, y_size, own_width, split, counts, queries, keys, values, attended, normed1, normed2,
                stream0, stream1, stream2, grad_normed3, turn, gains, facts, head_one, *refs):
    count = len(split)
    weights, refs = refs[: count - 1], refs[count - 1 :]
    sums, refs = refs[:count], refs[count:]
    code_out, code_in, class_sum, head_two, squares, refs = *refs[:5], refs[5:]
    grads, refs = refs[:count], refs[count:]
    core_in, refs = refs[:count], refs[count:]
    x_in, refs = refs[:count], refs[count:]
    y_in, refs = refs[:count], refs[count:]
    z_in, refs = refs[:count], refs[count:]
    trade, refs = refs[:count], refs[count:]
    (whole, rows_out, given, grad_mixed, grad_gated, hidden, grad_stream1, grad_attended, grad_stream0,
     z_sems, y_sems, c_sems, own_sems, rc_sems, rx_sems,
     ry_sems, rz_sems, tr_sems, co_sems, fr_sems, hd_sems, sq_sems) = refs
    p = Place(z_size, y_size, 2)
    n, me, x = p.n, p.me, p.x
    length, width = stream0.shape
    hidden_width = hidden.shape[1]
    own_rows = code_out.shape[0]
    gate_at, out_at, down_at, qkv_at, gain_at = range(5)
    late = [qkv_at, gain_at]
    halved = [k for k in (down_at, gate_at, out_at) if split[k]]
    plain = [k for k in (down_at, gate_at, out_at) if not split[k]]
    for k in range(count - 1):
        pltpu.make_async_copy(weights[k], grads[k], own_sems.at[k]).start()
    p.greet(True)
    mate = (me, 1 - x)
    spread = Spread(p, whole, z_sems, y_sems, c_sems)
    send(head_one, head_two, hd_sems, (), mate)

    def weight(k):
        pltpu.make_async_copy(weights[k], grads[k], own_sems.at[k]).wait()

    def slot_of(dz, dy):
        return dz * y_size + dy

    order = [(dz, dy) for dz in range(z_size - 1, -1, -1) for dy in range(y_size - 1, -1, -1)]

    def block_of(k, f):
        rows = counts[k]
        return grads[k].at[pl.ds(pl.multiple_of(f * rows, rows), rows)]

    def to_twin(kinds):
        for dz, dy in order:
            slot = slot_of(dz, dy)
            for k in kinds:
                send(block_of(k, p.at(dz, dy, 1)), core_in[k].at[slot], rc_sems, (k, slot), p.twin())

    def half_of(k, ref, which):
        columns = sums[k].shape[1] // 2
        return ref.at[:, pl.ds(pl.multiple_of(which * columns, columns), columns)]

    def ref_of(k, ref, which):
        return half_of(k, ref, which) if split[k] else ref

    def twin_sums(kinds, dz):
        def body(dy, carry):
            slot = slot_of(dz, dy)
            for k in kinds:
                arrival(core_in[k].at[slot], rc_sems, (k, slot))
                own = block_of(k, p.at(dz, dy))[...].astype(F32)
                core_in[k][slot] = (own + core_in[k][slot].astype(F32)).astype(BF)
                if split[k]:
                    send(half_of(k, core_in[k].at[slot], 1 - x), x_in[k].at[slot], rx_sems, (k, slot), mate)
            return carry

        lax.fori_loop(0, y_size, body, 0)

    def y_slot(dz, dy):
        return dz * (y_size - 1) + dy - 1

    def send_y(kinds, dz):
        for dy in range(1, y_size):
            for k in kinds:
                source = ref_of(k, core_in[k].at[slot_of(dz, dy)], x)
                at = y_slot(dz, dy)
                send(source, y_in[k].at[at], ry_sems, (k, at), (p.at(0, dy), x))

    def take_x(dz):
        def body(dy, carry):
            slot = slot_of(dz, dy)
            for k in halved:
                arrival(x_in[k].at[slot], rx_sems, (k, slot))
                mine = half_of(k, core_in[k].at[slot], x)
                mine[...] = (mine[...].astype(F32) + x_in[k][slot].astype(F32)).astype(BF)
            return carry

        lax.fori_loop(0, y_size, body, 0)
        send_y(halved, dz)

    def take_y(kinds, dz):
        for k in kinds:
            mine = ref_of(k, core_in[k].at[slot_of(dz, 0)], x)
            total = mine[...].astype(F32)
            for dy in range(1, y_size):
                at = y_slot(dz, dy)
                arrival(y_in[k].at[at], ry_sems, (k, at))
                total = total + y_in[k][at].astype(F32)
            mine[...] = total.astype(BF)
            if dz:
                send(mine, z_in[k].at[dz - 1], rz_sems, (k, dz - 1), (p.at(dz, 0), x))

    def settle(kinds):
        for k in kinds:
            mine = ref_of(k, core_in[k].at[0], x)
            total = mine[...].astype(F32)
            for dz in range(1, z_size):
                arrival(z_in[k].at[dz - 1], rz_sems, (k, dz - 1))
                total = total + z_in[k][dz - 1].astype(F32)
            source = ref_of(k, trade[k].at[0], x)
            source[...] = total.astype(BF)
            target = source if split[k] else trade[k].at[1]
            send(source, target, tr_sems, (k,), mate)

    def collect(kinds):
        summed = jnp.zeros((1, 1), F32)
        for k in kinds:
            if split[k]:
                arrival(half_of(k, trade[k].at[0], 1 - x), tr_sems, (k,))
                total = trade[k][0].astype(F32)
            else:
                arrival(trade[k].at[1], tr_sems, (k,))
                total = trade[k][0].astype(F32) + trade[k][1].astype(F32)
            sums[k][...] = total
            summed = summed + square(total)
        return summed

    def square(value):
        return jnp.sum(jnp.sum(value * value, 0, keepdims=True), 1, keepdims=True)

    def norm_back(stream, row, grad_out):
        inverse = lax.rsqrt(jnp.mean(stream * stream, -1, keepdims=True) + NORM_EPS)
        weighted = grad_out * gains[row : row + 1, :]
        inner = jnp.mean(weighted * stream, -1, keepdims=True)
        grad = inverse * weighted - stream * (inverse * inverse * inverse) * inner
        return grad, jnp.sum(grad_out * stream * inverse, 0, keepdims=True)

    grad_stream2, gain_three = norm_back(stream2[...], 2, grad_normed3[...])
    grad_stream1[...] = grad_stream2
    grad_stream0[...] = grad_stream2.astype(BF)
    weight(gate_at)
    weight(down_at)
    step = 512
    for at in range(0, hidden_width, step):
        gate = product(normed2[...], grads[gate_at][at : at + step, :], BY_LANES)
        up = product(normed2[...], grads[gate_at][hidden_width + at : hidden_width + at + step, :], BY_LANES)
        back = jnp.dot(grad_stream0[...], grads[down_at][:, at : at + step], preferred_element_type=F32)
        sigma = 1.0 / (1.0 + jnp.exp(-gate))
        hidden[:, at : at + step] = (gate * sigma * up).astype(BF)
        grad_gated[:, at : at + step] = (back * up * sigma * (1.0 + gate * (1.0 - sigma))).astype(BF)
        grad_gated[:, hidden_width + at : hidden_width + at + step] = (back * gate * sigma).astype(BF)
    for at in range(0, hidden_width, step):
        grads[down_at][:, at : at + step] = product(
            grad_stream0[...], hidden[:, at : at + step], BY_ROWS
        ).astype(BF)
    to_twin([down_at])
    grad_normed2 = jnp.dot(grad_gated[...], grads[gate_at][...], preferred_element_type=F32)
    for at in range(0, 2 * hidden_width, step):
        grads[gate_at][at : at + step, :] = product(
            grad_gated[:, at : at + step], normed2[...], BY_ROWS
        ).astype(BF)
    to_twin([gate_at])
    grad_middle, gain_two = norm_back(stream1[...], 1, grad_normed2)
    grad_stream1[...] = grad_stream1[...] + grad_middle
    grad_stream0[...] = grad_stream1[...].astype(BF)
    weight(out_at)
    grad_attended[...] = jnp.dot(
        grad_stream0[...], grads[out_at][...], preferred_element_type=F32
    ).astype(BF)
    grads[out_at][...] = product(grad_stream0[...], attended[...], BY_ROWS).astype(BF)
    to_twin([out_at])

    lane = lax.broadcasted_iota(jnp.int32, (length, 128), 1)
    low = lax.rem(lane, HEAD_DIM) < HEAD_DIM // 2
    scale = HEAD_DIM ** (-0.5)

    def turn_back(grad):
        scaled = grad * turn[1]
        other = jnp.where(
            low, pltpu.roll(scaled, 128 - HEAD_DIM // 2, 1), -pltpu.roll(scaled, HEAD_DIM // 2, 1)
        )
        return grad * turn[0] + other

    def pair(j, carry):
        base = pl.multiple_of(j * 128, 128)
        at = pl.ds(base, 128)
        q, k, v, grad = queries[:, at], keys[:, at], values[:, at], grad_attended[:, at]
        q_two, grad_two = both_heads(q), both_heads(grad)
        probs = attention_probs(q_two, k)
        grad_probs = product(grad_two, v, BY_LANES)
        inner = jnp.sum(probs * grad_probs, -1, keepdims=True)
        grad_scores = (probs * (grad_probs - inner)).astype(BF)
        grad_v = product(probs.astype(BF), grad_two, BY_ROWS)
        grad_q = one_row(jnp.dot(grad_scores, k, preferred_element_type=F32))
        grad_k = product(grad_scores, q_two, BY_ROWS)
        grad_mixed[:, at] = turn_back(grad_q * scale).astype(BF)
        grad_mixed[:, pl.ds(width + base, 128)] = turn_back(grad_k * scale).astype(BF)
        grad_mixed[:, pl.ds(2 * width + base, 128)] = grad_v.astype(BF)
        return carry

    pairs = width // 128
    for s in range(z_size):
        dz = z_size - 1 - s
        twin_sums(halved, dz)
        twin_sums(plain, dz)
        send_y(plain, dz)
        lax.fori_loop(s * pairs // z_size, (s + 1) * pairs // z_size, pair, 0)

    weight(qkv_at)
    grad_normed1 = jnp.dot(grad_mixed[...], grads[qkv_at][...], preferred_element_type=F32)
    grad_first, gain_one = norm_back(stream0[...], 0, grad_normed1)
    grad_stream0[...] = (grad_stream1[...] + grad_first).astype(BF)
    spread.start(grad_stream0)
    whole[me] = grad_stream0[...]
    step = 3 * width // 6
    for at in range(0, 3 * width, step):
        grads[qkv_at][at : at + step, :] = product(
            grad_mixed[:, at : at + step], normed1[...], BY_ROWS
        ).astype(BF)
    row = lax.broadcasted_iota(jnp.int32, (16, width), 0)
    all_gains = jnp.where(row == 2, gain_three, 0.0)
    all_gains = jnp.where(row == 0, gain_one, jnp.where(row == 1, gain_two, all_gains))

    def gain_block(f, carry):
        turned = pltpu.roll(all_gains, lax.rem(width - f * own_width, width), 1)[:, :128]
        own = lax.broadcasted_iota(jnp.int32, turned.shape, 1) < own_width
        block_of(gain_at, f)[...] = jnp.where(own, turned, 0.0).astype(BF)
        return carry

    lax.fori_loop(0, n, gain_block, 0)
    to_twin(late)
    for s in range(1, z_size):
        spread.step_z(s)
        spread.step_y(s - 1)
        twin_sums(late, z_size - s)
        take_y(plain, z_size - s)
    twin_sums(late, 0)
    spread.step_y(z_size - 1)
    for dz in range(z_size - 1, -1, -1):
        take_x(dz)
        send_y(late, dz)
    take_y(plain, 0)
    for z in range(z_size):
        spread.take_twin(z)

    rows_out[x] = whole[:, 0:16, :].astype(F32)[:, 0, :]
    send(rows_out.at[x], rows_out.at[x], fr_sems, (), mate)

    blocks = 4
    rows = own_rows // blocks
    iota = lax.broadcasted_iota(jnp.int32, (rows, length // 2), 0) + me * own_rows

    def code_block(r, carry):
        base = (iota + r * rows).astype(F32)

        def add(image, total):
            ids = facts[x, image]
            hot = jnp.concatenate(
                [jnp.where(base == ids[h : h + 1, :], 1.0, 0.0) for h in range(2)], 1
            ).astype(BF)
            return total + jnp.dot(hot, whole[image], preferred_element_type=F32)

        total = lax.fori_loop(0, n, add, jnp.zeros((rows, width), F32), unroll=4)
        at = pl.ds(pl.multiple_of(r * rows, rows), rows)
        code_out[at] = total.astype(BF)
        send(code_out.at[at], code_in.at[at], co_sems, (r,), mate)
        return carry

    for r in range(z_size):
        lax.fori_loop(r * blocks // z_size, (r + 1) * blocks // z_size, code_block, 0)
        take_y(halved, z_size - 1 - r)
        take_y(late, z_size - 1 - r)
    settle(plain + halved)

    arrival(head_two, hd_sems, ())
    total_squares = square(head_one[...].astype(F32) + head_two[...].astype(F32))

    arrival(rows_out.at[1 - x], fr_sems, ())
    firsts = rows_out[...].reshape(2 * n, width)
    shift = lax.rem(width - me * own_width, width)
    firsts = pltpu.roll(firsts, shift, 1)[:, :128]
    firsts = jnp.where(lax.broadcasted_iota(jnp.int32, firsts.shape, 1) < own_width, firsts, 0.0)
    classes = facts[:, :, 4, :].reshape(2 * n, 128)[:, 0:1]
    class_iota = lax.broadcasted_iota(jnp.int32, (2 * n, class_sum.shape[1]), 1).astype(F32)
    hot = jnp.where(class_iota == classes, 1.0, 0.0).astype(BF)
    class_grad = product(firsts.astype(BF), hot, BY_ROWS)
    class_sum[...] = class_grad
    total_squares = total_squares + square(class_grad)

    total_squares = total_squares + collect(plain + halved)
    settle(late)
    for r in range(blocks):
        at = pl.ds(r * rows, rows)
        arrival(code_in.at[at], co_sems, (r,))
        total_squares = total_squares + square(code_out[at].astype(F32) + code_in[at].astype(F32))
    total_squares = total_squares + collect(late)

    given[me] = jnp.broadcast_to(total_squares, (8, 128))
    for k in range(1, n):
        send(given.at[me], given.at[me], sq_sems, (k,), (lax.rem(me + k, n), x))

    spread.finish()
    departure(head_one, hd_sems, ())
    departure(rows_out.at[x], fr_sems, ())
    for r in range(blocks):
        departure(code_out.at[pl.ds(r * rows, rows)], co_sems, (r,))
    for k in range(count):
        departure(ref_of(k, trade[k].at[0], x), tr_sems, (k,))
        for dz in range(z_size):
            if dz:
                departure(z_in[k].at[dz - 1], rz_sems, (k, dz - 1))
            for dy in range(y_size):
                slot = slot_of(dz, dy)
                departure(core_in[k].at[slot], rc_sems, (k, slot))
                if split[k]:
                    departure(x_in[k].at[slot], rx_sems, (k, slot))
                if dy:
                    departure(y_in[k].at[y_slot(dz, dy)], ry_sems, (k, y_slot(dz, dy)))
    for k in range(1, n):
        arrival(given.at[0], sq_sems, (k,))
    squares[...] = jnp.sum(given[...], 0)
    for k in range(1, n):
        departure(given.at[0], sq_sems, (k,))


def tail_phase(layer, facts, head_one, weights, split, class_rows, own_width, n):
    z_size, y_size = geometry(n)
    length, width = layer[0].shape
    hidden_width = weights[2].shape[1]
    own_rows = head_one.shape[0]
    shapes = [(w.shape[0] // n, w.shape[1]) for w in weights] + [(16, 128)]
    count, spots = len(shapes), z_size * y_size
    halves = [(s[0], s[1] // 2) if h else s for s, h in zip(shapes, split)]
    dma = pltpu.SemaphoreType.DMA
    buffers = [((n * s[0], s[1]), BF) for s in shapes]
    buffers += [((spots,) + s, BF) for s in shapes]
    buffers += [((spots,) + s if h else (16, 128), BF) for s, h in zip(halves, split)]
    buffers += [((z_size * (y_size - 1),) + s, BF) for s in halves]
    buffers += [((z_size - 1,) + s, BF) for s in halves]
    buffers += [((2,) + s, BF) for s in shapes]
    buffers += [((n, length, width), BF), ((2, n, width), F32), ((n, 8, 128), F32),
                ((length, 3 * width), BF), ((length, 2 * hidden_width), BF), ((length, hidden_width), BF),
                ((length, width), F32), ((length, width), BF), ((length, width), BF)]
    sems = [
        dma((2, 2, z_size)), dma((2, z_size, y_size)), dma((2, z_size, y_size)),
        dma((count,)), dma((2, count, spots)), dma((2, count, spots)), dma((2, count, spots)),
        dma((2, count, z_size)), dma((2, count)), dma((2, 4)), dma((2,)), dma((2,)), dma((2, n)),
    ]
    vmem, hbm = pl.BlockSpec(memory_space=pltpu.VMEM), pl.BlockSpec(memory_space=pl.ANY)
    counts = tuple(s[0] for s in shapes)
    half = jax.ShapeDtypeStruct((own_rows, width), BF)
    outs = pl.pallas_call(
        functools.partial(tail_kernel, z_size, y_size, own_width, split, counts),
        out_shape=[jax.ShapeDtypeStruct(s, F32) for s in shapes]
        + [half, half, jax.ShapeDtypeStruct((128, class_rows), F32), half,
           jax.ShapeDtypeStruct((8, 128), F32)],
        in_specs=[vmem] * (len(layer) + 2) + [hbm] * len(weights),
        out_specs=[vmem] * (count + 5),
        scratch_shapes=[pltpu.VMEM(shape, kind) for shape, kind in buffers] + sems,
        compiler_params=pltpu.CompilerParams(
            collective_id=2, has_side_effects=True, vmem_limit_bytes=60 * 2**20
        ),
        name="tail",
    )(*layer, facts, head_one, *weights)
    code_one, code_two, class_sum, head_two, squares = outs[count:]
    return outs[:count], (code_one, code_two), class_sum, head_two, squares[0, 0]


BY_ROWS = (((0,), (0,)), ((), ()))
BY_LANES = (((1,), (1,)), ((), ()))


def product(left, right, dims):
    return lax.dot_general(left, right, dims, preferred_element_type=F32)


def both_heads(pair):
    lane = lax.broadcasted_iota(jnp.int32, pair.shape, 1)
    zero = jnp.zeros_like(pair)
    first, second = jnp.where(lane < HEAD_DIM, pair, zero), jnp.where(lane < HEAD_DIM, zero, pair)
    return jnp.concatenate([first, second], 0)


def one_row(two):
    length = two.shape[0] // 2
    lane = lax.broadcasted_iota(jnp.int32, (length, 128), 1)
    return jnp.where(lane < HEAD_DIM, two[:length], two[length:])


def attention_probs(q_two, k):
    length = k.shape[0]
    query = lax.rem(lax.broadcasted_iota(jnp.int32, (2 * length, length), 0), length)
    causal = query >= lax.broadcasted_iota(jnp.int32, (2 * length, length), 1)
    scores = jnp.where(causal, product(q_two, k, BY_LANES) * HEAD_DIM ** (-0.5), -1e30)
    expo = jnp.exp(scores - jnp.max(scores, -1, keepdims=True))
    return expo / jnp.sum(expo, -1, keepdims=True)


def layer_kernel(stream0, gains, turn, qkv_hbm, out_hbm, gate_hbm, down_hbm,
                 normed1, queries, keys, values, attended, stream1, normed2, stream2, normed3,
                 hidden, qkv_w, out_w, gate_w, down_w, sems):
    moves = [
        pltpu.make_async_copy(src, dst, sems.at[i])
        for i, (src, dst) in enumerate(
            ((qkv_hbm, qkv_w), (out_hbm, out_w), (gate_hbm, gate_w), (down_hbm, down_w))
        )
    ]
    for move in moves:
        move.start()
    length, width = stream0.shape
    hidden_width = hidden.shape[1]

    def rms(stream, row):
        inverse = lax.rsqrt(jnp.mean(stream * stream, -1, keepdims=True) + NORM_EPS)
        return (stream * inverse * gains[row : row + 1, :]).astype(BF)

    normed1[...] = rms(stream0[...], 0)
    lane = lax.broadcasted_iota(jnp.int32, (length, 128), 1)
    low = lax.rem(lane, HEAD_DIM) < HEAD_DIM // 2

    def turned(part):
        other = jnp.where(
            low, -pltpu.roll(part, 128 - HEAD_DIM // 2, 1), pltpu.roll(part, HEAD_DIM // 2, 1)
        )
        return (part * turn[0] + other * turn[1]).astype(BF)

    moves[0].wait()

    def pair(j, carry):
        base = pl.multiple_of(j * 128, 128)
        at = pl.ds(base, 128)
        x = normed1[...]
        q = turned(product(x, qkv_w[at, :], BY_LANES))
        k = turned(product(x, qkv_w[pl.ds(width + base, 128), :], BY_LANES))
        v = product(x, qkv_w[pl.ds(2 * width + base, 128), :], BY_LANES).astype(BF)
        queries[:, at], keys[:, at], values[:, at] = q, k, v
        probs = attention_probs(both_heads(q), k).astype(BF)
        attended[:, at] = one_row(jnp.dot(probs, v, preferred_element_type=F32)).astype(BF)
        return carry

    lax.fori_loop(0, width // 128, pair, 0, unroll=2)
    moves[1].wait()
    stream1[...] = stream0[...] + product(attended[...], out_w[...], BY_LANES)
    normed2[...] = rms(stream1[...], 1)
    moves[2].wait()
    step = 512
    for at in range(0, hidden_width, step):
        gate = product(normed2[...], gate_w[at : at + step, :], BY_LANES)
        up = product(normed2[...], gate_w[hidden_width + at : hidden_width + at + step, :], BY_LANES)
        hidden[:, at : at + step] = (gate * (1.0 / (1.0 + jnp.exp(-gate))) * up).astype(BF)
    moves[3].wait()
    stream2[...] = stream1[...] + product(hidden[...], down_w[...], BY_LANES)
    normed3[...] = rms(stream2[...], 2)


def layer_forward(stream0, gains, turn, qkv_w, out_w, gate_w, down_w):
    length, width = stream0.shape
    hidden_width = down_w.shape[1]
    vmem, hbm = pl.BlockSpec(memory_space=pltpu.VMEM), pl.BlockSpec(memory_space=pl.ANY)
    half, full = jax.ShapeDtypeStruct((length, width), BF), jax.ShapeDtypeStruct((length, width), F32)
    outs = [half] * 5 + [full, half, full, half]
    return pl.pallas_call(
        layer_kernel,
        out_shape=outs,
        in_specs=[vmem] * 3 + [hbm] * 4,
        out_specs=[vmem] * len(outs),
        scratch_shapes=[pltpu.VMEM((length, hidden_width), BF)]
        + [pltpu.VMEM(w.shape, BF) for w in (qkv_w, out_w, gate_w, down_w)]
        + [pltpu.SemaphoreType.DMA((4,))],
        compiler_params=pltpu.CompilerParams(vmem_limit_bytes=56 * 2**20),
        name="layer",
    )(stream0, gains, turn, qkv_w, out_w, gate_w, down_w)


def adam_update(weight, first, second, grad, rate, decay):
    first_new = BETA_ONE * first + (1.0 - BETA_ONE) * grad
    second_new = BETA_TWO * second + (1.0 - BETA_TWO) * grad * grad
    first_hat = first_new / (1.0 - BETA_ONE**STEP)
    second_hat = second_new / (1.0 - BETA_TWO**STEP)
    weight_new = weight - rate * (first_hat / (jnp.sqrt(second_hat) + ADAM_EPS) + decay * weight)
    return (weight_new, first_new, second_new)


def dot(subscripts, left, right):
    return jnp.einsum(subscripts, left, right, preferred_element_type=F32)


def local(*args):
    class_ids, null_mask, code_ids, lengths = args[:4]
    masters, firsts, seconds = args[4::3], args[5::3], args[6::3]
    code_table, class_table, qkv_weight, out_weight, gate_up, down_weight, head_weight, gains = (
        masters
    )
    rates = (0.5, 0.5, 0.05, 0.05, 0.05, 0.05, 0.05, 0.5)
    decays = (0.1, 0.1, 0.1, 0.1, 0.1, 0.1, 0.1, 0.0)
    n = lax.axis_size("fsdp")
    me = lax.axis_index("fsdp")
    batch, length = code_ids.shape
    width = qkv_weight.shape[1]
    hidden_width = down_weight.shape[1]
    table_rows, own_width = class_table.shape
    own_rows = code_table.shape[0]
    heads = width // HEAD_DIM
    rows = (qkv_weight.shape[0], gate_up.shape[0], out_weight.shape[0], down_weight.shape[0])

    classes = jnp.where(null_mask == 1, table_rows - 1, class_ids)
    previous = jnp.concatenate([jnp.full((1, 1), -1, code_ids.dtype), code_ids[:, :-1]], 1)
    pair = jnp.stack([classes[0], lengths[0]])[None].astype(F32)
    own_gains = gains.astype(BF).astype(F32)
    facts = jnp.concatenate(
        [
            previous.astype(F32).reshape(2, -1),
            code_ids.astype(F32).reshape(2, -1),
            jnp.pad(pair, ((0, 0), (0, length // 2 - 2))),
            jnp.pad(own_gains, ((0, 0), (0, length // 2 - own_width))),
        ],
        0,
    )
    class_b = jnp.pad(class_table.T.astype(BF), ((0, 128 - own_width), (0, -table_rows % 128)))
    reps = lax.axis_size("rep")
    wholes, stream0, facts = front(
        facts,
        code_table,
        class_b,
        [gate_up, qkv_weight, out_weight, down_weight],
        own_width,
        length,
        reps,
        n,
    )
    gate_w, qkv_w, out_w, down_w = (w.reshape(-1, w.shape[-1]) for w in wholes)
    stream0 = stream0[None]
    images = n * batch
    tokens = images * length
    every_fact, facts = facts, facts[lax.axis_index("rep")]
    gains32 = facts[:, 5:8, :own_width].transpose(1, 0, 2).reshape(3, width)
    all_codes = facts[:, 2:4].reshape(images, length).astype(jnp.int32)
    previous = facts[:, 0:2].reshape(tokens).astype(jnp.int32)
    all_classes = facts[:, 4, 0].astype(jnp.int32)
    all_lengths = facts[:, 4, 1].astype(jnp.int32)
    all_counted = (jnp.arange(length)[None, :] < all_lengths[:, None]).astype(F32)
    own_ids = jnp.arange(own_rows) + me * own_rows
    lookup = (previous[:, None] == own_ids[None, :]).astype(BF)

    cosine, sine = rotary_tables(length, HEAD_DIM)
    turn = jnp.stack([jnp.concatenate([t, t], -1) for t in (cosine, sine)])
    split4 = (batch, length, heads, HEAD_DIM)
    gain_rows = jnp.pad(gains32, ((0, 5), (0, 0)))
    kept = layer_forward(
        stream0[0], gain_rows, turn, qkv_w, out_w, gate_w, down_w
    )
    (normed1, queries, keys_rot, values, attended, stream1, normed2, stream2, normed3) = (
        t[None] for t in kept
    )
    head_b = head_weight.astype(BF)
    in_kernel = reps == 2 and size_of(head_scratch(n, length, width, own_rows, reps)[0]) < 52 * 2**20
    if in_kernel:
        grad_normed3, grad_head, totals = head_phase(normed3[0], head_weight, every_fact, reps, n)
        loss_sum, token_count = totals[0, 0], totals[1, 0]
    else:
        token_count = lax.psum(jnp.sum(all_counted), "rep")
        normed3_all = lax.all_gather(normed3, "fsdp", axis=0, tiled=True).reshape(tokens, width)
        logits = dot("td,vd->tv", normed3_all, head_b)
        onehot = all_codes.reshape(tokens)[:, None] == own_ids[None, :]
        local_top = jnp.max(logits, -1)
        local_sum = jnp.sum(jnp.exp(logits - local_top[:, None]), -1)
        local_pick = jnp.sum(jnp.where(onehot, logits, 0.0), -1)
        stats = lax.all_gather(jnp.stack([local_top, local_sum, local_pick]), "fsdp", axis=0)
        ltop = jnp.max(stats[:, 0], 0)
        lse = jnp.log(jnp.sum(stats[:, 1] * jnp.exp(stats[:, 0] - ltop[None]), 0)) + ltop
        picked = jnp.sum(stats[:, 2], 0)
        loss_sum = lax.psum(jnp.sum(jnp.where(all_counted.reshape(tokens) > 0, lse - picked, 0.0)), "rep")
        weight_t = all_counted.reshape(tokens) * (1.0 / token_count)
        soft = jnp.exp(logits - lse[:, None])
        grad_logits = ((soft - onehot.astype(F32)) * weight_t[:, None]).astype(BF)
        grad_normed3 = dot("tv,vd->td", grad_logits, head_b).astype(BF).reshape(images, length, width)
        grad_normed3 = lax.psum_scatter(grad_normed3, "fsdp", scatter_dimension=0, tiled=True)
        grad_normed3 = grad_normed3.astype(F32)
        grad_head = dot("tv,td->vd", grad_logits, normed3_all)

    if in_kernel:
        kinds = (queries, keys_rot, values, attended, normed1, normed2, stream0, stream1, stream2)
        layer = [t[0] for t in kinds] + [grad_normed3, turn, gain_rows]
        sums, codes, grad_classes, head_two, squares = tail_phase(
            layer,
            every_fact,
            grad_head,
            [gate_w, out_w, down_w, qkv_w],
            (True, True, False, False, False),
            table_rows + -table_rows % 128,
            own_width,
            n,
        )
        grad_codes, grad_head = (
            one.astype(F32) + two.astype(F32) for one, two in (codes, (grad_head, head_two))
        )
        grad_gate_up, grad_out, grad_down, grad_qkv, gain_part = sums
        grad_gains = gain_part[:3, :own_width]
        grad_classes = grad_classes[:own_width, :table_rows].T
    else:
        gated = dot("btd,fd->btf", normed2, gate_w)
        gate_part = gated[..., :hidden_width]
        up_part = gated[..., hidden_width:]
        hidden = (jax.nn.silu(gate_part) * up_part).astype(BF)
        inverse1, inverse2, inverse3 = (
            lax.rsqrt(jnp.mean(t * t, -1, keepdims=True) + NORM_EPS) for t in (stream0, stream1, stream2)
        )
        grad_stream2, gain_three = norm_backward(stream2, inverse3, gains32[2], grad_normed3)
        grad_branch = grad_stream2.astype(BF)
        grad_down = dot("btd,btf->df", grad_branch, hidden)
        grad_hidden = dot("btd,df->btf", grad_branch, down_w)
        sigma = jax.nn.sigmoid(gate_part)
        grad_gate = grad_hidden * up_part * sigma * (1.0 + gate_part * (1.0 - sigma))
        grad_up = grad_hidden * gate_part * sigma
        grad_gated = jnp.concatenate([grad_gate, grad_up], -1).astype(BF)
        grad_gate_up = dot("btf,btd->fd", grad_gated, normed2)
        grad_normed2 = dot("btf,fd->btd", grad_gated, gate_w)
        grad_middle, gain_two = norm_backward(stream1, inverse2, gains32[1], grad_normed2)
        grad_stream1 = grad_stream2 + grad_middle
        grad_attn = grad_stream1.astype(BF)
        grad_out = dot("bte,btd->ed", grad_attn, attended)
        grad_attended = dot("bte,ed->btd", grad_attn, out_w).astype(BF)
        queries, keys_rot, values, grad_attended = (
            t.reshape(split4) for t in (queries, keys_rot, values, grad_attended)
        )
        probs32 = jax.nn.softmax(attention_scores(queries, keys_rot), -1)
        probs = probs32.astype(BF)
        grad_probs = dot("bqhd,bkhd->bhqk", grad_attended, values)
        grad_values = dot("bhqk,bqhd->bkhd", probs, grad_attended)
        grad_scores = probs32 * (grad_probs - jnp.sum(probs32 * grad_probs, -1, keepdims=True))
        grad_scores = grad_scores.astype(BF)
        scale = HEAD_DIM ** (-0.5)
        grad_queries = dot("bhqk,bkhd->bqhd", grad_scores, keys_rot) * scale
        grad_keys = dot("bhqk,bqhd->bkhd", grad_scores, queries) * scale
        grad_mixed = jnp.concatenate(
            [
                rotate_back(grad_queries, cosine, sine).reshape(batch, length, width),
                rotate_back(grad_keys, cosine, sine).reshape(batch, length, width),
                grad_values.reshape(batch, length, width),
            ],
            -1,
        ).astype(BF)
        grad_qkv = dot("bte,btd->ed", grad_mixed, normed1)
        grad_normed1 = dot("bte,ed->btd", grad_mixed, qkv_w)
        grad_first, gain_one = norm_backward(stream0, inverse1, gains32[0], grad_normed1)
        grad_stream0 = grad_stream1 + grad_first

        grad_gains = jnp.stack([gain_one, gain_two, gain_three])
        blocks = [
            g.astype(BF).reshape(n, -1, g.shape[-1]) for g in (grad_qkv, grad_gate_up, grad_out, grad_down)
        ]
        layer_part = lax.psum_scatter(pack_rows(*blocks), "fsdp", scatter_dimension=0, tiled=False)
        rows_all = lax.all_gather(grad_stream0.astype(BF), "fsdp", axis=0, tiled=True)
        grad_codes = dot("tv,td->vd", lookup, rows_all.reshape(tokens, width))
        class_part = lax.dynamic_slice(rows_all[:, 0], (0, me * own_width), (images, own_width))
        class_spot = (all_classes[:, None] == jnp.arange(table_rows)[None, :]).astype(BF)
        grad_classes = dot("iv,id->vd", class_spot, class_part)
        summed = lax.psum(
            (grad_codes.astype(BF), grad_head.astype(BF), layer_part, grad_classes), "rep"
        )
        grad_codes, grad_head, layer_part, grad_classes = (s.astype(F32) for s in summed)
        grad_gains = lax.psum(grad_gains, ("fsdp", "rep"))
        grad_gains = lax.dynamic_slice(grad_gains, (0, me * own_width), (3, own_width))
        grad_qkv, grad_gate_up, grad_out, grad_down = unpack_rows(layer_part, rows, hidden_width)
    reduced = (
        grad_codes, grad_classes, grad_qkv, grad_out, grad_gate_up, grad_down, grad_head, grad_gains
    )
    if not in_kernel:
        squares = lax.psum(sum(jnp.sum(piece * piece) for piece in reduced), "fsdp")
    grad_norm = jnp.sqrt(squares)
    factor = jnp.minimum(1.0, 1.0 / CLIP_INV / (grad_norm + 1e-06))
    results = [loss_sum, token_count, grad_norm]
    for index in range(8):
        results.extend(
            adam_update(
                masters[index],
                firsts[index],
                seconds[index],
                reduced[index] * factor,
                rates[index],
                decays[index],
            )
        )
    return tuple(results)


def solution(mesh):
    split = P(("fsdp", "rep"))
    by_row, by_column = P("fsdp", None), P(None, "fsdp")
    weights = (by_row,) * 3 + (by_column,) * 3 + (by_row,) * 15 + (by_column,) * 3
    return jax.shard_map(
        local,
        mesh=mesh,
        in_specs=(split, split, P(("fsdp", "rep"), None), split) + weights,
        out_specs=(P(), P(), P()) + weights,
        check_vma=False,
    )
```
